32 devices in a mesh: gx: 4 (over z), gy: 8 (over y, x, core).
Axes of the slice: x: 2, y: 2, z: 4, core: 2. Of those that a mesh axis runs over, the one named last changes fastest.
Arguments:
- leaf_up: float32 [96, 128, 456], P('gx', 'gy'), may hold values from -6 to 6
- parent_in: float32 [48, 64, 456], P('gx', 'gy'), may hold values from -6 to 6
- leaf_lists: int32 [96, 128, 40], P('gx', 'gy'), may hold values from 0 to 1, as said below
- parent_lists: int32 [48, 64, 40], P('gx', 'gy'), may hold values from 0 to 1, as said below
- up_transfer: float32 [4, 456, 456], replicated, may hold values from -0.125 to 0.125
- down_transfer: float32 [4, 456, 456], replicated, may hold values from -0.25 to 0.25
- check_inverse: float32 [456, 456], replicated, may hold values from -0.25 to 0.25
Outputs:
- leaf_down: float32 [96, 128, 456], P('gx', 'gy')
- parent_up: float32 [48, 64, 456], P('gx', 'gy')
The draws below stay inside these ranges and needn't reach their ends.
Inputs may be any that keep to these rules, and one draw needn't show every extreme that they name: `leaf_lists`: A flag is 1 only where the box at that offset lies in the grid, its parent touches or equals the box's parent, and it holds surface points. `parent_lists`: A flag is 1 only where the parent at that offset lies in the grid, its parent touches or equals the box's parent, and it holds surface points.
All inputs are finite; a program needn't handle non-finite values.
Results may differ from the reference program's by a relative error of at most 0.0001.
Values sent between devices are 32-bit elements; how exact they have to be, the bound alone decides.
No kernel may reach another device: no remote copies, remote signals or barrier semaphores. Data moves between devices by JAX's collectives and lax.ppermute only.
A program may use at most 64 MiB of HBM per device.

```python
import math
import jax
import jax.numpy as jnp
import numpy as np
from jax import lax

ORDER = 6
DENS = 456
NX = 96
NY = 128
PX = 48
PY = 64


def offset_table_drawn():
    chosen = [(a, b) for a in range(-3, 4) for b in range(-3, 4) if max(abs(a), abs(b)) >= 2]
    return np.array(chosen, dtype=np.int32)


def occupancy(key):
    drawn = jax.random.randint(key, (NX, NY), 0, 4)
    return (drawn > 0).astype(jnp.int32)


def list_mask(occupied, row_count, col_count):
    row_place = jnp.arange(row_count, dtype=jnp.int32)[:, None]
    col_place = jnp.arange(col_count, dtype=jnp.int32)[None, :]
    columns = []
    for offset_pair in offset_table_drawn():
        source_row = row_place + int(offset_pair[0])
        source_col = col_place + int(offset_pair[1])
        inside = (source_row >= 0) & (source_row < row_count) & (source_col >= 0) & (source_col < col_count)
        nearby = (jnp.abs(source_row // 2 - row_place // 2) <= 1) & (jnp.abs(source_col // 2 - col_place // 2) <= 1)
        holder = occupied[jnp.clip(source_row, 0, row_count - 1), jnp.clip(source_col, 0, col_count - 1)]
        columns.append(jnp.where(inside & nearby, holder, 0))
    return jnp.stack(columns, axis=2).astype(jnp.int32)


def draw_leaf_lists(key, part):
    occupied = occupancy(key)
    return list_mask(occupied, NX, NY)


def draw_parent_lists(key, part):
    occupied = occupancy(key)
    parent_held = occupied.reshape(PX, 2, PY, 2).max(axis=(1, 3))
    return list_mask(parent_held, PX, PY)


def block_scale(stream_key, shape, pieces, smallest, high):
    gain = 1.0
    for dim, blocks in pieces:
        steps = jax.random.uniform(jax.random.fold_in(jax.random.fold_in(stream_key, 6), dim), (blocks,), jnp.float32, smallest / len(pieces), high / len(pieces))
        gain = gain * jnp.repeat(jnp.exp(steps), shape[dim] // blocks).reshape((-1,) + (1,) * (len(shape) - 1 - dim))
    return gain


def centred(rng, dims, scale, bound, shards=(), kind=jnp.bfloat16):
    values = jax.random.normal(rng, dims, jnp.float32) * scale
    if len(shards) > 0:
        values = block_scale(rng, dims, shards, -0.22, 0.18) * values
    return jnp.clip(values, min=-bound, max=bound).astype(kind)


def setup_inputs(seed: int = 0) -> dict:
    seeds = jax.random.split(jax.random.key(seed), 8)
    return {
        "leaf_up": centred(seeds[0], (NX, NY, DENS), 1.0, 6.0, ((0, 4), (1, 8)), jnp.float32),
        "parent_in": centred(seeds[1], (PX, PY, DENS), 1.0, 6.0, ((0, 4), (1, 8)), jnp.float32),
        "leaf_lists": draw_leaf_lists(jax.random.fold_in(seeds[7], 71), 0),
        "parent_lists": draw_parent_lists(jax.random.fold_in(seeds[7], 71), 0),
        "up_transfer": centred(seeds[4], (4, DENS, DENS), (4 * DENS) ** -0.5, 0.125, (), jnp.float32),
        "down_transfer": centred(seeds[5], (4, DENS, DENS), DENS ** -0.5, 0.25, (), jnp.float32),
        "check_inverse": centred(seeds[6], (DENS, DENS), DENS ** -0.5, 0.25, (), jnp.float32),
    }


stokes_scale = 1.0 / (8.0 * math.pi)

def offset_table():
    chosen = [(a, b) for a in range(-3, 4) for b in range(-3, 4) if max(abs(a), abs(b)) >= 2]
    return np.array(chosen, dtype=np.int32)

def surface_points():
    grid_line = np.linspace(-1.0, 1.0, ORDER)
    points = []
    for i in range(ORDER):
        for j in range(ORDER):
            for k in range(ORDER):
                if min(i, j, k) == 0 or max(i, j, k) == ORDER - 1:
                    points.append((grid_line[i], grid_line[j], grid_line[k]))
    return np.array(points, dtype=np.float32).T

def kernel_matrix(shift_row, shift_col):
    surface = surface_points()
    spacing = 0.525 * (surface[:, :, None] - surface[:, None, :])
    components = (jnp.asarray(spacing[0]) - shift_row, jnp.asarray(spacing[1]) - shift_col, jnp.asarray(spacing[2]) + 0.0 * shift_row)
    squared = components[0] * components[0] + components[1] * components[1] + components[2] * components[2]
    inverse = 1.0 / jnp.sqrt(squared)
    cubed = inverse * inverse * inverse
    blocks = []
    for a in range(3):
        line_blocks = []
        for b in range(3):
            entry = components[a] * components[b] * cubed
            if a == b:
                entry = entry + inverse
            line_blocks.append(entry * stokes_scale)
        blocks.append(jnp.concatenate(line_blocks, axis=1))
    return jnp.concatenate(blocks, axis=0)

def interact(padded, lists, row_count, col_count):
    features = padded.shape[2]
    offsets = jnp.asarray(offset_table()).reshape(10, 4, 2)
    picks = jnp.arange(40, dtype=jnp.int32).reshape(10, 4)

    def advance(running, cluster):
        pairs_now, picks_now = cluster
        sources = []
        matrices = []
        for member in range(4):
            offset_pair = pairs_now[member]
            source = lax.dynamic_slice(padded, (offset_pair[0] + 3, offset_pair[1] + 3, jnp.int32(0)), (row_count, col_count, features))
            weight = lax.dynamic_slice_in_dim(lists, picks_now[member], 1, 2).astype(jnp.float32)
            sources.append((source * weight).reshape(row_count * col_count, features))
            matrices.append(kernel_matrix(offset_pair[0].astype(jnp.float32), offset_pair[1].astype(jnp.float32)))
        stacked_source = jnp.concatenate(sources, axis=1)
        stacked_matrix = jnp.concatenate(matrices, axis=1)
        product = lax.dot_general(stacked_source, stacked_matrix, (((1,), (1,)), ((), ())), precision=lax.Precision.HIGHEST, preferred_element_type=jnp.float32)
        return (running + product, None)
    start = jnp.zeros((row_count * col_count, features), jnp.float32)
    running, _ = lax.scan(advance, start, (offsets, picks))
    return running

def gather_children(leaf_values, up_transfer):
    row_count, col_count, features = leaf_values.shape
    grouped = leaf_values.reshape(row_count // 2, 2, col_count // 2, 2, features)
    operators = up_transfer.reshape(2, 2, features, features)
    return jnp.einsum('acbdk,cdjk->abj', grouped, operators, precision=lax.Precision.HIGHEST)

def spread_children(parent_values, down_transfer):
    row_count, col_count, features = parent_values.shape
    operators = down_transfer.reshape(2, 2, features, features)
    spread = jnp.einsum('abk,cdjk->acbdj', parent_values, operators, precision=lax.Precision.HIGHEST)
    return spread.reshape(2 * row_count, 2 * col_count, features)

def apply_inverse(check_values, check_inverse):
    return lax.dot_general(check_values, check_inverse, (((1,), (1,)), ((), ())), precision=lax.Precision.HIGHEST, preferred_element_type=jnp.float32)

def reference(leaf_up, parent_in, leaf_lists, parent_lists, up_transfer, down_transfer, check_inverse):
    features = leaf_up.shape[2]
    parent_up = gather_children(leaf_up, up_transfer)
    parent_padded = jnp.pad(parent_up, ((3, 3), (3, 3), (0, 0)))
    parent_check = interact(parent_padded, parent_lists, PX, PY)
    parent_local = parent_in + apply_inverse(parent_check, check_inverse).reshape(PX, PY, features)
    leaf_padded = jnp.pad(leaf_up, ((3, 3), (3, 3), (0, 0)))
    leaf_check = interact(leaf_padded, leaf_lists, NX, NY).reshape(NX, NY, features)
    leaf_check = leaf_check + spread_children(parent_local, down_transfer)
    leaf_down = apply_inverse(leaf_check.reshape(NX * NY, features), check_inverse).reshape(NX, NY, features)
    return (leaf_down, parent_up)
```

```python
import functools
import math

import jax
import jax.numpy as jnp
import ml_dtypes
import numpy as np
from jax import lax
from jax.experimental import pallas as pl
from jax.experimental.pallas import tpu as pltpu
from jax.sharding import PartitionSpec as P

ORDER = 6
HALO = 4
KEPT = 14
BF16, F32 = jnp.bfloat16, jnp.float32

INNER = [(a, b) for a in range(-2, 3) for b in range(-2, 3) if max(abs(a), abs(b)) == 2]
SIDES = (
    [(3, b) for b in range(-2, 3)],
    [(-3, b) for b in range(-2, 3)],
    [(a, 3) for a in range(-2, 3)],
    [(a, -3) for a in range(-2, 3)],
)
CORNERS = ([(3, 3)], [(3, -3)], [(-3, 3)], [(-3, -3)])
GROUPS = (INNER,) + SIDES + CORNERS


def offset_table():
    return [(a, b) for a in range(-3, 4) for b in range(-3, 4) if max(abs(a), abs(b)) >= 2]


def surface_points():
    grid = np.linspace(-1.0, 1.0, ORDER)
    keys = [
        (i, j, k)
        for i in range(ORDER)
        for j in range(ORDER)
        for k in range(ORDER)
        if min(i, j, k) == 0 or max(i, j, k) == ORDER - 1
    ]
    return keys, np.array([[grid[i] for i in key] for key in keys])


def translation(points, dx, dy):
    r = 0.525 * (points[:, None, :] - points[None, :, :]) - np.array([dx, dy, 0.0])
    dist = np.sqrt((r * r).sum(-1))
    n = len(points)
    out = np.zeros((3, n, 3, n))
    for a in range(3):
        for b in range(3):
            out[a, :, b, :] = (float(a == b) / dist + r[..., a] * r[..., b] / dist**3) / (8 * math.pi)
    return out.reshape(3 * n, 3 * n)


def split(x):
    high = x.astype(ml_dtypes.bfloat16)
    return high, (x - high.astype(np.float64)).astype(ml_dtypes.bfloat16)


@functools.lru_cache(maxsize=None)
def operators():
    keys, points = surface_points()
    n = len(keys)
    place = {key: i for i, key in enumerate(keys)}
    mirror = [place[(i, j, ORDER - 1 - k)] for i, j, k in keys]
    mats = {o: translation(points, *o) for o in offset_table()}
    half = 3 * n // 2
    rotation = np.zeros((3 * n, 512))
    back = np.zeros((512, 3 * n))
    tables = {}
    for s, sign in enumerate((1, -1)):
        pairs = np.zeros((3 * n, half))
        col = 0
        for a in range(3):
            flip = sign if a < 2 else -sign
            for i in range(n):
                if i < mirror[i]:
                    pairs[a * n + i, col] = 1.0
                    pairs[a * n + mirror[i], col] = flip
                    col += 1
        blocks = {o: 0.5 * pairs.T @ m @ pairs for o, m in mats.items()}
        gram = sum((1 + 0.05 * o[0] + 0.02 * o[1]) * b.T @ b for o, b in blocks.items())
        _, vecs = np.linalg.eigh(gram)
        vecs = vecs[:, ::-1]
        vecs = vecs * np.sign(vecs[np.abs(vecs).argmax(0), np.arange(half)])
        modes = pairs @ vecs / math.sqrt(2.0)
        rotation[:, 256 * s : 256 * s + half] = modes
        rotation[:, 256 * s + half : 256 * s + half + KEPT] = modes[:, :KEPT]
        rotation[:, 256 * s + half + KEPT : 256 * s + half + 2 * KEPT] = modes[:, :KEPT]
        back[256 * s : 256 * s + half] = pairs.T
        for o, m in mats.items():
            high, low = split((0.5 * pairs.T @ m @ modes).T)
            tile = np.zeros((256, 256), ml_dtypes.bfloat16)
            tile[:half, :half] = high
            tile[half : half + KEPT, :half] = high[:KEPT]
            tile[half + KEPT : half + 2 * KEPT, :half] = low[:KEPT]
            tables[s, o] = tile
    stacked = [tables[s, o] for group in GROUPS for s in range(2) for o in group]
    return (
        np.concatenate(split(rotation), axis=0).reshape(2, 3 * n, 512),
        back.astype(ml_dtypes.bfloat16),
        np.concatenate(stacked, axis=0),
    )


def dot(a, b):
    return lax.dot_general(a, b, (((1,), (0,)), ((), ())), preferred_element_type=F32)


def dot_t(a, b):
    return lax.dot_general(a, b, (((1,), (1,)), ((), ())), preferred_element_type=F32)


def parts(x):
    high = x.astype(BF16)
    return high, (x - high.astype(F32)).astype(BF16)


def times(x, weight):
    xh, xl = parts(x)
    wh, wl = weight
    return dot(xh, wh) + (dot(xl, wh) + dot(xh, wl))


def times_t(x, weight):
    xh, xl = parts(x)
    wh, wl = weight
    return dot_t(xh, wh) + (dot_t(xl, wh) + dot_t(xh, wl))


def step_kernel(
    own_ref, before_ref, after_ref, left_ref, right_ref, pin_ref, llist_ref, plist_ref,
    up_hbm, down_hbm, inv_hbm, rot_ref, back_ref, table_hbm,
    out_ref, pup_ref,
    ext, modes, pmodes, pext, lut, lhs, acc, spread, up_v, down_v, inv_v, table, sems,
):
    rows, cols, dens = own_ref.shape
    pr, pc = rows // 2, cols // 2
    boxes = pr * pc
    tiles = [(t, 128 * t, min(128, dens - 128 * t)) for t in range(4)]

    def strided(ref, row, at, count):
        return jnp.concatenate(
            [ref[t, row, pl.ds(at, count, stride=2), :] for t in range(4)], axis=1
        )

    copies = [
        pltpu.make_async_copy(src, dst, sems.at[i])
        for i, (src, dst) in enumerate(
            ((up_hbm, up_v), (table_hbm, table), (down_hbm, down_v), (inv_hbm, inv_v))
        )
    ]
    for c in copies:
        c.start()

    ext[...] = jnp.zeros_like(ext)
    for t, at, width in tiles:
        cut = slice(at, at + width)
        to = slice(0, width)
        ext[t, HALO : HALO + rows, 8 : 8 + cols, to] = own_ref[:, :, cut]
        ext[t, 0:HALO, 8 : 8 + cols, to] = before_ref[:, :, cut]
        ext[t, HALO + rows :, 8 : 8 + cols, to] = after_ref[:, :, cut]
        ext[t, :, 8 - HALO : 8, to] = left_ref[:, :, cut]
        ext[t, :, 8 + cols : 8 + cols + HALO, to] = right_ref[:, :, cut]

    lane = lax.broadcasted_iota(jnp.int32, (1, 512), 1) % 256
    half = dens // 2
    is_low = (lane >= half) & (lane < half + KEPT)
    rot = (rot_ref[0], rot_ref[1])

    def to_modes(x):
        y = times(x, rot)
        return jnp.where(is_low, y - y.astype(BF16).astype(F32), y)

    wide = cols + 16
    used = rows + 4
    chunk = used // 4
    for i in range(4):
        rng = slice(2 + i * chunk, 2 + (i + 1) * chunk)
        x = jnp.concatenate(
            [ext[t, rng, :, :].reshape(chunk * wide, 128) for t in range(4)], axis=1
        )
        y = to_modes(x[:, :dens])
        for t in range(4):
            modes[t, i * chunk : (i + 1) * chunk, :, :] = y[:, 128 * t : 128 * t + 128].reshape(
                chunk, wide, 128
            )

    copies[0].wait()
    hp = pr + 4
    wp = wide // 2
    parent = jnp.zeros((hp * wp, dens), F32)
    for c in range(2):
        for d in range(2):
            x = jnp.concatenate(
                [strided(ext, 2 * i + c, d, wp) for i in range(hp)], axis=0
            )
            parent = parent + times_t(x[:, :dens], parts(up_v[2 * c + d]))
    pext[...] = parent.reshape(hp, wp, dens)
    pup_ref[...] = pext[2 : 2 + pr, 4 : 4 + pc, :]
    pmodes[0] = jnp.zeros((wp, 512), F32)
    pmodes[hp + 1] = jnp.zeros((wp, 512), F32)
    pmodes[1 : hp + 1] = to_modes(parent).reshape(hp, wp, 512)

    def source(cs, ds, px, py):
        return ((cs * 2 + ds) * 3 + px + 1) * 3 + py + 1

    for cs in range(2):
        for ds in range(2):
            for px in (-1, 0, 1):
                for py in (-1, 0, 1):
                    x = jnp.concatenate(
                        [
                            strided(modes, 2 + 2 * (i + px) + cs, 8 + 2 * py + ds, pc)
                            for i in range(pr)
                        ],
                        axis=0,
                    )
                    lut[source(cs, ds, px, py)] = x.astype(BF16)

    offsets = offset_table()
    spread[0, :, :, 0 : len(offsets)] = llist_ref[...].astype(F32)
    flags = []
    for c in range(2):
        for d in range(2):
            flags.append(
                jnp.concatenate(
                    [spread[0, 2 * i + c, pl.ds(d, pc, stride=2), :] for i in range(pr)], axis=0
                )
            )
    pflags = plist_ref[...].reshape(boxes, len(offsets)).astype(F32)

    def masked(flag, o, x):
        m = jnp.broadcast_to(flag[:, o : o + 1], (boxes, 128)).astype(BF16)
        return [x[:, 128 * t : 128 * t + 128] * m for t in range(4)]

    copies[1].wait()
    acc[...] = jnp.zeros_like(acc)
    start = 0
    for group in GROUPS:
        dx, dy = group[0]
        depth = 256 * len(group)
        classes = [
            2 * c + d
            for c in range(2)
            for d in range(2)
            if len(group) == 16
            or all(-2 - c <= o[0] <= 3 - c and -2 - d <= o[1] <= 3 - d for o in group)
        ]
        for k, (dx, dy) in enumerate(group):
            o = offsets.index((dx, dy))
            for n, cls in enumerate(classes):
                px, cs = divmod(cls // 2 + dx, 2)
                py, ds = divmod(cls % 2 + dy, 2)
                pieces = masked(flags[cls], o, lut[source(cs, ds, px, py)])
                for t in range(4):
                    at = (t // 2) * depth + 256 * k + 128 * (t % 2)
                    lhs[boxes * n : boxes * (n + 1), at : at + 128] = pieces[t]
            x = pmodes[3 + dx : 3 + dx + pr, 4 + dy : 4 + dy + pc, :].reshape(boxes, 512).astype(BF16)
            pieces = masked(pflags, o, x)
            n = len(classes)
            for t in range(4):
                at = (t // 2) * depth + 256 * k + 128 * (t % 2)
                lhs[boxes * n : boxes * (n + 1), at : at + 128] = pieces[t]
        total = boxes * (len(classes) + 1)
        for s in range(2):
            r = dot(
                lhs[0:total, s * depth : (s + 1) * depth],
                table[start + s * depth : start + (s + 1) * depth, :],
            )
            for n, cls in enumerate(classes + [4]):
                acc[boxes * cls : boxes * (cls + 1), 256 * s : 256 * (s + 1)] += r[
                    boxes * n : boxes * (n + 1)
                ]
        start += 2 * depth

    def natural(x):
        xh, xl = parts(x)
        return dot(xh, back_ref[...]) + dot(xl, back_ref[...])

    copies[2].wait()
    copies[3].wait()
    inverse = parts(inv_v[...])
    local = pin_ref[...].reshape(boxes, dens) + times_t(
        natural(acc[4 * boxes : 5 * boxes]), inverse
    )
    for c in range(2):
        for d in range(2):
            cls = 2 * c + d
            check = natural(acc[boxes * cls : boxes * (cls + 1)])
            check = check + times_t(local, parts(down_v[cls]))
            result = times_t(check, inverse)
            for t, at, width in tiles:
                for i in range(pr):
                    spread[t, 2 * i + c, pl.ds(d, pc, stride=2), 0:width] = result[
                        pc * i : pc * (i + 1), at : at + width
                    ]
    for t, at, width in tiles:
        out_ref[:, :, at : at + width] = spread[t, :, :, 0:width]


def step(own, before, after, left, right, pin, llist, plist, up, down, inv):
    rows, cols, dens = own.shape
    pr, pc = rows // 2, cols // 2
    boxes = pr * pc
    rotation, back, table = operators()
    vmem = pl.BlockSpec(memory_space=pltpu.VMEM)
    hbm = pl.BlockSpec(memory_space=pl.ANY)
    wide = cols + 16
    return pl.pallas_call(
        step_kernel,
        out_shape=(
            jax.ShapeDtypeStruct((rows, cols, dens), F32),
            jax.ShapeDtypeStruct((pr, pc, dens), F32),
        ),
        in_specs=[vmem] * 8 + [hbm] * 3 + [vmem] * 2 + [hbm],
        out_specs=(vmem, vmem),
        scratch_shapes=[
            pltpu.VMEM((4, rows + 2 * HALO, wide, 128), F32),
            pltpu.VMEM((4, rows + 4, wide, 128), F32),
            pltpu.VMEM((pr + 6, wide // 2, 512), F32),
            pltpu.VMEM((pr + 4, wide // 2, dens), F32),
            pltpu.VMEM((36, boxes, 512), BF16),
            pltpu.VMEM((5 * boxes, 512 * len(INNER)), BF16),
            pltpu.VMEM((5 * boxes, 512), F32),
            pltpu.VMEM((4, rows, cols, 128), F32),
            pltpu.VMEM(up.shape, F32),
            pltpu.VMEM(down.shape, F32),
            pltpu.VMEM(inv.shape, F32),
            pltpu.VMEM(table.shape, BF16),
            pltpu.SemaphoreType.DMA((4,)),
        ],
        compiler_params=pltpu.CompilerParams(vmem_limit_bytes=58 * 1024 * 1024),
    )(
        own, before, after, left, right, pin, llist, plist, up, down, inv,
        jnp.asarray(rotation), jnp.asarray(back), jnp.asarray(table),
    )


def shifted(low, high, axis):
    peers = lax.axis_size(axis)
    up = [(i, i + 1) for i in range(peers - 1)]
    down = [(j, i) for i, j in up]
    return lax.ppermute(high, axis, up), lax.ppermute(low, axis, down)


def local(leaf_up, parent_in, leaf_lists, parent_lists, up_transfer, down_transfer, check_inverse):
    rows, cols, _ = leaf_up.shape
    before, after = shifted(leaf_up[:HALO], leaf_up[rows - HALO :], "gx")
    tall = lambda s: jnp.concatenate([before[:, s], leaf_up[:, s], after[:, s]], axis=0)
    left, right = shifted(tall(slice(0, HALO)), tall(slice(cols - HALO, cols)), "gy")
    return step(
        leaf_up, before, after, left, right, parent_in, leaf_lists, parent_lists,
        up_transfer, down_transfer, check_inverse,
    )


def solution(mesh):
    block = P("gx", "gy", None)
    return jax.shard_map(
        local,
        mesh=mesh,
        in_specs=(block,) * 4 + (P(),) * 3,
        out_specs=(block, block),
        check_vma=False,
    )
```

```python
import functools
import math

import jax
import jax.numpy as jnp
import ml_dtypes
import numpy as np
from jax import lax
from jax.experimental import pallas as pl
from jax.experimental.pallas import tpu as pltpu
from jax.sharding import PartitionSpec as P

ORDER = 6
HALO = 4
KEPT = 14
BF16, F32 = jnp.bfloat16, jnp.float32

INNER = [(a, b) for a in range(-2, 3) for b in range(-2, 3) if max(abs(a), abs(b)) == 2]
SIDES = (
    [(3, b) for b in range(-2, 3)],
    [(-3, b) for b in range(-2, 3)],
    [(a, 3) for a in range(-2, 3)],
    [(a, -3) for a in range(-2, 3)],
)
CORNERS = ([(3, 3)], [(3, -3)], [(-3, 3)], [(-3, -3)])
GROUPS = (INNER,) + SIDES + CORNERS


def offset_table():
    return [(a, b) for a in range(-3, 4) for b in range(-3, 4) if max(abs(a), abs(b)) >= 2]


def surface_points():
    grid = np.linspace(-1.0, 1.0, ORDER)
    keys = [
        (i, j, k)
        for i in range(ORDER)
        for j in range(ORDER)
        for k in range(ORDER)
        if min(i, j, k) == 0 or max(i, j, k) == ORDER - 1
    ]
    return keys, np.array([[grid[i] for i in key] for key in keys])


def translation(points, dx, dy):
    r = 0.525 * (points[:, None, :] - points[None, :, :]) - np.array([dx, dy, 0.0])
    dist = np.sqrt((r * r).sum(-1))
    n = len(points)
    out = np.zeros((3, n, 3, n))
    for a in range(3):
        for b in range(3):
            out[a, :, b, :] = (float(a == b) / dist + r[..., a] * r[..., b] / dist**3) / (8 * math.pi)
    return out.reshape(3 * n, 3 * n)


def split(x):
    high = x.astype(ml_dtypes.bfloat16)
    return high, (x - high.astype(np.float64)).astype(ml_dtypes.bfloat16)


@functools.lru_cache(maxsize=None)
def operators():
    keys, points = surface_points()
    n = len(keys)
    place = {key: i for i, key in enumerate(keys)}
    mirror = [place[(i, j, ORDER - 1 - k)] for i, j, k in keys]
    mats = {o: translation(points, *o) for o in offset_table()}
    half = 3 * n // 2
    rotation = np.zeros((3 * n, 512))
    back = np.zeros((512, 3 * n))
    tables = {}
    for s, sign in enumerate((1, -1)):
        pairs = np.zeros((3 * n, half))
        col = 0
        for a in range(3):
            flip = sign if a < 2 else -sign
            for i in range(n):
                if i < mirror[i]:
                    pairs[a * n + i, col] = 1.0
                    pairs[a * n + mirror[i], col] = flip
                    col += 1
        blocks = {o: 0.5 * pairs.T @ m @ pairs for o, m in mats.items()}
        gram = sum((1 + 0.05 * o[0] + 0.02 * o[1]) * b.T @ b for o, b in blocks.items())
        _, vecs = np.linalg.eigh(gram)
        vecs = vecs[:, ::-1]
        vecs = vecs * np.sign(vecs[np.abs(vecs).argmax(0), np.arange(half)])
        modes = pairs @ vecs / math.sqrt(2.0)
        rotation[:, 256 * s : 256 * s + half] = modes
        rotation[:, 256 * s + half : 256 * s + half + KEPT] = modes[:, :KEPT]
        rotation[:, 256 * s + half + KEPT : 256 * s + half + 2 * KEPT] = modes[:, :KEPT]
        back[256 * s : 256 * s + half] = pairs.T
        for o, m in mats.items():
            high, low = split((0.5 * pairs.T @ m @ modes).T)
            tile = np.zeros((256, 256), ml_dtypes.bfloat16)
            tile[:half, :half] = high
            tile[half : half + KEPT, :half] = high[:KEPT]
            tile[half + KEPT : half + 2 * KEPT, :half] = low[:KEPT]
            tables[s, o] = tile
    stacked = [tables[s, o] for group in GROUPS for s in range(2) for o in group]
    return (
        np.concatenate(split(rotation), axis=0).reshape(2, 3 * n, 512),
        back.astype(ml_dtypes.bfloat16),
        np.concatenate(stacked, axis=0),
    )


def dot(a, b):
    return lax.dot_general(a, b, (((1,), (0,)), ((), ())), preferred_element_type=F32)


def dot_t(a, b):
    return lax.dot_general(a, b, (((1,), (1,)), ((), ())), preferred_element_type=F32)


def parts(x):
    high = x.astype(BF16)
    return high, (x - high.astype(F32)).astype(BF16)


def times(x, weight):
    xh, xl = parts(x)
    wh, wl = weight
    return dot(xh, wh) + (dot(xl, wh) + dot(xh, wl))


def times_t(x, weight):
    xh, xl = parts(x)
    wh, wl = weight
    return dot_t(xh, wh) + (dot_t(xl, wh) + dot_t(xh, wl))


def step_kernel(
    own_ref, before_ref, after_ref, left_ref, right_ref, pin_ref, llist_ref, plist_ref,
    up_hbm, down_hbm, inv_hbm, rot_ref, back_ref, table_hbm,
    out_ref, pup_ref,
    ext, modes, pmodes, pext, lut, lhs, acc, spread, up_v, down_v, inv_v, table, sems,
):
    rows, cols, dens = own_ref.shape
    pr, pc = rows // 2, cols // 2
    boxes = pr * pc
    tiles = [(t, 128 * t, min(128, dens - 128 * t)) for t in range(4)]

    def strided(ref, row, at, count):
        return jnp.concatenate(
            [ref[t, row, pl.ds(at, count, stride=2), :] for t in range(4)], axis=1
        )

    copies = [
        pltpu.make_async_copy(src, dst, sems.at[i])
        for i, (src, dst) in enumerate(
            ((up_hbm, up_v), (table_hbm, table), (down_hbm, down_v), (inv_hbm, inv_v))
        )
    ]
    for c in copies:
        c.start()

    ext[...] = jnp.zeros_like(ext)
    for t, at, width in tiles:
        cut = slice(at, at + width)
        to = slice(0, width)
        ext[t, HALO : HALO + rows, 8 : 8 + cols, to] = own_ref[:, :, cut]
        ext[t, 0:HALO, 8 : 8 + cols, to] = before_ref[:, :, cut]
        ext[t, HALO + rows :, 8 : 8 + cols, to] = after_ref[:, :, cut]
        ext[t, :, 8 - HALO : 8, to] = left_ref[:, :, cut]
        ext[t, :, 8 + cols : 8 + cols + HALO, to] = right_ref[:, :, cut]

    lane = lax.broadcasted_iota(jnp.int32, (1, 512), 1) % 256
    half = dens // 2
    is_low = (lane >= half) & (lane < half + KEPT)
    rot = (rot_ref[0], rot_ref[1])

    def to_modes(x):
        y = times(x, rot)
        return jnp.where(is_low, y - y.astype(BF16).astype(F32), y)

    wide = cols + 16
    used = rows + 4
    chunk = used // 4
    for i in range(4):
        rng = slice(2 + i * chunk, 2 + (i + 1) * chunk)
        x = jnp.concatenate(
            [ext[t, rng, :, :].reshape(chunk * wide, 128) for t in range(4)], axis=1
        )
        y = to_modes(x[:, :dens])
        for t in range(4):
            modes[t, i * chunk : (i + 1) * chunk, :, :] = y[:, 128 * t : 128 * t + 128].reshape(
                chunk, wide, 128
            )

    copies[0].wait()
    hp = pr + 4
    wp = wide // 2
    parent = jnp.zeros((hp * wp, dens), F32)
    for c in range(2):
        for d in range(2):
            x = jnp.concatenate(
                [strided(ext, 2 * i + c, d, wp) for i in range(hp)], axis=0
            )
            parent = parent + times_t(x[:, :dens], parts(up_v[2 * c + d]))
    pext[...] = parent.reshape(hp, wp, dens)
    pup_ref[...] = pext[2 : 2 + pr, 4 : 4 + pc, :]
    pmodes[0] = jnp.zeros((wp, 512), F32)
    pmodes[hp + 1] = jnp.zeros((wp, 512), F32)
    pmodes[1 : hp + 1] = to_modes(parent).reshape(hp, wp, 512)

    def source(cs, ds, px, py):
        return ((cs * 2 + ds) * 3 + px + 1) * 3 + py + 1

    for cs in range(2):
        for ds in range(2):
            for px in (-1, 0, 1):
                for py in (-1, 0, 1):
                    x = jnp.concatenate(
                        [
                            strided(modes, 2 + 2 * (i + px) + cs, 8 + 2 * py + ds, pc)
                            for i in range(pr)
                        ],
                        axis=0,
                    )
                    lut[source(cs, ds, px, py)] = x.astype(BF16)

    offsets = offset_table()
    spread[0, :, :, 0 : len(offsets)] = llist_ref[...].astype(F32)
    flags = []
    for c in range(2):
        for d in range(2):
            flags.append(
                jnp.concatenate(
                    [spread[0, 2 * i + c, pl.ds(d, pc, stride=2), :] for i in range(pr)], axis=0
                )
            )
    pflags = plist_ref[...].reshape(boxes, len(offsets)).astype(F32)

    def masked(flag, o, x):
        m = jnp.broadcast_to(flag[:, o : o + 1], (boxes, 128)).astype(BF16)
        return [x[:, 128 * t : 128 * t + 128] * m for t in range(4)]

    copies[1].wait()
    acc[...] = jnp.zeros_like(acc)
    start = 0
    for group in GROUPS:
        dx, dy = group[0]
        depth = 256 * len(group)
        classes = [
            2 * c + d
            for c in range(2)
            for d in range(2)
            if len(group) == 16
            or all(-2 - c <= o[0] <= 3 - c and -2 - d <= o[1] <= 3 - d for o in group)
        ]
        for k, (dx, dy) in enumerate(group):
            o = offsets.index((dx, dy))
            for n, cls in enumerate(classes):
                px, cs = divmod(cls // 2 + dx, 2)
                py, ds = divmod(cls % 2 + dy, 2)
                pieces = masked(flags[cls], o, lut[source(cs, ds, px, py)])
                for t in range(4):
                    at = (t // 2) * depth + 256 * k + 128 * (t % 2)
                    lhs[boxes * n : boxes * (n + 1), at : at + 128] = pieces[t]
            x = pmodes[3 + dx : 3 + dx + pr, 4 + dy : 4 + dy + pc, :].reshape(boxes, 512).astype(BF16)
            pieces = masked(pflags, o, x)
            n = len(classes)
            for t in range(4):
                at = (t // 2) * depth + 256 * k + 128 * (t % 2)
                lhs[boxes * n : boxes * (n + 1), at : at + 128] = pieces[t]
        total = boxes * (len(classes) + 1)
        for s in range(2):
            r = dot(
                lhs[0:total, s * depth : (s + 1) * depth],
                table[start + s * depth : start + (s + 1) * depth, :],
            )
            for n, cls in enumerate(classes + [4]):
                acc[boxes * cls : boxes * (cls + 1), 256 * s : 256 * (s + 1)] += r[
                    boxes * n : boxes * (n + 1)
                ]
        start += 2 * depth

    def natural(x):
        xh, xl = parts(x)
        return dot(xh, back_ref[...]) + dot(xl, back_ref[...])

    copies[2].wait()
    copies[3].wait()
    inverse = parts(inv_v[...])
    local = pin_ref[...].reshape(boxes, dens) + times_t(
        natural(acc[4 * boxes : 5 * boxes]), inverse
    )
    for c in range(2):
        for d in range(2):
            cls = 2 * c + d
            check = natural(acc[boxes * cls : boxes * (cls + 1)])
            check = check + times_t(local, parts(down_v[cls]))
            result = times_t(check, inverse)
            for t, at, width in tiles:
                for i in range(pr):
                    spread[t, 2 * i + c, pl.ds(d, pc, stride=2), 0:width] = result[
                        pc * i : pc * (i + 1), at : at + width
                    ]
    for t, at, width in tiles:
        out_ref[:, :, at : at + width] = spread[t, :, :, 0:width]


def step(own, before, after, left, right, pin, llist, plist, up, down, inv):
    rows, cols, dens = own.shape
    pr, pc = rows // 2, cols // 2
    boxes = pr * pc
    rotation, back, table = operators()
    vmem = pl.BlockSpec(memory_space=pltpu.VMEM)
    hbm = pl.BlockSpec(memory_space=pl.ANY)
    wide = cols + 16
    return pl.pallas_call(
        step_kernel,
        out_shape=(
            jax.ShapeDtypeStruct((rows, cols, dens), F32),
            jax.ShapeDtypeStruct((pr, pc, dens), F32),
        ),
        in_specs=[vmem] * 8 + [hbm] * 3 + [vmem] * 2 + [hbm],
        out_specs=(vmem, vmem),
        scratch_shapes=[
            pltpu.VMEM((4, rows + 2 * HALO, wide, 128), F32),
            pltpu.VMEM((4, rows + 4, wide, 128), F32),
            pltpu.VMEM((pr + 6, wide // 2, 512), F32),
            pltpu.VMEM((pr + 4, wide // 2, dens), F32),
            pltpu.VMEM((36, boxes, 512), BF16),
            pltpu.VMEM((5 * boxes, 512 * len(INNER)), BF16),
            pltpu.VMEM((5 * boxes, 512), F32),
            pltpu.VMEM((4, rows, cols, 128), F32),
            pltpu.VMEM(up.shape, F32),
            pltpu.VMEM(down.shape, F32),
            pltpu.VMEM(inv.shape, F32),
            pltpu.VMEM(table.shape, BF16),
            pltpu.SemaphoreType.DMA((4,)),
        ],
        compiler_params=pltpu.CompilerParams(vmem_limit_bytes=58 * 1024 * 1024),
    )(
        own, before, after, left, right, pin, llist, plist, up, down, inv,
        jnp.asarray(rotation), jnp.asarray(back), jnp.asarray(table),
    )


def shifted(low, high, axis):
    peers = lax.axis_size(axis)
    even = lax.axis_index(axis) % 2 == 0
    pairs = [[i, i + 1] for i in range(0, peers, 2)]
    others = [[i, (i + 1) % peers] for i in range(1, peers, 2)]
    first = lax.all_gather(jnp.where(even, high, low), axis, axis_index_groups=pairs)
    second = lax.all_gather(jnp.where(even, low, high), axis, axis_index_groups=others)
    return jnp.where(even, second[0], first[0]), jnp.where(even, first[1], second[1])


def local(leaf_up, parent_in, leaf_lists, parent_lists, up_transfer, down_transfer, check_inverse):
    rows, cols, _ = leaf_up.shape
    before, after = shifted(leaf_up[:HALO], leaf_up[rows - HALO :], "gx")
    tall = lambda s: jnp.concatenate([before[:, s], leaf_up[:, s], after[:, s]], axis=0)
    left, right = shifted(tall(slice(0, HALO)), tall(slice(cols - HALO, cols)), "gy")
    return step(
        leaf_up, before, after, left, right, parent_in, leaf_lists, parent_lists,
        up_transfer, down_transfer, check_inverse,
    )


def solution(mesh):
    block = P("gx", "gy", None)
    return jax.shard_map(
        local,
        mesh=mesh,
        in_specs=(block,) * 4 + (P(),) * 3,
        out_specs=(block, block),
        check_vma=False,
    )
```

```python
import functools
import math

import jax
import jax.numpy as jnp
import ml_dtypes
import numpy as np
from jax import lax
from jax.experimental import pallas as pl
from jax.experimental.pallas import tpu as pltpu
from jax.sharding import PartitionSpec as P

ORDER = 6
HALO = 4
KEPT = 14
BF16, F32 = jnp.bfloat16, jnp.float32

def offset_table():
    return [(a, b) for a in range(-3, 4) for b in range(-3, 4) if max(abs(a), abs(b)) >= 2]


def surface_points():
    grid = np.linspace(-1.0, 1.0, ORDER)
    keys = [
        (i, j, k)
        for i in range(ORDER)
        for j in range(ORDER)
        for k in range(ORDER)
        if min(i, j, k) == 0 or max(i, j, k) == ORDER - 1
    ]
    return keys, np.array([[grid[i] for i in key] for key in keys])


def translation(points, dx, dy):
    r = 0.525 * (points[:, None, :] - points[None, :, :]) - np.array([dx, dy, 0.0])
    dist = np.sqrt((r * r).sum(-1))
    n = len(points)
    out = np.zeros((3, n, 3, n))
    for a in range(3):
        for b in range(3):
            out[a, :, b, :] = (float(a == b) / dist + r[..., a] * r[..., b] / dist**3) / (8 * math.pi)
    return out.reshape(3 * n, 3 * n)


def split(x):
    high = x.astype(ml_dtypes.bfloat16)
    return high, (x - high.astype(np.float64)).astype(ml_dtypes.bfloat16)


@functools.lru_cache(maxsize=None)
def operators():
    keys, points = surface_points()
    n = len(keys)
    place = {key: i for i, key in enumerate(keys)}
    mirror = [place[(i, j, ORDER - 1 - k)] for i, j, k in keys]
    mats = {o: translation(points, *o) for o in offset_table()}
    half = 3 * n // 2
    rotation = np.zeros((3 * n, 512))
    back = np.zeros((512, 3 * n))
    tables = {}
    for s, sign in enumerate((1, -1)):
        pairs = np.zeros((3 * n, half))
        col = 0
        for a in range(3):
            flip = sign if a < 2 else -sign
            for i in range(n):
                if i < mirror[i]:
                    pairs[a * n + i, col] = 1.0
                    pairs[a * n + mirror[i], col] = flip
                    col += 1
        blocks = {o: 0.5 * pairs.T @ m @ pairs for o, m in mats.items()}
        gram = sum((1 + 0.05 * o[0] + 0.02 * o[1]) * b.T @ b for o, b in blocks.items())
        _, vecs = np.linalg.eigh(gram)
        vecs = vecs[:, ::-1]
        vecs = vecs * np.sign(vecs[np.abs(vecs).argmax(0), np.arange(half)])
        modes = pairs @ vecs / math.sqrt(2.0)
        rotation[:, 256 * s : 256 * s + half] = modes
        rotation[:, 256 * s + half : 256 * s + half + KEPT] = modes[:, :KEPT]
        rotation[:, 256 * s + half + KEPT : 256 * s + half + 2 * KEPT] = modes[:, :KEPT]
        back[256 * s : 256 * s + half] = pairs.T
        for o, m in mats.items():
            high, low = split((0.5 * pairs.T @ m @ modes).T)
            tile = np.zeros((256, 256), ml_dtypes.bfloat16)
            tile[:half, :half] = high
            tile[half : half + KEPT, :half] = high[:KEPT]
            tile[half + KEPT : half + 2 * KEPT, :half] = low[:KEPT]
            tables[s, o] = tile
    return (
        np.stack(split(rotation)),
        back.astype(ml_dtypes.bfloat16),
        np.stack([np.stack([tables[s, o] for s in range(2)]) for o in offset_table()]),
    )


@functools.lru_cache(maxsize=None)
def plan():
    offsets = offset_table()
    entries, picks = [], []
    for c in range(2):
        for d in range(2):
            for o, (dx, dy) in enumerate(offsets):
                px, cs = divmod(c + dx, 2)
                py, ds = divmod(d + dy, 2)
                if abs(px) <= 1 and abs(py) <= 1:
                    entries.append((cs * 3 + px + 1) * 6 + ds * 3 + py + 1)
                    picks.append(o)
    return entries, picks


def dot(a, b):
    return lax.dot_general(a, b, (((1,), (0,)), ((), ())), preferred_element_type=F32)


def dot_t(a, b):
    return lax.dot_general(a, b, (((1,), (1,)), ((), ())), preferred_element_type=F32)


def parts(x):
    high = x.astype(BF16)
    return high, (x - high.astype(F32)).astype(BF16)


def times(x, weight):
    xh, xl = parts(x)
    wh, wl = weight
    return dot(xh, wh) + (dot(xl, wh) + dot(xh, wl))


def times_t(x, weight):
    xh, xl = parts(x)
    wh, wl = weight
    return dot_t(xh, wh) + (dot_t(xl, wh) + dot_t(xh, wl))


def step_kernel(
    entry_ref, pick_ref,
    own_ref, before_ref, after_ref, left_ref, right_ref, pin_ref, llist_ref, plist_ref,
    up_hbm, down_hbm, inv_hbm, rot_ref, back_ref, table_hbm,
    out_ref, pup_ref,
    own_t, ends_t, strip_t, modes, pmodes, flat, masks, lut, acc, plocal,
    up_v, down_v, inv_v, table, sems,
):
    rows, cols, dens = own_ref.shape
    pr, pc = rows // 2, cols // 2
    gr, gc = pr // 2, pc // 2
    boxes, pboxes = pr * pc, gr * gc
    used = boxes + pboxes
    high = lut.shape[2]
    count = masks.shape[0] // 4
    classes = [(c, d) for c in range(2) for d in range(2)]
    tiles = [(t, 128 * t, min(128, dens - 128 * t)) for t in range(4)]
    copies = [
        pltpu.make_async_copy(src, dst, sems.at[i])
        for i, (src, dst) in enumerate(
            ((up_hbm, up_v), (table_hbm, table), (down_hbm, down_v), (inv_hbm, inv_v))
        )
    ]
    for c in copies:
        c.start()

    for t, at, width in tiles:
        cut, to = slice(at, at + width), slice(0, width)
        if width < 128:
            own_t[t] = jnp.zeros_like(own_t[t])
            ends_t[t] = jnp.zeros_like(ends_t[t])
            strip_t[t] = jnp.zeros_like(strip_t[t])
        own_t[t, :, :, to] = own_ref[:, :, cut]
        ends_t[t, 0:HALO, :, to] = before_ref[:, :, cut]
        ends_t[t, HALO:, :, to] = after_ref[:, :, cut]
        strip_t[t, :, 0:HALO, to] = left_ref[:, :, cut]
        strip_t[t, :, HALO:, to] = right_ref[:, :, cut]

    flat[0, :, :, 0 : llist_ref.shape[2]] = llist_ref[...].astype(F32)
    flat[1, 0:pr, 0:pc, 0 : plist_ref.shape[2]] = plist_ref[...].astype(F32)
    entries, picks = plan()
    for n, (c, d) in enumerate(classes):
        flag = jnp.concatenate(
            [flat[0, 2 * i + c, pl.ds(d, pc, stride=2), :] for i in range(pr)]
            + [flat[1, 2 * i + c, pl.ds(d, gc, stride=2), :] for i in range(gr)]
            + [jnp.zeros((high - used, 128), F32)],
            axis=0,
        )
        for k in range(count):
            o = picks[count * n + k]
            masks[count * n + k] = jnp.broadcast_to(flag[:, o : o + 1], (high, 128)).astype(BF16)

    copies[0].wait()
    parent = None
    for n, (c, d) in enumerate(classes):
        x = jnp.concatenate(
            [
                jnp.concatenate(
                    [own_t[t, 2 * i + c, pl.ds(d, pc, stride=2), :] for i in range(pr)]
                    + [ends_t[t, 2 * i + c, pl.ds(d, pc, stride=2), :] for i in range(HALO)]
                    + [strip_t[t, 2 * i + c, pl.ds(d, HALO, stride=2), :] for i in range(pr + 4)],
                    axis=0,
                )
                for t in range(4)
            ],
            axis=1,
        )
        part = times_t(x[:, :dens], parts(up_v[n]))
        parent = part if parent is None else parent + part
    pup_ref[...] = parent[0:boxes].reshape(pr, pc, dens)

    lane = lax.broadcasted_iota(jnp.int32, (1, 512), 1) % 256
    half = dens // 2
    is_low = (lane >= half) & (lane < half + KEPT)
    rot = (rot_ref[0], rot_ref[1])

    def to_modes(x):
        y = times(x, rot)
        return jnp.where(is_low, y - y.astype(BF16).astype(F32), y)

    y = to_modes(own_ref[...].reshape(rows * cols, dens))
    z = to_modes(
        jnp.concatenate([before_ref[HALO - 2 :], after_ref[0:2]], axis=0).reshape(4 * cols, dens)
    )
    w = jnp.concatenate(
        [strip_t[t, 2 : rows + 6].reshape((rows + 4) * 8, 128) for t in range(4)], axis=1
    )
    w = to_modes(w[:, :dens])
    p = to_modes(parent)
    for t in range(4):
        cut = slice(128 * t, 128 * t + 128)
        modes[t, 2 : 2 + rows, 8 : 8 + cols, :] = y[:, cut].reshape(rows, cols, 128)
        ends = z[:, cut].reshape(4, cols, 128)
        modes[t, 0:2, 8 : 8 + cols, :] = ends[0:2]
        modes[t, 2 + rows :, 8 : 8 + cols, :] = ends[2:4]
        strip = w[:, cut].reshape(rows + 4, 8, 128)
        modes[t, :, 4:8, :] = strip[:, 0:4]
        modes[t, :, 8 + cols : 12 + cols, :] = strip[:, 4:8]
        pmodes[t, 2 : 2 + pr, 4 : 4 + pc, :] = p[0:boxes, cut].reshape(pr, pc, 128)
        ends = p[boxes : boxes + 4 * pc, cut].reshape(4, pc, 128)
        pmodes[t, 0:2, 4 : 4 + pc, :] = ends[0:2]
        pmodes[t, 2 + pr :, 4 : 4 + pc, :] = ends[2:4]
        strip = p[boxes + 4 * pc :, cut].reshape(pr + 4, 4, 128)
        pmodes[t, :, 2:4, :] = strip[:, 0:2]
        pmodes[t, :, 4 + pc : 6 + pc, :] = strip[:, 2:4]

    def gather(i, carry):
        base = 2 * (i % 3) + i // 3
        for ds in range(2):
            for py in (-1, 0, 1):
                e = i * 6 + ds * 3 + py + 1
                for t in range(4):
                    x = jnp.concatenate(
                        [
                            modes[t, base + 2 * j, pl.ds(8 + 2 * py + ds, pc, stride=2), :]
                            for j in range(pr)
                        ]
                        + [
                            pmodes[t, base + 2 * j, pl.ds(4 + 2 * py + ds, gc, stride=2), :]
                            for j in range(gr)
                        ]
                        + [jnp.zeros((high - used, 128), F32)],
                        axis=0,
                    )
                    lut[e, t // 2, :, 128 * (t % 2) : 128 * (t % 2) + 128] = x.astype(BF16)
        return carry

    lax.fori_loop(0, 6, gather, 0)

    copies[1].wait()

    def interact(j, carry):
        n, s = j // 2, j % 2
        total = jnp.zeros((high, 256), F32)
        for k in range(count):
            i = n * count + k
            m = masks[i]
            x = lut[entry_ref[i], s]
            x = jnp.concatenate([x[:, :128] * m, x[:, 128:] * m], axis=1)
            total = total + dot(x, table[pick_ref[i], s])
        acc[s, n] = total
        return carry

    lax.fori_loop(0, 8, interact, 0)

    check = []
    for n in range(4):
        check_n = None
        for s in range(2):
            xh, xl = parts(acc[s, n])
            b = back_ref[256 * s : 256 * (s + 1)]
            part = dot(xh, b) + dot(xl, b)
            check_n = part if check_n is None else check_n + part
        check.append(check_n)

    copies[2].wait()
    copies[3].wait()
    inverse = parts(inv_v[...])
    for n, (c, d) in enumerate(classes):
        for t, at, width in tiles:
            for j in range(gr):
                plocal[t, 2 * j + c, pl.ds(d, gc, stride=2), 0:width] = check[n][
                    boxes + gc * j : boxes + gc * (j + 1), at : at + width
                ]
    x = jnp.concatenate([plocal[t].reshape(boxes, 128) for t in range(4)], axis=1)[:, :dens]
    local = pin_ref[...].reshape(boxes, dens) + times_t(x, inverse)
    x = jnp.concatenate(
        [check[n][0:boxes] + times_t(local, parts(down_v[n])) for n in range(4)], axis=0
    )
    result = times_t(x, inverse)
    for n, (c, d) in enumerate(classes):
        for t, at, width in tiles:
            for j in range(pr):
                r = boxes * n + pc * j
                flat[t, 2 * j + c, pl.ds(d, pc, stride=2), 0:width] = result[
                    r : r + pc, at : at + width
                ]
    for t, at, width in tiles:
        out_ref[:, :, at : at + width] = flat[t, :, :, 0:width]


def step(own, before, after, left, right, pin, llist, plist, up, down, inv):
    rows, cols, dens = own.shape
    pr, pc = rows // 2, cols // 2
    rotation, back, table = operators()
    entries, picks = plan()
    high = -(-(pr * pc * 5 // 4) // 16) * 16
    vmem = pl.BlockSpec(memory_space=pltpu.VMEM)
    hbm = pl.BlockSpec(memory_space=pl.ANY)
    smem = pl.BlockSpec(memory_space=pltpu.SMEM)
    return pl.pallas_call(
        step_kernel,
        out_shape=(
            jax.ShapeDtypeStruct((rows, cols, dens), F32),
            jax.ShapeDtypeStruct((pr, pc, dens), F32),
        ),
        in_specs=[smem] * 2 + [vmem] * 8 + [hbm] * 3 + [vmem] * 2 + [hbm],
        out_specs=(vmem, vmem),
        scratch_shapes=[
            pltpu.VMEM((4, rows, cols, 128), F32),
            pltpu.VMEM((4, 2 * HALO, cols, 128), F32),
            pltpu.VMEM((4, rows + 2 * HALO, 8, 128), F32),
            pltpu.VMEM((4, rows + 4, cols + 16, 128), F32),
            pltpu.VMEM((4, pr + 4, pc + 8, 128), F32),
            pltpu.VMEM((4, rows, cols, 128), F32),
            pltpu.VMEM((len(entries), high, 128), BF16),
            pltpu.VMEM((36, 2, high, 256), BF16),
            pltpu.VMEM((2, 4, high, 256), F32),
            pltpu.VMEM((4, pr, pc, 128), F32),
            pltpu.VMEM(up.shape, F32),
            pltpu.VMEM(down.shape, F32),
            pltpu.VMEM(inv.shape, F32),
            pltpu.VMEM(table.shape, BF16),
            pltpu.SemaphoreType.DMA((4,)),
        ],
        compiler_params=pltpu.CompilerParams(vmem_limit_bytes=56 * 1024 * 1024),
    )(
        jnp.asarray(entries, jnp.int32), jnp.asarray(picks, jnp.int32),
        own, before, after, left, right, pin, llist, plist, up, down, inv,
        jnp.asarray(rotation), jnp.asarray(back), jnp.asarray(table),
    )


def shifted(low, high, axis):
    peers = lax.axis_size(axis)
    up = [(i, i + 1) for i in range(peers - 1)]
    down = [(j, i) for i, j in up]
    return lax.ppermute(high, axis, up), lax.ppermute(low, axis, down)


def local(leaf_up, parent_in, leaf_lists, parent_lists, up_transfer, down_transfer, check_inverse):
    rows, cols, _ = leaf_up.shape
    before, after = shifted(leaf_up[:HALO], leaf_up[rows - HALO :], "gx")
    tall = lambda s: jnp.concatenate([before[:, s], leaf_up[:, s], after[:, s]], axis=0)
    left, right = shifted(tall(slice(0, HALO)), tall(slice(cols - HALO, cols)), "gy")
    return step(
        leaf_up, before, after, left, right, parent_in, leaf_lists, parent_lists,
        up_transfer, down_transfer, check_inverse,
    )


def solution(mesh):
    block = P("gx", "gy", None)
    return jax.shard_map(
        local,
        mesh=mesh,
        in_specs=(block,) * 4 + (P(),) * 3,
        out_specs=(block, block),
        check_vma=False,
    )
```

```python
import functools
import math

import jax
import jax.numpy as jnp
import ml_dtypes
import numpy as np
from jax import lax
from jax.experimental import pallas as pl
from jax.experimental.pallas import tpu as pltpu
from jax.sharding import PartitionSpec as P

ORDER = 6
HALO = 4
KEPT = 14
BF16, F32 = jnp.bfloat16, jnp.float32

def offset_table():
    return [(a, b) for a in range(-3, 4) for b in range(-3, 4) if max(abs(a), abs(b)) >= 2]


def surface_points():
    grid = np.linspace(-1.0, 1.0, ORDER)
    keys = [
        (i, j, k)
        for i in range(ORDER)
        for j in range(ORDER)
        for k in range(ORDER)
        if min(i, j, k) == 0 or max(i, j, k) == ORDER - 1
    ]
    return keys, np.array([[grid[i] for i in key] for key in keys])


def translation(points, dx, dy):
    r = 0.525 * (points[:, None, :] - points[None, :, :]) - np.array([dx, dy, 0.0])
    dist = np.sqrt((r * r).sum(-1))
    n = len(points)
    out = np.zeros((3, n, 3, n))
    for a in range(3):
        for b in range(3):
            out[a, :, b, :] = (float(a == b) / dist + r[..., a] * r[..., b] / dist**3) / (8 * math.pi)
    return out.reshape(3 * n, 3 * n)


def split(x):
    high = x.astype(ml_dtypes.bfloat16)
    return high, (x - high.astype(np.float64)).astype(ml_dtypes.bfloat16)


@functools.lru_cache(maxsize=None)
def operators():
    keys, points = surface_points()
    n = len(keys)
    place = {key: i for i, key in enumerate(keys)}
    mirror = [place[(i, j, ORDER - 1 - k)] for i, j, k in keys]
    mats = {o: translation(points, *o) for o in offset_table()}
    half = 3 * n // 2
    rotation = np.zeros((3 * n, 512))
    back = np.zeros((512, 3 * n))
    tables = {}
    for s, sign in enumerate((1, -1)):
        pairs = np.zeros((3 * n, half))
        col = 0
        for a in range(3):
            flip = sign if a < 2 else -sign
            for i in range(n):
                if i < mirror[i]:
                    pairs[a * n + i, col] = 1.0
                    pairs[a * n + mirror[i], col] = flip
                    col += 1
        blocks = {o: 0.5 * pairs.T @ m @ pairs for o, m in mats.items()}
        gram = sum((1 + 0.05 * o[0] + 0.02 * o[1]) * b.T @ b for o, b in blocks.items())
        _, vecs = np.linalg.eigh(gram)
        vecs = vecs[:, ::-1]
        vecs = vecs * np.sign(vecs[np.abs(vecs).argmax(0), np.arange(half)])
        modes = pairs @ vecs / math.sqrt(2.0)
        rotation[:, 256 * s : 256 * s + half] = modes
        rotation[:, 256 * s + half : 256 * s + half + KEPT] = modes[:, :KEPT]
        rotation[:, 256 * s + half + KEPT : 256 * s + half + 2 * KEPT] = modes[:, :KEPT]
        back[256 * s : 256 * s + half] = pairs.T
        for o, m in mats.items():
            high, low = split((0.5 * pairs.T @ m @ modes).T)
            tile = np.zeros((256, 256), ml_dtypes.bfloat16)
            tile[:half, :half] = high
            tile[half : half + KEPT, :half] = high[:KEPT]
            tile[half + KEPT : half + 2 * KEPT, :half] = low[:KEPT]
            tables[s, o] = tile
    return (
        np.stack(split(rotation)),
        back.astype(ml_dtypes.bfloat16),
        np.stack([np.stack([tables[s, o] for s in range(2)]) for o in offset_table()]),
    )


@functools.lru_cache(maxsize=None)
def plan():
    offsets = offset_table()
    entries, picks = [], []
    for c in range(2):
        for d in range(2):
            for o, (dx, dy) in enumerate(offsets):
                px, cs = divmod(c + dx, 2)
                py, ds = divmod(d + dy, 2)
                if abs(px) <= 1 and abs(py) <= 1:
                    entries.append((cs * 3 + px + 1) * 6 + ds * 3 + py + 1)
                    picks.append(o)
    return entries, picks


def dot(a, b):
    return lax.dot_general(a, b, (((1,), (0,)), ((), ())), preferred_element_type=F32)


def dot_t(a, b):
    return lax.dot_general(a, b, (((1,), (1,)), ((), ())), preferred_element_type=F32)


def parts(x):
    high = x.astype(BF16)
    return high, (x - high.astype(F32)).astype(BF16)


def times(x, weight):
    xh, xl = parts(x)
    wh, wl = weight
    return dot(xh, wh) + (dot(xl, wh) + dot(xh, wl))


def times_t(x, weight):
    xh, xl = parts(x)
    wh, wl = weight
    return dot_t(xh, wh) + (dot_t(xl, wh) + dot_t(xh, wl))


def step_kernel(
    entry_ref, pick_ref, even_ref,
    own_ref, end0_ref, end1_ref, strip0_ref, strip1_ref, pin_ref, llist_ref, plist_ref,
    up_hbm, down_hbm, inv_hbm, rot_ref, back_ref, table_hbm,
    out_ref, pup_ref,
    own_t, ends_t, strip_t, modes, pmodes, flat, masks, lut, acc, plocal,
    up_v, down_v, inv_v, table, sems,
):
    rows, cols, dens = own_ref.shape
    pr, pc = rows // 2, cols // 2
    gr, gc = pr // 2, pc // 2
    boxes, pboxes = pr * pc, gr * gc
    used = boxes + pboxes
    high = lut.shape[2]
    count = masks.shape[0] // 4
    classes = [(c, d) for c in range(2) for d in range(2)]
    tiles = [(t, 128 * t, min(128, dens - 128 * t)) for t in range(4)]
    copies = [
        pltpu.make_async_copy(src, dst, sems.at[i])
        for i, (src, dst) in enumerate(
            ((up_hbm, up_v), (table_hbm, table), (down_hbm, down_v), (inv_hbm, inv_v))
        )
    ]
    for c in copies:
        c.start()

    even_x, even_y = even_ref[0] == 1, even_ref[1] == 1

    for t, at, width in tiles:
        cut, to = slice(at, at + width), slice(0, width)
        if width < 128:
            own_t[t] = jnp.zeros_like(own_t[t])
            ends_t[t] = jnp.zeros_like(ends_t[t])
            strip_t[t] = jnp.zeros_like(strip_t[t])
        own_t[t, :, :, to] = own_ref[:, :, cut]
        first, second = end0_ref[:, :, cut], end1_ref[:, :, cut]
        ends_t[t, 0:HALO, :, to] = jnp.where(even_x, second, first)
        ends_t[t, HALO:, :, to] = jnp.where(even_x, first, second)
        first, second = strip0_ref[:, :, cut], strip1_ref[:, :, cut]
        strip_t[t, :, 0:HALO, to] = jnp.where(even_y, second, first)
        strip_t[t, :, HALO:, to] = jnp.where(even_y, first, second)

    flat[0, :, :, 0 : llist_ref.shape[2]] = llist_ref[...].astype(F32)
    flat[1, 0:pr, 0:pc, 0 : plist_ref.shape[2]] = plist_ref[...].astype(F32)
    entries, picks = plan()
    for n, (c, d) in enumerate(classes):
        flag = jnp.concatenate(
            [flat[0, 2 * i + c, pl.ds(d, pc, stride=2), :] for i in range(pr)]
            + [flat[1, 2 * i + c, pl.ds(d, gc, stride=2), :] for i in range(gr)]
            + [jnp.zeros((high - used, 128), F32)],
            axis=0,
        )
        for k in range(count):
            o = picks[count * n + k]
            masks[count * n + k] = jnp.broadcast_to(flag[:, o : o + 1], (high, 128)).astype(BF16)

    copies[0].wait()
    parent = None
    for n, (c, d) in enumerate(classes):
        x = jnp.concatenate(
            [
                jnp.concatenate(
                    [own_t[t, 2 * i + c, pl.ds(d, pc, stride=2), :] for i in range(pr)]
                    + [ends_t[t, 2 * i + c, pl.ds(d, pc, stride=2), :] for i in range(HALO)]
                    + [strip_t[t, 2 * i + c, pl.ds(d, HALO, stride=2), :] for i in range(pr + 4)],
                    axis=0,
                )
                for t in range(4)
            ],
            axis=1,
        )
        part = times_t(x[:, :dens], parts(up_v[n]))
        parent = part if parent is None else parent + part
    pup_ref[...] = parent[0:boxes].reshape(pr, pc, dens)

    lane = lax.broadcasted_iota(jnp.int32, (1, 512), 1) % 256
    half = dens // 2
    is_low = (lane >= half) & (lane < half + KEPT)
    rot = (rot_ref[0], rot_ref[1])

    def to_modes(x):
        y = times(x, rot)
        return jnp.where(is_low, y - y.astype(BF16).astype(F32), y)

    y = to_modes(own_ref[...].reshape(rows * cols, dens))
    z = jnp.concatenate(
        [ends_t[t, HALO - 2 : HALO + 2].reshape(4 * cols, 128) for t in range(4)], axis=1
    )
    z = to_modes(z[:, :dens])
    w = jnp.concatenate(
        [strip_t[t, 2 : rows + 6].reshape((rows + 4) * 8, 128) for t in range(4)], axis=1
    )
    w = to_modes(w[:, :dens])
    p = to_modes(parent)
    for t in range(4):
        cut = slice(128 * t, 128 * t + 128)
        modes[t, 2 : 2 + rows, 8 : 8 + cols, :] = y[:, cut].reshape(rows, cols, 128)
        ends = z[:, cut].reshape(4, cols, 128)
        modes[t, 0:2, 8 : 8 + cols, :] = ends[0:2]
        modes[t, 2 + rows :, 8 : 8 + cols, :] = ends[2:4]
        strip = w[:, cut].reshape(rows + 4, 8, 128)
        modes[t, :, 4:8, :] = strip[:, 0:4]
        modes[t, :, 8 + cols : 12 + cols, :] = strip[:, 4:8]
        pmodes[t, 2 : 2 + pr, 4 : 4 + pc, :] = p[0:boxes, cut].reshape(pr, pc, 128)
        ends = p[boxes : boxes + 4 * pc, cut].reshape(4, pc, 128)
        pmodes[t, 0:2, 4 : 4 + pc, :] = ends[0:2]
        pmodes[t, 2 + pr :, 4 : 4 + pc, :] = ends[2:4]
        strip = p[boxes + 4 * pc :, cut].reshape(pr + 4, 4, 128)
        pmodes[t, :, 2:4, :] = strip[:, 0:2]
        pmodes[t, :, 4 + pc : 6 + pc, :] = strip[:, 2:4]

    def gather(i, carry):
        base = 2 * (i % 3) + i // 3
        for ds in range(2):
            for py in (-1, 0, 1):
                e = i * 6 + ds * 3 + py + 1
                for t in range(4):
                    x = jnp.concatenate(
                        [
                            modes[t, base + 2 * j, pl.ds(8 + 2 * py + ds, pc, stride=2), :]
                            for j in range(pr)
                        ]
                        + [
                            pmodes[t, base + 2 * j, pl.ds(4 + 2 * py + ds, gc, stride=2), :]
                            for j in range(gr)
                        ]
                        + [jnp.zeros((high - used, 128), F32)],
                        axis=0,
                    )
                    lut[e, t // 2, :, 128 * (t % 2) : 128 * (t % 2) + 128] = x.astype(BF16)
        return carry

    lax.fori_loop(0, 6, gather, 0)

    copies[1].wait()

    def interact(j, carry):
        n, s = j // 2, j % 2
        total = jnp.zeros((high, 256), F32)
        for k in range(count):
            i = n * count + k
            m = masks[i]
            x = lut[entry_ref[i], s]
            x = jnp.concatenate([x[:, :128] * m, x[:, 128:] * m], axis=1)
            total = total + dot(x, table[pick_ref[i], s])
        acc[s, n] = total
        return carry

    lax.fori_loop(0, 8, interact, 0)

    check = []
    for n in range(4):
        check_n = None
        for s in range(2):
            xh, xl = parts(acc[s, n])
            b = back_ref[256 * s : 256 * (s + 1)]
            part = dot(xh, b) + dot(xl, b)
            check_n = part if check_n is None else check_n + part
        check.append(check_n)

    copies[2].wait()
    copies[3].wait()
    inverse = parts(inv_v[...])
    for n, (c, d) in enumerate(classes):
        for t, at, width in tiles:
            for j in range(gr):
                plocal[t, 2 * j + c, pl.ds(d, gc, stride=2), 0:width] = check[n][
                    boxes + gc * j : boxes + gc * (j + 1), at : at + width
                ]
    x = jnp.concatenate([plocal[t].reshape(boxes, 128) for t in range(4)], axis=1)[:, :dens]
    local = pin_ref[...].reshape(boxes, dens) + times_t(x, inverse)
    x = jnp.concatenate(
        [check[n][0:boxes] + times_t(local, parts(down_v[n])) for n in range(4)], axis=0
    )
    result = times_t(x, inverse)
    for n, (c, d) in enumerate(classes):
        for t, at, width in tiles:
            for j in range(pr):
                r = boxes * n + pc * j
                flat[t, 2 * j + c, pl.ds(d, pc, stride=2), 0:width] = result[
                    r : r + pc, at : at + width
                ]
    for t, at, width in tiles:
        out_ref[:, :, at : at + width] = flat[t, :, :, 0:width]


def step(even, own, ends, strips, pin, llist, plist, up, down, inv):
    rows, cols, dens = own.shape
    pr, pc = rows // 2, cols // 2
    rotation, back, table = operators()
    entries, picks = plan()
    high = -(-(pr * pc * 5 // 4) // 16) * 16
    vmem = pl.BlockSpec(memory_space=pltpu.VMEM)
    hbm = pl.BlockSpec(memory_space=pl.ANY)
    smem = pl.BlockSpec(memory_space=pltpu.SMEM)
    return pl.pallas_call(
        step_kernel,
        out_shape=(
            jax.ShapeDtypeStruct((rows, cols, dens), F32),
            jax.ShapeDtypeStruct((pr, pc, dens), F32),
        ),
        in_specs=[smem] * 3 + [vmem] * 8 + [hbm] * 3 + [vmem] * 2 + [hbm],
        out_specs=(vmem, vmem),
        scratch_shapes=[
            pltpu.VMEM((4, rows, cols, 128), F32),
            pltpu.VMEM((4, 2 * HALO, cols, 128), F32),
            pltpu.VMEM((4, rows + 2 * HALO, 8, 128), F32),
            pltpu.VMEM((4, rows + 4, cols + 16, 128), F32),
            pltpu.VMEM((4, pr + 4, pc + 8, 128), F32),
            pltpu.VMEM((4, rows, cols, 128), F32),
            pltpu.VMEM((len(entries), high, 128), BF16),
            pltpu.VMEM((36, 2, high, 256), BF16),
            pltpu.VMEM((2, 4, high, 256), F32),
            pltpu.VMEM((4, pr, pc, 128), F32),
            pltpu.VMEM(up.shape, F32),
            pltpu.VMEM(down.shape, F32),
            pltpu.VMEM(inv.shape, F32),
            pltpu.VMEM(table.shape, BF16),
            pltpu.SemaphoreType.DMA((4,)),
        ],
        compiler_params=pltpu.CompilerParams(vmem_limit_bytes=56 * 1024 * 1024),
    )(
        jnp.asarray(entries, jnp.int32), jnp.asarray(picks, jnp.int32), even,
        own, *ends, *strips, pin, llist, plist, up, down, inv,
        jnp.asarray(rotation), jnp.asarray(back), jnp.asarray(table),
    )


def swapped(low, high, axis, odd_first):
    peers = lax.axis_size(axis)
    even = lax.axis_index(axis) % 2 == 0
    strips = (jnp.where(even, high, low), jnp.where(even, low, high))
    got = [None, None]
    for kind in (1, 0) if odd_first else (0, 1):
        pairs = [(i, i + 1) for i in range(kind, peers - 1, 2)]
        got[kind] = lax.ppermute(strips[kind], axis, pairs + [(j, i) for i, j in pairs])
    return got


def local(leaf_up, parent_in, leaf_lists, parent_lists, up_transfer, down_transfer, check_inverse):
    rows, cols, _ = leaf_up.shape
    even = [lax.axis_index(axis) % 2 == 0 for axis in ("gx", "gy")]
    ends = swapped(leaf_up[:HALO], leaf_up[rows - HALO :], "gx", False)
    before = jnp.where(even[0], ends[1], ends[0])
    after = jnp.where(even[0], ends[0], ends[1])
    tall = lambda s: jnp.concatenate([before[:, s], leaf_up[:, s], after[:, s]], axis=0)
    strips = swapped(tall(slice(0, HALO)), tall(slice(cols - HALO, cols)), "gy", True)
    return step(
        jnp.stack(even).astype(jnp.int32), leaf_up, ends, strips, parent_in, leaf_lists, parent_lists,
        up_transfer, down_transfer, check_inverse,
    )


def solution(mesh):
    block = P("gx", "gy", None)
    return jax.shard_map(
        local,
        mesh=mesh,
        in_specs=(block,) * 4 + (P(),) * 3,
        out_specs=(block, block),
        check_vma=False,
    )
```

```python
import functools
import math

import jax
import jax.numpy as jnp
import ml_dtypes
import numpy as np
from jax import lax
from jax.experimental import pallas as pl
from jax.experimental.pallas import tpu as pltpu
from jax.sharding import PartitionSpec as P

ORDER = 6
HALO = 4
KEPT = 14
BF16, F32 = jnp.bfloat16, jnp.float32

def offset_table():
    return [(a, b) for a in range(-3, 4) for b in range(-3, 4) if max(abs(a), abs(b)) >= 2]


def surface_points():
    grid = np.linspace(-1.0, 1.0, ORDER)
    keys = [
        (i, j, k)
        for i in range(ORDER)
        for j in range(ORDER)
        for k in range(ORDER)
        if min(i, j, k) == 0 or max(i, j, k) == ORDER - 1
    ]
    return keys, np.array([[grid[i] for i in key] for key in keys])


def translation(points, dx, dy):
    r = 0.525 * (points[:, None, :] - points[None, :, :]) - np.array([dx, dy, 0.0])
    dist = np.sqrt((r * r).sum(-1))
    n = len(points)
    out = np.zeros((3, n, 3, n))
    for a in range(3):
        for b in range(3):
            out[a, :, b, :] = (float(a == b) / dist + r[..., a] * r[..., b] / dist**3) / (8 * math.pi)
    return out.reshape(3 * n, 3 * n)


def split(x):
    high = x.astype(ml_dtypes.bfloat16)
    return high, (x - high.astype(np.float64)).astype(ml_dtypes.bfloat16)


@functools.lru_cache(maxsize=None)
def operators():
    keys, points = surface_points()
    n = len(keys)
    place = {key: i for i, key in enumerate(keys)}
    mirror = [place[(i, j, ORDER - 1 - k)] for i, j, k in keys]
    mats = {o: translation(points, *o) for o in offset_table()}
    half = 3 * n // 2
    rotation = np.zeros((3 * n, 512))
    back = np.zeros((512, 3 * n))
    tables = {}
    for s, sign in enumerate((1, -1)):
        pairs = np.zeros((3 * n, half))
        col = 0
        for a in range(3):
            flip = sign if a < 2 else -sign
            for i in range(n):
                if i < mirror[i]:
                    pairs[a * n + i, col] = 1.0
                    pairs[a * n + mirror[i], col] = flip
                    col += 1
        blocks = {o: 0.5 * pairs.T @ m @ pairs for o, m in mats.items()}
        gram = sum((1 + 0.05 * o[0] + 0.02 * o[1]) * b.T @ b for o, b in blocks.items())
        _, vecs = np.linalg.eigh(gram)
        vecs = vecs[:, ::-1]
        vecs = vecs * np.sign(vecs[np.abs(vecs).argmax(0), np.arange(half)])
        modes = pairs @ vecs / math.sqrt(2.0)
        rotation[:, 256 * s : 256 * s + half] = modes
        rotation[:, 256 * s + half : 256 * s + half + KEPT] = modes[:, :KEPT]
        rotation[:, 256 * s + half + KEPT : 256 * s + half + 2 * KEPT] = modes[:, :KEPT]
        back[256 * s : 256 * s + half] = pairs.T
        for o, m in mats.items():
            high, low = split((0.5 * pairs.T @ m @ modes).T)
            tile = np.zeros((256, 256), ml_dtypes.bfloat16)
            tile[:half, :half] = high
            tile[half : half + KEPT, :half] = high[:KEPT]
            tile[half + KEPT : half + 2 * KEPT, :half] = low[:KEPT]
            tables[s, o] = tile
    return (
        np.stack(split(rotation)),
        back.astype(ml_dtypes.bfloat16),
        np.stack([np.stack([tables[s, o] for s in range(2)]) for o in offset_table()]),
    )


@functools.lru_cache(maxsize=None)
def plan():
    offsets = offset_table()
    entries, picks = [], []
    for c in range(2):
        for d in range(2):
            for o, (dx, dy) in enumerate(offsets):
                px, cs = divmod(c + dx, 2)
                py, ds = divmod(d + dy, 2)
                if abs(px) <= 1 and abs(py) <= 1:
                    entries.append((cs * 3 + px + 1) * 6 + ds * 3 + py + 1)
                    picks.append(o)
    return entries, picks


def flag_order():
    _, picks = plan()
    count = len(picks) // 4
    order = np.zeros((4, 128, 128), ml_dtypes.bfloat16)
    for i, o in enumerate(picks):
        order[i // count, o, i % count] = 1
    return order


def dot(a, b):
    return lax.dot_general(a, b, (((1,), (0,)), ((), ())), preferred_element_type=F32)


def dot_t(a, b):
    return lax.dot_general(a, b, (((1,), (1,)), ((), ())), preferred_element_type=F32)


def parts(x):
    high = x.astype(BF16)
    return high, (x - high.astype(F32)).astype(BF16)


def times(x, weight):
    xh, xl = parts(x)
    wh, wl = weight
    return dot(xh, wh) + (dot(xl, wh) + dot(xh, wl))


def times_t(x, weight):
    xh, xl = parts(x)
    wh, wl = weight
    return dot_t(xh, wh) + (dot_t(xl, wh) + dot_t(xh, wl))


def split_into(ref, x):
    ref[0], ref[1] = parts(x)
    return ref[0], ref[1]


def lanes(ref, *at):
    pieces = [ref[(t,) + at] for t in range(4)]
    pieces = [p.reshape(-1, 128) for p in pieces]
    return jnp.concatenate(pieces, axis=1)


def cut_tiles(dens):
    return [(t, slice(128 * t, min(128 * t + 128, dens)), slice(0, min(128, dens - 128 * t))) for t in range(4)]


def modes_of(x, rot_ref, dens):
    y = times(x[:, :dens], (rot_ref[0], rot_ref[1]))
    lane = lax.broadcasted_iota(jnp.int32, (1, 512), 1) % 256
    half = dens // 2
    is_low = (lane >= half) & (lane < half + KEPT)
    return jnp.where(is_low, y - y.astype(BF16).astype(F32), y)


def class_pairs():
    return [(c, d) for c in range(2) for d in range(2)]


def own_kernel(own_ref, rot_ref, up_hbm, pup_ref, modes_ref, upw_ref, own_t, up_v, sems):
    rows, cols, dens = own_ref.shape
    pr, pc = rows // 2, cols // 2
    copies = [pltpu.make_async_copy(up_hbm.at[n], up_v.at[n], sems.at[n]) for n in range(4)]
    for c in copies:
        c.start()
    y = modes_of(own_ref[...].reshape(rows * cols, dens), rot_ref, dens)
    for t, cut, to in cut_tiles(dens):
        modes_ref[t] = y[:, 128 * t : 128 * t + 128].reshape(rows, cols, 128)
        own_t[t, :, :, to] = own_ref[:, :, cut]
    parent = None
    for n, (c, d) in enumerate(class_pairs()):
        copies[n].wait()
        weight = split_into(upw_ref.at[n], up_v[n])
        x = jnp.concatenate(
            [
                jnp.concatenate(
                    [own_t[t, 2 * i + c, pl.ds(d, pc, stride=2), :] for i in range(pr)], axis=0
                )
                for t in range(4)
            ],
            axis=1,
        )
        part = times_t(x[:, :dens], weight)
        parent = part if parent is None else parent + part
    pup_ref[...] = parent.reshape(pr, pc, dens)


def side_kernel(
    even_ref, strip0_ref, strip1_ref, own_modes_ref, pup_ref, rot_ref, upw_ref,
    llist_ref, plist_ref, order_ref, down_hbm, inv_hbm,
    lut_hbm, edge_ref, pmodes_ref, flag_ref, downw_hbm, invw_hbm,
    strip_t, modes, flat, lut, down_v, inv_v, downw, invw, sems, out_sems,
):
    rows, _, dens = strip0_ref.shape
    cols = own_modes_ref.shape[2]
    pr, pc = rows // 2, cols // 2
    gr, gc = pr // 2, pc // 2
    used = pr * pc + gr * gc
    high = lut.shape[2]
    copies = [
        pltpu.make_async_copy(down_hbm, down_v, sems.at[0]),
        pltpu.make_async_copy(inv_hbm, inv_v, sems.at[1]),
    ]
    for c in copies:
        c.start()
    even = even_ref[1] == 1
    for t, cut, to in cut_tiles(dens):
        first, second = strip0_ref[:, :, cut], strip1_ref[:, :, cut]
        strip_t[t, :, 0:HALO, to] = jnp.where(even, second, first)
        strip_t[t, :, HALO:, to] = jnp.where(even, first, second)

    w = modes_of(lanes(strip_t), rot_ref, dens)
    parent = None
    for n, (c, d) in enumerate(class_pairs()):
        x = jnp.concatenate(
            [
                jnp.concatenate(
                    [strip_t[t, 2 * i + c, pl.ds(d, HALO, stride=2), :] for i in range(pr)], axis=0
                )
                for t in range(4)
            ],
            axis=1,
        )
        part = times_t(x[:, :dens], (upw_ref[n, 0], upw_ref[n, 1]))
        parent = part if parent is None else parent + part
    p = modes_of(
        jnp.concatenate([pup_ref[...].reshape(pr * pc, dens), parent], axis=0), rot_ref, dens
    )
    for t in range(4):
        cut = slice(128 * t, 128 * t + 128)
        modes[t, 2 : 2 + rows, 8 : 8 + cols, :] = own_modes_ref[t]
        strip = w[:, cut].reshape(rows, 8, 128)
        modes[t, 2 : 2 + rows, 4:8, :] = strip[:, 0:4]
        modes[t, 2 : 2 + rows, 8 + cols : 12 + cols, :] = strip[:, 4:8]
        edge_ref[t, 0:2] = modes[t, 2:4]
        edge_ref[t, 2:4] = modes[t, rows : rows + 2]
        pmodes_ref[t, 2 : 2 + pr, 4 : 4 + pc, :] = p[: pr * pc, cut].reshape(pr, pc, 128)
        strip = p[pr * pc :, cut].reshape(pr, 4, 128)
        pmodes_ref[t, 2 : 2 + pr, 2:4, :] = strip[:, 0:2]
        pmodes_ref[t, 2 : 2 + pr, 4 + pc : 6 + pc, :] = strip[:, 2:4]

    def gather(i, carry):
        base = 2 * (i % 3) + i // 3
        for ds in range(2):
            for py in (-1, 0, 1):
                e = i * 6 + ds * 3 + py + 1
                for t in range(4):
                    x = jnp.concatenate(
                        [
                            modes[t, base + 2 * j, pl.ds(8 + 2 * py + ds, pc, stride=2), :]
                            for j in range(pr)
                        ]
                        + [
                            pmodes_ref[t, base + 2 * j, pl.ds(4 + 2 * py + ds, gc, stride=2), :]
                            for j in range(gr)
                        ]
                        + [jnp.zeros((high - used, 128), F32)],
                        axis=0,
                    )
                    lut[e, t // 2, :, 128 * (t % 2) : 128 * (t % 2) + 128] = x.astype(BF16)
        return carry

    lax.fori_loop(0, 6, gather, 0)
    out = [pltpu.make_async_copy(lut, lut_hbm, out_sems.at[0])]
    out[0].start()

    copies[0].wait()
    copies[1].wait()
    for n in range(4):
        split_into(downw.at[n], down_v[n])
    split_into(invw, inv_v[...])
    out.append(pltpu.make_async_copy(downw, downw_hbm, out_sems.at[1]))
    out.append(pltpu.make_async_copy(invw, invw_hbm, out_sems.at[2]))
    out[1].start()
    out[2].start()

    flat[0, :, :, 0 : llist_ref.shape[2]] = llist_ref[...].astype(F32)
    flat[1, 0:pr, 0:pc, 0 : plist_ref.shape[2]] = plist_ref[...].astype(F32)
    listed = lax.broadcasted_iota(jnp.int32, (1, 128), 1) < llist_ref.shape[2]
    for n, (c, d) in enumerate(class_pairs()):
        flag = jnp.concatenate(
            [flat[0, 2 * i + c, pl.ds(d, pc, stride=2), :] for i in range(pr)]
            + [flat[1, 2 * i + c, pl.ds(d, gc, stride=2), :] for i in range(gr)]
            + [jnp.zeros((high - used, 128), F32)],
            axis=0,
        )
        flag_ref[n] = dot(jnp.where(listed, flag, 0.0).astype(BF16), order_ref[n])
    for c in out:
        c.wait()


def close_kernel(
    entry_ref, pick_ref, even_ref,
    end0_ref, end1_ref, edge_ref, pside_ref, rot_ref, upw_ref, pin_ref, flag_ref, back_ref, table,
    lut_hbm, downw_hbm, invw_hbm,
    out_ref,
    ends_t, edge, pmodes, lut, acc, flat, plocal, downw, invw, sems,
):
    rows, cols, dens = out_ref.shape
    pr, pc = rows // 2, cols // 2
    gr, gc = pr // 2, pc // 2
    boxes, pboxes = pr * pc, gr * gc
    high = lut.shape[2]
    wide = end0_ref.shape[1]
    count = entry_ref.shape[0] // 4
    copies = [
        pltpu.make_async_copy(src, dst, sems.at[i])
        for i, (src, dst) in enumerate(((lut_hbm, lut), (downw_hbm, downw), (invw_hbm, invw)))
    ]
    for c in copies:
        c.start()
    even = even_ref[0] == 1
    for t, cut, to in cut_tiles(dens):
        first, second = end0_ref[:, :, cut], end1_ref[:, :, cut]
        ends_t[t, 0:HALO, :, to] = jnp.where(even, second, first)
        ends_t[t, HALO:, :, to] = jnp.where(even, first, second)
    z = modes_of(lanes(ends_t, slice(HALO - 2, HALO + 2)), rot_ref, dens)
    parent = None
    for n, (c, d) in enumerate(class_pairs()):
        x = jnp.concatenate(
            [
                jnp.concatenate(
                    [ends_t[t, 2 * i + c, pl.ds(d, wide // 2, stride=2), :] for i in range(HALO)],
                    axis=0,
                )
                for t in range(4)
            ],
            axis=1,
        )
        part = times_t(x[:, :dens], (upw_ref[n, 0], upw_ref[n, 1]))
        parent = part if parent is None else parent + part
    p = modes_of(parent, rot_ref, dens)
    for t in range(4):
        cut = slice(128 * t, 128 * t + 128)
        end = z[:, cut].reshape(4, wide, 128)
        edge[t, 0:2, 4 : 4 + wide, :] = end[0:2]
        edge[t, 2:4] = edge_ref[t, 0:2]
        edge[t, 4:6] = edge_ref[t, 2:4]
        edge[t, 6:8, 4 : 4 + wide, :] = end[2:4]
        end = p[:, cut].reshape(4, wide // 2, 128)
        pmodes[t, 0:2, 2 : 2 + wide // 2, :] = end[0:2]
        pmodes[t, 2 : 2 + pr] = pside_ref[t, 2 : 2 + pr]
        pmodes[t, 2 + pr :, 2 : 2 + wide // 2, :] = end[2:4]

    copies[0].wait()

    def patch(cs, carry):
        for ds in range(2):
            for py in (-1, 0, 1):
                for t in range(4):
                    at = slice(128 * (t % 2), 128 * (t % 2) + 128)
                    mine = pl.ds(8 + 2 * py + ds, pc, stride=2)
                    theirs = pl.ds(4 + 2 * py + ds, gc, stride=2)
                    e = cs * 18 + ds * 3 + py + 1
                    x = jnp.concatenate([edge[t, cs + 2 * j, mine, :] for j in range(2)], axis=0)
                    lut[e, t // 2, 0:16, at] = x.astype(BF16)
                    x = jnp.concatenate([pmodes[t, cs + 2 * j, theirs, :] for j in range(4)], axis=0)
                    lut[e, t // 2, boxes : boxes + 16, at] = x.astype(BF16)
                    e = e + 12
                    x = jnp.concatenate([edge[t, 4 + cs + 2 * j, mine, :] for j in range(2)], axis=0)
                    lut[e, t // 2, boxes - 16 : boxes, at] = x.astype(BF16)
                    x = jnp.concatenate(
                        [pmodes[t, 4 + cs + 2 * j, theirs, :] for j in range(4, gr)]
                        + [jnp.zeros((high - boxes - pboxes, 128), F32)],
                        axis=0,
                    )
                    lut[e, t // 2, boxes + 16 : high, at] = x.astype(BF16)
        return carry

    lax.fori_loop(0, 2, patch, 0)

    def interact(j, carry):
        n, s = j // 2, j % 2
        total = jnp.zeros((high, 256), F32)
        flag = flag_ref[n]
        for k in range(count):
            i = n * count + k
            m = jnp.broadcast_to(flag[:, k : k + 1], (high, 128)).astype(BF16)
            x = lut[entry_ref[i], s]
            x = jnp.concatenate([x[:, :128] * m, x[:, 128:] * m], axis=1)
            total = total + dot(x, table[pick_ref[i], s])
        acc[s, n] = total
        return carry

    lax.fori_loop(0, 8, interact, 0)

    check = []
    for n in range(4):
        check_n = None
        for s in range(2):
            xh, xl = parts(acc[s, n])
            b = back_ref[256 * s : 256 * (s + 1)]
            part = dot(xh, b) + dot(xl, b)
            check_n = part if check_n is None else check_n + part
        check.append(check_n)

    copies[1].wait()
    copies[2].wait()
    inverse = (invw[0], invw[1])
    for n, (c, d) in enumerate(class_pairs()):
        for t, cut, to in cut_tiles(dens):
            for j in range(gr):
                plocal[t, 2 * j + c, pl.ds(d, gc, stride=2), to] = check[n][
                    boxes + gc * j : boxes + gc * (j + 1), cut
                ]
    local = pin_ref[...].reshape(boxes, dens) + times_t(lanes(plocal)[:, :dens], inverse)
    x = jnp.concatenate(
        [check[n][0:boxes] + times_t(local, (downw[n, 0], downw[n, 1])) for n in range(4)], axis=0
    )
    result = times_t(x, inverse)
    for n, (c, d) in enumerate(class_pairs()):
        for t, cut, to in cut_tiles(dens):
            for j in range(pr):
                r = boxes * n + pc * j
                flat[t, 2 * j + c, pl.ds(d, pc, stride=2), to] = result[r : r + pc, cut]
    for t, cut, to in cut_tiles(dens):
        out_ref[:, :, cut] = flat[t, :, :, to]


VMEM = pl.BlockSpec(memory_space=pltpu.VMEM)
HBM = pl.BlockSpec(memory_space=pl.ANY)
SMEM = pl.BlockSpec(memory_space=pltpu.SMEM)


def params(mib):
    return pltpu.CompilerParams(vmem_limit_bytes=mib * 1024 * 1024)


def cost(rows, tiles, reads):
    return pl.CostEstimate(flops=2 * rows * tiles * 256 * 256, bytes_accessed=reads, transcendentals=0)


def own_step(own, rotation, up):
    rows, cols, dens = own.shape
    return pl.pallas_call(
        own_kernel,
        out_shape=(
            jax.ShapeDtypeStruct((rows // 2, cols // 2, dens), F32),
            jax.ShapeDtypeStruct((4, rows, cols, 128), F32),
            jax.ShapeDtypeStruct((4, 2, dens, dens), BF16),
        ),
        in_specs=[VMEM, VMEM, HBM],
        out_specs=(VMEM,) * 3,
        scratch_shapes=[
            pltpu.VMEM((4, rows, cols, 128), F32),
            pltpu.VMEM(up.shape, F32),
            pltpu.SemaphoreType.DMA((4,)),
        ],
        compiler_params=params(24),
        cost_estimate=cost(rows * cols, 24, up.size * 4),
    )(own, rotation, up)


def side_step(even, strips, own_modes, pup, rotation, upw, llist, plist, order, down, inv):
    rows, cols = own_modes.shape[1:3]
    dens = pup.shape[2]
    pr, pc = rows // 2, cols // 2
    high = -(-(pr * pc * 5 // 4) // 16) * 16
    table = (36, 2, high, 256)
    return pl.pallas_call(
        side_kernel,
        out_shape=(
            jax.ShapeDtypeStruct(table, BF16),
            jax.ShapeDtypeStruct((4, 4, cols + 16, 128), F32),
            jax.ShapeDtypeStruct((4, pr + 4, pc + 8, 128), F32),
            jax.ShapeDtypeStruct((4, high, 128), F32),
            jax.ShapeDtypeStruct((4, 2, dens, dens), BF16),
            jax.ShapeDtypeStruct((2, dens, dens), BF16),
        ),
        in_specs=[SMEM] + [VMEM] * 9 + [HBM] * 2,
        out_specs=(HBM, VMEM, VMEM, VMEM, HBM, HBM),
        scratch_shapes=[
            pltpu.VMEM((4, rows, 8, 128), F32),
            pltpu.VMEM((4, rows + 4, cols + 16, 128), F32),
            pltpu.VMEM((2, rows, cols, 128), F32),
            pltpu.VMEM(table, BF16),
            pltpu.VMEM(down.shape, F32),
            pltpu.VMEM(inv.shape, F32),
            pltpu.VMEM((4, 2, dens, dens), BF16),
            pltpu.VMEM((2, dens, dens), BF16),
            pltpu.SemaphoreType.DMA((2,)),
            pltpu.SemaphoreType.DMA((3,)),
        ],
        compiler_params=params(32),
        cost_estimate=cost(rows * cols, 24, down.size * 8),
    )(even, *strips, own_modes, pup, rotation, upw, llist, plist, order, down, inv)


def close_step(even, ends, edge, pmodes, rotation, upw, pin, flags, back, table, lut, downw, invw, shape):
    rows, cols, dens = shape
    pr, pc = rows // 2, cols // 2
    entries, picks = plan()
    return pl.pallas_call(
        close_kernel,
        out_shape=jax.ShapeDtypeStruct(shape, F32),
        in_specs=[SMEM] * 3 + [VMEM] * 10 + [HBM] * 3,
        out_specs=VMEM,
        scratch_shapes=[
            pltpu.VMEM((4, 2 * HALO, cols + 2 * HALO, 128), F32),
            pltpu.VMEM((4, 8, cols + 16, 128), F32),
            pltpu.VMEM((4, pr + 4, pc + 8, 128), F32),
            pltpu.VMEM(lut.shape, BF16),
            pltpu.VMEM((2, 4, lut.shape[2], 256), F32),
            pltpu.VMEM((4, rows, cols, 128), F32),
            pltpu.VMEM((4, pr, pc, 128), F32),
            pltpu.VMEM(downw.shape, BF16),
            pltpu.VMEM(invw.shape, BF16),
            pltpu.SemaphoreType.DMA((3,)),
        ],
        compiler_params=params(40),
        cost_estimate=cost(rows * cols, 150, table.size * 2),
    )(
        jnp.asarray(entries, jnp.int32), jnp.asarray(picks, jnp.int32), even,
        *ends, edge, pmodes, rotation, upw, pin, flags, back, table, lut, downw, invw,
    )


def swapped(low, high, axis, odd_first):
    peers = lax.axis_size(axis)
    even = lax.axis_index(axis) % 2 == 0
    strips = (jnp.where(even, high, low), jnp.where(even, low, high))
    got = [None, None]
    for kind in (1, 0) if odd_first else (0, 1):
        pairs = [(i, i + 1) for i in range(kind, peers - 1, 2)]
        got[kind] = lax.ppermute(strips[kind], axis, pairs + [(j, i) for i, j in pairs])
    return got


def local(leaf_up, parent_in, leaf_lists, parent_lists, up_transfer, down_transfer, check_inverse):
    rows, cols, _ = leaf_up.shape
    even = [lax.axis_index(axis) % 2 == 0 for axis in ("gx", "gy")]
    flag = jnp.stack(even).astype(jnp.int32)
    rotation, back, table = (jnp.asarray(x) for x in operators())
    order = jnp.asarray(flag_order())
    strips = swapped(leaf_up[:, :HALO], leaf_up[:, cols - HALO :], "gy", True)
    parent_up, own_modes, upw = own_step(leaf_up, rotation, up_transfer)
    left = jnp.where(even[1], strips[1], strips[0])
    right = jnp.where(even[1], strips[0], strips[1])
    broad = lambda s: jnp.concatenate([left[s], leaf_up[s], right[s]], axis=1)
    ends = swapped(broad(slice(0, HALO)), broad(slice(rows - HALO, rows)), "gx", False)
    lut, edge, pmodes, flags, downw, invw = side_step(
        flag, strips, own_modes, parent_up, rotation, upw, leaf_lists, parent_lists, order,
        down_transfer, check_inverse,
    )
    leaf_down = close_step(
        flag, ends, edge, pmodes, rotation, upw, parent_in, flags, back, table, lut, downw, invw,
        leaf_up.shape,
    )
    return leaf_down, parent_up


def solution(mesh):
    block = P("gx", "gy", None)
    return jax.shard_map(
        local,
        mesh=mesh,
        in_specs=(block,) * 4 + (P(),) * 3,
        out_specs=(block, block),
        check_vma=False,
    )
```

```python
import functools
import math

import jax
import jax.numpy as jnp
import ml_dtypes
import numpy as np
from jax import lax
from jax.experimental import pallas as pl
from jax.experimental.pallas import tpu as pltpu
from jax.sharding import PartitionSpec as P

ORDER = 6
HALO = 4
KEPT = 14
BF16, F32 = jnp.bfloat16, jnp.float32

INNER = [(a, b) for a in range(-2, 3) for b in range(-2, 3) if max(abs(a), abs(b)) == 2]
SIDES = (
    [(3, b) for b in range(-2, 3)],
    [(-3, b) for b in range(-2, 3)],
    [(a, 3) for a in range(-2, 3)],
    [(a, -3) for a in range(-2, 3)],
)
SIDE_CLASSES = ((0, 1), (2, 3), (0, 2), (1, 3))
CORNERS = [(3, 3), (3, -3), (-3, 3), (-3, -3)]


def offset_table():
    return [(a, b) for a in range(-3, 4) for b in range(-3, 4) if max(abs(a), abs(b)) >= 2]


def surface_points():
    grid = np.linspace(-1.0, 1.0, ORDER)
    keys = [
        (i, j, k)
        for i in range(ORDER)
        for j in range(ORDER)
        for k in range(ORDER)
        if min(i, j, k) == 0 or max(i, j, k) == ORDER - 1
    ]
    return keys, np.array([[grid[i] for i in key] for key in keys])


def translation(points, dx, dy):
    r = 0.525 * (points[:, None, :] - points[None, :, :]) - np.array([dx, dy, 0.0])
    dist = np.sqrt((r * r).sum(-1))
    n = len(points)
    out = np.zeros((3, n, 3, n))
    for a in range(3):
        for b in range(3):
            out[a, :, b, :] = (float(a == b) / dist + r[..., a] * r[..., b] / dist**3) / (8 * math.pi)
    return out.reshape(3 * n, 3 * n)


def split(x):
    high = x.astype(ml_dtypes.bfloat16)
    return high, (x - high.astype(np.float64)).astype(ml_dtypes.bfloat16)


@functools.lru_cache(maxsize=None)
def operators():
    keys, points = surface_points()
    n = len(keys)
    place = {key: i for i, key in enumerate(keys)}
    mirror = [place[(i, j, ORDER - 1 - k)] for i, j, k in keys]
    mats = {o: translation(points, *o) for o in offset_table()}
    half = 3 * n // 2
    rotation = np.zeros((3 * n, 512), ml_dtypes.bfloat16)
    back = np.zeros((512, 3 * n))
    sequence = INNER + [o for side in SIDES for o in side] + CORNERS
    table = np.zeros((2, len(sequence), 256, 256), ml_dtypes.bfloat16)
    for s, sign in enumerate((1, -1)):
        pairs = np.zeros((3 * n, half))
        firsts = []
        for a in range(3):
            flip = sign if a < 2 else -sign
            for i in range(n):
                if i < mirror[i]:
                    pairs[a * n + i, len(firsts)] = 1.0
                    pairs[a * n + mirror[i], len(firsts)] = flip
                    firsts.append(a * n + i)
        blocks = {o: 0.25 * pairs.T @ m @ pairs for o, m in mats.items()}
        gram = sum((1 + 0.05 * o[0] + 0.02 * o[1]) * b.T @ b for o, b in blocks.items())
        _, vecs = np.linalg.eigh(gram)
        vecs = vecs[:, ::-1]
        vecs = vecs * np.sign(vecs[np.abs(vecs).argmax(0), np.arange(half)])
        modes = (pairs @ vecs / math.sqrt(2.0)).astype(ml_dtypes.bfloat16)
        rotation[:, 256 * s : 256 * s + half] = modes
        rotation[:, 256 * s + half : 256 * s + half + KEPT] = modes[:, :KEPT]
        rotation[:, 256 * s + half + KEPT : 256 * s + half + 2 * KEPT] = modes[:, :KEPT]
        back[256 * s : 256 * s + half] = pairs.T
        undo = np.linalg.inv(modes[firsts].astype(np.float64))
        for q, o in enumerate(sequence):
            high, low = split(undo @ blocks[o].T)
            table[s, q, :half, :half] = high
            table[s, q, half : half + KEPT, :half] = high[:KEPT]
            table[s, q, half + KEPT : half + 2 * KEPT, :half] = low[:KEPT]
    return rotation, back.astype(ml_dtypes.bfloat16), table.reshape(2, -1, 256)


@functools.lru_cache(maxsize=None)
def plan():
    offsets = offset_table()
    picks = [(n, o) for o in INNER for n in range(4)]
    picks += [(n, o) for side, ns in zip(SIDES, SIDE_CLASSES) for o in side for n in ns]
    picks += list(enumerate(CORNERS))
    products = []
    for n, (dx, dy) in picks:
        px, cs = divmod(n // 2 + dx, 2)
        py, ds = divmod(n % 2 + dy, 2)
        products.append((n, offsets.index((dx, dy)), (cs * 3 + px + 1) * 6 + ds * 3 + py + 1))
    return products


def dot(a, b):
    return lax.dot_general(a, b, (((1,), (0,)), ((), ())), preferred_element_type=F32)


def dot_t(a, b):
    return lax.dot_general(a, b, (((1,), (1,)), ((), ())), preferred_element_type=F32)


def parts(x):
    high = x.astype(BF16)
    return high, (x - high.astype(F32)).astype(BF16)


def times_t(x, weight):
    xh, xl = parts(x)
    wh, wl = weight
    return dot_t(xh, wh) + (dot_t(xl, wh) + dot_t(xh, wl))


def lanes(ref, *at):
    pieces = [ref[(t,) + at] for t in range(4)]
    pieces = [p.reshape(-1, 128) for p in pieces]
    return jnp.concatenate(pieces, axis=1)


def cut_tiles(dens):
    return [(t, slice(128 * t, min(128 * t + 128, dens)), slice(0, min(128, dens - 128 * t))) for t in range(4)]


def modes_of(x, rot_ref, dens):
    xh, xl = parts(x[:, :dens])
    y = dot(xh, rot_ref[...]) + dot(xl, rot_ref[...])
    lane = lax.broadcasted_iota(jnp.int32, (1, 512), 1) % 256
    half = dens // 2
    is_low = (lane >= half) & (lane < half + KEPT)
    return jnp.where(is_low, y - y.astype(BF16).astype(F32), y)


def class_pairs():
    return [(c, d) for c in range(2) for d in range(2)]


def own_kernel(
    own_ref, rot_ref, llist_ref, plist_ref, up_hbm, down_hbm, inv_hbm,
    modes_ref, masks_ref, upw_ref, downw_ref, invw_ref,
    flat, weights, sems,
):
    rows, cols, dens = own_ref.shape
    pr, pc = rows // 2, cols // 2
    gr, gc = pr // 2, pc // 2
    used = pr * pc + gr * gc
    high = masks_ref.shape[1]
    sources = [up_hbm.at[n] for n in range(4)] + [down_hbm.at[n] for n in range(4)] + [inv_hbm]
    copies = [
        pltpu.make_async_copy(src, weights.at[n], sems.at[n]) for n, src in enumerate(sources)
    ]
    for c in copies:
        c.start()
    y = modes_of(own_ref[...].reshape(rows * cols, dens), rot_ref, dens)
    for t in range(4):
        modes_ref[t] = y[:, 128 * t : 128 * t + 128].reshape(rows, cols, 128)

    flat[0, :, :, 0 : llist_ref.shape[2]] = llist_ref[...].astype(F32)
    flat[1, 0:pr, 0:pc, 0 : plist_ref.shape[2]] = plist_ref[...].astype(F32)
    flags = [
        jnp.concatenate(
            [flat[0, 2 * i + c, pl.ds(d, pc, stride=2), :] for i in range(pr)]
            + [flat[1, 2 * i + c, pl.ds(d, gc, stride=2), :] for i in range(gr)]
            + [jnp.zeros((high - used, 128), F32)],
            axis=0,
        )
        for c, d in class_pairs()
    ]
    for i, (n, o, _) in enumerate(plan()):
        masks_ref[i] = jnp.broadcast_to(flags[n][:, o : o + 1], (high, 128)).astype(BF16)

    for n in range(9):
        copies[n].wait()
        target = (upw_ref.at[n] if n < 4 else downw_ref.at[n - 4]) if n < 8 else invw_ref
        target[0], target[1] = parts(weights[n])


def children(ref, dens, counts, c, d):
    return jnp.concatenate(
        [
            jnp.concatenate(
                [ref[t, 2 * i + c, pl.ds(d, counts[1], stride=2), :] for i in range(counts[0])],
                axis=0,
            )
            for t in range(4)
        ],
        axis=1,
    )[:, :dens]


def side_kernel(
    even_ref, strip0_ref, strip1_ref, own_ref, own_modes_ref, rot_ref, upw_ref,
    pup_ref, lut, edge_ref, pmodes_ref,
    own_t, strip_t, modes,
):
    rows, cols, dens = own_ref.shape
    pr, pc = rows // 2, cols // 2
    gr, gc = pr // 2, pc // 2
    boxes = pr * pc
    used = boxes + gr * gc
    high = lut.shape[2]
    even = even_ref[1] == 1
    for t, cut, to in cut_tiles(dens):
        own_t[t, :, :, to] = own_ref[:, :, cut]
        first, second = strip0_ref[:, :, cut], strip1_ref[:, :, cut]
        strip_t[t, :, 0:HALO, to] = jnp.where(even, second, first)
        strip_t[t, :, HALO:, to] = jnp.where(even, first, second)

    parent = None
    for n, (c, d) in enumerate(class_pairs()):
        x = jnp.concatenate(
            [children(own_t, dens, (pr, pc), c, d), children(strip_t, dens, (pr, HALO), c, d)],
            axis=0,
        )
        part = times_t(x, (upw_ref[n, 0], upw_ref[n, 1]))
        parent = part if parent is None else parent + part
    pup_ref[...] = parent[:boxes].reshape(pr, pc, dens)
    y = modes_of(jnp.concatenate([lanes(strip_t)[:, :dens], parent], axis=0), rot_ref, dens)
    w, p = y[: rows * 8], y[rows * 8 :]
    for t in range(4):
        cut = slice(128 * t, 128 * t + 128)
        modes[t, 2 : 2 + rows, 8 : 8 + cols, :] = own_modes_ref[t]
        strip = w[:, cut].reshape(rows, 8, 128)
        modes[t, 2 : 2 + rows, 4:8, :] = strip[:, 0:4]
        modes[t, 2 : 2 + rows, 8 + cols : 12 + cols, :] = strip[:, 4:8]
        edge_ref[t, 0:2] = modes[t, 2:4]
        edge_ref[t, 2:4] = modes[t, rows : rows + 2]
        pmodes_ref[t, 2 : 2 + pr, 4 : 4 + pc, :] = p[:boxes, cut].reshape(pr, pc, 128)
        strip = p[boxes:, cut].reshape(pr, 4, 128)
        pmodes_ref[t, 2 : 2 + pr, 2:4, :] = strip[:, 0:2]
        pmodes_ref[t, 2 : 2 + pr, 4 + pc : 6 + pc, :] = strip[:, 2:4]

    def gather(i, carry):
        base = 2 * (i % 3) + i // 3
        for ds in range(2):
            for py in (-1, 0, 1):
                e = i * 6 + ds * 3 + py + 1
                for t in range(4):
                    x = jnp.concatenate(
                        [
                            modes[t, base + 2 * j, pl.ds(8 + 2 * py + ds, pc, stride=2), :]
                            for j in range(pr)
                        ]
                        + [
                            pmodes_ref[t, base + 2 * j, pl.ds(4 + 2 * py + ds, gc, stride=2), :]
                            for j in range(gr)
                        ]
                        + [jnp.zeros((high - used, 128), F32)],
                        axis=0,
                    )
                    lut[e, t // 2, :, 128 * (t % 2) : 128 * (t % 2) + 128] = x.astype(BF16)
        return carry

    lax.fori_loop(0, 6, gather, 0)


def close_kernel(
    entry_ref, side_ref, even_ref,
    end0_ref, end1_ref, edge_ref, pside_ref, rot_ref, upw_ref, pin_ref, masks, back_ref,
    lut_ref, downw, invw, table_hbm,
    out_ref,
    ends_t, edge, pmodes, lut, acc, flat, plocal, table, sem, table_sems,
):
    rows, cols, dens = out_ref.shape
    pr, pc = rows // 2, cols // 2
    gr, gc = pr // 2, pc // 2
    boxes, pboxes = pr * pc, gr * gc
    high = lut.shape[2]
    wide = end0_ref.shape[1]
    copy = pltpu.make_async_copy(lut_ref, lut, sem)
    copy.start()
    inner, side, corner = len(INNER), len(SIDES[0]), len(CORNERS)

    def piece(i, at, depth):
        rows = pl.ds(at if isinstance(at, int) else pl.multiple_of(at, 256), depth)
        return pltpu.make_async_copy(
            table_hbm.at[:, rows, :], table.at[:, rows, :], table_sems.at[i]
        )

    def inner_piece(g):
        return piece(g, 1024 * g, 1024)

    def side_piece(g):
        return piece(inner // 4 + g, 256 * (inner + side * g), 256 * side)

    corner_piece = piece(
        inner // 4 + len(SIDES), 256 * (inner + side * len(SIDES)), 256 * corner
    )
    for g in range(inner // 4):
        inner_piece(g).start()
    for g in range(len(SIDES)):
        side_piece(g).start()
    corner_piece.start()
    even = even_ref[0] == 1
    for t, cut, to in cut_tiles(dens):
        first, second = end0_ref[:, :, cut], end1_ref[:, :, cut]
        ends_t[t, 0:HALO, :, to] = jnp.where(even, second, first)
        ends_t[t, HALO:, :, to] = jnp.where(even, first, second)
    parent = None
    for n, (c, d) in enumerate(class_pairs()):
        x = children(ends_t, dens, (HALO, wide // 2), c, d)
        part = times_t(x, (upw_ref[n, 0], upw_ref[n, 1]))
        parent = part if parent is None else parent + part
    x = lanes(ends_t, slice(HALO - 2, HALO + 2))[:, :dens]
    y = modes_of(jnp.concatenate([x, parent], axis=0), rot_ref, dens)
    z, p = y[: 4 * wide], y[4 * wide :]
    for t in range(4):
        cut = slice(128 * t, 128 * t + 128)
        end = z[:, cut].reshape(4, wide, 128)
        edge[t, 0:2, 4 : 4 + wide, :] = end[0:2]
        edge[t, 2:4] = edge_ref[t, 0:2]
        edge[t, 4:6] = edge_ref[t, 2:4]
        edge[t, 6:8, 4 : 4 + wide, :] = end[2:4]
        end = p[:, cut].reshape(4, wide // 2, 128)
        pmodes[t, 0:2, 2 : 2 + wide // 2, :] = end[0:2]
        pmodes[t, 2 : 2 + pr] = pside_ref[t, 2 : 2 + pr]
        pmodes[t, 2 + pr :, 2 : 2 + wide // 2, :] = end[2:4]

    copy.wait()

    def patch(cs, carry):
        for ds in range(2):
            for py in (-1, 0, 1):
                for t in range(4):
                    at = slice(128 * (t % 2), 128 * (t % 2) + 128)
                    mine = pl.ds(8 + 2 * py + ds, pc, stride=2)
                    theirs = pl.ds(4 + 2 * py + ds, gc, stride=2)
                    e = cs * 18 + ds * 3 + py + 1
                    x = jnp.concatenate([edge[t, cs + 2 * j, mine, :] for j in range(2)], axis=0)
                    lut[e, t // 2, 0:16, at] = x.astype(BF16)
                    x = jnp.concatenate([pmodes[t, cs + 2 * j, theirs, :] for j in range(4)], axis=0)
                    lut[e, t // 2, boxes : boxes + 16, at] = x.astype(BF16)
                    e = e + 12
                    x = jnp.concatenate([edge[t, 4 + cs + 2 * j, mine, :] for j in range(2)], axis=0)
                    lut[e, t // 2, boxes - 16 : boxes, at] = x.astype(BF16)
                    x = jnp.concatenate(
                        [pmodes[t, 4 + cs + 2 * j, theirs, :] for j in range(4, gr)]
                        + [jnp.zeros((high - boxes - pboxes, 128), F32)],
                        axis=0,
                    )
                    lut[e, t // 2, boxes + 16 : high, at] = x.astype(BF16)
        return carry

    lax.fori_loop(0, 2, patch, 0)

    def listed(i, s):
        m = masks[i]
        x = lut[entry_ref[i], s]
        return jnp.concatenate([x[:, :128] * m, x[:, 128:] * m], axis=1)

    acc[...] = jnp.zeros_like(acc)

    def inner_part(g, carry):
        inner_piece(g).wait()
        for s in range(2):
            x = jnp.concatenate(
                [
                    jnp.concatenate([listed((4 * g + k) * 4 + n, s) for k in range(4)], axis=1)
                    for n in range(4)
                ],
                axis=0,
            )
            acc[s] += dot(x, table[s, pl.ds(pl.multiple_of(1024 * g, 1024), 1024), :])
        return carry

    lax.fori_loop(0, inner // 4, inner_part, 0)

    def side_part(g, carry):
        side_piece(g).wait()
        for s in range(2):
            first = 4 * inner + 2 * side * g
            x = jnp.concatenate(
                [
                    jnp.concatenate([listed(first + 2 * k + j, s) for k in range(side)], axis=1)
                    for j in range(2)
                ],
                axis=0,
            )
            at = pl.multiple_of(256 * (inner + side * g), 256)
            r = dot(x, table[s, pl.ds(at, 256 * side), :])
            for j in range(2):
                to = pl.ds(pl.multiple_of(side_ref[2 * g + j] * high, high), high)
                acc[s, to, :] += r[high * j : high * (j + 1)]
        return carry

    lax.fori_loop(0, len(SIDES), side_part, 0)
    corner_piece.wait()
    for n in range(corner):
        for s in range(2):
            at = 256 * (inner + len(SIDES) * side + n)
            x = listed(4 * inner + 2 * side * len(SIDES) + n, s)
            acc[s, high * n : high * (n + 1), :] += dot(x, table[s, at : at + 256, :])

    check = None
    for s in range(2):
        xh, xl = parts(acc[s])
        b = back_ref[256 * s : 256 * (s + 1)]
        part = dot(xh, b) + dot(xl, b)
        check = part if check is None else check + part

    inverse = (invw[0], invw[1])
    for n, (c, d) in enumerate(class_pairs()):
        for t, cut, to in cut_tiles(dens):
            for j in range(gr):
                r = high * n + boxes + gc * j
                plocal[t, 2 * j + c, pl.ds(d, gc, stride=2), to] = check[r : r + gc, cut]
    local = pin_ref[...].reshape(boxes, dens) + times_t(lanes(plocal)[:, :dens], inverse)
    x = jnp.concatenate(
        [
            check[high * n : high * n + boxes] + times_t(local, (downw[n, 0], downw[n, 1]))
            for n in range(4)
        ],
        axis=0,
    )
    result = times_t(x, inverse)
    for n, (c, d) in enumerate(class_pairs()):
        for t, cut, to in cut_tiles(dens):
            for j in range(pr):
                r = boxes * n + pc * j
                flat[t, 2 * j + c, pl.ds(d, pc, stride=2), to] = result[r : r + pc, cut]
    for t, cut, to in cut_tiles(dens):
        out_ref[:, :, cut] = flat[t, :, :, to]


VMEM = pl.BlockSpec(memory_space=pltpu.VMEM)
HBM = pl.BlockSpec(memory_space=pl.ANY)
SMEM = pl.BlockSpec(memory_space=pltpu.SMEM)


def params(mib):
    return pltpu.CompilerParams(vmem_limit_bytes=mib * 1024 * 1024)


def cost(rows, tiles, reads):
    return pl.CostEstimate(flops=2 * rows * tiles * 256 * 256, bytes_accessed=reads, transcendentals=0)


def own_step(own, rotation, llist, plist, up, down, inv):
    rows, cols, dens = own.shape
    pr, pc = rows // 2, cols // 2
    high = -(-(pr * pc * 5 // 4) // 16) * 16
    return pl.pallas_call(
        own_kernel,
        out_shape=(
            jax.ShapeDtypeStruct((4, rows, cols, 128), F32),
            jax.ShapeDtypeStruct((len(plan()), high, 128), BF16),
            jax.ShapeDtypeStruct((4, 2, dens, dens), BF16),
            jax.ShapeDtypeStruct((4, 2, dens, dens), BF16),
            jax.ShapeDtypeStruct((2, dens, dens), BF16),
        ),
        in_specs=[VMEM] * 4 + [HBM] * 3,
        out_specs=(VMEM,) * 5,
        scratch_shapes=[
            pltpu.VMEM((2, rows, cols, 128), F32),
            pltpu.VMEM((9, dens, dens), F32),
            pltpu.SemaphoreType.DMA((9,)),
        ],
        compiler_params=params(22),
        cost_estimate=cost(rows * cols, 24, up.size * 4),
    )(own, rotation, llist, plist, up, down, inv)


def side_step(even, strips, own, own_modes, rotation, upw):
    rows, cols, dens = own.shape
    pr, pc = rows // 2, cols // 2
    high = -(-(pr * pc * 5 // 4) // 16) * 16
    return pl.pallas_call(
        side_kernel,
        out_shape=(
            jax.ShapeDtypeStruct((pr, pc, dens), F32),
            jax.ShapeDtypeStruct((36, 2, high, 256), BF16),
            jax.ShapeDtypeStruct((4, 4, cols + 16, 128), F32),
            jax.ShapeDtypeStruct((4, pr + 4, pc + 8, 128), F32),
        ),
        in_specs=[SMEM] + [VMEM] * 6,
        out_specs=(VMEM,) * 4,
        scratch_shapes=[
            pltpu.VMEM((4, rows, cols, 128), F32),
            pltpu.VMEM((4, rows, 8, 128), F32),
            pltpu.VMEM((4, rows + 4, cols + 16, 128), F32),
        ],
        compiler_params=params(16),
        cost_estimate=cost(rows * cols, 24, upw.size * 2),
    )(even, *strips, own, own_modes, rotation, upw)


def close_step(even, ends, edge, pmodes, rotation, upw, pin, masks, back, table, lut, downw, invw, shape):
    rows, cols, dens = shape
    pr, pc = rows // 2, cols // 2
    return pl.pallas_call(
        close_kernel,
        out_shape=jax.ShapeDtypeStruct(shape, F32),
        in_specs=[SMEM] * 3 + [VMEM] * 12 + [HBM],
        out_specs=VMEM,
        scratch_shapes=[
            pltpu.VMEM((4, 2 * HALO, cols + 2 * HALO, 128), F32),
            pltpu.VMEM((4, 8, cols + 16, 128), F32),
            pltpu.VMEM((4, pr + 4, pc + 8, 128), F32),
            pltpu.VMEM(lut.shape, BF16),
            pltpu.VMEM((2, 4 * lut.shape[2], 256), F32),
            pltpu.VMEM((4, rows, cols, 128), F32),
            pltpu.VMEM((4, pr, pc, 128), F32),
            pltpu.VMEM(table.shape, BF16),
            pltpu.SemaphoreType.DMA,
            pltpu.SemaphoreType.DMA((len(INNER) // 4 + len(SIDES) + 1,)),
        ],
        compiler_params=params(36),
        cost_estimate=cost(rows * cols, 150, table.size * 2),
    )(
        jnp.asarray([e for _, _, e in plan()], jnp.int32),
        jnp.asarray([n for pair in SIDE_CLASSES for n in pair], jnp.int32), even,
        *ends, edge, pmodes, rotation, upw, pin, masks, back, lut, downw, invw, table,
    )


def swapped(low, high, axis, odd_first):
    peers = lax.axis_size(axis)
    even = lax.axis_index(axis) % 2 == 0
    strips = (jnp.where(even, high, low), jnp.where(even, low, high))
    got = [None, None]
    for kind in (1, 0) if odd_first else (0, 1):
        pairs = [(i, i + 1) for i in range(kind, peers - 1, 2)]
        got[kind] = lax.ppermute(strips[kind], axis, pairs + [(j, i) for i, j in pairs])
    return got


def local(leaf_up, parent_in, leaf_lists, parent_lists, up_transfer, down_transfer, check_inverse):
    rows, cols, _ = leaf_up.shape
    even = [lax.axis_index(axis) % 2 == 0 for axis in ("gx", "gy")]
    flag = jnp.stack(even).astype(jnp.int32)
    rotation, back, table = (jnp.asarray(x) for x in operators())
    strips = swapped(leaf_up[:, :HALO], leaf_up[:, cols - HALO :], "gy", True)
    own_modes, masks, upw, downw, invw = own_step(
        leaf_up, rotation, leaf_lists, parent_lists, up_transfer, down_transfer, check_inverse
    )
    left = jnp.where(even[1], strips[1], strips[0])
    right = jnp.where(even[1], strips[0], strips[1])
    broad = lambda s: jnp.concatenate([left[s], leaf_up[s], right[s]], axis=1)
    ends = swapped(broad(slice(0, HALO)), broad(slice(rows - HALO, rows)), "gx", False)
    parent_up, lut, edge, pmodes = side_step(flag, strips, leaf_up, own_modes, rotation, upw)
    leaf_down = close_step(
        flag, ends, edge, pmodes, rotation, upw, parent_in, masks, back, table, lut, downw, invw,
        leaf_up.shape,
    )
    return leaf_down, parent_up


def solution(mesh):
    block = P("gx", "gy", None)
    return jax.shard_map(
        local,
        mesh=mesh,
        in_specs=(block,) * 4 + (P(),) * 3,
        out_specs=(block, block),
        check_vma=False,
    )
```

```python
import functools
import math

import jax
import jax.numpy as jnp
import ml_dtypes
import numpy as np
from jax import lax
from jax.experimental import pallas as pl
from jax.experimental.pallas import tpu as pltpu
from jax.sharding import PartitionSpec as P

ORDER = 6
HALO = 4
KEPT = 14
BF16, F32 = jnp.bfloat16, jnp.float32

INNER = [(a, b) for a in range(-2, 3) for b in range(-2, 3) if max(abs(a), abs(b)) == 2]
SIDES = (
    [(3, b) for b in range(-2, 3)],
    [(-3, b) for b in range(-2, 3)],
    [(a, 3) for a in range(-2, 3)],
    [(a, -3) for a in range(-2, 3)],
)
SIDE_CLASSES = ((0, 1), (2, 3), (0, 2), (1, 3))
CORNERS = [(3, 3), (3, -3), (-3, 3), (-3, -3)]
SEQUENCE = INNER + [o for side in SIDES for o in side] + CORNERS
BASES = sorted({(abs(a), abs(b)) for a, b in SEQUENCE})


def offset_table():
    return [(a, b) for a in range(-3, 4) for b in range(-3, 4) if max(abs(a), abs(b)) >= 2]


def surface_points():
    grid = np.linspace(-1.0, 1.0, ORDER)
    keys = [
        (i, j, k)
        for i in range(ORDER)
        for j in range(ORDER)
        for k in range(ORDER)
        if min(i, j, k) == 0 or max(i, j, k) == ORDER - 1
    ]
    return keys, np.array([[grid[i] for i in key] for key in keys])


def translation(points, dx, dy):
    r = 0.525 * (points[:, None, :] - points[None, :, :]) - np.array([dx, dy, 0.0])
    dist = np.sqrt((r * r).sum(-1))
    n = len(points)
    out = np.zeros((3, n, 3, n))
    for a in range(3):
        for b in range(3):
            out[a, :, b, :] = (float(a == b) / dist + r[..., a] * r[..., b] / dist**3) / (8 * math.pi)
    return out.reshape(3 * n, 3 * n)


def split(x):
    high = x.astype(ml_dtypes.bfloat16)
    return high, (x - high.astype(np.float64)).astype(ml_dtypes.bfloat16)


@functools.lru_cache(maxsize=None)
def operators():
    keys, points = surface_points()
    n = len(keys)
    points_of = {key: i for i, key in enumerate(keys)}
    mirror = [points_of[(i, j, ORDER - 1 - k)] for i, j, k in keys]
    mats = {o: translation(points, *o) for o in offset_table()}
    half = 3 * n // 2
    rotation = np.zeros((3 * n, 512), ml_dtypes.bfloat16)
    back = np.zeros((512, 3 * n))
    table = np.zeros((2, len(BASES), 256, 256), ml_dtypes.bfloat16)
    signs = np.ones((4, 2, 256, 256), ml_dtypes.bfloat16)
    for s, sign in enumerate((1, -1)):
        pairs = np.zeros((3 * n, half))
        firsts = []
        for a in range(3):
            flip = sign if a < 2 else -sign
            for i in range(n):
                if i < mirror[i]:
                    pairs[a * n + i, len(firsts)] = 1.0
                    pairs[a * n + mirror[i], len(firsts)] = flip
                    firsts.append(a * n + i)
        blocks = {o: 0.25 * pairs.T @ m @ pairs for o, m in mats.items()}
        gram = sum(b.T @ b for b in blocks.values())
        place = {f: i for i, f in enumerate(firsts)}
        modes, parity, weight = [], [], []
        for sx in (1, -1):
            for sy in (1, -1):
                basis = []
                for i, f in enumerate(firsts):
                    a, (kx, ky, kz) = f // n, keys[f % n]
                    if kx < ORDER // 2 and ky < ORDER // 2:
                        v = np.zeros(half)
                        for fx in range(2):
                            for fy in range(2):
                                key = (ORDER - 1 - kx if fx else kx, ORDER - 1 - ky if fy else ky, kz)
                                sign_x = (sx if a != 0 else -sx) if fx else 1
                                sign_y = (sy if a != 1 else -sy) if fy else 1
                                v[place[a * n + points_of[key]]] = 0.5 * sign_x * sign_y
                        basis.append(v)
                basis = np.array(basis).T
                w, vecs = np.linalg.eigh(basis.T @ gram @ basis)
                vecs = basis @ vecs
                vecs = vecs * np.sign(vecs[np.abs(np.round(vecs, 9)).argmax(0), np.arange(len(w))])
                modes.append(vecs)
                weight.append(w)
                parity += [(sx, sy)] * len(w)
        order = np.argsort(-np.concatenate(weight), kind="stable")
        vecs = np.concatenate(modes, axis=1)[:, order]
        parity = np.array(parity)[order]
        modes = (pairs @ vecs / math.sqrt(2.0)).astype(ml_dtypes.bfloat16)
        lows = np.concatenate([modes, modes[:, :KEPT], modes[:, :KEPT]], axis=1)
        rotation[:, 256 * s : 256 * (s + 1)] = lows
        outs, out_parity = [], []
        for sx in (1, -1):
            for sy in (1, -1):
                for f in firsts:
                    a, (kx, ky, kz) = f // n, keys[f % n]
                    if kx < ORDER // 2 and ky < ORDER // 2:
                        v = np.zeros(half)
                        for fx in range(2):
                            for fy in range(2):
                                key = (ORDER - 1 - kx if fx else kx, ORDER - 1 - ky if fy else ky, kz)
                                sign_x = (sx if a != 0 else -sx) if fx else 1
                                sign_y = (sy if a != 1 else -sy) if fy else 1
                                v[place[a * n + points_of[key]]] = sign_x * sign_y
                        outs.append(v)
                        out_parity.append((sx, sy))
        outs = np.array(outs).T
        out_parity = np.array(out_parity)
        back[256 * s : 256 * s + half] = (pairs @ outs).T
        undo = np.linalg.inv(modes[firsts].astype(np.float64))
        for q, o in enumerate(BASES):
            high, low = split(undo @ blocks[o].T @ outs * 0.25)
            table[s, q, :half, :half] = high
            table[s, q, half : half + KEPT, :half] = high[:KEPT]
            table[s, q, half + KEPT : half + 2 * KEPT, :half] = low[:KEPT]
        ins = np.concatenate([parity, parity[:KEPT], parity[:KEPT]], axis=0)
        for f in range(4):
            row = np.ones(256)
            row[: len(ins)] = (ins[:, 0] if f // 2 else 1) * (ins[:, 1] if f % 2 else 1)
            col = np.ones(256)
            col[:half] = (out_parity[:, 0] if f // 2 else 1) * (out_parity[:, 1] if f % 2 else 1)
            signs[f, s] = row[:, None] * col[None, :]
    return rotation, back.astype(ml_dtypes.bfloat16), table, signs


@functools.lru_cache(maxsize=None)
def plan():
    offsets = offset_table()
    picks = [(n, o) for o in INNER for n in range(4)]
    picks += [(n, o) for side, ns in zip(SIDES, SIDE_CLASSES) for o in side for n in ns]
    picks += list(enumerate(CORNERS))
    products = []
    for n, (dx, dy) in picks:
        px, cs = divmod(n // 2 + dx, 2)
        py, ds = divmod(n % 2 + dy, 2)
        products.append((n, offsets.index((dx, dy)), (cs * 3 + px + 1) * 6 + ds * 3 + py + 1))
    return products


def dot(a, b):
    return lax.dot_general(a, b, (((1,), (0,)), ((), ())), preferred_element_type=F32)


def dot_t(a, b):
    return lax.dot_general(a, b, (((1,), (1,)), ((), ())), preferred_element_type=F32)


def parts(x):
    high = x.astype(BF16)
    return high, (x - high.astype(F32)).astype(BF16)


def times_t(x, weight):
    xh, xl = parts(x)
    wh, wl = weight
    both = dot_t(jnp.concatenate([xh, xl], axis=0), wh)
    return both[: x.shape[0]] + (both[x.shape[0] :] + dot_t(xh, wl))


def times_exact(x, weight):
    both = dot(jnp.concatenate(parts(x), axis=0), weight)
    return both[: x.shape[0]] + both[x.shape[0] :]


def lanes(ref, *at):
    pieces = [ref[(t,) + at] for t in range(4)]
    pieces = [p.reshape(-1, 128) for p in pieces]
    return jnp.concatenate(pieces, axis=1)


def cut_tiles(dens):
    return [(t, slice(128 * t, min(128 * t + 128, dens)), slice(0, min(128, dens - 128 * t))) for t in range(4)]


def modes_of(x, rot_ref, dens):
    y = times_exact(x[:, :dens], rot_ref[...])
    lane = lax.broadcasted_iota(jnp.int32, (1, 512), 1) % 256
    half = dens // 2
    is_low = (lane >= half) & (lane < half + KEPT)
    return jnp.where(is_low, y - y.astype(BF16).astype(F32), y)


def class_pairs():
    return [(c, d) for c in range(2) for d in range(2)]


def fetch(pairs, sems, first=0):
    copies = [
        pltpu.make_async_copy(src, dst, sems.at[first + i]) for i, (src, dst) in enumerate(pairs)
    ]
    for c in copies:
        c.start()
    return copies


def own_kernel(
    own_hbm, rot_hbm, llist_hbm, plist_hbm, up_hbm, down_hbm, inv_hbm,
    modes_hbm, masks_hbm, split_hbm,
    own_ref, rot_ref, llist_ref, plist_ref, modes, masks, flat, weights, halves, sems, out_sems,
):
    rows, cols, dens = own_ref.shape
    pr, pc = rows // 2, cols // 2
    gr, gc = pr // 2, pc // 2
    used = pr * pc + gr * gc
    high = masks.shape[1]
    pairs = [(llist_hbm, llist_ref), (plist_hbm, plist_ref), (own_hbm, own_ref), (rot_hbm, rot_ref)]
    pairs += [(up_hbm.at[n], weights.at[n]) for n in range(4)]
    pairs += [(down_hbm.at[n], weights.at[4 + n]) for n in range(4)] + [(inv_hbm, weights.at[8])]
    copies = fetch(pairs, sems)
    copies[2].wait()
    copies[3].wait()
    y = modes_of(own_ref[...].reshape(rows * cols, dens), rot_ref, dens)
    for t in range(4):
        modes[t] = y[:, 128 * t : 128 * t + 128].reshape(rows, cols, 128)
    out = fetch([(modes, modes_hbm)], out_sems, 0)

    for n in range(9):
        copies[4 + n].wait()
        halves[n, 0], halves[n, 1] = parts(weights[n])
        out += fetch([(halves.at[n], split_hbm.at[n])], out_sems, 1 + n)

    copies[0].wait()
    copies[1].wait()
    flat[0, :, :, 0 : llist_ref.shape[2]] = llist_ref[...].astype(F32)
    flat[1, 0:pr, 0:pc, 0 : plist_ref.shape[2]] = plist_ref[...].astype(F32)
    flags = [
        jnp.concatenate(
            [flat[0, 2 * i + c, pl.ds(d, pc, stride=2), :] for i in range(pr)]
            + [flat[1, 2 * i + c, pl.ds(d, gc, stride=2), :] for i in range(gr)]
            + [jnp.zeros((high - used, 128), F32)],
            axis=0,
        )
        for c, d in class_pairs()
    ]
    for i, (n, o, _) in enumerate(plan()):
        masks[i] = jnp.broadcast_to(flags[n][:, o : o + 1], (high, 128)).astype(BF16)
    out += fetch([(masks, masks_hbm)], out_sems, 10)
    for c in out:
        c.wait()


def children(ref, dens, counts, c, d):
    return jnp.concatenate(
        [
            jnp.concatenate(
                [ref[t, 2 * i + c, pl.ds(d, counts[1], stride=2), :] for i in range(counts[0])],
                axis=0,
            )
            for t in range(4)
        ],
        axis=1,
    )[:, :dens]


def rest_kernel(
    entry_ref, side_ref, base_ref, even_ref,
    strip0_ref, strip1_ref, end0_ref, end1_ref,
    own_hbm, modes_hbm, masks_hbm, split_hbm, rot_hbm, back_hbm, pin_hbm, table_hbm, signs_hbm,
    out_ref, pup_ref,
    own_ref, own_t, strip_t, ends_t, own_modes, modes, pmodes, masks, split_v, rot_ref, back, pin_ref,
    bases, signs, table, lut, acc, flat, plocal, sems,
):
    rows, cols, dens = out_ref.shape
    pr, pc = rows // 2, cols // 2
    gr, gc = pr // 2, pc // 2
    boxes, pboxes = pr * pc, gr * gc
    high = lut.shape[2]
    wide = end0_ref.shape[1]
    copies = fetch(
        (
            (own_hbm, own_ref), (split_hbm.at[0:4], split_v.at[0:4]), (rot_hbm, rot_ref),
            (modes_hbm, own_modes), (table_hbm, bases), (signs_hbm, signs), (masks_hbm, masks),
            (back_hbm, back), (pin_hbm, pin_ref), (split_hbm.at[4:9], split_v.at[4:9]),
        ),
        sems,
    )
    even_x, even_y = even_ref[0] == 1, even_ref[1] == 1
    for t, cut, to in cut_tiles(dens):
        first, second = strip0_ref[:, :, cut], strip1_ref[:, :, cut]
        strip_t[t, :, 0:HALO, to] = jnp.where(even_y, second, first)
        strip_t[t, :, HALO:, to] = jnp.where(even_y, first, second)
        first, second = end0_ref[:, :, cut], end1_ref[:, :, cut]
        ends_t[t, 0:HALO, :, to] = jnp.where(even_x, second, first)
        ends_t[t, HALO:, :, to] = jnp.where(even_x, first, second)
    copies[0].wait()
    for t, cut, to in cut_tiles(dens):
        own_t[t, :, :, to] = own_ref[:, :, cut]

    copies[1].wait()
    parent = None
    for n, (c, d) in enumerate(class_pairs()):
        x = jnp.concatenate(
            [
                children(own_t, dens, (pr, pc), c, d),
                children(strip_t, dens, (pr, HALO), c, d),
                children(ends_t, dens, (HALO, wide // 2), c, d),
            ],
            axis=0,
        )
        part = times_t(x, (split_v[n, 0], split_v[n, 1]))
        parent = part if parent is None else parent + part
    pup_ref[...] = parent[:boxes].reshape(pr, pc, dens)

    copies[2].wait()
    x = [lanes(strip_t)[:, :dens], lanes(ends_t, slice(HALO - 2, HALO + 2))[:, :dens], parent]
    y = modes_of(jnp.concatenate(x, axis=0), rot_ref, dens)
    sizes = [8 * rows, 4 * wide, boxes, 4 * pr, 2 * wide]
    starts = [sum(sizes[:i]) for i in range(6)]
    copies[3].wait()
    for t in range(4):
        cut = slice(128 * t, 128 * t + 128)
        pieces = [y[starts[i] : starts[i + 1], cut] for i in range(5)]
        modes[t, 2 : 2 + rows, 8 : 8 + cols, :] = own_modes[t]
        strip = pieces[0].reshape(rows, 8, 128)
        modes[t, 2 : 2 + rows, 4:8, :] = strip[:, 0:4]
        modes[t, 2 : 2 + rows, 8 + cols : 12 + cols, :] = strip[:, 4:8]
        end = pieces[1].reshape(4, wide, 128)
        modes[t, 0:2, 4 : 4 + wide, :] = end[0:2]
        modes[t, 2 + rows :, 4 : 4 + wide, :] = end[2:4]
        pmodes[t, 2 : 2 + pr, 4 : 4 + pc, :] = pieces[2].reshape(pr, pc, 128)
        strip = pieces[3].reshape(pr, 4, 128)
        pmodes[t, 2 : 2 + pr, 2:4, :] = strip[:, 0:2]
        pmodes[t, 2 : 2 + pr, 4 + pc : 6 + pc, :] = strip[:, 2:4]
        end = pieces[4].reshape(4, wide // 2, 128)
        pmodes[t, 0:2, 2 : 2 + wide // 2, :] = end[0:2]
        pmodes[t, 2 + pr :, 2 : 2 + wide // 2, :] = end[2:4]

    def gather(i, carry):
        base = 2 * (i % 3) + i // 3
        for ds in range(2):
            for py in (-1, 0, 1):
                e = i * 6 + ds * 3 + py + 1
                for t in range(4):
                    x = jnp.concatenate(
                        [
                            modes[t, base + 2 * j, pl.ds(8 + 2 * py + ds, pc, stride=2), :]
                            for j in range(pr)
                        ]
                        + [
                            pmodes[t, base + 2 * j, pl.ds(4 + 2 * py + ds, gc, stride=2), :]
                            for j in range(gr)
                        ]
                        + [jnp.zeros((high - used, 128), F32)],
                        axis=0,
                    )
                    lut[e, t // 2, :, 128 * (t % 2) : 128 * (t % 2) + 128] = x.astype(BF16)
        return carry

    used = boxes + pboxes
    lax.fori_loop(0, 6, gather, 0)

    copies[4].wait()
    copies[5].wait()

    def mirror(q, carry):
        for s in range(2):
            at = pl.ds(pl.multiple_of(256 * q, 256), 256)
            table[s, at, :] = bases[s, base_ref[2 * q]] * signs[base_ref[2 * q + 1], s]
        return carry

    lax.fori_loop(0, len(SEQUENCE), mirror, 0)
    copies[6].wait()

    def listed(i, s):
        m = masks[i]
        x = lut[entry_ref[i], s]
        return jnp.concatenate([x[:, :128] * m, x[:, 128:] * m], axis=1)

    acc[...] = jnp.zeros_like(acc)
    inner, side, corner = len(INNER), len(SIDES[0]), len(CORNERS)

    def inner_part(g, carry):
        for s in range(2):
            x = jnp.concatenate(
                [
                    jnp.concatenate([listed((4 * g + k) * 4 + n, s) for k in range(4)], axis=1)
                    for n in range(4)
                ],
                axis=0,
            )
            acc[s] += dot(x, table[s, pl.ds(pl.multiple_of(1024 * g, 1024), 1024), :])
        return carry

    lax.fori_loop(0, inner // 4, inner_part, 0)

    def side_part(g, carry):
        for s in range(2):
            first = 4 * inner + 2 * side * g
            x = jnp.concatenate(
                [
                    jnp.concatenate([listed(first + 2 * k + j, s) for k in range(side)], axis=1)
                    for j in range(2)
                ],
                axis=0,
            )
            at = pl.multiple_of(256 * (inner + side * g), 256)
            r = dot(x, table[s, pl.ds(at, 256 * side), :])
            for j in range(2):
                to = pl.ds(pl.multiple_of(side_ref[2 * g + j] * high, high), high)
                acc[s, to, :] += r[high * j : high * (j + 1)]
        return carry

    lax.fori_loop(0, len(SIDES), side_part, 0)
    for n in range(corner):
        for s in range(2):
            at = 256 * (inner + len(SIDES) * side + n)
            x = listed(4 * inner + 2 * side * len(SIDES) + n, s)
            acc[s, high * n : high * (n + 1), :] += dot(x, table[s, at : at + 256, :])

    for c in copies[7:]:
        c.wait()
    check = None
    for s in range(2):
        part = times_exact(acc[s], back[256 * s : 256 * (s + 1)])
        check = part if check is None else check + part

    inverse = (split_v[8, 0], split_v[8, 1])
    for n, (c, d) in enumerate(class_pairs()):
        for t, cut, to in cut_tiles(dens):
            for j in range(gr):
                r = high * n + boxes + gc * j
                plocal[t, 2 * j + c, pl.ds(d, gc, stride=2), to] = check[r : r + gc, cut]
    local = pin_ref[...].reshape(boxes, dens) + times_t(lanes(plocal)[:, :dens], inverse)
    x = jnp.concatenate(
        [
            check[high * n : high * n + boxes]
            + times_t(local, (split_v[4 + n, 0], split_v[4 + n, 1]))
            for n in range(4)
        ],
        axis=0,
    )
    result = times_t(x, inverse)
    for n, (c, d) in enumerate(class_pairs()):
        for t, cut, to in cut_tiles(dens):
            for j in range(pr):
                r = boxes * n + pc * j
                flat[t, 2 * j + c, pl.ds(d, pc, stride=2), to] = result[r : r + pc, cut]
    for t, cut, to in cut_tiles(dens):
        out_ref[:, :, cut] = flat[t, :, :, to]


VMEM = pl.BlockSpec(memory_space=pltpu.VMEM)
HBM = pl.BlockSpec(memory_space=pltpu.HBM)
SMEM = pl.BlockSpec(memory_space=pltpu.SMEM)


def params(mib):
    return pltpu.CompilerParams(vmem_limit_bytes=mib * 1024 * 1024)


def cost(rows, tiles, reads):
    return pl.CostEstimate(flops=2 * rows * tiles * 256 * 256, bytes_accessed=reads, transcendentals=0)


def height(boxes):
    return -(-(boxes * 5 // 4) // 16) * 16


def own_step(own, rotation, llist, plist, up, down, inv):
    rows, cols, dens = own.shape
    masks = (len(plan()), height(rows * cols // 4), 128)
    return pl.pallas_call(
        own_kernel,
        out_shape=(
            jax.ShapeDtypeStruct((4, rows, cols, 128), F32),
            jax.ShapeDtypeStruct(masks, BF16),
            jax.ShapeDtypeStruct((9, 2, dens, dens), BF16),
        ),
        in_specs=[HBM] * 7,
        out_specs=(HBM,) * 3,
        scratch_shapes=[
            pltpu.VMEM(own.shape, F32),
            pltpu.VMEM(rotation.shape, BF16),
            pltpu.VMEM(llist.shape, jnp.int32),
            pltpu.VMEM(plist.shape, jnp.int32),
            pltpu.VMEM((4, rows, cols, 128), F32),
            pltpu.VMEM(masks, BF16),
            pltpu.VMEM((2, rows, cols, 128), F32),
            pltpu.VMEM((9, dens, dens), F32),
            pltpu.VMEM((9, 2, dens, dens), BF16),
            pltpu.SemaphoreType.DMA((13,)),
            pltpu.SemaphoreType.DMA((11,)),
        ],
        compiler_params=params(58),
        cost_estimate=cost(rows * cols, 24, up.size * 4),
    )(own, rotation, llist, plist, up, down, inv)


def rest_step(even, strips, ends, own, modes, masks, halves, rotation, back, pin, table, signs):
    rows, cols, dens = own.shape
    pr, pc = rows // 2, cols // 2
    high = height(pr * pc)
    bases = [x for a, b in SEQUENCE for x in (BASES.index((abs(a), abs(b))), 2 * (a < 0) + (b < 0))]
    return pl.pallas_call(
        rest_kernel,
        out_shape=(
            jax.ShapeDtypeStruct(own.shape, F32),
            jax.ShapeDtypeStruct((pr, pc, dens), F32),
        ),
        in_specs=[SMEM] * 4 + [VMEM] * 4 + [HBM] * 9,
        out_specs=(VMEM, VMEM),
        scratch_shapes=[
            pltpu.VMEM(own.shape, F32),
            pltpu.VMEM((4, rows, cols, 128), F32),
            pltpu.VMEM((4, rows, 2 * HALO, 128), F32),
            pltpu.VMEM((4, 2 * HALO, cols + 2 * HALO, 128), F32),
            pltpu.VMEM((4, rows, cols, 128), F32),
            pltpu.VMEM((4, rows + 4, cols + 16, 128), F32),
            pltpu.VMEM((4, pr + 4, pc + 8, 128), F32),
            pltpu.VMEM(masks.shape, BF16),
            pltpu.VMEM(halves.shape, BF16),
            pltpu.VMEM(rotation.shape, BF16),
            pltpu.VMEM(back.shape, BF16),
            pltpu.VMEM(pin.shape, F32),
            pltpu.VMEM(table.shape, BF16),
            pltpu.VMEM(signs.shape, BF16),
            pltpu.VMEM((2, 256 * len(SEQUENCE), 256), BF16),
            pltpu.VMEM((36, 2, high, 256), BF16),
            pltpu.VMEM((2, 4 * high, 256), F32),
            pltpu.VMEM((4, rows, cols, 128), F32),
            pltpu.VMEM((4, pr, pc, 128), F32),
            pltpu.SemaphoreType.DMA((10,)),
        ],
        compiler_params=params(58),
        cost_estimate=cost(rows * cols, 150, table.size * 2),
    )(
        jnp.asarray([e for _, _, e in plan()], jnp.int32),
        jnp.asarray([n for pair in SIDE_CLASSES for n in pair], jnp.int32),
        jnp.asarray(bases, jnp.int32), even,
        *strips, *ends, own, modes, masks, halves, rotation, back, pin, table, signs,
    )


def swapped(low, high, axis, odd_first):
    peers = lax.axis_size(axis)
    even = lax.axis_index(axis) % 2 == 0
    strips = (jnp.where(even, high, low), jnp.where(even, low, high))
    got = [None, None]
    for kind in (1, 0) if odd_first else (0, 1):
        pairs = [(i, i + 1) for i in range(kind, peers - 1, 2)]
        got[kind] = lax.ppermute(strips[kind], axis, pairs + [(j, i) for i, j in pairs])
    return got


def local(leaf_up, parent_in, leaf_lists, parent_lists, up_transfer, down_transfer, check_inverse):
    rows, cols, _ = leaf_up.shape
    even = [lax.axis_index(axis) % 2 == 0 for axis in ("gx", "gy")]
    flag = jnp.stack(even).astype(jnp.int32)
    rotation, back, table, signs = (jnp.asarray(x) for x in operators())
    strips = swapped(leaf_up[:, :HALO], leaf_up[:, cols - HALO :], "gy", True)
    modes, masks, halves = own_step(
        leaf_up, rotation, leaf_lists, parent_lists, up_transfer, down_transfer, check_inverse
    )
    left = jnp.where(even[1], strips[1], strips[0])
    right = jnp.where(even[1], strips[0], strips[1])
    broad = lambda s: jnp.concatenate([left[s], leaf_up[s], right[s]], axis=1)
    ends = swapped(broad(slice(0, HALO)), broad(slice(rows - HALO, rows)), "gx", False)
    leaf_down, parent_up = rest_step(
        flag, strips, ends, leaf_up, modes, masks, halves, rotation, back, parent_in, table, signs
    )
    return leaf_down, parent_up


def solution(mesh):
    block = P("gx", "gy", None)
    return jax.shard_map(
        local,
        mesh=mesh,
        in_specs=(block,) * 4 + (P(),) * 3,
        out_specs=(block, block),
        check_vma=False,
    )
```

```python
import functools
import math

import jax
import jax.numpy as jnp
import ml_dtypes
import numpy as np
from jax import lax
from jax.experimental import pallas as pl
from jax.experimental.pallas import tpu as pltpu
from jax.sharding import PartitionSpec as P

ORDER = 6
HALO = 4
KEPT = 14
BF16, F32 = jnp.bfloat16, jnp.float32

def offset_table():
    return [(a, b) for a in range(-3, 4) for b in range(-3, 4) if max(abs(a), abs(b)) >= 2]


BASES = sorted({(abs(a), abs(b)) for a, b in offset_table()})


def surface_points():
    grid = np.linspace(-1.0, 1.0, ORDER)
    keys = [
        (i, j, k)
        for i in range(ORDER)
        for j in range(ORDER)
        for k in range(ORDER)
        if min(i, j, k) == 0 or max(i, j, k) == ORDER - 1
    ]
    return keys, np.array([[grid[i] for i in key] for key in keys])


def translation(points, dx, dy):
    r = 0.525 * (points[:, None, :] - points[None, :, :]) - np.array([dx, dy, 0.0])
    dist = np.sqrt((r * r).sum(-1))
    n = len(points)
    out = np.zeros((3, n, 3, n))
    for a in range(3):
        for b in range(3):
            out[a, :, b, :] = (float(a == b) / dist + r[..., a] * r[..., b] / dist**3) / (8 * math.pi)
    return out.reshape(3 * n, 3 * n)


def split(x):
    high = x.astype(ml_dtypes.bfloat16)
    return high, (x - high.astype(np.float64)).astype(ml_dtypes.bfloat16)


@functools.lru_cache(maxsize=None)
def operators():
    keys, points = surface_points()
    n = len(keys)
    points_of = {key: i for i, key in enumerate(keys)}
    mirror = [points_of[(i, j, ORDER - 1 - k)] for i, j, k in keys]
    mats = {o: translation(points, *o) for o in offset_table()}
    half = 3 * n // 2
    rotation = np.zeros((3 * n, 512), ml_dtypes.bfloat16)
    back = np.zeros((512, 3 * n))
    table = np.zeros((2, len(BASES), 256, 256), ml_dtypes.bfloat16)
    signs = np.ones((4, 2, 256, 256), ml_dtypes.bfloat16)
    for s, sign in enumerate((1, -1)):
        pairs = np.zeros((3 * n, half))
        firsts = []
        for a in range(3):
            flip = sign if a < 2 else -sign
            for i in range(n):
                if i < mirror[i]:
                    pairs[a * n + i, len(firsts)] = 1.0
                    pairs[a * n + mirror[i], len(firsts)] = flip
                    firsts.append(a * n + i)
        blocks = {o: 0.25 * pairs.T @ m @ pairs for o, m in mats.items()}
        gram = sum(b.T @ b for b in blocks.values())
        place = {f: i for i, f in enumerate(firsts)}
        modes, parity, weight = [], [], []
        for sx in (1, -1):
            for sy in (1, -1):
                basis = []
                for i, f in enumerate(firsts):
                    a, (kx, ky, kz) = f // n, keys[f % n]
                    if kx < ORDER // 2 and ky < ORDER // 2:
                        v = np.zeros(half)
                        for fx in range(2):
                            for fy in range(2):
                                key = (ORDER - 1 - kx if fx else kx, ORDER - 1 - ky if fy else ky, kz)
                                sign_x = (sx if a != 0 else -sx) if fx else 1
                                sign_y = (sy if a != 1 else -sy) if fy else 1
                                v[place[a * n + points_of[key]]] = 0.5 * sign_x * sign_y
                        basis.append(v)
                basis = np.array(basis).T
                w, vecs = np.linalg.eigh(basis.T @ gram @ basis)
                vecs = basis @ vecs
                vecs = vecs * np.sign(vecs[np.abs(np.round(vecs, 9)).argmax(0), np.arange(len(w))])
                modes.append(vecs)
                weight.append(w)
                parity += [(sx, sy)] * len(w)
        order = np.argsort(-np.concatenate(weight), kind="stable")
        vecs = np.concatenate(modes, axis=1)[:, order]
        parity = np.array(parity)[order]
        modes = (pairs @ vecs / math.sqrt(2.0)).astype(ml_dtypes.bfloat16)
        lows = np.concatenate([modes, modes[:, :KEPT], modes[:, :KEPT]], axis=1)
        rotation[:, 256 * s : 256 * (s + 1)] = lows
        outs, out_parity = [], []
        for sx in (1, -1):
            for sy in (1, -1):
                for f in firsts:
                    a, (kx, ky, kz) = f // n, keys[f % n]
                    if kx < ORDER // 2 and ky < ORDER // 2:
                        v = np.zeros(half)
                        for fx in range(2):
                            for fy in range(2):
                                key = (ORDER - 1 - kx if fx else kx, ORDER - 1 - ky if fy else ky, kz)
                                sign_x = (sx if a != 0 else -sx) if fx else 1
                                sign_y = (sy if a != 1 else -sy) if fy else 1
                                v[place[a * n + points_of[key]]] = sign_x * sign_y
                        outs.append(v)
                        out_parity.append((sx, sy))
        outs = np.array(outs).T
        out_parity = np.array(out_parity)
        back[256 * s : 256 * s + half] = (pairs @ outs).T
        undo = np.linalg.inv(modes[firsts].astype(np.float64))
        for q, o in enumerate(BASES):
            high, low = split(undo @ blocks[o].T @ outs * 0.25)
            table[s, q, :half, :half] = high
            table[s, q, half : half + KEPT, :half] = high[:KEPT]
            table[s, q, half + KEPT : half + 2 * KEPT, :half] = low[:KEPT]
        ins = np.concatenate([parity, parity[:KEPT], parity[:KEPT]], axis=0)
        for f in range(4):
            row = np.ones(256)
            row[: len(ins)] = (ins[:, 0] if f // 2 else 1) * (ins[:, 1] if f % 2 else 1)
            col = np.ones(256)
            col[:half] = (out_parity[:, 0] if f // 2 else 1) * (out_parity[:, 1] if f % 2 else 1)
            signs[f, s] = row[:, None] * col[None, :]
    return rotation, back.astype(ml_dtypes.bfloat16), table, signs


@functools.lru_cache(maxsize=None)
def plan():
    products = []
    for c, d in class_pairs():
        for o, (dx, dy) in enumerate(offset_table()):
            px, cs = divmod(c + dx, 2)
            py, ds = divmod(d + dy, 2)
            if abs(px) <= 1 and abs(py) <= 1:
                products.append((o, (cs * 3 + px + 1) * 6 + ds * 3 + py + 1))
    return products


def class_pairs():
    return [(c, d) for c in range(2) for d in range(2)]


def dot(a, b):
    return lax.dot_general(a, b, (((1,), (0,)), ((), ())), preferred_element_type=F32)


def dot_t(a, b):
    return lax.dot_general(a, b, (((1,), (1,)), ((), ())), preferred_element_type=F32)


def parts(x):
    high = x.astype(BF16)
    return high, (x - high.astype(F32)).astype(BF16)


def times_t(x, weight):
    xh, xl = parts(x)
    wh, wl = weight
    both = dot_t(jnp.concatenate([xh, xl], axis=0), wh)
    return both[: x.shape[0]] + (both[x.shape[0] :] + dot_t(xh, wl))


def times_exact(x, weight):
    both = dot(jnp.concatenate(parts(x), axis=0), weight)
    return both[: x.shape[0]] + both[x.shape[0] :]


def lanes(ref, *at):
    pieces = [ref[(t,) + at] for t in range(4)]
    pieces = [p.reshape(-1, 128) for p in pieces]
    return jnp.concatenate(pieces, axis=1)


def cut_tiles(dens):
    return [(t, slice(128 * t, min(128 * t + 128, dens)), slice(0, min(128, dens - 128 * t))) for t in range(4)]


def modes_of(x, rot_ref, dens):
    y = times_exact(x[:, :dens], rot_ref[...])
    lane = lax.broadcasted_iota(jnp.int32, (1, 512), 1) % 256
    half = dens // 2
    is_low = (lane >= half) & (lane < half + KEPT)
    return jnp.where(is_low, y - y.astype(BF16).astype(F32), y)


def children(ref, dens, counts, c, d):
    return jnp.concatenate(
        [
            jnp.concatenate(
                [ref[t, 2 * i + c, pl.ds(d, counts[1], stride=2), :] for i in range(counts[0])],
                axis=0,
            )
            for t in range(4)
        ],
        axis=1,
    )[:, :dens]


def near_kernel(
    even_ref, strip0_ref, strip1_ref, own_ref, rot_ref, up_ref, llist_ref, plist_ref,
    pup_ref, lut, edge_ref, pmodes_ref, masks_ref, upw_ref,
    own_t, strip_t, modes, flat,
):
    rows, cols, dens = own_ref.shape
    pr, pc = rows // 2, cols // 2
    gr, gc = pr // 2, pc // 2
    boxes = pr * pc
    used = boxes + gr * gc
    high = lut.shape[2]
    count = masks_ref.shape[0] // 4
    even = even_ref[1] == 1
    for t, cut, to in cut_tiles(dens):
        own_t[t, :, :, to] = own_ref[:, :, cut]
        first, second = strip0_ref[:, :, cut], strip1_ref[:, :, cut]
        strip_t[t, :, 0:HALO, to] = jnp.where(even, second, first)
        strip_t[t, :, HALO:, to] = jnp.where(even, first, second)

    parent = None
    for n, (c, d) in enumerate(class_pairs()):
        upw_ref[n, 0], upw_ref[n, 1] = parts(up_ref[n])
        x = jnp.concatenate(
            [children(own_t, dens, (pr, pc), c, d), children(strip_t, dens, (pr, HALO), c, d)],
            axis=0,
        )
        part = times_t(x, (upw_ref[n, 0], upw_ref[n, 1]))
        parent = part if parent is None else parent + part
    pup_ref[...] = parent[:boxes].reshape(pr, pc, dens)
    y = modes_of(own_ref[...].reshape(rows * cols, dens), rot_ref, dens)
    z = modes_of(jnp.concatenate([lanes(strip_t)[:, :dens], parent], axis=0), rot_ref, dens)
    w, p = z[: rows * 8], z[rows * 8 :]
    for t in range(4):
        cut = slice(128 * t, 128 * t + 128)
        modes[t, 2 : 2 + rows, 8 : 8 + cols, :] = y[:, cut].reshape(rows, cols, 128)
        strip = w[:, cut].reshape(rows, 8, 128)
        modes[t, 2 : 2 + rows, 4:8, :] = strip[:, 0:4]
        modes[t, 2 : 2 + rows, 8 + cols : 12 + cols, :] = strip[:, 4:8]
        edge_ref[t, 0:2] = modes[t, 2:4]
        edge_ref[t, 2:4] = modes[t, rows : rows + 2]
        pmodes_ref[t, 2 : 2 + pr, 4 : 4 + pc, :] = p[:boxes, cut].reshape(pr, pc, 128)
        strip = p[boxes:, cut].reshape(pr, 4, 128)
        pmodes_ref[t, 2 : 2 + pr, 2:4, :] = strip[:, 0:2]
        pmodes_ref[t, 2 : 2 + pr, 4 + pc : 6 + pc, :] = strip[:, 2:4]

    def gather(i, carry):
        base = 2 * (i % 3) + i // 3
        for ds in range(2):
            for py in (-1, 0, 1):
                e = i * 6 + ds * 3 + py + 1
                for t in range(4):
                    x = jnp.concatenate(
                        [
                            modes[t, base + 2 * j, pl.ds(8 + 2 * py + ds, pc, stride=2), :]
                            for j in range(pr)
                        ]
                        + [
                            pmodes_ref[t, base + 2 * j, pl.ds(4 + 2 * py + ds, gc, stride=2), :]
                            for j in range(gr)
                        ]
                        + [jnp.zeros((high - used, 128), F32)],
                        axis=0,
                    )
                    lut[e, t // 2, :, 128 * (t % 2) : 128 * (t % 2) + 128] = x.astype(BF16)
        return carry

    lax.fori_loop(0, 6, gather, 0)

    flat[0, :, :, 0 : llist_ref.shape[2]] = llist_ref[...].astype(F32)
    flat[1, 0:pr, 0:pc, 0 : plist_ref.shape[2]] = plist_ref[...].astype(F32)
    for n, (c, d) in enumerate(class_pairs()):
        flag = jnp.concatenate(
            [flat[0, 2 * i + c, pl.ds(d, pc, stride=2), :] for i in range(pr)]
            + [flat[1, 2 * i + c, pl.ds(d, gc, stride=2), :] for i in range(gr)]
            + [jnp.zeros((high - used, 128), F32)],
            axis=0,
        )
        for k in range(count):
            o = plan()[count * n + k][0]
            masks_ref[count * n + k] = jnp.broadcast_to(flag[:, o : o + 1], (high, 128)).astype(BF16)


def close_kernel(
    entry_ref, pick_ref, base_ref, even_ref,
    end0_ref, end1_ref, edge_ref, pside_ref, upw_ref, masks, lut_ref,
    rot_ref, pin_ref, back, bases, signs, down_ref, inv_ref,
    out_ref,
    ends_t, edge, pmodes, lut, table, acc, flat, plocal, sem,
):
    rows, cols, dens = out_ref.shape
    pr, pc = rows // 2, cols // 2
    gr, gc = pr // 2, pc // 2
    boxes, pboxes = pr * pc, gr * gc
    high = lut.shape[2]
    wide = end0_ref.shape[1]
    count = masks.shape[0] // 4
    copy = pltpu.make_async_copy(lut_ref, lut, sem)
    copy.start()
    even = even_ref[0] == 1
    for t, cut, to in cut_tiles(dens):
        first, second = end0_ref[:, :, cut], end1_ref[:, :, cut]
        ends_t[t, 0:HALO, :, to] = jnp.where(even, second, first)
        ends_t[t, HALO:, :, to] = jnp.where(even, first, second)
    parent = None
    for n, (c, d) in enumerate(class_pairs()):
        x = children(ends_t, dens, (HALO, wide // 2), c, d)
        part = times_t(x, (upw_ref[n, 0], upw_ref[n, 1]))
        parent = part if parent is None else parent + part
    x = lanes(ends_t, slice(HALO - 2, HALO + 2))[:, :dens]
    y = modes_of(jnp.concatenate([x, parent], axis=0), rot_ref, dens)
    z, p = y[: 4 * wide], y[4 * wide :]
    for t in range(4):
        cut = slice(128 * t, 128 * t + 128)
        end = z[:, cut].reshape(4, wide, 128)
        edge[t, 0:2, 4 : 4 + wide, :] = end[0:2]
        edge[t, 2:4] = edge_ref[t, 0:2]
        edge[t, 4:6] = edge_ref[t, 2:4]
        edge[t, 6:8, 4 : 4 + wide, :] = end[2:4]
        end = p[:, cut].reshape(4, wide // 2, 128)
        pmodes[t, 0:2, 2 : 2 + wide // 2, :] = end[0:2]
        pmodes[t, 2 : 2 + pr] = pside_ref[t, 2 : 2 + pr]
        pmodes[t, 2 + pr :, 2 : 2 + wide // 2, :] = end[2:4]

    def mirror(q, carry):
        for s in range(2):
            table[s, q] = bases[s, base_ref[2 * q]] * signs[base_ref[2 * q + 1], s]
        return carry

    lax.fori_loop(0, len(offset_table()), mirror, 0)

    copy.wait()

    def patch(cs, carry):
        for ds in range(2):
            for py in (-1, 0, 1):
                for t in range(4):
                    at = slice(128 * (t % 2), 128 * (t % 2) + 128)
                    mine = pl.ds(8 + 2 * py + ds, pc, stride=2)
                    theirs = pl.ds(4 + 2 * py + ds, gc, stride=2)
                    e = cs * 18 + ds * 3 + py + 1
                    x = jnp.concatenate([edge[t, cs + 2 * j, mine, :] for j in range(2)], axis=0)
                    lut[e, t // 2, 0:16, at] = x.astype(BF16)
                    x = jnp.concatenate([pmodes[t, cs + 2 * j, theirs, :] for j in range(4)], axis=0)
                    lut[e, t // 2, boxes : boxes + 16, at] = x.astype(BF16)
                    e = e + 12
                    x = jnp.concatenate([edge[t, 4 + cs + 2 * j, mine, :] for j in range(2)], axis=0)
                    lut[e, t // 2, boxes - 16 : boxes, at] = x.astype(BF16)
                    x = jnp.concatenate(
                        [pmodes[t, 4 + cs + 2 * j, theirs, :] for j in range(4, gr)]
                        + [jnp.zeros((high - boxes - pboxes, 128), F32)],
                        axis=0,
                    )
                    lut[e, t // 2, boxes + 16 : high, at] = x.astype(BF16)
        return carry

    lax.fori_loop(0, 2, patch, 0)

    def interact(j, carry):
        n, s = j // 2, j % 2
        total = jnp.zeros((high, 256), F32)
        for k in range(count):
            i = n * count + k
            m = masks[i]
            x = lut[entry_ref[i], s]
            x = jnp.concatenate([x[:, :128] * m, x[:, 128:] * m], axis=1)
            total = total + dot(x, table[s, pick_ref[i]])
        acc[s, n] = total
        return carry

    lax.fori_loop(0, 8, interact, 0)

    check = None
    for s in range(2):
        part = times_exact(acc[s].reshape(4 * high, 256), back[256 * s : 256 * (s + 1)])
        check = part if check is None else check + part

    inverse = parts(inv_ref[...])
    for n, (c, d) in enumerate(class_pairs()):
        for t, cut, to in cut_tiles(dens):
            for j in range(gr):
                r = high * n + boxes + gc * j
                plocal[t, 2 * j + c, pl.ds(d, gc, stride=2), to] = check[r : r + gc, cut]
    local = pin_ref[...].reshape(boxes, dens) + times_t(lanes(plocal)[:, :dens], inverse)
    x = jnp.concatenate(
        [
            check[high * n : high * n + boxes] + times_t(local, parts(down_ref[n]))
            for n in range(4)
        ],
        axis=0,
    )
    result = times_t(x, inverse)
    for n, (c, d) in enumerate(class_pairs()):
        for t, cut, to in cut_tiles(dens):
            for j in range(pr):
                r = boxes * n + pc * j
                flat[t, 2 * j + c, pl.ds(d, pc, stride=2), to] = result[r : r + pc, cut]
    for t, cut, to in cut_tiles(dens):
        out_ref[:, :, cut] = flat[t, :, :, to]


VMEM = pl.BlockSpec(memory_space=pltpu.VMEM)
SMEM = pl.BlockSpec(memory_space=pltpu.SMEM)


def params(mib):
    return pltpu.CompilerParams(vmem_limit_bytes=mib * 1024 * 1024)


def cost(rows, tiles, reads):
    return pl.CostEstimate(flops=2 * rows * tiles * 256 * 256, bytes_accessed=reads, transcendentals=0)


def height(boxes):
    return -(-(boxes * 5 // 4) // 16) * 16


def near_step(even, strips, own, rotation, up, llist, plist):
    rows, cols, dens = own.shape
    pr, pc = rows // 2, cols // 2
    high = height(pr * pc)
    return pl.pallas_call(
        near_kernel,
        out_shape=(
            jax.ShapeDtypeStruct((pr, pc, dens), F32),
            jax.ShapeDtypeStruct((36, 2, high, 256), BF16),
            jax.ShapeDtypeStruct((4, 4, cols + 16, 128), F32),
            jax.ShapeDtypeStruct((4, pr + 4, pc + 8, 128), F32),
            jax.ShapeDtypeStruct((len(plan()), high, 128), BF16),
            jax.ShapeDtypeStruct((4, 2, dens, dens), BF16),
        ),
        in_specs=[SMEM] + [VMEM] * 7,
        out_specs=(VMEM,) * 6,
        scratch_shapes=[
            pltpu.VMEM((4, rows, cols, 128), F32),
            pltpu.VMEM((4, rows, 2 * HALO, 128), F32),
            pltpu.VMEM((4, rows + 4, cols + 16, 128), F32),
            pltpu.VMEM((2, rows, cols, 128), F32),
        ],
        compiler_params=params(24),
        cost_estimate=cost(rows * cols, 48, up.size * 4),
    )(even, *strips, own, rotation, up, llist, plist)


def close_step(even, ends, edge, pmodes, upw, masks, lut, rotation, pin, back, bases, signs, down, inv, shape):
    rows, cols, dens = shape
    pr, pc = rows // 2, cols // 2
    high = height(pr * pc)
    offsets = offset_table()
    mirrors = [x for a, b in offsets for x in (BASES.index((abs(a), abs(b))), 2 * (a < 0) + (b < 0))]
    return pl.pallas_call(
        close_kernel,
        out_shape=jax.ShapeDtypeStruct(shape, F32),
        in_specs=[SMEM] * 4 + [VMEM] * 14,
        out_specs=VMEM,
        scratch_shapes=[
            pltpu.VMEM((4, 2 * HALO, cols + 2 * HALO, 128), F32),
            pltpu.VMEM((4, 8, cols + 16, 128), F32),
            pltpu.VMEM((4, pr + 4, pc + 8, 128), F32),
            pltpu.VMEM(lut.shape, BF16),
            pltpu.VMEM((2, len(offsets), 256, 256), BF16),
            pltpu.VMEM((2, 4, high, 256), F32),
            pltpu.VMEM((4, rows, cols, 128), F32),
            pltpu.VMEM((4, pr, pc, 128), F32),
            pltpu.SemaphoreType.DMA,
        ],
        compiler_params=params(30),
        cost_estimate=cost(rows * cols, 150, bases.size * 2),
    )(
        jnp.asarray([e for _, e in plan()], jnp.int32), jnp.asarray([o for o, _ in plan()], jnp.int32),
        jnp.asarray(mirrors, jnp.int32), even,
        *ends, edge, pmodes, upw, masks, lut, rotation, pin, back, bases, signs, down, inv,
    )


def swapped(low, high, axis, odd_first):
    peers = lax.axis_size(axis)
    even = lax.axis_index(axis) % 2 == 0
    strips = (jnp.where(even, high, low), jnp.where(even, low, high))
    got = [None, None]
    for kind in (1, 0) if odd_first else (0, 1):
        pairs = [(i, i + 1) for i in range(kind, peers - 1, 2)]
        got[kind] = lax.ppermute(strips[kind], axis, pairs + [(j, i) for i, j in pairs])
    return got


def local(leaf_up, parent_in, leaf_lists, parent_lists, up_transfer, down_transfer, check_inverse):
    rows, cols, _ = leaf_up.shape
    even = [lax.axis_index(axis) % 2 == 0 for axis in ("gx", "gy")]
    flag = jnp.stack(even).astype(jnp.int32)
    rotation, back, table, signs = (jnp.asarray(x) for x in operators())
    strips = swapped(leaf_up[:, :HALO], leaf_up[:, cols - HALO :], "gy", True)
    left = jnp.where(even[1], strips[1], strips[0])
    right = jnp.where(even[1], strips[0], strips[1])
    broad = lambda s: jnp.concatenate([left[s], leaf_up[s], right[s]], axis=1)
    ends = swapped(broad(slice(0, HALO)), broad(slice(rows - HALO, rows)), "gx", False)
    parent_up, lut, edge, pmodes, masks, upw = near_step(
        flag, strips, leaf_up, rotation, up_transfer, leaf_lists, parent_lists
    )
    leaf_down = close_step(
        flag, ends, edge, pmodes, upw, masks, lut, rotation, parent_in, back, table, signs,
        down_transfer, check_inverse, leaf_up.shape,
    )
    return leaf_down, parent_up


def solution(mesh):
    block = P("gx", "gy", None)
    return jax.shard_map(
        local,
        mesh=mesh,
        in_specs=(block,) * 4 + (P(),) * 3,
        out_specs=(block, block),
        check_vma=False,
    )
```

```python
import functools
import math

import jax
import jax.numpy as jnp
import ml_dtypes
import numpy as np
from jax import lax
from jax.experimental import pallas as pl
from jax.experimental.pallas import tpu as pltpu
from jax.sharding import PartitionSpec as P

ORDER = 6
HALO = 4
KEPT = 14
BF16, F32 = jnp.bfloat16, jnp.float32

def offset_table():
    return [(a, b) for a in range(-3, 4) for b in range(-3, 4) if max(abs(a), abs(b)) >= 2]


BASES = sorted({(abs(a), abs(b)) for a, b in offset_table()})


def surface_points():
    grid = np.linspace(-1.0, 1.0, ORDER)
    keys = [
        (i, j, k)
        for i in range(ORDER)
        for j in range(ORDER)
        for k in range(ORDER)
        if min(i, j, k) == 0 or max(i, j, k) == ORDER - 1
    ]
    return keys, np.array([[grid[i] for i in key] for key in keys])


def translation(points, dx, dy):
    r = 0.525 * (points[:, None, :] - points[None, :, :]) - np.array([dx, dy, 0.0])
    dist = np.sqrt((r * r).sum(-1))
    n = len(points)
    out = np.zeros((3, n, 3, n))
    for a in range(3):
        for b in range(3):
            out[a, :, b, :] = (float(a == b) / dist + r[..., a] * r[..., b] / dist**3) / (8 * math.pi)
    return out.reshape(3 * n, 3 * n)


def split(x):
    high = x.astype(ml_dtypes.bfloat16)
    return high, (x - high.astype(np.float64)).astype(ml_dtypes.bfloat16)


@functools.lru_cache(maxsize=None)
def operators():
    keys, points = surface_points()
    n = len(keys)
    points_of = {key: i for i, key in enumerate(keys)}
    mirror = [points_of[(i, j, ORDER - 1 - k)] for i, j, k in keys]
    mats = {o: translation(points, *o) for o in offset_table()}
    half = 3 * n // 2
    rotation = np.zeros((3 * n, 512), ml_dtypes.bfloat16)
    back = np.zeros((512, 3 * n))
    table = np.zeros((2, len(BASES), 256, 256), ml_dtypes.bfloat16)
    signs = np.ones((4, 2, 256, 256), ml_dtypes.bfloat16)
    for s, sign in enumerate((1, -1)):
        pairs = np.zeros((3 * n, half))
        firsts = []
        for a in range(3):
            flip = sign if a < 2 else -sign
            for i in range(n):
                if i < mirror[i]:
                    pairs[a * n + i, len(firsts)] = 1.0
                    pairs[a * n + mirror[i], len(firsts)] = flip
                    firsts.append(a * n + i)
        blocks = {o: 0.25 * pairs.T @ m @ pairs for o, m in mats.items()}
        gram = sum(b.T @ b for b in blocks.values())
        place = {f: i for i, f in enumerate(firsts)}
        modes, parity, weight = [], [], []
        for sx in (1, -1):
            for sy in (1, -1):
                basis = []
                for i, f in enumerate(firsts):
                    a, (kx, ky, kz) = f // n, keys[f % n]
                    if kx < ORDER // 2 and ky < ORDER // 2:
                        v = np.zeros(half)
                        for fx in range(2):
                            for fy in range(2):
                                key = (ORDER - 1 - kx if fx else kx, ORDER - 1 - ky if fy else ky, kz)
                                sign_x = (sx if a != 0 else -sx) if fx else 1
                                sign_y = (sy if a != 1 else -sy) if fy else 1
                                v[place[a * n + points_of[key]]] = 0.5 * sign_x * sign_y
                        basis.append(v)
                basis = np.array(basis).T
                w, vecs = np.linalg.eigh(basis.T @ gram @ basis)
                vecs = basis @ vecs
                vecs = vecs * np.sign(vecs[np.abs(np.round(vecs, 9)).argmax(0), np.arange(len(w))])
                modes.append(vecs)
                weight.append(w)
                parity += [(sx, sy)] * len(w)
        order = np.argsort(-np.concatenate(weight), kind="stable")
        vecs = np.concatenate(modes, axis=1)[:, order]
        parity = np.array(parity)[order]
        modes = (pairs @ vecs / math.sqrt(2.0)).astype(ml_dtypes.bfloat16)
        lows = np.concatenate([modes, modes[:, :KEPT], modes[:, :KEPT]], axis=1)
        rotation[:, 256 * s : 256 * (s + 1)] = lows
        outs, out_parity = [], []
        for sx in (1, -1):
            for sy in (1, -1):
                for f in firsts:
                    a, (kx, ky, kz) = f // n, keys[f % n]
                    if kx < ORDER // 2 and ky < ORDER // 2:
                        v = np.zeros(half)
                        for fx in range(2):
                            for fy in range(2):
                                key = (ORDER - 1 - kx if fx else kx, ORDER - 1 - ky if fy else ky, kz)
                                sign_x = (sx if a != 0 else -sx) if fx else 1
                                sign_y = (sy if a != 1 else -sy) if fy else 1
                                v[place[a * n + points_of[key]]] = sign_x * sign_y
                        outs.append(v)
                        out_parity.append((sx, sy))
        outs = np.array(outs).T
        out_parity = np.array(out_parity)
        back[256 * s : 256 * s + half] = (pairs @ outs).T
        undo = np.linalg.inv(modes[firsts].astype(np.float64))
        for q, o in enumerate(BASES):
            high, low = split(undo @ blocks[o].T @ outs * 0.25)
            table[s, q, :half, :half] = high
            table[s, q, half : half + KEPT, :half] = high[:KEPT]
            table[s, q, half + KEPT : half + 2 * KEPT, :half] = low[:KEPT]
        ins = np.concatenate([parity, parity[:KEPT], parity[:KEPT]], axis=0)
        for f in range(4):
            row = np.ones(256)
            row[: len(ins)] = (ins[:, 0] if f // 2 else 1) * (ins[:, 1] if f % 2 else 1)
            col = np.ones(256)
            col[:half] = (out_parity[:, 0] if f // 2 else 1) * (out_parity[:, 1] if f % 2 else 1)
            signs[f, s] = row[:, None] * col[None, :]
    whole = [
        table[:, BASES.index((abs(a), abs(b)))] * signs[2 * (a < 0) + (b < 0)]
        for a, b in offset_table()
    ]
    return rotation, back.astype(ml_dtypes.bfloat16), np.stack(whole, axis=1)


@functools.lru_cache(maxsize=None)
def plan():
    products = []
    for c, d in class_pairs():
        for o, (dx, dy) in enumerate(offset_table()):
            px, cs = divmod(c + dx, 2)
            py, ds = divmod(d + dy, 2)
            if abs(px) <= 1 and abs(py) <= 1:
                products.append((o, (cs * 3 + px + 1) * 6 + ds * 3 + py + 1))
    return products


def class_pairs():
    return [(c, d) for c in range(2) for d in range(2)]


def dot(a, b):
    return lax.dot_general(a, b, (((1,), (0,)), ((), ())), preferred_element_type=F32)


def dot_t(a, b):
    return lax.dot_general(a, b, (((1,), (1,)), ((), ())), preferred_element_type=F32)


def parts(x):
    high = x.astype(BF16)
    return high, (x - high.astype(F32)).astype(BF16)


def times_t(x, weight):
    xh, xl = parts(x)
    wh, wl = weight
    both = dot_t(jnp.concatenate([xh, xl], axis=0), wh)
    return both[: x.shape[0]] + (both[x.shape[0] :] + dot_t(xh, wl))


def times_exact(x, weight):
    both = dot(jnp.concatenate(parts(x), axis=0), weight)
    return both[: x.shape[0]] + both[x.shape[0] :]


def lanes(ref, *at):
    pieces = [ref[(t,) + at] for t in range(4)]
    pieces = [p.reshape(-1, 128) for p in pieces]
    return jnp.concatenate(pieces, axis=1)


def cut_tiles(dens):
    return [(t, slice(128 * t, min(128 * t + 128, dens)), slice(0, min(128, dens - 128 * t))) for t in range(4)]


def modes_of(x, rot_ref, dens):
    y = times_exact(x[:, :dens], rot_ref[...])
    lane = lax.broadcasted_iota(jnp.int32, (1, 512), 1) % 256
    half = dens // 2
    is_low = (lane >= half) & (lane < half + KEPT)
    return jnp.where(is_low, y - y.astype(BF16).astype(F32), y)


def children(ref, dens, counts, c, d):
    return jnp.concatenate(
        [
            jnp.concatenate(
                [ref[t, 2 * i + c, pl.ds(d, counts[1], stride=2), :] for i in range(counts[0])],
                axis=0,
            )
            for t in range(4)
        ],
        axis=1,
    )[:, :dens]


def own_kernel(own_ref, rot_ref, modes_ref):
    rows, cols, dens = own_ref.shape
    y = modes_of(own_ref[...].reshape(rows * cols, dens), rot_ref, dens)
    for t in range(4):
        modes_ref[t] = y[:, 128 * t : 128 * t + 128].reshape(rows, cols, 128)


def near_kernel(
    even_ref, strip0_ref, strip1_ref, own_ref, own_modes_ref, rot_ref, up_ref, llist_ref, plist_ref,
    pup_ref, lut, edge_ref, pmodes_ref, masks_ref, upw_ref,
    own_t, strip_t, modes, flat,
):
    rows, cols, dens = own_ref.shape
    pr, pc = rows // 2, cols // 2
    gr, gc = pr // 2, pc // 2
    boxes = pr * pc
    used = boxes + gr * gc
    high = lut.shape[2]
    count = masks_ref.shape[0] // 4
    even = even_ref[1] == 1
    for t, cut, to in cut_tiles(dens):
        own_t[t, :, :, to] = own_ref[:, :, cut]
        first, second = strip0_ref[:, :, cut], strip1_ref[:, :, cut]
        strip_t[t, :, 0:HALO, to] = jnp.where(even, second, first)
        strip_t[t, :, HALO:, to] = jnp.where(even, first, second)

    parent = None
    for n, (c, d) in enumerate(class_pairs()):
        upw_ref[n, 0], upw_ref[n, 1] = parts(up_ref[n])
        x = jnp.concatenate(
            [children(own_t, dens, (pr, pc), c, d), children(strip_t, dens, (pr, HALO), c, d)],
            axis=0,
        )
        part = times_t(x, (upw_ref[n, 0], upw_ref[n, 1]))
        parent = part if parent is None else parent + part
    pup_ref[...] = parent[:boxes].reshape(pr, pc, dens)
    z = modes_of(jnp.concatenate([lanes(strip_t)[:, :dens], parent], axis=0), rot_ref, dens)
    w, p = z[: rows * 8], z[rows * 8 :]
    for t in range(4):
        cut = slice(128 * t, 128 * t + 128)
        modes[t, 2 : 2 + rows, 8 : 8 + cols, :] = own_modes_ref[t]
        strip = w[:, cut].reshape(rows, 8, 128)
        modes[t, 2 : 2 + rows, 4:8, :] = strip[:, 0:4]
        modes[t, 2 : 2 + rows, 8 + cols : 12 + cols, :] = strip[:, 4:8]
        edge_ref[t, 0:2] = modes[t, 2:4]
        edge_ref[t, 2:4] = modes[t, rows : rows + 2]
        pmodes_ref[t, 2 : 2 + pr, 4 : 4 + pc, :] = p[:boxes, cut].reshape(pr, pc, 128)
        strip = p[boxes:, cut].reshape(pr, 4, 128)
        pmodes_ref[t, 2 : 2 + pr, 2:4, :] = strip[:, 0:2]
        pmodes_ref[t, 2 : 2 + pr, 4 + pc : 6 + pc, :] = strip[:, 2:4]

    def gather(i, carry):
        base = 2 * (i % 3) + i // 3
        for ds in range(2):
            for py in (-1, 0, 1):
                e = i * 6 + ds * 3 + py + 1
                for t in range(4):
                    x = jnp.concatenate(
                        [
                            modes[t, base + 2 * j, pl.ds(8 + 2 * py + ds, pc, stride=2), :]
                            for j in range(pr)
                        ]
                        + [
                            pmodes_ref[t, base + 2 * j, pl.ds(4 + 2 * py + ds, gc, stride=2), :]
                            for j in range(gr)
                        ]
                        + [jnp.zeros((high - used, 128), F32)],
                        axis=0,
                    )
                    lut[e, t // 2, :, 128 * (t % 2) : 128 * (t % 2) + 128] = x.astype(BF16)
        return carry

    lax.fori_loop(0, 6, gather, 0)

    flat[0, :, :, 0 : llist_ref.shape[2]] = llist_ref[...].astype(F32)
    flat[1, 0:pr, 0:pc, 0 : plist_ref.shape[2]] = plist_ref[...].astype(F32)
    for n, (c, d) in enumerate(class_pairs()):
        flag = jnp.concatenate(
            [flat[0, 2 * i + c, pl.ds(d, pc, stride=2), :] for i in range(pr)]
            + [flat[1, 2 * i + c, pl.ds(d, gc, stride=2), :] for i in range(gr)]
            + [jnp.zeros((high - used, 128), F32)],
            axis=0,
        )
        for k in range(count):
            o = plan()[count * n + k][0]
            masks_ref[count * n + k] = jnp.broadcast_to(flag[:, o : o + 1], (high, 128)).astype(BF16)


def close_kernel(
    entry_ref, pick_ref, even_ref,
    end0_ref, end1_ref, edge_ref, pside_ref, upw_ref, masks, lut_ref,
    rot_ref, pin_ref, back, table, down_ref, inv_ref,
    out_ref,
    ends_t, edge, pmodes, lut, acc, flat, plocal, sem,
):
    rows, cols, dens = out_ref.shape
    pr, pc = rows // 2, cols // 2
    gr, gc = pr // 2, pc // 2
    boxes, pboxes = pr * pc, gr * gc
    high = lut.shape[2]
    wide = end0_ref.shape[1]
    count = masks.shape[0] // 4
    copy = pltpu.make_async_copy(lut_ref, lut, sem)
    copy.start()
    even = even_ref[0] == 1
    for t, cut, to in cut_tiles(dens):
        first, second = end0_ref[:, :, cut], end1_ref[:, :, cut]
        ends_t[t, 0:HALO, :, to] = jnp.where(even, second, first)
        ends_t[t, HALO:, :, to] = jnp.where(even, first, second)
    parent = None
    for n, (c, d) in enumerate(class_pairs()):
        x = children(ends_t, dens, (HALO, wide // 2), c, d)
        part = times_t(x, (upw_ref[n, 0], upw_ref[n, 1]))
        parent = part if parent is None else parent + part
    x = lanes(ends_t, slice(HALO - 2, HALO + 2))[:, :dens]
    y = modes_of(jnp.concatenate([x, parent], axis=0), rot_ref, dens)
    z, p = y[: 4 * wide], y[4 * wide :]
    for t in range(4):
        cut = slice(128 * t, 128 * t + 128)
        end = z[:, cut].reshape(4, wide, 128)
        edge[t, 0:2, 4 : 4 + wide, :] = end[0:2]
        edge[t, 2:4] = edge_ref[t, 0:2]
        edge[t, 4:6] = edge_ref[t, 2:4]
        edge[t, 6:8, 4 : 4 + wide, :] = end[2:4]
        end = p[:, cut].reshape(4, wide // 2, 128)
        pmodes[t, 0:2, 2 : 2 + wide // 2, :] = end[0:2]
        pmodes[t, 2 : 2 + pr] = pside_ref[t, 2 : 2 + pr]
        pmodes[t, 2 + pr :, 2 : 2 + wide // 2, :] = end[2:4]

    copy.wait()

    def patch(cs, carry):
        for ds in range(2):
            for py in (-1, 0, 1):
                for t in range(4):
                    at = slice(128 * (t % 2), 128 * (t % 2) + 128)
                    mine = pl.ds(8 + 2 * py + ds, pc, stride=2)
                    theirs = pl.ds(4 + 2 * py + ds, gc, stride=2)
                    e = cs * 18 + ds * 3 + py + 1
                    x = jnp.concatenate([edge[t, cs + 2 * j, mine, :] for j in range(2)], axis=0)
                    lut[e, t // 2, 0:16, at] = x.astype(BF16)
                    x = jnp.concatenate([pmodes[t, cs + 2 * j, theirs, :] for j in range(4)], axis=0)
                    lut[e, t // 2, boxes : boxes + 16, at] = x.astype(BF16)
                    e = e + 12
                    x = jnp.concatenate([edge[t, 4 + cs + 2 * j, mine, :] for j in range(2)], axis=0)
                    lut[e, t // 2, boxes - 16 : boxes, at] = x.astype(BF16)
                    x = jnp.concatenate(
                        [pmodes[t, 4 + cs + 2 * j, theirs, :] for j in range(4, gr)]
                        + [jnp.zeros((high - boxes - pboxes, 128), F32)],
                        axis=0,
                    )
                    lut[e, t // 2, boxes + 16 : high, at] = x.astype(BF16)
        return carry

    lax.fori_loop(0, 2, patch, 0)

    def interact(j, carry):
        n, s = j // 2, j % 2
        total = jnp.zeros((high, 256), F32)
        for k in range(count):
            i = n * count + k
            m = masks[i]
            x = lut[entry_ref[i], s]
            x = jnp.concatenate([x[:, :128] * m, x[:, 128:] * m], axis=1)
            total = total + dot(x, table[s, pick_ref[i]])
        acc[s, n] = total
        return carry

    lax.fori_loop(0, 8, interact, 0)

    check = None
    for s in range(2):
        part = times_exact(acc[s].reshape(4 * high, 256), back[256 * s : 256 * (s + 1)])
        check = part if check is None else check + part

    inverse = parts(inv_ref[...])
    for n, (c, d) in enumerate(class_pairs()):
        for t, cut, to in cut_tiles(dens):
            for j in range(gr):
                r = high * n + boxes + gc * j
                plocal[t, 2 * j + c, pl.ds(d, gc, stride=2), to] = check[r : r + gc, cut]
    local = pin_ref[...].reshape(boxes, dens) + times_t(lanes(plocal)[:, :dens], inverse)
    x = jnp.concatenate(
        [
            check[high * n : high * n + boxes] + times_t(local, parts(down_ref[n]))
            for n in range(4)
        ],
        axis=0,
    )
    result = times_t(x, inverse)
    for n, (c, d) in enumerate(class_pairs()):
        for t, cut, to in cut_tiles(dens):
            for j in range(pr):
                r = boxes * n + pc * j
                flat[t, 2 * j + c, pl.ds(d, pc, stride=2), to] = result[r : r + pc, cut]
    for t, cut, to in cut_tiles(dens):
        out_ref[:, :, cut] = flat[t, :, :, to]


VMEM = pl.BlockSpec(memory_space=pltpu.VMEM)
SMEM = pl.BlockSpec(memory_space=pltpu.SMEM)


def params(mib):
    return pltpu.CompilerParams(vmem_limit_bytes=mib * 1024 * 1024)


def cost(rows, tiles, reads):
    return pl.CostEstimate(flops=2 * rows * tiles * 256 * 256, bytes_accessed=reads, transcendentals=0)


def height(boxes):
    return -(-(boxes * 5 // 4) // 16) * 16


def own_step(own, rotation):
    rows, cols, _ = own.shape
    return pl.pallas_call(
        own_kernel,
        out_shape=jax.ShapeDtypeStruct((4, rows, cols, 128), F32),
        in_specs=[VMEM] * 2,
        out_specs=VMEM,
        compiler_params=params(16),
        cost_estimate=cost(rows * cols, 48, 16 * 1024 * 1024),
    )(own, rotation)


def near_step(even, strips, own, own_modes, rotation, up, llist, plist):
    rows, cols, dens = own.shape
    pr, pc = rows // 2, cols // 2
    high = height(pr * pc)
    return pl.pallas_call(
        near_kernel,
        out_shape=(
            jax.ShapeDtypeStruct((pr, pc, dens), F32),
            jax.ShapeDtypeStruct((36, 2, high, 256), BF16),
            jax.ShapeDtypeStruct((4, 4, cols + 16, 128), F32),
            jax.ShapeDtypeStruct((4, pr + 4, pc + 8, 128), F32),
            jax.ShapeDtypeStruct((len(plan()), high, 128), BF16),
            jax.ShapeDtypeStruct((4, 2, dens, dens), BF16),
        ),
        in_specs=[SMEM] + [VMEM] * 8,
        out_specs=(VMEM,) * 6,
        scratch_shapes=[
            pltpu.VMEM((4, rows, cols, 128), F32),
            pltpu.VMEM((4, rows, 2 * HALO, 128), F32),
            pltpu.VMEM((4, rows + 4, cols + 16, 128), F32),
            pltpu.VMEM((2, rows, cols, 128), F32),
        ],
        compiler_params=params(24),
        cost_estimate=cost(rows * cols, 48, up.size * 4),
    )(even, *strips, own, own_modes, rotation, up, llist, plist)


def close_step(even, ends, edge, pmodes, upw, masks, lut, rotation, pin, back, table, down, inv, shape):
    rows, cols, dens = shape
    pr, pc = rows // 2, cols // 2
    high = height(pr * pc)
    return pl.pallas_call(
        close_kernel,
        out_shape=jax.ShapeDtypeStruct(shape, F32),
        in_specs=[SMEM] * 3 + [VMEM] * 13,
        out_specs=VMEM,
        scratch_shapes=[
            pltpu.VMEM((4, 2 * HALO, cols + 2 * HALO, 128), F32),
            pltpu.VMEM((4, 8, cols + 16, 128), F32),
            pltpu.VMEM((4, pr + 4, pc + 8, 128), F32),
            pltpu.VMEM(lut.shape, BF16),
            pltpu.VMEM((2, 4, high, 256), F32),
            pltpu.VMEM((4, rows, cols, 128), F32),
            pltpu.VMEM((4, pr, pc, 128), F32),
            pltpu.SemaphoreType.DMA,
        ],
        compiler_params=params(24),
        cost_estimate=cost(rows * cols, 150, table.size * 2),
    )(
        jnp.asarray([e for _, e in plan()], jnp.int32), jnp.asarray([o for o, _ in plan()], jnp.int32),
        even, *ends, edge, pmodes, upw, masks, lut, rotation, pin, back, table, down, inv,
    )


def swapped(low, high, axis, odd_first):
    peers = lax.axis_size(axis)
    even = lax.axis_index(axis) % 2 == 0
    strips = (jnp.where(even, high, low), jnp.where(even, low, high))
    got = [None, None]
    for kind in (1, 0) if odd_first else (0, 1):
        pairs = [(i, i + 1) for i in range(kind, peers - 1, 2)]
        got[kind] = lax.ppermute(strips[kind], axis, pairs + [(j, i) for i, j in pairs])
    return got


def local(leaf_up, parent_in, leaf_lists, parent_lists, up_transfer, down_transfer, check_inverse):
    rows, cols, _ = leaf_up.shape
    even = [lax.axis_index(axis) % 2 == 0 for axis in ("gx", "gy")]
    flag = jnp.stack(even).astype(jnp.int32)
    rotation, back, table = (jnp.asarray(x) for x in operators())
    strips = swapped(leaf_up[:, :HALO], leaf_up[:, cols - HALO :], "gy", True)
    *strips, own_modes = lax.optimization_barrier((*strips, own_step(leaf_up, rotation)))
    left = jnp.where(even[1], strips[1], strips[0])
    right = jnp.where(even[1], strips[0], strips[1])
    broad = lambda s: jnp.concatenate([left[s], leaf_up[s], right[s]], axis=1)
    ends = swapped(broad(slice(0, HALO)), broad(slice(rows - HALO, rows)), "gx", False)
    parent_up, lut, edge, pmodes, masks, upw = near_step(
        flag, strips, leaf_up, own_modes, rotation, up_transfer, leaf_lists, parent_lists
    )
    leaf_down = close_step(
        flag, ends, edge, pmodes, upw, masks, lut, rotation, parent_in, back, table,
        down_transfer, check_inverse, leaf_up.shape,
    )
    return leaf_down, parent_up


def solution(mesh):
    block = P("gx", "gy", None)
    return jax.shard_map(
        local,
        mesh=mesh,
        in_specs=(block,) * 4 + (P(),) * 3,
        out_specs=(block, block),
        check_vma=False,
    )
```

```python
import functools
import math

import jax
import jax.numpy as jnp
import ml_dtypes
import numpy as np
from jax import lax
from jax.experimental import pallas as pl
from jax.experimental.pallas import tpu as pltpu
from jax.sharding import PartitionSpec as P

ORDER = 6
HALO = 4
KEPT = 14
BF16, F32 = jnp.bfloat16, jnp.float32

def offset_table():
    return [(a, b) for a in range(-3, 4) for b in range(-3, 4) if max(abs(a), abs(b)) >= 2]


BASES = sorted({(abs(a), abs(b)) for a, b in offset_table()})


def surface_points():
    grid = np.linspace(-1.0, 1.0, ORDER)
    keys = [
        (i, j, k)
        for i in range(ORDER)
        for j in range(ORDER)
        for k in range(ORDER)
        if min(i, j, k) == 0 or max(i, j, k) == ORDER - 1
    ]
    return keys, np.array([[grid[i] for i in key] for key in keys])


def translation(points, dx, dy):
    r = 0.525 * (points[:, None, :] - points[None, :, :]) - np.array([dx, dy, 0.0])
    dist = np.sqrt((r * r).sum(-1))
    n = len(points)
    out = np.zeros((3, n, 3, n))
    for a in range(3):
        for b in range(3):
            out[a, :, b, :] = (float(a == b) / dist + r[..., a] * r[..., b] / dist**3) / (8 * math.pi)
    return out.reshape(3 * n, 3 * n)


def split(x):
    high = x.astype(ml_dtypes.bfloat16)
    return high, (x - high.astype(np.float64)).astype(ml_dtypes.bfloat16)


@functools.lru_cache(maxsize=None)
def operators():
    keys, points = surface_points()
    n = len(keys)
    points_of = {key: i for i, key in enumerate(keys)}
    mirror = [points_of[(i, j, ORDER - 1 - k)] for i, j, k in keys]
    mats = {o: translation(points, *o) for o in offset_table()}
    half = 3 * n // 2
    rotation = np.zeros((3 * n, 512), ml_dtypes.bfloat16)
    back = np.zeros((512, 3 * n))
    table = np.zeros((2, len(BASES), 256, 256), ml_dtypes.bfloat16)
    signs = np.ones((4, 2, 256, 256), ml_dtypes.bfloat16)
    for s, sign in enumerate((1, -1)):
        pairs = np.zeros((3 * n, half))
        firsts = []
        for a in range(3):
            flip = sign if a < 2 else -sign
            for i in range(n):
                if i < mirror[i]:
                    pairs[a * n + i, len(firsts)] = 1.0
                    pairs[a * n + mirror[i], len(firsts)] = flip
                    firsts.append(a * n + i)
        blocks = {o: 0.25 * pairs.T @ m @ pairs for o, m in mats.items()}
        gram = sum(b.T @ b for b in blocks.values())
        place = {f: i for i, f in enumerate(firsts)}
        modes, parity, weight = [], [], []
        for sx in (1, -1):
            for sy in (1, -1):
                basis = []
                for i, f in enumerate(firsts):
                    a, (kx, ky, kz) = f // n, keys[f % n]
                    if kx < ORDER // 2 and ky < ORDER // 2:
                        v = np.zeros(half)
                        for fx in range(2):
                            for fy in range(2):
                                key = (ORDER - 1 - kx if fx else kx, ORDER - 1 - ky if fy else ky, kz)
                                sign_x = (sx if a != 0 else -sx) if fx else 1
                                sign_y = (sy if a != 1 else -sy) if fy else 1
                                v[place[a * n + points_of[key]]] = 0.5 * sign_x * sign_y
                        basis.append(v)
                basis = np.array(basis).T
                w, vecs = np.linalg.eigh(basis.T @ gram @ basis)
                vecs = basis @ vecs
                vecs = vecs * np.sign(vecs[np.abs(np.round(vecs, 9)).argmax(0), np.arange(len(w))])
                modes.append(vecs)
                weight.append(w)
                parity += [(sx, sy)] * len(w)
        order = np.argsort(-np.concatenate(weight), kind="stable")
        vecs = np.concatenate(modes, axis=1)[:, order]
        parity = np.array(parity)[order]
        modes = (pairs @ vecs / math.sqrt(2.0)).astype(ml_dtypes.bfloat16)
        lows = np.concatenate([modes, modes[:, :KEPT], modes[:, :KEPT]], axis=1)
        rotation[:, 256 * s : 256 * (s + 1)] = lows
        outs, out_parity = [], []
        for sx in (1, -1):
            for sy in (1, -1):
                for f in firsts:
                    a, (kx, ky, kz) = f // n, keys[f % n]
                    if kx < ORDER // 2 and ky < ORDER // 2:
                        v = np.zeros(half)
                        for fx in range(2):
                            for fy in range(2):
                                key = (ORDER - 1 - kx if fx else kx, ORDER - 1 - ky if fy else ky, kz)
                                sign_x = (sx if a != 0 else -sx) if fx else 1
                                sign_y = (sy if a != 1 else -sy) if fy else 1
                                v[place[a * n + points_of[key]]] = sign_x * sign_y
                        outs.append(v)
                        out_parity.append((sx, sy))
        outs = np.array(outs).T
        out_parity = np.array(out_parity)
        back[256 * s : 256 * s + half] = (pairs @ outs).T
        undo = np.linalg.inv(modes[firsts].astype(np.float64))
        for q, o in enumerate(BASES):
            high, low = split(undo @ blocks[o].T @ outs * 0.25)
            table[s, q, :half, :half] = high
            table[s, q, half : half + KEPT, :half] = high[:KEPT]
            table[s, q, half + KEPT : half + 2 * KEPT, :half] = low[:KEPT]
        ins = np.concatenate([parity, parity[:KEPT], parity[:KEPT]], axis=0)
        for f in range(4):
            row = np.ones(256)
            row[: len(ins)] = (ins[:, 0] if f // 2 else 1) * (ins[:, 1] if f % 2 else 1)
            col = np.ones(256)
            col[:half] = (out_parity[:, 0] if f // 2 else 1) * (out_parity[:, 1] if f % 2 else 1)
            signs[f, s] = row[:, None] * col[None, :]
    whole = [
        table[:, BASES.index((abs(a), abs(b)))] * signs[2 * (a < 0) + (b < 0)]
        for a, b in offset_table()
    ]
    return rotation, back.astype(ml_dtypes.bfloat16), np.stack(whole, axis=1)


@functools.lru_cache(maxsize=None)
def plan():
    products = []
    offsets = offset_table()
    for c, d in class_pairs():
        for o in sorted(range(len(offsets)), key=lambda o: (abs(offsets[o][1]) == 3, o)):
            dx, dy = offsets[o]
            px, cs = divmod(c + dx, 2)
            py, ds = divmod(d + dy, 2)
            if abs(px) <= 1 and abs(py) <= 1:
                products.append((o, (cs * 3 + px + 1) * 6 + ds * 3 + py + 1))
    return products


def class_pairs():
    return [(c, d) for c in range(2) for d in range(2)]


def dot(a, b):
    return lax.dot_general(a, b, (((1,), (0,)), ((), ())), preferred_element_type=F32)


def dot_t(a, b):
    return lax.dot_general(a, b, (((1,), (1,)), ((), ())), preferred_element_type=F32)


def parts(x):
    high = x.astype(BF16)
    return high, (x - high.astype(F32)).astype(BF16)


def times_t(x, weight):
    xh, xl = parts(x)
    wh, wl = weight
    both = dot_t(jnp.concatenate([xh, xl], axis=0), wh)
    return both[: x.shape[0]] + (both[x.shape[0] :] + dot_t(xh, wl))


def times_exact(x, weight):
    both = dot(jnp.concatenate(parts(x), axis=0), weight)
    return both[: x.shape[0]] + both[x.shape[0] :]


def lanes(ref, *at):
    pieces = [ref[(t,) + at] for t in range(4)]
    pieces = [p.reshape(-1, 128) for p in pieces]
    return jnp.concatenate(pieces, axis=1)


def cut_tiles(dens):
    return [(t, slice(128 * t, min(128 * t + 128, dens)), slice(0, min(128, dens - 128 * t))) for t in range(4)]


def modes_of(x, rot_ref, dens):
    y = times_exact(x[:, :dens], rot_ref[...])
    lane = lax.broadcasted_iota(jnp.int32, (1, 512), 1) % 256
    half = dens // 2
    is_low = (lane >= half) & (lane < half + KEPT)
    return jnp.where(is_low, y - y.astype(BF16).astype(F32), y)


def children(ref, dens, counts, c, d):
    return jnp.concatenate(
        [
            jnp.concatenate(
                [ref[t, 2 * i + c, pl.ds(d, counts[1], stride=2), :] for i in range(counts[0])],
                axis=0,
            )
            for t in range(4)
        ],
        axis=1,
    )[:, :dens]


def own_kernel(own_ref, rot_ref, modes_ref):
    rows, cols, dens = own_ref.shape
    y = modes_of(own_ref[...].reshape(rows * cols, dens), rot_ref, dens)
    for t in range(4):
        modes_ref[t] = y[:, 128 * t : 128 * t + 128].reshape(rows, cols, 128)


def near_kernel(
    even_ref, strip0_ref, strip1_ref, own_ref, own_modes_ref, rot_ref, up_ref, llist_ref, plist_ref,
    pup_ref, lut, edge_ref, pmodes_ref, masks_ref, upw_ref,
    own_t, strip_t, modes, flat,
):
    rows, cols, dens = own_ref.shape
    pr, pc = rows // 2, cols // 2
    gr, gc = pr // 2, pc // 2
    boxes = pr * pc
    used = boxes + gr * gc
    high = lut.shape[2]
    count = masks_ref.shape[0] // 4
    even = even_ref[1] == 1
    for t, cut, to in cut_tiles(dens):
        own_t[t, :, :, to] = own_ref[:, :, cut]
        first, second = strip0_ref[:, :, cut], strip1_ref[:, :, cut]
        strip_t[t, :, 0:HALO, to] = jnp.where(even, second, first)
        strip_t[t, :, HALO:, to] = jnp.where(even, first, second)

    parent = None
    for n, (c, d) in enumerate(class_pairs()):
        upw_ref[n, 0], upw_ref[n, 1] = parts(up_ref[n])
        x = jnp.concatenate(
            [children(own_t, dens, (pr, pc), c, d), children(strip_t, dens, (pr, HALO), c, d)],
            axis=0,
        )
        part = times_t(x, (upw_ref[n, 0], upw_ref[n, 1]))
        parent = part if parent is None else parent + part
    pup_ref[...] = parent[:boxes].reshape(pr, pc, dens)
    z = modes_of(jnp.concatenate([lanes(strip_t)[:, :dens], parent], axis=0), rot_ref, dens)
    w, p = z[: rows * 8], z[rows * 8 :]
    for t in range(4):
        cut = slice(128 * t, 128 * t + 128)
        modes[t, 2 : 2 + rows, 8 : 8 + cols, :] = own_modes_ref[t]
        strip = w[:, cut].reshape(rows, 8, 128)
        modes[t, 2 : 2 + rows, 4:8, :] = strip[:, 0:4]
        modes[t, 2 : 2 + rows, 8 + cols : 12 + cols, :] = strip[:, 4:8]
        edge_ref[t, 0:2] = modes[t, 2:4]
        edge_ref[t, 2:4] = modes[t, rows : rows + 2]
        pmodes_ref[t, 2 : 2 + pr, 4 : 4 + pc, :] = p[:boxes, cut].reshape(pr, pc, 128)
        strip = p[boxes:, cut].reshape(pr, 4, 128)
        pmodes_ref[t, 2 : 2 + pr, 2:4, :] = strip[:, 0:2]
        pmodes_ref[t, 2 : 2 + pr, 4 + pc : 6 + pc, :] = strip[:, 2:4]

    def gather(i, carry):
        base = 2 * (i % 3) + i // 3
        for ds in range(2):
            for py in (-1, 0, 1):
                e = i * 6 + ds * 3 + py + 1
                for t in range(4):
                    x = jnp.concatenate(
                        [
                            modes[t, base + 2 * j, pl.ds(8 + 2 * py + ds, pc, stride=2), :]
                            for j in range(pr)
                        ]
                        + [
                            pmodes_ref[t, base + 2 * j, pl.ds(4 + 2 * py + ds, gc, stride=2), :]
                            for j in range(gr)
                        ]
                        + [jnp.zeros((high - used, 128), F32)],
                        axis=0,
                    )
                    lut[e, t // 2, :, 128 * (t % 2) : 128 * (t % 2) + 128] = x.astype(BF16)
        return carry

    lax.fori_loop(0, 6, gather, 0)

    flat[0, :, :, 0 : llist_ref.shape[2]] = llist_ref[...].astype(F32)
    flat[1, 0:pr, 0:pc, 0 : plist_ref.shape[2]] = plist_ref[...].astype(F32)
    for n, (c, d) in enumerate(class_pairs()):
        flag = jnp.concatenate(
            [flat[0, 2 * i + c, pl.ds(d, pc, stride=2), :] for i in range(pr)]
            + [flat[1, 2 * i + c, pl.ds(d, gc, stride=2), :] for i in range(gr)]
            + [jnp.zeros((high - used, 128), F32)],
            axis=0,
        )
        for k in range(count):
            o = plan()[count * n + k][0]
            masks_ref[count * n + k] = jnp.broadcast_to(flag[:, o : o + 1], (high, 128)).astype(BF16)


def close_kernel(
    entry_ref, pick_ref, even_ref,
    end0_ref, end1_ref, edge_ref, pside_ref, upw_ref, masks, lut_ref,
    rot_ref, pin_ref, back, table, down_ref, inv_ref,
    out_ref,
    ends_t, edge, pmodes, lut, acc, flat, plocal, sem,
):
    rows, cols, dens = out_ref.shape
    pr, pc = rows // 2, cols // 2
    gr, gc = pr // 2, pc // 2
    boxes, pboxes = pr * pc, gr * gc
    high = lut.shape[2]
    wide = end0_ref.shape[1]
    count = masks.shape[0] // 4
    copy = pltpu.make_async_copy(lut_ref, lut, sem)
    copy.start()
    even = even_ref[0] == 1
    for t, cut, to in cut_tiles(dens):
        first, second = end0_ref[:, :, cut], end1_ref[:, :, cut]
        ends_t[t, 0:HALO, :, to] = jnp.where(even, second, first)
        ends_t[t, HALO:, :, to] = jnp.where(even, first, second)
    parent = None
    for n, (c, d) in enumerate(class_pairs()):
        x = children(ends_t, dens, (HALO, wide // 2), c, d)
        part = times_t(x, (upw_ref[n, 0], upw_ref[n, 1]))
        parent = part if parent is None else parent + part
    x = lanes(ends_t, slice(HALO - 2, HALO + 2))[:, :dens]
    y = modes_of(jnp.concatenate([x, parent], axis=0), rot_ref, dens)
    z, p = y[: 4 * wide], y[4 * wide :]
    for t in range(4):
        cut = slice(128 * t, 128 * t + 128)
        end = z[:, cut].reshape(4, wide, 128)
        edge[t, 0:2, 4 : 4 + wide, :] = end[0:2]
        edge[t, 2:4] = edge_ref[t, 0:2]
        edge[t, 4:6] = edge_ref[t, 2:4]
        edge[t, 6:8, 4 : 4 + wide, :] = end[2:4]
        end = p[:, cut].reshape(4, wide // 2, 128)
        pmodes[t, 0:2, 2 : 2 + wide // 2, :] = end[0:2]
        pmodes[t, 2 : 2 + pr] = pside_ref[t, 2 : 2 + pr]
        pmodes[t, 2 + pr :, 2 : 2 + wide // 2, :] = end[2:4]

    copy.wait()

    def patch(cs, carry):
        for ds in range(2):
            for py in (-1, 0, 1):
                for t in range(4):
                    at = slice(128 * (t % 2), 128 * (t % 2) + 128)
                    mine = pl.ds(8 + 2 * py + ds, pc, stride=2)
                    theirs = pl.ds(4 + 2 * py + ds, gc, stride=2)
                    e = cs * 18 + ds * 3 + py + 1
                    x = jnp.concatenate([edge[t, cs + 2 * j, mine, :] for j in range(2)], axis=0)
                    lut[e, t // 2, 0:16, at] = x.astype(BF16)
                    x = jnp.concatenate([pmodes[t, cs + 2 * j, theirs, :] for j in range(4)], axis=0)
                    lut[e, t // 2, boxes : boxes + 16, at] = x.astype(BF16)
                    e = e + 12
                    x = jnp.concatenate([edge[t, 4 + cs + 2 * j, mine, :] for j in range(2)], axis=0)
                    lut[e, t // 2, boxes - 16 : boxes, at] = x.astype(BF16)
                    x = jnp.concatenate(
                        [pmodes[t, 4 + cs + 2 * j, theirs, :] for j in range(4, gr)]
                        + [jnp.zeros((high - boxes - pboxes, 128), F32)],
                        axis=0,
                    )
                    lut[e, t // 2, boxes + 16 : high, at] = x.astype(BF16)
        return carry

    lax.fori_loop(0, 2, patch, 0)

    shared = sum(abs(offset_table()[o][1]) < 3 for o, _ in plan()[:count])

    def listed(i, s):
        m = masks[i]
        x = lut[entry_ref[i], s]
        return jnp.concatenate([x[:, :128] * m, x[:, 128:] * m], axis=1)

    def interact(j, carry):
        n, s = 2 * (j // 2), j % 2
        total = jnp.zeros((2 * high, 256), F32)
        for k in range(shared):
            i = n * count + k
            x = jnp.concatenate([listed(i, s), listed(i + count, s)], axis=0)
            total = total + dot(x, table[s, pick_ref[i]])
        for d in range(2):
            part = total[high * d : high * (d + 1)]
            for k in range(shared, count):
                i = (n + d) * count + k
                part = part + dot(listed(i, s), table[s, pick_ref[i]])
            acc[s, n + d] = part
        return carry

    lax.fori_loop(0, 4, interact, 0)

    check = None
    for s in range(2):
        part = times_exact(acc[s].reshape(4 * high, 256), back[256 * s : 256 * (s + 1)])
        check = part if check is None else check + part

    inverse = parts(inv_ref[...])
    for n, (c, d) in enumerate(class_pairs()):
        for t, cut, to in cut_tiles(dens):
            for j in range(gr):
                r = high * n + boxes + gc * j
                plocal[t, 2 * j + c, pl.ds(d, gc, stride=2), to] = check[r : r + gc, cut]
    local = pin_ref[...].reshape(boxes, dens) + times_t(lanes(plocal)[:, :dens], inverse)
    x = jnp.concatenate(
        [
            check[high * n : high * n + boxes] + times_t(local, parts(down_ref[n]))
            for n in range(4)
        ],
        axis=0,
    )
    result = times_t(x, inverse)
    for n, (c, d) in enumerate(class_pairs()):
        for t, cut, to in cut_tiles(dens):
            for j in range(pr):
                r = boxes * n + pc * j
                flat[t, 2 * j + c, pl.ds(d, pc, stride=2), to] = result[r : r + pc, cut]
    for t, cut, to in cut_tiles(dens):
        out_ref[:, :, cut] = flat[t, :, :, to]


VMEM = pl.BlockSpec(memory_space=pltpu.VMEM)
SMEM = pl.BlockSpec(memory_space=pltpu.SMEM)


def params(mib):
    return pltpu.CompilerParams(vmem_limit_bytes=mib * 1024 * 1024)


def cost(rows, tiles, reads):
    return pl.CostEstimate(flops=2 * rows * tiles * 256 * 256, bytes_accessed=reads, transcendentals=0)


def height(boxes):
    return -(-(boxes * 5 // 4) // 16) * 16


def own_step(own, rotation):
    rows, cols, _ = own.shape
    return pl.pallas_call(
        own_kernel,
        out_shape=jax.ShapeDtypeStruct((4, rows, cols, 128), F32),
        in_specs=[VMEM] * 2,
        out_specs=VMEM,
        compiler_params=params(16),
        cost_estimate=cost(rows * cols, 48, 64 * 1024 * 1024),
    )(own, rotation)


def near_step(even, strips, own, own_modes, rotation, up, llist, plist):
    rows, cols, dens = own.shape
    pr, pc = rows // 2, cols // 2
    high = height(pr * pc)
    return pl.pallas_call(
        near_kernel,
        out_shape=(
            jax.ShapeDtypeStruct((pr, pc, dens), F32),
            jax.ShapeDtypeStruct((36, 2, high, 256), BF16),
            jax.ShapeDtypeStruct((4, 4, cols + 16, 128), F32),
            jax.ShapeDtypeStruct((4, pr + 4, pc + 8, 128), F32),
            jax.ShapeDtypeStruct((len(plan()), high, 128), BF16),
            jax.ShapeDtypeStruct((4, 2, dens, dens), BF16),
        ),
        in_specs=[SMEM] + [VMEM] * 8,
        out_specs=(VMEM,) * 6,
        scratch_shapes=[
            pltpu.VMEM((4, rows, cols, 128), F32),
            pltpu.VMEM((4, rows, 2 * HALO, 128), F32),
            pltpu.VMEM((4, rows + 4, cols + 16, 128), F32),
            pltpu.VMEM((2, rows, cols, 128), F32),
        ],
        compiler_params=params(24),
        cost_estimate=cost(rows * cols, 48, up.size * 4),
    )(even, *strips, own, own_modes, rotation, up, llist, plist)


def close_step(even, ends, edge, pmodes, upw, masks, lut, rotation, pin, back, table, down, inv, shape):
    rows, cols, dens = shape
    pr, pc = rows // 2, cols // 2
    high = height(pr * pc)
    return pl.pallas_call(
        close_kernel,
        out_shape=jax.ShapeDtypeStruct(shape, F32),
        in_specs=[SMEM] * 3 + [VMEM] * 13,
        out_specs=VMEM,
        scratch_shapes=[
            pltpu.VMEM((4, 2 * HALO, cols + 2 * HALO, 128), F32),
            pltpu.VMEM((4, 8, cols + 16, 128), F32),
            pltpu.VMEM((4, pr + 4, pc + 8, 128), F32),
            pltpu.VMEM(lut.shape, BF16),
            pltpu.VMEM((2, 4, high, 256), F32),
            pltpu.VMEM((4, rows, cols, 128), F32),
            pltpu.VMEM((4, pr, pc, 128), F32),
            pltpu.SemaphoreType.DMA,
        ],
        compiler_params=params(24),
        cost_estimate=cost(rows * cols, 150, table.size * 2),
    )(
        jnp.asarray([e for _, e in plan()], jnp.int32), jnp.asarray([o for o, _ in plan()], jnp.int32),
        even, *ends, edge, pmodes, upw, masks, lut, rotation, pin, back, table, down, inv,
    )


def swapped(low, high, axis, odd_first):
    peers = lax.axis_size(axis)
    even = lax.axis_index(axis) % 2 == 0
    strips = (jnp.where(even, high, low), jnp.where(even, low, high))
    got = [None, None]
    for kind in (1, 0) if odd_first else (0, 1):
        pairs = [(i, i + 1) for i in range(kind, peers - 1, 2)]
        got[kind] = lax.ppermute(strips[kind], axis, pairs + [(j, i) for i, j in pairs])
    return got


def local(leaf_up, parent_in, leaf_lists, parent_lists, up_transfer, down_transfer, check_inverse):
    rows, cols, _ = leaf_up.shape
    even = [lax.axis_index(axis) % 2 == 0 for axis in ("gx", "gy")]
    flag = jnp.stack(even).astype(jnp.int32)
    rotation, back, table = (jnp.asarray(x) for x in operators())
    strips = swapped(leaf_up[:, :HALO], leaf_up[:, cols - HALO :], "gy", True)
    *strips, own_modes = lax.optimization_barrier((*strips, own_step(leaf_up, rotation)))
    left = jnp.where(even[1], strips[1], strips[0])
    right = jnp.where(even[1], strips[0], strips[1])
    broad = lambda s: jnp.concatenate([left[s], leaf_up[s], right[s]], axis=1)
    ends = swapped(broad(slice(0, HALO)), broad(slice(rows - HALO, rows)), "gx", False)
    parent_up, lut, edge, pmodes, masks, upw = near_step(
        flag, strips, leaf_up, own_modes, rotation, up_transfer, leaf_lists, parent_lists
    )
    leaf_down = close_step(
        flag, ends, edge, pmodes, upw, masks, lut, rotation, parent_in, back, table,
        down_transfer, check_inverse, leaf_up.shape,
    )
    return leaf_down, parent_up


def solution(mesh):
    block = P("gx", "gy", None)
    return jax.shard_map(
        local,
        mesh=mesh,
        in_specs=(block,) * 4 + (P(),) * 3,
        out_specs=(block, block),
        check_vma=False,
    )
```

```python
import functools
import math

import jax
import jax.numpy as jnp
import ml_dtypes
import numpy as np
from jax import lax
from jax.experimental import pallas as pl
from jax.experimental.pallas import tpu as pltpu
from jax.sharding import PartitionSpec as P

ORDER = 6
HALO = 4
KEPT = 14
BF16, F32 = jnp.bfloat16, jnp.float32

def offset_table():
    return [(a, b) for a in range(-3, 4) for b in range(-3, 4) if max(abs(a), abs(b)) >= 2]


BASES = sorted({(abs(a), abs(b)) for a, b in offset_table()})


def surface_points():
    grid = np.linspace(-1.0, 1.0, ORDER)
    keys = [
        (i, j, k)
        for i in range(ORDER)
        for j in range(ORDER)
        for k in range(ORDER)
        if min(i, j, k) == 0 or max(i, j, k) == ORDER - 1
    ]
    return keys, np.array([[grid[i] for i in key] for key in keys])


def translation(points, dx, dy):
    r = 0.525 * (points[:, None, :] - points[None, :, :]) - np.array([dx, dy, 0.0])
    dist = np.sqrt((r * r).sum(-1))
    n = len(points)
    out = np.zeros((3, n, 3, n))
    for a in range(3):
        for b in range(3):
            out[a, :, b, :] = (float(a == b) / dist + r[..., a] * r[..., b] / dist**3) / (8 * math.pi)
    return out.reshape(3 * n, 3 * n)


def split(x):
    high = x.astype(ml_dtypes.bfloat16)
    return high, (x - high.astype(np.float64)).astype(ml_dtypes.bfloat16)


@functools.lru_cache(maxsize=None)
def operators():
    keys, points = surface_points()
    n = len(keys)
    points_of = {key: i for i, key in enumerate(keys)}
    mirror = [points_of[(i, j, ORDER - 1 - k)] for i, j, k in keys]
    mats = {o: translation(points, *o) for o in offset_table()}
    half = 3 * n // 2
    rotation = np.zeros((3 * n, 512), ml_dtypes.bfloat16)
    back = np.zeros((512, 3 * n))
    table = np.zeros((2, len(BASES), 256, 256), ml_dtypes.bfloat16)
    signs = np.ones((4, 2, 256, 256), ml_dtypes.bfloat16)
    for s, sign in enumerate((1, -1)):
        pairs = np.zeros((3 * n, half))
        firsts = []
        for a in range(3):
            flip = sign if a < 2 else -sign
            for i in range(n):
                if i < mirror[i]:
                    pairs[a * n + i, len(firsts)] = 1.0
                    pairs[a * n + mirror[i], len(firsts)] = flip
                    firsts.append(a * n + i)
        blocks = {o: 0.25 * pairs.T @ m @ pairs for o, m in mats.items()}
        gram = sum(b.T @ b for b in blocks.values())
        place = {f: i for i, f in enumerate(firsts)}
        modes, parity, weight = [], [], []
        for sx in (1, -1):
            for sy in (1, -1):
                basis = []
                for i, f in enumerate(firsts):
                    a, (kx, ky, kz) = f // n, keys[f % n]
                    if kx < ORDER // 2 and ky < ORDER // 2:
                        v = np.zeros(half)
                        for fx in range(2):
                            for fy in range(2):
                                key = (ORDER - 1 - kx if fx else kx, ORDER - 1 - ky if fy else ky, kz)
                                sign_x = (sx if a != 0 else -sx) if fx else 1
                                sign_y = (sy if a != 1 else -sy) if fy else 1
                                v[place[a * n + points_of[key]]] = 0.5 * sign_x * sign_y
                        basis.append(v)
                basis = np.array(basis).T
                w, vecs = np.linalg.eigh(basis.T @ gram @ basis)
                vecs = basis @ vecs
                vecs = vecs * np.sign(vecs[np.abs(np.round(vecs, 9)).argmax(0), np.arange(len(w))])
                modes.append(vecs)
                weight.append(w)
                parity += [(sx, sy)] * len(w)
        order = np.argsort(-np.concatenate(weight), kind="stable")
        vecs = np.concatenate(modes, axis=1)[:, order]
        parity = np.array(parity)[order]
        modes = (pairs @ vecs / math.sqrt(2.0)).astype(ml_dtypes.bfloat16)
        lows = np.concatenate([modes, modes[:, :KEPT], modes[:, :KEPT]], axis=1)
        rotation[:, 256 * s : 256 * (s + 1)] = lows
        outs, out_parity = [], []
        for sx in (1, -1):
            for sy in (1, -1):
                for f in firsts:
                    a, (kx, ky, kz) = f // n, keys[f % n]
                    if kx < ORDER // 2 and ky < ORDER // 2:
                        v = np.zeros(half)
                        for fx in range(2):
                            for fy in range(2):
                                key = (ORDER - 1 - kx if fx else kx, ORDER - 1 - ky if fy else ky, kz)
                                sign_x = (sx if a != 0 else -sx) if fx else 1
                                sign_y = (sy if a != 1 else -sy) if fy else 1
                                v[place[a * n + points_of[key]]] = sign_x * sign_y
                        outs.append(v)
                        out_parity.append((sx, sy))
        outs = np.array(outs).T
        out_parity = np.array(out_parity)
        back[256 * s : 256 * s + half] = (pairs @ outs).T
        undo = np.linalg.inv(modes[firsts].astype(np.float64))
        for q, o in enumerate(BASES):
            high, low = split(undo @ blocks[o].T @ outs * 0.25)
            table[s, q, :half, :half] = high
            table[s, q, half : half + KEPT, :half] = high[:KEPT]
            table[s, q, half + KEPT : half + 2 * KEPT, :half] = low[:KEPT]
        ins = np.concatenate([parity, parity[:KEPT], parity[:KEPT]], axis=0)
        for f in range(4):
            row = np.ones(256)
            row[: len(ins)] = (ins[:, 0] if f // 2 else 1) * (ins[:, 1] if f % 2 else 1)
            col = np.ones(256)
            col[:half] = (out_parity[:, 0] if f // 2 else 1) * (out_parity[:, 1] if f % 2 else 1)
            signs[f, s] = row[:, None] * col[None, :]
    whole = [
        table[:, BASES.index((abs(a), abs(b)))] * signs[2 * (a < 0) + (b < 0)]
        for a, b in offset_table()
    ]
    return rotation, back.astype(ml_dtypes.bfloat16), np.stack(whole, axis=1)


@functools.lru_cache(maxsize=None)
def plan():
    products = []
    offsets = offset_table()
    for c, d in class_pairs():
        for o in sorted(range(len(offsets)), key=lambda o: (abs(offsets[o][1]) == 3, o)):
            dx, dy = offsets[o]
            px, cs = divmod(c + dx, 2)
            py, ds = divmod(d + dy, 2)
            if abs(px) <= 1 and abs(py) <= 1:
                products.append((o, (cs * 3 + px + 1) * 6 + ds * 3 + py + 1))
    return products


def class_pairs():
    return [(c, d) for c in range(2) for d in range(2)]


def dot(a, b):
    return lax.dot_general(a, b, (((1,), (0,)), ((), ())), preferred_element_type=F32)


def dot_t(a, b):
    return lax.dot_general(a, b, (((1,), (1,)), ((), ())), preferred_element_type=F32)


def parts(x):
    high = x.astype(BF16)
    return high, (x - high.astype(F32)).astype(BF16)


def times_t(x, weight):
    xh, xl = parts(x)
    wh, wl = weight
    both = dot_t(jnp.concatenate([xh, xl], axis=0), wh)
    return both[: x.shape[0]] + (both[x.shape[0] :] + dot_t(xh, wl))


def times_exact(x, weight):
    both = dot(jnp.concatenate(parts(x), axis=0), weight)
    return both[: x.shape[0]] + both[x.shape[0] :]


def lanes(ref, *at):
    pieces = [ref[(t,) + at] for t in range(4)]
    pieces = [p.reshape(-1, 128) for p in pieces]
    return jnp.concatenate(pieces, axis=1)


def cut_tiles(dens):
    return [(t, slice(128 * t, min(128 * t + 128, dens)), slice(0, min(128, dens - 128 * t))) for t in range(4)]


def modes_of(x, rot_ref, dens):
    y = times_exact(x[:, :dens], rot_ref[...])
    lane = lax.broadcasted_iota(jnp.int32, (1, 512), 1) % 256
    half = dens // 2
    is_low = (lane >= half) & (lane < half + KEPT)
    return jnp.where(is_low, y - y.astype(BF16).astype(F32), y)


def children(ref, dens, counts, c, d):
    return jnp.concatenate(
        [
            jnp.concatenate(
                [ref[t, 2 * i + c, pl.ds(d, counts[1], stride=2), :] for i in range(counts[0])],
                axis=0,
            )
            for t in range(4)
        ],
        axis=1,
    )[:, :dens]


def own_kernel(own_ref, rot_ref, modes_ref, tiled_ref, rot_out):
    rows, cols, dens = own_ref.shape
    rot_out[...] = rot_ref[...]
    y = modes_of(own_ref[...].reshape(rows * cols, dens), rot_ref, dens)
    for t, cut, to in cut_tiles(dens):
        modes_ref[t] = y[:, 128 * t : 128 * t + 128].reshape(rows, cols, 128)
        tiled_ref[t, :, :, to] = own_ref[:, :, cut]


def pass_kernel(
    even_ref, strip0_ref, strip1_ref, own_t, own_modes_ref, rot_ref, up_ref,
    pup_ref, modes, pmodes, send0_ref, send1_ref,
    strip_t,
):
    rows, _, dens = strip0_ref.shape
    cols = own_modes_ref.shape[2]
    pr, pc = rows // 2, cols // 2
    boxes = pr * pc
    wide = cols + 2 * HALO
    even_x, even_y = even_ref[0] == 1, even_ref[1] == 1
    for t, cut, to in cut_tiles(dens):
        first, second = strip0_ref[:, :, cut], strip1_ref[:, :, cut]
        strip_t[t, :, 0:HALO, to] = jnp.where(even_y, second, first)
        strip_t[t, :, HALO:, to] = jnp.where(even_y, first, second)

    parent = None
    for n, (c, d) in enumerate(class_pairs()):
        x = jnp.concatenate(
            [children(own_t, dens, (pr, pc), c, d), children(strip_t, dens, (pr, HALO), c, d)],
            axis=0,
        )
        part = times_t(x, parts(up_ref[n]))
        parent = part if parent is None else parent + part
    pup_ref[...] = parent[:boxes].reshape(pr, pc, dens)
    z = modes_of(jnp.concatenate([lanes(strip_t)[:, :dens], parent], axis=0), rot_ref, dens)
    w, p = z[: rows * 8], z[rows * 8 :]
    for t in range(4):
        cut = slice(128 * t, 128 * t + 128)
        modes[t, 2 : 2 + rows, 8 : 8 + cols, :] = own_modes_ref[t]
        strip = w[:, cut].reshape(rows, 8, 128)
        modes[t, 2 : 2 + rows, 4:8, :] = strip[:, 0:4]
        modes[t, 2 : 2 + rows, 8 + cols : 12 + cols, :] = strip[:, 4:8]
        pmodes[t, 2 : 2 + pr, 4 : 4 + pc, :] = p[:boxes, cut].reshape(pr, pc, 128)
        strip = p[boxes:, cut].reshape(pr, 4, 128)
        pmodes[t, 2 : 2 + pr, 2:4, :] = strip[:, 0:2]
        pmodes[t, 2 : 2 + pr, 4 + pc : 6 + pc, :] = strip[:, 2:4]
        low, high = modes[t, 2:4, 4 : 4 + wide, :], modes[t, rows : rows + 2, 4 : 4 + wide, :]
        send0_ref[t, :, 0:wide, :] = jnp.where(even_x, high, low)
        send1_ref[t, :, 0:wide, :] = jnp.where(even_x, low, high)
        low, high = pmodes[t, 2:4, 2 : 6 + pc, :], pmodes[t, pr : pr + 2, 2 : 6 + pc, :]
        send0_ref[t, :, wide : wide + 4 + pc, :] = jnp.where(even_x, high, low)
        send1_ref[t, :, wide : wide + 4 + pc, :] = jnp.where(even_x, low, high)


def near_kernel(modes, pmodes_ref, llist_ref, plist_ref, lut, masks_ref, flat):
    rows, cols = modes.shape[1] - 4, modes.shape[2] - 16
    pr, pc = rows // 2, cols // 2
    gr, gc = pr // 2, pc // 2
    used = pr * pc + gr * gc
    high = lut.shape[2]
    count = masks_ref.shape[0] // 4

    def gather(i, carry):
        base = 2 * (i % 3) + i // 3
        for ds in range(2):
            for py in (-1, 0, 1):
                e = i * 6 + ds * 3 + py + 1
                for t in range(4):
                    x = jnp.concatenate(
                        [
                            modes[t, base + 2 * j, pl.ds(8 + 2 * py + ds, pc, stride=2), :]
                            for j in range(pr)
                        ]
                        + [
                            pmodes_ref[t, base + 2 * j, pl.ds(4 + 2 * py + ds, gc, stride=2), :]
                            for j in range(gr)
                        ]
                        + [jnp.zeros((high - used, 128), F32)],
                        axis=0,
                    )
                    lut[e, t // 2, :, 128 * (t % 2) : 128 * (t % 2) + 128] = x.astype(BF16)
        return carry

    lax.fori_loop(0, 6, gather, 0)

    flat[0, :, :, 0 : llist_ref.shape[2]] = llist_ref[...].astype(F32)
    flat[1, 0:pr, 0:pc, 0 : plist_ref.shape[2]] = plist_ref[...].astype(F32)
    for n, (c, d) in enumerate(class_pairs()):
        flag = jnp.concatenate(
            [flat[0, 2 * i + c, pl.ds(d, pc, stride=2), :] for i in range(pr)]
            + [flat[1, 2 * i + c, pl.ds(d, gc, stride=2), :] for i in range(gr)]
            + [jnp.zeros((high - used, 128), F32)],
            axis=0,
        )
        for k in range(count):
            o = plan()[count * n + k][0]
            masks_ref[count * n + k] = jnp.broadcast_to(flag[:, o : o + 1], (high, 128)).astype(BF16)


def close_kernel(
    entry_ref, pick_ref, even_ref,
    got0_ref, got1_ref, modes, pside_ref, masks, lut_ref,
    pin_ref, back, table, down_ref, inv_ref,
    out_ref,
    edge, pmodes, lut, acc, flat, plocal, sem,
):
    rows, cols, dens = out_ref.shape
    pr, pc = rows // 2, cols // 2
    gr, gc = pr // 2, pc // 2
    boxes, pboxes = pr * pc, gr * gc
    high = lut.shape[2]
    wide = cols + 2 * HALO
    count = masks.shape[0] // 4
    copy = pltpu.make_async_copy(lut_ref, lut, sem)
    copy.start()
    even = even_ref[0] == 1
    for t in range(4):
        before = jnp.where(even, got1_ref[t], got0_ref[t])
        after = jnp.where(even, got0_ref[t], got1_ref[t])
        edge[t, 0:2, 4 : 4 + wide, :] = before[:, 0:wide]
        edge[t, 2:4] = modes[t, 2:4]
        edge[t, 4:6] = modes[t, rows : rows + 2]
        edge[t, 6:8, 4 : 4 + wide, :] = after[:, 0:wide]
        pmodes[t, 0:2, 2 : 6 + pc, :] = before[:, wide : wide + 4 + pc]
        pmodes[t, 2 : 2 + pr] = pside_ref[t, 2 : 2 + pr]
        pmodes[t, 2 + pr :, 2 : 6 + pc, :] = after[:, wide : wide + 4 + pc]

    copy.wait()

    def patch(cs, carry):
        for ds in range(2):
            for py in (-1, 0, 1):
                for t in range(4):
                    at = slice(128 * (t % 2), 128 * (t % 2) + 128)
                    mine = pl.ds(8 + 2 * py + ds, pc, stride=2)
                    theirs = pl.ds(4 + 2 * py + ds, gc, stride=2)
                    e = cs * 18 + ds * 3 + py + 1
                    x = jnp.concatenate([edge[t, cs + 2 * j, mine, :] for j in range(2)], axis=0)
                    lut[e, t // 2, 0:16, at] = x.astype(BF16)
                    x = jnp.concatenate([pmodes[t, cs + 2 * j, theirs, :] for j in range(4)], axis=0)
                    lut[e, t // 2, boxes : boxes + 16, at] = x.astype(BF16)
                    e = e + 12
                    x = jnp.concatenate([edge[t, 4 + cs + 2 * j, mine, :] for j in range(2)], axis=0)
                    lut[e, t // 2, boxes - 16 : boxes, at] = x.astype(BF16)
                    x = jnp.concatenate(
                        [pmodes[t, 4 + cs + 2 * j, theirs, :] for j in range(4, gr)]
                        + [jnp.zeros((high - boxes - pboxes, 128), F32)],
                        axis=0,
                    )
                    lut[e, t // 2, boxes + 16 : high, at] = x.astype(BF16)
        return carry

    lax.fori_loop(0, 2, patch, 0)

    shared = sum(abs(offset_table()[o][1]) < 3 for o, _ in plan()[:count])

    def listed(i, s):
        m = masks[i]
        x = lut[entry_ref[i], s]
        return jnp.concatenate([x[:, :128] * m, x[:, 128:] * m], axis=1)

    def interact(j, carry):
        n, s = 2 * (j // 2), j % 2
        total = jnp.zeros((2 * high, 256), F32)
        for k in range(shared):
            i = n * count + k
            x = jnp.concatenate([listed(i, s), listed(i + count, s)], axis=0)
            total = total + dot(x, table[s, pick_ref[i]])
        for d in range(2):
            part = total[high * d : high * (d + 1)]
            for k in range(shared, count):
                i = (n + d) * count + k
                part = part + dot(listed(i, s), table[s, pick_ref[i]])
            acc[s, n + d] = part
        return carry

    lax.fori_loop(0, 4, interact, 0)

    check = None
    for s in range(2):
        part = times_exact(acc[s].reshape(4 * high, 256), back[256 * s : 256 * (s + 1)])
        check = part if check is None else check + part

    inverse = parts(inv_ref[...])
    for n, (c, d) in enumerate(class_pairs()):
        for t, cut, to in cut_tiles(dens):
            for j in range(gr):
                r = high * n + boxes + gc * j
                plocal[t, 2 * j + c, pl.ds(d, gc, stride=2), to] = check[r : r + gc, cut]
    local = pin_ref[...].reshape(boxes, dens) + times_t(lanes(plocal)[:, :dens], inverse)
    x = jnp.concatenate(
        [
            check[high * n : high * n + boxes] + times_t(local, parts(down_ref[n]))
            for n in range(4)
        ],
        axis=0,
    )
    result = times_t(x, inverse)
    for n, (c, d) in enumerate(class_pairs()):
        for t, cut, to in cut_tiles(dens):
            for j in range(pr):
                r = boxes * n + pc * j
                flat[t, 2 * j + c, pl.ds(d, pc, stride=2), to] = result[r : r + pc, cut]
    for t, cut, to in cut_tiles(dens):
        out_ref[:, :, cut] = flat[t, :, :, to]


VMEM = pl.BlockSpec(memory_space=pltpu.VMEM)
SMEM = pl.BlockSpec(memory_space=pltpu.SMEM)


def params(mib):
    return pltpu.CompilerParams(vmem_limit_bytes=mib * 1024 * 1024)


def cost(rows, tiles, reads):
    return pl.CostEstimate(flops=2 * rows * tiles * 256 * 256, bytes_accessed=reads, transcendentals=0)


def height(boxes):
    return -(-(boxes * 5 // 4) // 16) * 16


def own_step(own, rotation):
    rows, cols, _ = own.shape
    tiled = jax.ShapeDtypeStruct((4, rows, cols, 128), F32)
    return pl.pallas_call(
        own_kernel,
        out_shape=(tiled, tiled, jax.ShapeDtypeStruct(rotation.shape, BF16)),
        in_specs=[VMEM] * 2,
        out_specs=(VMEM,) * 3,
        compiler_params=params(16),
        cost_estimate=cost(rows * cols, 48, 64 * 1024 * 1024),
    )(own, rotation)


def pass_step(even, strips, tiled, own_modes, rotation, up):
    rows, cols = tiled.shape[1:3]
    dens = up.shape[1]
    pr, pc = rows // 2, cols // 2
    send = jax.ShapeDtypeStruct((4, 2, cols + 2 * HALO + 8 * ((pc + 11) // 8), 128), F32)
    return pl.pallas_call(
        pass_kernel,
        out_shape=(
            jax.ShapeDtypeStruct((pr, pc, dens), F32),
            jax.ShapeDtypeStruct((4, rows + 4, cols + 16, 128), F32),
            jax.ShapeDtypeStruct((4, pr + 4, pc + 8, 128), F32),
            send,
            send,
        ),
        in_specs=[SMEM] + [VMEM] * 6,
        out_specs=(VMEM,) * 5,
        scratch_shapes=[pltpu.VMEM((4, rows, 2 * HALO, 128), F32)],
        compiler_params=params(16),
        cost_estimate=cost(rows * cols, 32, up.size * 4),
    )(even, *strips, tiled, own_modes, rotation, up)


def near_step(modes, pmodes, llist, plist):
    rows, cols, _ = llist.shape
    high = height(rows * cols // 4)
    return pl.pallas_call(
        near_kernel,
        out_shape=(
            jax.ShapeDtypeStruct((36, 2, high, 256), BF16),
            jax.ShapeDtypeStruct((len(plan()), high, 128), BF16),
        ),
        in_specs=[VMEM] * 4,
        out_specs=(VMEM,) * 2,
        scratch_shapes=[pltpu.VMEM((2, rows, cols, 128), F32)],
        compiler_params=params(16),
        cost_estimate=cost(rows * cols, 48, 16 * 1024 * 1024),
    )(modes, pmodes, llist, plist)


def close_step(even, ends, modes, pmodes, masks, lut, pin, back, table, down, inv, shape):
    rows, cols, dens = shape
    pr, pc = rows // 2, cols // 2
    high = height(pr * pc)
    return pl.pallas_call(
        close_kernel,
        out_shape=jax.ShapeDtypeStruct(shape, F32),
        in_specs=[SMEM] * 3 + [VMEM] * 11,
        out_specs=VMEM,
        scratch_shapes=[
            pltpu.VMEM((4, 8, cols + 16, 128), F32),
            pltpu.VMEM((4, pr + 4, pc + 8, 128), F32),
            pltpu.VMEM(lut.shape, BF16),
            pltpu.VMEM((2, 4, high, 256), F32),
            pltpu.VMEM((4, rows, cols, 128), F32),
            pltpu.VMEM((4, pr, pc, 128), F32),
            pltpu.SemaphoreType.DMA,
        ],
        compiler_params=params(24),
        cost_estimate=cost(rows * cols, 150, table.size * 2),
    )(
        jnp.asarray([e for _, e in plan()], jnp.int32), jnp.asarray([o for o, _ in plan()], jnp.int32),
        even, *ends, modes, pmodes, masks, lut, pin, back, table, down, inv,
    )


def swapped(strips, axis, odd_first):
    peers = lax.axis_size(axis)
    got = [None, None]
    for kind in (1, 0) if odd_first else (0, 1):
        pairs = [(i, i + 1) for i in range(kind, peers - 1, 2)]
        got[kind] = lax.ppermute(strips[kind], axis, pairs + [(j, i) for i, j in pairs])
    return got


def local(leaf_up, parent_in, leaf_lists, parent_lists, up_transfer, down_transfer, check_inverse):
    cols = leaf_up.shape[1]
    even = [lax.axis_index(axis) % 2 == 0 for axis in ("gx", "gy")]
    flag = jnp.stack(even).astype(jnp.int32)
    rotation, back, table = (jnp.asarray(x) for x in operators())
    low, high = leaf_up[:, :HALO], leaf_up[:, cols - HALO :]
    strips = (jnp.where(even[1], high, low), jnp.where(even[1], low, high))
    strips = swapped(strips, "gy", True)
    own_modes, tiled, rotation = own_step(leaf_up, rotation)
    parent_up, modes, pmodes, *sends = pass_step(flag, strips, tiled, own_modes, rotation, up_transfer)
    ends = swapped(sends, "gx", False)
    lut, masks = near_step(modes, pmodes, leaf_lists, parent_lists)
    leaf_down = close_step(
        flag, ends, modes, pmodes, masks, lut, parent_in, back, table,
        down_transfer, check_inverse, leaf_up.shape,
    )
    return leaf_down, parent_up


def solution(mesh):
    block = P("gx", "gy", None)
    return jax.shard_map(
        local,
        mesh=mesh,
        in_specs=(block,) * 4 + (P(),) * 3,
        out_specs=(block, block),
        check_vma=False,
    )
```

```python
import functools
import math

import jax
import jax.numpy as jnp
import ml_dtypes
import numpy as np
from jax import lax
from jax.experimental import pallas as pl
from jax.experimental.pallas import tpu as pltpu
from jax.sharding import PartitionSpec as P

ORDER = 6
HALO = 4
KEPT = 14
BF16, F32 = jnp.bfloat16, jnp.float32

def offset_table():
    return [(a, b) for a in range(-3, 4) for b in range(-3, 4) if max(abs(a), abs(b)) >= 2]


BASES = sorted({(abs(a), abs(b)) for a, b in offset_table()})


def surface_points():
    grid = np.linspace(-1.0, 1.0, ORDER)
    keys = [
        (i, j, k)
        for i in range(ORDER)
        for j in range(ORDER)
        for k in range(ORDER)
        if min(i, j, k) == 0 or max(i, j, k) == ORDER - 1
    ]
    return keys, np.array([[grid[i] for i in key] for key in keys])


def translation(points, dx, dy):
    r = 0.525 * (points[:, None, :] - points[None, :, :]) - np.array([dx, dy, 0.0])
    dist = np.sqrt((r * r).sum(-1))
    n = len(points)
    out = np.zeros((3, n, 3, n))
    for a in range(3):
        for b in range(3):
            out[a, :, b, :] = (float(a == b) / dist + r[..., a] * r[..., b] / dist**3) / (8 * math.pi)
    return out.reshape(3 * n, 3 * n)


def split(x):
    high = x.astype(ml_dtypes.bfloat16)
    return high, (x - high.astype(np.float64)).astype(ml_dtypes.bfloat16)


@functools.lru_cache(maxsize=None)
def operators():
    keys, points = surface_points()
    n = len(keys)
    points_of = {key: i for i, key in enumerate(keys)}
    mirror = [points_of[(i, j, ORDER - 1 - k)] for i, j, k in keys]
    mats = {o: translation(points, *o) for o in offset_table()}
    half = 3 * n // 2
    rotation = np.zeros((3 * n, 512), ml_dtypes.bfloat16)
    back = np.zeros((512, 3 * n))
    table = np.zeros((2, len(BASES), 256, 256), ml_dtypes.bfloat16)
    signs = np.ones((4, 2, 256, 256), ml_dtypes.bfloat16)
    for s, sign in enumerate((1, -1)):
        pairs = np.zeros((3 * n, half))
        firsts = []
        for a in range(3):
            flip = sign if a < 2 else -sign
            for i in range(n):
                if i < mirror[i]:
                    pairs[a * n + i, len(firsts)] = 1.0
                    pairs[a * n + mirror[i], len(firsts)] = flip
                    firsts.append(a * n + i)
        blocks = {o: 0.25 * pairs.T @ m @ pairs for o, m in mats.items()}
        gram = sum(b.T @ b for b in blocks.values())
        place = {f: i for i, f in enumerate(firsts)}
        modes, parity, weight = [], [], []
        for sx in (1, -1):
            for sy in (1, -1):
                basis = []
                for i, f in enumerate(firsts):
                    a, (kx, ky, kz) = f // n, keys[f % n]
                    if kx < ORDER // 2 and ky < ORDER // 2:
                        v = np.zeros(half)
                        for fx in range(2):
                            for fy in range(2):
                                key = (ORDER - 1 - kx if fx else kx, ORDER - 1 - ky if fy else ky, kz)
                                sign_x = (sx if a != 0 else -sx) if fx else 1
                                sign_y = (sy if a != 1 else -sy) if fy else 1
                                v[place[a * n + points_of[key]]] = 0.5 * sign_x * sign_y
                        basis.append(v)
                basis = np.array(basis).T
                w, vecs = np.linalg.eigh(basis.T @ gram @ basis)
                vecs = basis @ vecs
                vecs = vecs * np.sign(vecs[np.abs(np.round(vecs, 9)).argmax(0), np.arange(len(w))])
                modes.append(vecs)
                weight.append(w)
                parity += [(sx, sy)] * len(w)
        order = np.argsort(-np.concatenate(weight), kind="stable")
        vecs = np.concatenate(modes, axis=1)[:, order]
        parity = np.array(parity)[order]
        modes = (pairs @ vecs / math.sqrt(2.0)).astype(ml_dtypes.bfloat16)
        lows = np.concatenate([modes, modes[:, :KEPT], modes[:, :KEPT]], axis=1)
        rotation[:, 256 * s : 256 * (s + 1)] = lows
        outs, out_parity = [], []
        for sx in (1, -1):
            for sy in (1, -1):
                for f in firsts:
                    a, (kx, ky, kz) = f // n, keys[f % n]
                    if kx < ORDER // 2 and ky < ORDER // 2:
                        v = np.zeros(half)
                        for fx in range(2):
                            for fy in range(2):
                                key = (ORDER - 1 - kx if fx else kx, ORDER - 1 - ky if fy else ky, kz)
                                sign_x = (sx if a != 0 else -sx) if fx else 1
                                sign_y = (sy if a != 1 else -sy) if fy else 1
                                v[place[a * n + points_of[key]]] = sign_x * sign_y
                        outs.append(v)
                        out_parity.append((sx, sy))
        outs = np.array(outs).T
        out_parity = np.array(out_parity)
        back[256 * s : 256 * s + half] = (pairs @ outs).T
        undo = np.linalg.inv(modes[firsts].astype(np.float64))
        for q, o in enumerate(BASES):
            high, low = split(undo @ blocks[o].T @ outs * 0.25)
            table[s, q, :half, :half] = high
            table[s, q, half : half + KEPT, :half] = high[:KEPT]
            table[s, q, half + KEPT : half + 2 * KEPT, :half] = low[:KEPT]
        ins = np.concatenate([parity, parity[:KEPT], parity[:KEPT]], axis=0)
        for f in range(4):
            row = np.ones(256)
            row[: len(ins)] = (ins[:, 0] if f // 2 else 1) * (ins[:, 1] if f % 2 else 1)
            col = np.ones(256)
            col[:half] = (out_parity[:, 0] if f // 2 else 1) * (out_parity[:, 1] if f % 2 else 1)
            signs[f, s] = row[:, None] * col[None, :]
    whole = [
        table[:, BASES.index((abs(a), abs(b)))] * signs[2 * (a < 0) + (b < 0)]
        for a, b in offset_table()
    ]
    return rotation, back.astype(ml_dtypes.bfloat16), np.stack(whole, axis=1)


@functools.lru_cache(maxsize=None)
def plan():
    products = []
    offsets = offset_table()
    for c, d in class_pairs():
        for o in sorted(range(len(offsets)), key=lambda o: (abs(offsets[o][1]) == 3, o)):
            dx, dy = offsets[o]
            px, cs = divmod(c + dx, 2)
            py, ds = divmod(d + dy, 2)
            if abs(px) <= 1 and abs(py) <= 1:
                products.append((o, (cs * 3 + px + 1) * 6 + ds * 3 + py + 1))
    return products


def class_pairs():
    return [(c, d) for c in range(2) for d in range(2)]


def dot(a, b):
    return lax.dot_general(a, b, (((1,), (0,)), ((), ())), preferred_element_type=F32)


def dot_t(a, b):
    return lax.dot_general(a, b, (((1,), (1,)), ((), ())), preferred_element_type=F32)


def parts(x):
    high = x.astype(BF16)
    return high, (x - high.astype(F32)).astype(BF16)


def times_t(x, weight):
    xh, xl = parts(x)
    wh, wl = weight
    both = dot_t(jnp.concatenate([xh, xl], axis=0), wh)
    return both[: x.shape[0]] + (both[x.shape[0] :] + dot_t(xh, wl))


def times_exact(x, weight):
    both = dot(jnp.concatenate(parts(x), axis=0), weight)
    return both[: x.shape[0]] + both[x.shape[0] :]


def lanes(ref, *at):
    pieces = [ref[(t,) + at] for t in range(4)]
    pieces = [p.reshape(-1, 128) for p in pieces]
    return jnp.concatenate(pieces, axis=1)


def cut_tiles(dens):
    return [(t, slice(128 * t, min(128 * t + 128, dens)), slice(0, min(128, dens - 128 * t))) for t in range(4)]


def modes_of(x, rot_ref, dens):
    y = times_exact(x[:, :dens], rot_ref[...])
    lane = lax.broadcasted_iota(jnp.int32, (1, 512), 1) % 256
    half = dens // 2
    is_low = (lane >= half) & (lane < half + KEPT)
    return jnp.where(is_low, y - y.astype(BF16).astype(F32), y)


def children(ref, dens, counts, c, d):
    return jnp.concatenate(
        [
            jnp.concatenate(
                [ref[t, 2 * i + c, pl.ds(d, counts[1], stride=2), :] for i in range(counts[0])],
                axis=0,
            )
            for t in range(4)
        ],
        axis=1,
    )[:, :dens]


def own_kernel(own_ref, rot_ref, modes_ref, tiled_ref, rot_out):
    rows, cols, dens = own_ref.shape
    rot_out[...] = rot_ref[...]
    y = modes_of(own_ref[...].reshape(rows * cols, dens), rot_ref, dens)
    for t, cut, to in cut_tiles(dens):
        modes_ref[t] = y[:, 128 * t : 128 * t + 128].reshape(rows, cols, 128)
        tiled_ref[t, :, :, to] = own_ref[:, :, cut]


def pass_kernel(
    even_ref, strip0_ref, strip1_ref, own_t, own_modes_ref, rot_ref, up_ref,
    pup_ref, modes, pmodes, send0_ref, send1_ref,
    strip_t,
):
    rows, _, dens = strip0_ref.shape
    cols = own_modes_ref.shape[2]
    pr, pc = rows // 2, cols // 2
    boxes = pr * pc
    wide = cols + 2 * HALO
    even_x, even_y = even_ref[0] == 1, even_ref[1] == 1
    for t, cut, to in cut_tiles(dens):
        first, second = strip0_ref[:, :, cut], strip1_ref[:, :, cut]
        strip_t[t, :, 0:HALO, to] = jnp.where(even_y, second, first)
        strip_t[t, :, HALO:, to] = jnp.where(even_y, first, second)

    parent = None
    for n, (c, d) in enumerate(class_pairs()):
        x = jnp.concatenate(
            [children(own_t, dens, (pr, pc), c, d), children(strip_t, dens, (pr, HALO), c, d)],
            axis=0,
        )
        part = times_t(x, parts(up_ref[n]))
        parent = part if parent is None else parent + part
    pup_ref[...] = parent[:boxes].reshape(pr, pc, dens)
    z = modes_of(jnp.concatenate([lanes(strip_t)[:, :dens], parent], axis=0), rot_ref, dens)
    w, p = z[: rows * 8], z[rows * 8 :]
    for t in range(4):
        cut = slice(128 * t, 128 * t + 128)
        modes[t, 2 : 2 + rows, 8 : 8 + cols, :] = own_modes_ref[t]
        strip = w[:, cut].reshape(rows, 8, 128)
        modes[t, 2 : 2 + rows, 4:8, :] = strip[:, 0:4]
        modes[t, 2 : 2 + rows, 8 + cols : 12 + cols, :] = strip[:, 4:8]
        pmodes[t, 2 : 2 + pr, 4 : 4 + pc, :] = p[:boxes, cut].reshape(pr, pc, 128)
        strip = p[boxes:, cut].reshape(pr, 4, 128)
        pmodes[t, 2 : 2 + pr, 2:4, :] = strip[:, 0:2]
        pmodes[t, 2 : 2 + pr, 4 + pc : 6 + pc, :] = strip[:, 2:4]
        low, high = modes[t, 2:4, 4 : 4 + wide, :], modes[t, rows : rows + 2, 4 : 4 + wide, :]
        send0_ref[t, :, 0:wide, :] = jnp.where(even_x, high, low)
        send1_ref[t, :, 0:wide, :] = jnp.where(even_x, low, high)
        low, high = pmodes[t, 2:4, 2 : 6 + pc, :], pmodes[t, pr : pr + 2, 2 : 6 + pc, :]
        send0_ref[t, :, wide : wide + 4 + pc, :] = jnp.where(even_x, high, low)
        send1_ref[t, :, wide : wide + 4 + pc, :] = jnp.where(even_x, low, high)


def near_kernel(
    modes, pmodes_ref, llist_ref, plist_ref, down_ref, inv_ref,
    lut, masks_ref, downw_ref, invw_ref,
    flat,
):
    rows, cols = modes.shape[1] - 4, modes.shape[2] - 16
    pr, pc = rows // 2, cols // 2
    gr, gc = pr // 2, pc // 2
    used = pr * pc + gr * gc
    high = lut.shape[2]
    count = masks_ref.shape[0] // 4

    def gather(i, carry):
        base = 2 * (i % 3) + i // 3
        for ds in range(2):
            for py in (-1, 0, 1):
                e = i * 6 + ds * 3 + py + 1
                for t in range(4):
                    x = jnp.concatenate(
                        [
                            modes[t, base + 2 * j, pl.ds(8 + 2 * py + ds, pc, stride=2), :]
                            for j in range(pr)
                        ]
                        + [
                            pmodes_ref[t, base + 2 * j, pl.ds(4 + 2 * py + ds, gc, stride=2), :]
                            for j in range(gr)
                        ]
                        + [jnp.zeros((high - used, 128), F32)],
                        axis=0,
                    )
                    lut[e, t // 2, :, 128 * (t % 2) : 128 * (t % 2) + 128] = x.astype(BF16)
        return carry

    lax.fori_loop(0, 6, gather, 0)

    for n in range(4):
        downw_ref[n, 0], downw_ref[n, 1] = parts(down_ref[n])
    invw_ref[0], invw_ref[1] = parts(inv_ref[...])

    flat[0, :, :, 0 : llist_ref.shape[2]] = llist_ref[...].astype(F32)
    flat[1, 0:pr, 0:pc, 0 : plist_ref.shape[2]] = plist_ref[...].astype(F32)
    for n, (c, d) in enumerate(class_pairs()):
        flag = jnp.concatenate(
            [flat[0, 2 * i + c, pl.ds(d, pc, stride=2), :] for i in range(pr)]
            + [flat[1, 2 * i + c, pl.ds(d, gc, stride=2), :] for i in range(gr)]
            + [jnp.zeros((high - used, 128), F32)],
            axis=0,
        )
        for k in range(count):
            o = plan()[count * n + k][0]
            masks_ref[count * n + k] = jnp.broadcast_to(flag[:, o : o + 1], (high, 128)).astype(BF16)


def close_kernel(
    even_ref,
    got0_ref, got1_ref, modes, pside_ref, masks, lut,
    pin_ref, back, table, downw, invw,
    out_ref,
    edge, pmodes, fresh, acc, flat, plocal,
):
    rows, cols, dens = out_ref.shape
    pr, pc = rows // 2, cols // 2
    gr, gc = pr // 2, pc // 2
    boxes, pboxes = pr * pc, gr * gc
    high = lut.shape[2]
    wide = cols + 2 * HALO
    count = masks.shape[0] // 4
    even = even_ref[0] == 1
    for t in range(4):
        before = jnp.where(even, got1_ref[t], got0_ref[t])
        after = jnp.where(even, got0_ref[t], got1_ref[t])
        edge[t, 0:2, 4 : 4 + wide, :] = before[:, 0:wide]
        edge[t, 2:4] = modes[t, 2:4]
        edge[t, 4:6] = modes[t, rows : rows + 2]
        edge[t, 6:8, 4 : 4 + wide, :] = after[:, 0:wide]
        pmodes[t, 0:2, 2 : 6 + pc, :] = before[:, wide : wide + 4 + pc]
        pmodes[t, 2 : 2 + pr] = pside_ref[t, 2 : 2 + pr]
        pmodes[t, 2 + pr :, 2 : 6 + pc, :] = after[:, wide : wide + 4 + pc]

    def patch(cs, carry):
        for ds in range(2):
            for py in (-1, 0, 1):
                for t in range(4):
                    at = slice(128 * (t % 2), 128 * (t % 2) + 128)
                    mine = pl.ds(8 + 2 * py + ds, pc, stride=2)
                    theirs = pl.ds(4 + 2 * py + ds, gc, stride=2)
                    e = cs * 6 + ds * 3 + py + 1
                    x = jnp.concatenate([edge[t, cs + 2 * j, mine, :] for j in range(2)], axis=0)
                    fresh[0, e, t // 2, 0:16, at] = x.astype(BF16)
                    x = jnp.concatenate([pmodes[t, cs + 2 * j, theirs, :] for j in range(4)], axis=0)
                    fresh[0, e, t // 2, 16:32, at] = x.astype(BF16)
                    x = jnp.concatenate([edge[t, 4 + cs + 2 * j, mine, :] for j in range(2)], axis=0)
                    fresh[1, e, t // 2, 0:16, at] = x.astype(BF16)
                    x = jnp.concatenate(
                        [pmodes[t, 4 + cs + 2 * j, theirs, :] for j in range(4, gr)]
                        + [jnp.zeros((high - boxes - pboxes, 128), F32)],
                        axis=0,
                    )
                    fresh[1, e, t // 2, 16:32, at] = x.astype(BF16)
        return carry

    lax.fori_loop(0, 2, patch, 0)

    shared = sum(abs(offset_table()[o][1]) < 3 for o, _ in plan()[:count])

    def listed(i, s):
        e = plan()[i][1]
        px = e // 6 % 3 - 1
        m = masks[i]
        if px == 0:
            x = lut[e, s]
        else:
            new = fresh[(px + 1) // 2, e // 18 * 6 + e % 6, s]
            if px < 0:
                pieces = [new[0:16], lut[e, s, 16:boxes], new[16:32], lut[e, s, boxes + 16 : high]]
            else:
                pieces = [lut[e, s, 0 : boxes - 16], new[0:16], lut[e, s, boxes : boxes + 16], new[16:32]]
            x = jnp.concatenate(pieces, axis=0)
        return jnp.concatenate([x[:, :128] * m, x[:, 128:] * m], axis=1)

    for c in range(2):

        def interact(s, carry):
            n = 2 * c
            total = jnp.zeros((2 * high, 256), F32)
            for k in range(shared):
                i = n * count + k
                x = jnp.concatenate([listed(i, s), listed(i + count, s)], axis=0)
                total = total + dot(x, table[s, plan()[i][0]])
            for d in range(2):
                part = total[high * d : high * (d + 1)]
                for k in range(shared, count):
                    i = (n + d) * count + k
                    part = part + dot(listed(i, s), table[s, plan()[i][0]])
                acc[s, n + d] = part
            return carry

        lax.fori_loop(0, 2, interact, 0)

    check = None
    for s in range(2):
        part = times_exact(acc[s].reshape(4 * high, 256), back[256 * s : 256 * (s + 1)])
        check = part if check is None else check + part

    inverse = (invw[0], invw[1])
    for n, (c, d) in enumerate(class_pairs()):
        for t, cut, to in cut_tiles(dens):
            for j in range(gr):
                r = high * n + boxes + gc * j
                plocal[t, 2 * j + c, pl.ds(d, gc, stride=2), to] = check[r : r + gc, cut]
    local = pin_ref[...].reshape(boxes, dens) + times_t(lanes(plocal)[:, :dens], inverse)
    x = jnp.concatenate(
        [
            check[high * n : high * n + boxes] + times_t(local, (downw[n, 0], downw[n, 1]))
            for n in range(4)
        ],
        axis=0,
    )
    result = times_t(x, inverse)
    for n, (c, d) in enumerate(class_pairs()):
        for t, cut, to in cut_tiles(dens):
            for j in range(pr):
                r = boxes * n + pc * j
                flat[t, 2 * j + c, pl.ds(d, pc, stride=2), to] = result[r : r + pc, cut]
    for t, cut, to in cut_tiles(dens):
        out_ref[:, :, cut] = flat[t, :, :, to]


VMEM = pl.BlockSpec(memory_space=pltpu.VMEM)
SMEM = pl.BlockSpec(memory_space=pltpu.SMEM)


def params(mib):
    return pltpu.CompilerParams(vmem_limit_bytes=mib * 1024 * 1024)


def cost(rows, tiles, reads):
    return pl.CostEstimate(flops=2 * rows * tiles * 256 * 256, bytes_accessed=reads, transcendentals=0)


def height(boxes):
    return -(-(boxes * 5 // 4) // 16) * 16


def own_step(own, rotation):
    rows, cols, _ = own.shape
    tiled = jax.ShapeDtypeStruct((4, rows, cols, 128), F32)
    return pl.pallas_call(
        own_kernel,
        out_shape=(tiled, tiled, jax.ShapeDtypeStruct(rotation.shape, BF16)),
        in_specs=[VMEM] * 2,
        out_specs=(VMEM,) * 3,
        compiler_params=params(16),
        cost_estimate=cost(rows * cols, 48, 64 * 1024 * 1024),
    )(own, rotation)


def pass_step(even, strips, tiled, own_modes, rotation, up):
    rows, cols = tiled.shape[1:3]
    dens = up.shape[1]
    pr, pc = rows // 2, cols // 2
    send = jax.ShapeDtypeStruct((4, 2, cols + 2 * HALO + 8 * ((pc + 11) // 8), 128), F32)
    return pl.pallas_call(
        pass_kernel,
        out_shape=(
            jax.ShapeDtypeStruct((pr, pc, dens), F32),
            jax.ShapeDtypeStruct((4, rows + 4, cols + 16, 128), F32),
            jax.ShapeDtypeStruct((4, pr + 4, pc + 8, 128), F32),
            send,
            send,
        ),
        in_specs=[SMEM] + [VMEM] * 6,
        out_specs=(VMEM,) * 5,
        scratch_shapes=[pltpu.VMEM((4, rows, 2 * HALO, 128), F32)],
        compiler_params=params(16),
        cost_estimate=cost(rows * cols, 32, up.size * 4),
    )(even, *strips, tiled, own_modes, rotation, up)


def near_step(modes, pmodes, llist, plist, down, inv):
    rows, cols, _ = llist.shape
    high = height(rows * cols // 4)
    return pl.pallas_call(
        near_kernel,
        out_shape=(
            jax.ShapeDtypeStruct((36, 2, high, 256), BF16),
            jax.ShapeDtypeStruct((len(plan()), high, 128), BF16),
            jax.ShapeDtypeStruct((4, 2) + inv.shape, BF16),
            jax.ShapeDtypeStruct((2,) + inv.shape, BF16),
        ),
        in_specs=[VMEM] * 6,
        out_specs=(VMEM,) * 4,
        scratch_shapes=[pltpu.VMEM((2, rows, cols, 128), F32)],
        compiler_params=params(16),
        cost_estimate=cost(rows * cols, 48, 16 * 1024 * 1024),
    )(modes, pmodes, llist, plist, down, inv)


def close_step(even, ends, modes, pmodes, masks, lut, pin, back, table, downw, invw, shape):
    rows, cols, dens = shape
    pr, pc = rows // 2, cols // 2
    high = height(pr * pc)
    return pl.pallas_call(
        close_kernel,
        out_shape=jax.ShapeDtypeStruct(shape, F32),
        in_specs=[SMEM] + [VMEM] * 11,
        out_specs=VMEM,
        scratch_shapes=[
            pltpu.VMEM((4, 8, cols + 16, 128), F32),
            pltpu.VMEM((4, pr + 4, pc + 8, 128), F32),
            pltpu.VMEM((2, 12, 2, 32, 256), BF16),
            pltpu.VMEM((2, 4, high, 256), F32),
            pltpu.VMEM((4, rows, cols, 128), F32),
            pltpu.VMEM((4, pr, pc, 128), F32),
        ],
        compiler_params=params(24),
        cost_estimate=cost(rows * cols, 150, table.size * 2),
    )(
        even, *ends, modes, pmodes, masks, lut, pin, back, table, downw, invw,
    )


def swapped(strips, axis, odd_first):
    peers = lax.axis_size(axis)
    got = [None, None]
    for kind in (1, 0) if odd_first else (0, 1):
        pairs = [(i, i + 1) for i in range(kind, peers - 1, 2)]
        got[kind] = lax.ppermute(strips[kind], axis, pairs + [(j, i) for i, j in pairs])
    return got


def local(leaf_up, parent_in, leaf_lists, parent_lists, up_transfer, down_transfer, check_inverse):
    cols = leaf_up.shape[1]
    even = [lax.axis_index(axis) % 2 == 0 for axis in ("gx", "gy")]
    flag = jnp.stack(even).astype(jnp.int32)
    rotation, back, table = (jnp.asarray(x) for x in operators())
    low, high = leaf_up[:, :HALO], leaf_up[:, cols - HALO :]
    strips = (jnp.where(even[1], high, low), jnp.where(even[1], low, high))
    strips = swapped(strips, "gy", True)
    own_modes, tiled, rotation = own_step(leaf_up, rotation)
    parent_up, modes, pmodes, *sends = pass_step(flag, strips, tiled, own_modes, rotation, up_transfer)
    ends = swapped(sends, "gx", False)
    lut, masks, downw, invw = near_step(
        modes, pmodes, leaf_lists, parent_lists, down_transfer, check_inverse
    )
    leaf_down = close_step(
        flag, ends, modes, pmodes, masks, lut, parent_in, back, table,
        downw, invw, leaf_up.shape,
    )
    return leaf_down, parent_up


def solution(mesh):
    block = P("gx", "gy", None)
    return jax.shard_map(
        local,
        mesh=mesh,
        in_specs=(block,) * 4 + (P(),) * 3,
        out_specs=(block, block),
        check_vma=False,
    )
```

```python
import functools
import math

import jax
import jax.numpy as jnp
import ml_dtypes
import numpy as np
from jax import lax
from jax.experimental import pallas as pl
from jax.experimental.pallas import tpu as pltpu
from jax.sharding import PartitionSpec as P

ORDER = 6
HALO = 4
KEPT = 14
BF16, F32 = jnp.bfloat16, jnp.float32

def offset_table():
    return [(a, b) for a in range(-3, 4) for b in range(-3, 4) if max(abs(a), abs(b)) >= 2]


BASES = sorted({(abs(a), abs(b)) for a, b in offset_table()})


def surface_points():
    grid = np.linspace(-1.0, 1.0, ORDER)
    keys = [
        (i, j, k)
        for i in range(ORDER)
        for j in range(ORDER)
        for k in range(ORDER)
        if min(i, j, k) == 0 or max(i, j, k) == ORDER - 1
    ]
    return keys, np.array([[grid[i] for i in key] for key in keys])


def translation(points, dx, dy):
    r = 0.525 * (points[:, None, :] - points[None, :, :]) - np.array([dx, dy, 0.0])
    dist = np.sqrt((r * r).sum(-1))
    n = len(points)
    out = np.zeros((3, n, 3, n))
    for a in range(3):
        for b in range(3):
            out[a, :, b, :] = (float(a == b) / dist + r[..., a] * r[..., b] / dist**3) / (8 * math.pi)
    return out.reshape(3 * n, 3 * n)


def split(x):
    high = x.astype(ml_dtypes.bfloat16)
    return high, (x - high.astype(np.float64)).astype(ml_dtypes.bfloat16)


@functools.lru_cache(maxsize=None)
def operators():
    keys, points = surface_points()
    n = len(keys)
    points_of = {key: i for i, key in enumerate(keys)}
    mirror = [points_of[(i, j, ORDER - 1 - k)] for i, j, k in keys]
    mats = {o: translation(points, *o) for o in offset_table()}
    half = 3 * n // 2
    rotation = np.zeros((3 * n, 512), ml_dtypes.bfloat16)
    back = np.zeros((512, 3 * n))
    table = np.zeros((2, len(BASES), 256, 256), ml_dtypes.bfloat16)
    signs = np.ones((4, 2, 256, 256), ml_dtypes.bfloat16)
    for s, sign in enumerate((1, -1)):
        pairs = np.zeros((3 * n, half))
        firsts = []
        for a in range(3):
            flip = sign if a < 2 else -sign
            for i in range(n):
                if i < mirror[i]:
                    pairs[a * n + i, len(firsts)] = 1.0
                    pairs[a * n + mirror[i], len(firsts)] = flip
                    firsts.append(a * n + i)
        blocks = {o: 0.25 * pairs.T @ m @ pairs for o, m in mats.items()}
        gram = sum(b.T @ b for b in blocks.values())
        place = {f: i for i, f in enumerate(firsts)}
        modes, parity, weight = [], [], []
        for sx in (1, -1):
            for sy in (1, -1):
                basis = []
                for i, f in enumerate(firsts):
                    a, (kx, ky, kz) = f // n, keys[f % n]
                    if kx < ORDER // 2 and ky < ORDER // 2:
                        v = np.zeros(half)
                        for fx in range(2):
                            for fy in range(2):
                                key = (ORDER - 1 - kx if fx else kx, ORDER - 1 - ky if fy else ky, kz)
                                sign_x = (sx if a != 0 else -sx) if fx else 1
                                sign_y = (sy if a != 1 else -sy) if fy else 1
                                v[place[a * n + points_of[key]]] = 0.5 * sign_x * sign_y
                        basis.append(v)
                basis = np.array(basis).T
                w, vecs = np.linalg.eigh(basis.T @ gram @ basis)
                vecs = basis @ vecs
                vecs = vecs * np.sign(vecs[np.abs(np.round(vecs, 9)).argmax(0), np.arange(len(w))])
                modes.append(vecs)
                weight.append(w)
                parity += [(sx, sy)] * len(w)
        order = np.argsort(-np.concatenate(weight), kind="stable")
        vecs = np.concatenate(modes, axis=1)[:, order]
        parity = np.array(parity)[order]
        modes = (pairs @ vecs / math.sqrt(2.0)).astype(ml_dtypes.bfloat16)
        lows = np.concatenate([modes, modes[:, :KEPT], modes[:, :KEPT]], axis=1)
        rotation[:, 256 * s : 256 * (s + 1)] = lows
        outs, out_parity = [], []
        for sx in (1, -1):
            for sy in (1, -1):
                for f in firsts:
                    a, (kx, ky, kz) = f // n, keys[f % n]
                    if kx < ORDER // 2 and ky < ORDER // 2:
                        v = np.zeros(half)
                        for fx in range(2):
                            for fy in range(2):
                                key = (ORDER - 1 - kx if fx else kx, ORDER - 1 - ky if fy else ky, kz)
                                sign_x = (sx if a != 0 else -sx) if fx else 1
                                sign_y = (sy if a != 1 else -sy) if fy else 1
                                v[place[a * n + points_of[key]]] = sign_x * sign_y
                        outs.append(v)
                        out_parity.append((sx, sy))
        outs = np.array(outs).T
        out_parity = np.array(out_parity)
        back[256 * s : 256 * s + half] = (pairs @ outs).T
        undo = np.linalg.inv(modes[firsts].astype(np.float64))
        for q, o in enumerate(BASES):
            high, low = split(undo @ blocks[o].T @ outs * 0.25)
            table[s, q, :half, :half] = high
            table[s, q, half : half + KEPT, :half] = high[:KEPT]
            table[s, q, half + KEPT : half + 2 * KEPT, :half] = low[:KEPT]
        ins = np.concatenate([parity, parity[:KEPT], parity[:KEPT]], axis=0)
        for f in range(4):
            row = np.ones(256)
            row[: len(ins)] = (ins[:, 0] if f // 2 else 1) * (ins[:, 1] if f % 2 else 1)
            col = np.ones(256)
            col[:half] = (out_parity[:, 0] if f // 2 else 1) * (out_parity[:, 1] if f % 2 else 1)
            signs[f, s] = row[:, None] * col[None, :]
    whole = [
        table[:, BASES.index((abs(a), abs(b)))] * signs[2 * (a < 0) + (b < 0)]
        for a, b in offset_table()
    ]
    return rotation, back.astype(ml_dtypes.bfloat16), np.stack(whole, axis=1)


@functools.lru_cache(maxsize=None)
def plan():
    products = []
    offsets = offset_table()
    for c, d in class_pairs():
        for o in sorted(range(len(offsets)), key=lambda o: (abs(offsets[o][1]) == 3, o)):
            dx, dy = offsets[o]
            px, cs = divmod(c + dx, 2)
            py, ds = divmod(d + dy, 2)
            if abs(px) <= 1 and abs(py) <= 1:
                products.append((o, (cs * 3 + px + 1) * 6 + ds * 3 + py + 1))
    return products


def class_pairs():
    return [(c, d) for c in range(2) for d in range(2)]


def dot(a, b):
    return lax.dot_general(a, b, (((1,), (0,)), ((), ())), preferred_element_type=F32)


def dot_t(a, b):
    return lax.dot_general(a, b, (((1,), (1,)), ((), ())), preferred_element_type=F32)


def parts(x):
    high = x.astype(BF16)
    return high, (x - high.astype(F32)).astype(BF16)


def times_t(x, weight):
    xh, xl = parts(x)
    wh, wl = weight
    both = dot_t(jnp.concatenate([xh, xl], axis=0), wh)
    return both[: x.shape[0]] + (both[x.shape[0] :] + dot_t(xh, wl))


def times_exact(x, weight):
    both = dot(jnp.concatenate(parts(x), axis=0), weight)
    return both[: x.shape[0]] + both[x.shape[0] :]


def lanes(ref, *at):
    pieces = [ref[(t,) + at] for t in range(4)]
    pieces = [p.reshape(-1, 128) for p in pieces]
    return jnp.concatenate(pieces, axis=1)


def cut_tiles(dens):
    return [(t, slice(128 * t, min(128 * t + 128, dens)), slice(0, min(128, dens - 128 * t))) for t in range(4)]


def modes_of(x, rot_ref, dens):
    y = times_exact(x[:, :dens], rot_ref[...])
    lane = lax.broadcasted_iota(jnp.int32, (1, 512), 1) % 256
    half = dens // 2
    is_low = (lane >= half) & (lane < half + KEPT)
    return jnp.where(is_low, y - y.astype(BF16).astype(F32), y)


def children(ref, dens, counts, c, d):
    return jnp.concatenate(
        [
            jnp.concatenate(
                [ref[t, 2 * i + c, pl.ds(d, counts[1], stride=2), :] for i in range(counts[0])],
                axis=0,
            )
            for t in range(4)
        ],
        axis=1,
    )[:, :dens]


def own_kernel(own_ref, rot_ref, modes_ref, tiled_ref, rot_out):
    rows, cols, dens = own_ref.shape
    rot_out[...] = rot_ref[...]
    y = modes_of(own_ref[...].reshape(rows * cols, dens), rot_ref, dens)
    for t, cut, to in cut_tiles(dens):
        modes_ref[t] = y[:, 128 * t : 128 * t + 128].reshape(rows, cols, 128)
        tiled_ref[t, :, :, to] = own_ref[:, :, cut]


def split_kernel(weight_ref, after_ref, split_ref):
    def one(n, carry):
        split_ref[n, 0], split_ref[n, 1] = parts(weight_ref[n])
        return carry

    lax.fori_loop(0, weight_ref.shape[0], one, 0)


def pass_kernel(
    even_ref, strip0_ref, strip1_ref, own_t, own_modes_ref, rot_ref, upw_ref,
    pup_ref, modes, pmodes, send0_ref, send1_ref,
    strip_t,
):
    rows, _, dens = strip0_ref.shape
    cols = own_modes_ref.shape[2]
    pr, pc = rows // 2, cols // 2
    boxes = pr * pc
    wide = cols + 2 * HALO
    even_x, even_y = even_ref[0] == 1, even_ref[1] == 1
    for t, cut, to in cut_tiles(dens):
        first, second = strip0_ref[:, :, cut], strip1_ref[:, :, cut]
        strip_t[t, :, 0:HALO, to] = jnp.where(even_y, second, first)
        strip_t[t, :, HALO:, to] = jnp.where(even_y, first, second)

    parent = None
    for n, (c, d) in enumerate(class_pairs()):
        x = jnp.concatenate(
            [children(own_t, dens, (pr, pc), c, d), children(strip_t, dens, (pr, HALO), c, d)],
            axis=0,
        )
        part = times_t(x, (upw_ref[n, 0], upw_ref[n, 1]))
        parent = part if parent is None else parent + part
    pup_ref[...] = parent[:boxes].reshape(pr, pc, dens)
    z = modes_of(jnp.concatenate([lanes(strip_t)[:, :dens], parent], axis=0), rot_ref, dens)
    w, p = z[: rows * 8], z[rows * 8 :]
    for t in range(4):
        cut = slice(128 * t, 128 * t + 128)
        modes[t, 2 : 2 + rows, 8 : 8 + cols, :] = own_modes_ref[t]
        strip = w[:, cut].reshape(rows, 8, 128)
        modes[t, 2 : 2 + rows, 4:8, :] = strip[:, 0:4]
        modes[t, 2 : 2 + rows, 8 + cols : 12 + cols, :] = strip[:, 4:8]
        pmodes[t, 2 : 2 + pr, 4 : 4 + pc, :] = p[:boxes, cut].reshape(pr, pc, 128)
        strip = p[boxes:, cut].reshape(pr, 4, 128)
        pmodes[t, 2 : 2 + pr, 2:4, :] = strip[:, 0:2]
        pmodes[t, 2 : 2 + pr, 4 + pc : 6 + pc, :] = strip[:, 2:4]
        low, high = modes[t, 2:4, 4 : 4 + wide, :], modes[t, rows : rows + 2, 4 : 4 + wide, :]
        send0_ref[t, :, 0:wide, :] = jnp.where(even_x, high, low)
        send1_ref[t, :, 0:wide, :] = jnp.where(even_x, low, high)
        low, high = pmodes[t, 2:4, 2 : 6 + pc, :], pmodes[t, pr : pr + 2, 2 : 6 + pc, :]
        send0_ref[t, :, wide : wide + 4 + pc, :] = jnp.where(even_x, high, low)
        send1_ref[t, :, wide : wide + 4 + pc, :] = jnp.where(even_x, low, high)


def near_kernel(
    modes, pmodes_ref, llist_ref, plist_ref, down_ref, inv_ref,
    lut, masks_ref, downw_ref, invw_ref,
    flat,
):
    rows, cols = modes.shape[1] - 4, modes.shape[2] - 16
    pr, pc = rows // 2, cols // 2
    gr, gc = pr // 2, pc // 2
    used = pr * pc + gr * gc
    high = lut.shape[2]
    count = masks_ref.shape[0] // 4

    def gather(i, carry):
        base = 2 * (i % 3) + i // 3
        for ds in range(2):
            for py in (-1, 0, 1):
                e = i * 6 + ds * 3 + py + 1
                for t in range(4):
                    x = jnp.concatenate(
                        [
                            modes[t, base + 2 * j, pl.ds(8 + 2 * py + ds, pc, stride=2), :]
                            for j in range(pr)
                        ]
                        + [
                            pmodes_ref[t, base + 2 * j, pl.ds(4 + 2 * py + ds, gc, stride=2), :]
                            for j in range(gr)
                        ]
                        + [jnp.zeros((high - used, 128), F32)],
                        axis=0,
                    )
                    lut[e, t // 2, :, 128 * (t % 2) : 128 * (t % 2) + 128] = x.astype(BF16)
        return carry

    lax.fori_loop(0, 6, gather, 0)

    def halve(n, carry):
        downw_ref[n, 0], downw_ref[n, 1] = parts(down_ref[n])
        return carry

    lax.fori_loop(0, 4, halve, 0)
    invw_ref[0], invw_ref[1] = parts(inv_ref[...])

    flat[0, :, :, 0 : llist_ref.shape[2]] = llist_ref[...].astype(F32)
    flat[1, 0:pr, 0:pc, 0 : plist_ref.shape[2]] = plist_ref[...].astype(F32)
    for n, (c, d) in enumerate(class_pairs()):
        flag = jnp.concatenate(
            [flat[0, 2 * i + c, pl.ds(d, pc, stride=2), :] for i in range(pr)]
            + [flat[1, 2 * i + c, pl.ds(d, gc, stride=2), :] for i in range(gr)]
            + [jnp.zeros((high - used, 128), F32)],
            axis=0,
        )
        for k in range(count):
            o = plan()[count * n + k][0]
            masks_ref[count * n + k] = jnp.broadcast_to(flag[:, o : o + 1], (high, 128)).astype(BF16)


def close_kernel(
    entry_ref, pick_ref, even_ref,
    got0_ref, got1_ref, modes, pside_ref, masks, lut_ref,
    pin_ref, back, table, downw, invw,
    out_ref,
    edge, pmodes, lut, acc, flat, plocal, checks, sem,
):
    rows, cols, dens = out_ref.shape
    pr, pc = rows // 2, cols // 2
    gr, gc = pr // 2, pc // 2
    boxes, pboxes = pr * pc, gr * gc
    high = lut.shape[2]
    wide = cols + 2 * HALO
    count = masks.shape[0] // 4
    copy = pltpu.make_async_copy(lut_ref, lut, sem)
    copy.start()
    even = even_ref[0] == 1
    for t in range(4):
        before = jnp.where(even, got1_ref[t], got0_ref[t])
        after = jnp.where(even, got0_ref[t], got1_ref[t])
        edge[t, 0:2, 4 : 4 + wide, :] = before[:, 0:wide]
        edge[t, 2:4] = modes[t, 2:4]
        edge[t, 4:6] = modes[t, rows : rows + 2]
        edge[t, 6:8, 4 : 4 + wide, :] = after[:, 0:wide]
        pmodes[t, 0:2, 2 : 6 + pc, :] = before[:, wide : wide + 4 + pc]
        pmodes[t, 2 : 2 + pr] = pside_ref[t, 2 : 2 + pr]
        pmodes[t, 2 + pr :, 2 : 6 + pc, :] = after[:, wide : wide + 4 + pc]

    copy.wait()

    def patch(cs, carry):
        for ds in range(2):
            for py in (-1, 0, 1):
                for t in range(4):
                    at = slice(128 * (t % 2), 128 * (t % 2) + 128)
                    mine = pl.ds(8 + 2 * py + ds, pc, stride=2)
                    theirs = pl.ds(4 + 2 * py + ds, gc, stride=2)
                    e = cs * 18 + ds * 3 + py + 1
                    x = jnp.concatenate([edge[t, cs + 2 * j, mine, :] for j in range(2)], axis=0)
                    lut[e, t // 2, 0:16, at] = x.astype(BF16)
                    x = jnp.concatenate([pmodes[t, cs + 2 * j, theirs, :] for j in range(4)], axis=0)
                    lut[e, t // 2, boxes : boxes + 16, at] = x.astype(BF16)
                    e = e + 12
                    x = jnp.concatenate([edge[t, 4 + cs + 2 * j, mine, :] for j in range(2)], axis=0)
                    lut[e, t // 2, boxes - 16 : boxes, at] = x.astype(BF16)
                    x = jnp.concatenate(
                        [pmodes[t, 4 + cs + 2 * j, theirs, :] for j in range(4, gr)]
                        + [jnp.zeros((high - boxes - pboxes, 128), F32)],
                        axis=0,
                    )
                    lut[e, t // 2, boxes + 16 : high, at] = x.astype(BF16)
        return carry

    lax.fori_loop(0, 2, patch, 0)

    shared = sum(abs(offset_table()[o][1]) < 3 for o, _ in plan()[:count])

    def listed(i, s):
        m = masks[i]
        x = lut[entry_ref[i], s]
        return jnp.concatenate([x[:, :128] * m, x[:, 128:] * m], axis=1)

    def interact(j, carry):
        n, s = 2 * (j // 2), j % 2
        total = jnp.zeros((2 * high, 256), F32)
        for k in range(shared):
            i = n * count + k
            x = jnp.concatenate([listed(i, s), listed(i + count, s)], axis=0)
            total = total + dot(x, table[s, pick_ref[i]])
        for d in range(2):
            part = total[high * d : high * (d + 1)]
            for k in range(shared, count):
                i = (n + d) * count + k
                part = part + dot(listed(i, s), table[s, pick_ref[i]])
            acc[s, n + d] = part
        return carry

    lax.fori_loop(0, 4, interact, 0)

    check = None
    for s in range(2):
        part = times_exact(acc[s].reshape(4 * high, 256), back[256 * s : 256 * (s + 1)])
        check = part if check is None else check + part

    inverse = (invw[0], invw[1])
    for n, (c, d) in enumerate(class_pairs()):
        for t, cut, to in cut_tiles(dens):
            for j in range(gr):
                r = high * n + boxes + gc * j
                plocal[t, 2 * j + c, pl.ds(d, gc, stride=2), to] = check[r : r + gc, cut]
    local = pin_ref[...].reshape(boxes, dens) + times_t(lanes(plocal)[:, :dens], inverse)
    checks[...] = jnp.concatenate([check[high * n : high * n + boxes] for n in range(4)], axis=0)

    def spread(n, carry):
        at = pl.ds(pl.multiple_of(boxes * n, 8), boxes)
        checks[at, :] += times_t(local, (downw[n, 0], downw[n, 1]))
        return carry

    lax.fori_loop(0, 4, spread, 0)
    result = times_t(checks[...], inverse)
    for n, (c, d) in enumerate(class_pairs()):
        for t, cut, to in cut_tiles(dens):
            for j in range(pr):
                r = boxes * n + pc * j
                flat[t, 2 * j + c, pl.ds(d, pc, stride=2), to] = result[r : r + pc, cut]
    for t, cut, to in cut_tiles(dens):
        out_ref[:, :, cut] = flat[t, :, :, to]


VMEM = pl.BlockSpec(memory_space=pltpu.VMEM)
SMEM = pl.BlockSpec(memory_space=pltpu.SMEM)


def params(mib):
    return pltpu.CompilerParams(vmem_limit_bytes=mib * 1024 * 1024)


def cost(rows, tiles, reads):
    return pl.CostEstimate(flops=2 * rows * tiles * 256 * 256, bytes_accessed=reads, transcendentals=0)


def height(boxes):
    return -(-(boxes * 5 // 4) // 16) * 16


def own_step(own, rotation):
    rows, cols, _ = own.shape
    tiled = jax.ShapeDtypeStruct((4, rows, cols, 128), F32)
    return pl.pallas_call(
        own_kernel,
        out_shape=(tiled, tiled, jax.ShapeDtypeStruct(rotation.shape, BF16)),
        in_specs=[VMEM] * 2,
        out_specs=(VMEM,) * 3,
        compiler_params=params(12),
        cost_estimate=cost(rows * cols, 48, 64 * 1024 * 1024),
    )(own, rotation)


def split_step(weight, after):
    n, dens, _ = weight.shape
    return pl.pallas_call(
        split_kernel,
        out_shape=jax.ShapeDtypeStruct((n, 2, dens, dens), BF16),
        in_specs=[VMEM] * 2,
        out_specs=VMEM,
        compiler_params=params(12),
        cost_estimate=cost(8 * dens, 1, weight.size * 8),
    )(weight, after)


def pass_step(even, strips, tiled, own_modes, rotation, upw):
    rows, cols = tiled.shape[1:3]
    dens = upw.shape[2]
    pr, pc = rows // 2, cols // 2
    send = jax.ShapeDtypeStruct((4, 2, cols + 2 * HALO + 8 * ((pc + 11) // 8), 128), F32)
    return pl.pallas_call(
        pass_kernel,
        out_shape=(
            jax.ShapeDtypeStruct((pr, pc, dens), F32),
            jax.ShapeDtypeStruct((4, rows + 4, cols + 16, 128), F32),
            jax.ShapeDtypeStruct((4, pr + 4, pc + 8, 128), F32),
            send,
            send,
        ),
        in_specs=[SMEM] + [VMEM] * 6,
        out_specs=(VMEM,) * 5,
        scratch_shapes=[pltpu.VMEM((4, rows, 2 * HALO, 128), F32)],
        compiler_params=params(12),
        cost_estimate=cost(rows * cols, 32, upw.size * 2),
    )(even, *strips, tiled, own_modes, rotation, upw)


def near_step(modes, pmodes, llist, plist, down, inv):
    rows, cols, _ = llist.shape
    high = height(rows * cols // 4)
    return pl.pallas_call(
        near_kernel,
        out_shape=(
            jax.ShapeDtypeStruct((36, 2, high, 256), BF16),
            jax.ShapeDtypeStruct((len(plan()), high, 128), BF16),
            jax.ShapeDtypeStruct((4, 2) + inv.shape, BF16),
            jax.ShapeDtypeStruct((2,) + inv.shape, BF16),
        ),
        in_specs=[VMEM] * 6,
        out_specs=(VMEM,) * 4,
        scratch_shapes=[pltpu.VMEM((2, rows, cols, 128), F32)],
        compiler_params=params(12),
        cost_estimate=cost(rows * cols, 48, 16 * 1024 * 1024),
    )(modes, pmodes, llist, plist, down, inv)


def close_step(even, ends, modes, pmodes, masks, lut, pin, back, table, downw, invw, shape):
    rows, cols, dens = shape
    pr, pc = rows // 2, cols // 2
    high = height(pr * pc)
    return pl.pallas_call(
        close_kernel,
        out_shape=jax.ShapeDtypeStruct(shape, F32),
        in_specs=[SMEM] * 3 + [VMEM] * 11,
        out_specs=VMEM,
        scratch_shapes=[
            pltpu.VMEM((4, 8, cols + 16, 128), F32),
            pltpu.VMEM((4, pr + 4, pc + 8, 128), F32),
            pltpu.VMEM(lut.shape, BF16),
            pltpu.VMEM((2, 4, high, 256), F32),
            pltpu.VMEM((4, rows, cols, 128), F32),
            pltpu.VMEM((4, pr, pc, 128), F32),
            pltpu.VMEM((4 * pr * pc, dens), F32),
            pltpu.SemaphoreType.DMA,
        ],
        compiler_params=params(24),
        cost_estimate=cost(rows * cols, 150, table.size * 2),
    )(
        jnp.asarray([e for _, e in plan()], jnp.int32), jnp.asarray([o for o, _ in plan()], jnp.int32),
        even, *ends, modes, pmodes, masks, lut, pin, back, table, downw, invw,
    )


def swapped(strips, axis, odd_first):
    peers = lax.axis_size(axis)
    got = [None, None]
    for kind in (1, 0) if odd_first else (0, 1):
        pairs = [(i, i + 1) for i in range(kind, peers - 1, 2)]
        got[kind] = lax.ppermute(strips[kind], axis, pairs + [(j, i) for i, j in pairs])
    return got


def local(leaf_up, parent_in, leaf_lists, parent_lists, up_transfer, down_transfer, check_inverse):
    cols = leaf_up.shape[1]
    even = [lax.axis_index(axis) % 2 == 0 for axis in ("gx", "gy")]
    flag = jnp.stack(even).astype(jnp.int32)
    rotation, back, table = (jnp.asarray(x) for x in operators())
    low, high = leaf_up[:, :HALO], leaf_up[:, cols - HALO :]
    strips = (jnp.where(even[1], high, low), jnp.where(even[1], low, high))
    strips = swapped(strips, "gy", True)
    own_modes, tiled, rotation = own_step(leaf_up, rotation)
    upw = split_step(up_transfer, rotation)
    parent_up, modes, pmodes, *sends = pass_step(flag, strips, tiled, own_modes, rotation, upw)
    ends = swapped(sends, "gx", False)
    lut, masks, downw, invw = near_step(
        modes, pmodes, leaf_lists, parent_lists, down_transfer, check_inverse
    )
    leaf_down = close_step(
        flag, ends, modes, pmodes, masks, lut, parent_in, back, table,
        downw, invw, leaf_up.shape,
    )
    return leaf_down, parent_up


def solution(mesh):
    block = P("gx", "gy", None)
    return jax.shard_map(
        local,
        mesh=mesh,
        in_specs=(block,) * 4 + (P(),) * 3,
        out_specs=(block, block),
        check_vma=False,
    )
```

```python
import functools
import math

import jax
import jax.numpy as jnp
import ml_dtypes
import numpy as np
from jax import lax
from jax.experimental import pallas as pl
from jax.experimental.pallas import tpu as pltpu
from jax.sharding import PartitionSpec as P

ORDER = 6
HALO = 4
KEPT = 14
BF16, F32 = jnp.bfloat16, jnp.float32

def offset_table():
    return [(a, b) for a in range(-3, 4) for b in range(-3, 4) if max(abs(a), abs(b)) >= 2]


BASES = sorted({(abs(a), abs(b)) for a, b in offset_table()})


def surface_points():
    grid = np.linspace(-1.0, 1.0, ORDER)
    keys = [
        (i, j, k)
        for i in range(ORDER)
        for j in range(ORDER)
        for k in range(ORDER)
        if min(i, j, k) == 0 or max(i, j, k) == ORDER - 1
    ]
    return keys, np.array([[grid[i] for i in key] for key in keys])


def translation(points, dx, dy):
    r = 0.525 * (points[:, None, :] - points[None, :, :]) - np.array([dx, dy, 0.0])
    dist = np.sqrt((r * r).sum(-1))
    n = len(points)
    out = np.zeros((3, n, 3, n))
    for a in range(3):
        for b in range(3):
            out[a, :, b, :] = (float(a == b) / dist + r[..., a] * r[..., b] / dist**3) / (8 * math.pi)
    return out.reshape(3 * n, 3 * n)


def split(x):
    high = x.astype(ml_dtypes.bfloat16)
    return high, (x - high.astype(np.float64)).astype(ml_dtypes.bfloat16)


@functools.lru_cache(maxsize=None)
def operators():
    keys, points = surface_points()
    n = len(keys)
    points_of = {key: i for i, key in enumerate(keys)}
    mirror = [points_of[(i, j, ORDER - 1 - k)] for i, j, k in keys]
    mats = {o: translation(points, *o) for o in offset_table()}
    half = 3 * n // 2
    rotation = np.zeros((3 * n, 512), ml_dtypes.bfloat16)
    back = np.zeros((512, 3 * n))
    table = np.zeros((2, len(BASES), 256, 256), ml_dtypes.bfloat16)
    signs = np.ones((4, 2, 256, 256), ml_dtypes.bfloat16)
    for s, sign in enumerate((1, -1)):
        pairs = np.zeros((3 * n, half))
        firsts = []
        for a in range(3):
            flip = sign if a < 2 else -sign
            for i in range(n):
                if i < mirror[i]:
                    pairs[a * n + i, len(firsts)] = 1.0
                    pairs[a * n + mirror[i], len(firsts)] = flip
                    firsts.append(a * n + i)
        blocks = {o: 0.25 * pairs.T @ m @ pairs for o, m in mats.items()}
        gram = sum(b.T @ b for b in blocks.values())
        place = {f: i for i, f in enumerate(firsts)}
        modes, parity, weight = [], [], []
        for sx in (1, -1):
            for sy in (1, -1):
                basis = []
                for i, f in enumerate(firsts):
                    a, (kx, ky, kz) = f // n, keys[f % n]
                    if kx < ORDER // 2 and ky < ORDER // 2:
                        v = np.zeros(half)
                        for fx in range(2):
                            for fy in range(2):
                                key = (ORDER - 1 - kx if fx else kx, ORDER - 1 - ky if fy else ky, kz)
                                sign_x = (sx if a != 0 else -sx) if fx else 1
                                sign_y = (sy if a != 1 else -sy) if fy else 1
                                v[place[a * n + points_of[key]]] = 0.5 * sign_x * sign_y
                        basis.append(v)
                basis = np.array(basis).T
                w, vecs = np.linalg.eigh(basis.T @ gram @ basis)
                vecs = basis @ vecs
                vecs = vecs * np.sign(vecs[np.abs(np.round(vecs, 9)).argmax(0), np.arange(len(w))])
                modes.append(vecs)
                weight.append(w)
                parity += [(sx, sy)] * len(w)
        order = np.argsort(-np.concatenate(weight), kind="stable")
        vecs = np.concatenate(modes, axis=1)[:, order]
        parity = np.array(parity)[order]
        modes = (pairs @ vecs / math.sqrt(2.0)).astype(ml_dtypes.bfloat16)
        lows = np.concatenate([modes, modes[:, :KEPT], modes[:, :KEPT]], axis=1)
        rotation[:, 256 * s : 256 * (s + 1)] = lows
        outs, out_parity = [], []
        for sx in (1, -1):
            for sy in (1, -1):
                for f in firsts:
                    a, (kx, ky, kz) = f // n, keys[f % n]
                    if kx < ORDER // 2 and ky < ORDER // 2:
                        v = np.zeros(half)
                        for fx in range(2):
                            for fy in range(2):
                                key = (ORDER - 1 - kx if fx else kx, ORDER - 1 - ky if fy else ky, kz)
                                sign_x = (sx if a != 0 else -sx) if fx else 1
                                sign_y = (sy if a != 1 else -sy) if fy else 1
                                v[place[a * n + points_of[key]]] = sign_x * sign_y
                        outs.append(v)
                        out_parity.append((sx, sy))
        outs = np.array(outs).T
        out_parity = np.array(out_parity)
        back[256 * s : 256 * s + half] = (pairs @ outs).T
        undo = np.linalg.inv(modes[firsts].astype(np.float64))
        for q, o in enumerate(BASES):
            high, low = split(undo @ blocks[o].T @ outs * 0.25)
            table[s, q, :half, :half] = high
            table[s, q, half : half + KEPT, :half] = high[:KEPT]
            table[s, q, half + KEPT : half + 2 * KEPT, :half] = low[:KEPT]
        ins = np.concatenate([parity, parity[:KEPT], parity[:KEPT]], axis=0)
        for f in range(4):
            row = np.ones(256)
            row[: len(ins)] = (ins[:, 0] if f // 2 else 1) * (ins[:, 1] if f % 2 else 1)
            col = np.ones(256)
            col[:half] = (out_parity[:, 0] if f // 2 else 1) * (out_parity[:, 1] if f % 2 else 1)
            signs[f, s] = row[:, None] * col[None, :]
    whole = [
        table[:, BASES.index((abs(a), abs(b)))] * signs[2 * (a < 0) + (b < 0)]
        for a, b in offset_table()
    ]
    return rotation, back.astype(ml_dtypes.bfloat16), np.stack(whole, axis=1)


@functools.lru_cache(maxsize=None)
def plan():
    products = []
    offsets = offset_table()
    for c, d in class_pairs():
        for o in sorted(range(len(offsets)), key=lambda o: (abs(offsets[o][1]) == 3, o)):
            dx, dy = offsets[o]
            px, cs = divmod(c + dx, 2)
            py, ds = divmod(d + dy, 2)
            if abs(px) <= 1 and abs(py) <= 1:
                products.append((o, (cs * 3 + px + 1) * 6 + ds * 3 + py + 1))
    return products


def class_pairs():
    return [(c, d) for c in range(2) for d in range(2)]


def dot(a, b):
    return lax.dot_general(a, b, (((1,), (0,)), ((), ())), preferred_element_type=F32)


def dot_t(a, b):
    return lax.dot_general(a, b, (((1,), (1,)), ((), ())), preferred_element_type=F32)


def parts(x):
    high = x.astype(BF16)
    return high, (x - high.astype(F32)).astype(BF16)


def times_t(x, weight):
    xh, xl = parts(x)
    wh, wl = weight
    both = dot_t(jnp.concatenate([xh, xl], axis=0), wh)
    return both[: x.shape[0]] + (both[x.shape[0] :] + dot_t(xh, wl))


def times_exact(x, weight):
    both = dot(jnp.concatenate(parts(x), axis=0), weight)
    return both[: x.shape[0]] + both[x.shape[0] :]


def lanes(ref, *at):
    pieces = [ref[(t,) + at] for t in range(4)]
    pieces = [p.reshape(-1, 128) for p in pieces]
    return jnp.concatenate(pieces, axis=1)


def cut_tiles(dens):
    return [(t, slice(128 * t, min(128 * t + 128, dens)), slice(0, min(128, dens - 128 * t))) for t in range(4)]


def modes_of(x, rot_ref, dens):
    y = times_exact(x[:, :dens], rot_ref[...])
    lane = lax.broadcasted_iota(jnp.int32, (1, 512), 1) % 256
    half = dens // 2
    is_low = (lane >= half) & (lane < half + KEPT)
    return jnp.where(is_low, y - y.astype(BF16).astype(F32), y)


def children(ref, dens, counts, c, d):
    return jnp.concatenate(
        [
            jnp.concatenate(
                [ref[t, 2 * i + c, pl.ds(d, counts[1], stride=2), :] for i in range(counts[0])],
                axis=0,
            )
            for t in range(4)
        ],
        axis=1,
    )[:, :dens]


def own_kernel(own_ref, rot_ref, modes_ref, tiled_ref, rot_out):
    rows, cols, dens = own_ref.shape
    rot_out[...] = rot_ref[...]
    y = modes_of(own_ref[...].reshape(rows * cols, dens), rot_ref, dens)
    for t, cut, to in cut_tiles(dens):
        modes_ref[t] = y[:, 128 * t : 128 * t + 128].reshape(rows, cols, 128)
        tiled_ref[t, :, :, to] = own_ref[:, :, cut]


def pass_kernel(
    even_ref, strip0_ref, strip1_ref, own_t, own_modes_ref, rot_ref, up_ref,
    pup_ref, side_ref, pmodes, send0_ref, send1_ref,
    strip_t,
):
    rows, _, dens = strip0_ref.shape
    cols = own_modes_ref.shape[2]
    pr, pc = rows // 2, cols // 2
    boxes = pr * pc
    wide = cols + 4
    even_x, even_y = even_ref[0] == 1, even_ref[1] == 1
    for t, cut, to in cut_tiles(dens):
        first, second = strip0_ref[:, :, cut], strip1_ref[:, :, cut]
        strip_t[t, :, 0:HALO, to] = jnp.where(even_y, second, first)
        strip_t[t, :, HALO:, to] = jnp.where(even_y, first, second)

    parent = None
    for n, (c, d) in enumerate(class_pairs()):
        x = jnp.concatenate(
            [children(own_t, dens, (pr, pc), c, d), children(strip_t, dens, (pr, HALO), c, d)],
            axis=0,
        )
        part = times_t(x, parts(up_ref[n]))
        parent = part if parent is None else parent + part
    pup_ref[...] = parent[:boxes].reshape(pr, pc, dens)
    z = modes_of(jnp.concatenate([lanes(strip_t)[:, :dens], parent], axis=0), rot_ref, dens)
    w, p = z[: rows * 8], z[rows * 8 :]
    for t in range(4):
        cut = slice(128 * t, 128 * t + 128)
        side = w[:, cut].reshape(rows, 8, 128)
        side_ref[t] = side
        pmodes[t, 2 : 2 + pr, 4 : 4 + pc, :] = p[:boxes, cut].reshape(pr, pc, 128)
        strip = p[boxes:, cut].reshape(pr, 4, 128)
        pmodes[t, 2 : 2 + pr, 2:4, :] = strip[:, 0:2]
        pmodes[t, 2 : 2 + pr, 4 + pc : 6 + pc, :] = strip[:, 2:4]
        for at, x in ((0, side[:, 2:4]), (2, own_modes_ref[t]), (2 + cols, side[:, 4:6])):
            low, high = x[0:2], x[rows - 2 :]
            to = slice(at, at + x.shape[1])
            send0_ref[t, :, to, :] = jnp.where(even_x, high, low)
            send1_ref[t, :, to, :] = jnp.where(even_x, low, high)
        low, high = pmodes[t, 2:4, 2 : 6 + pc, :], pmodes[t, pr : pr + 2, 2 : 6 + pc, :]
        send0_ref[t, :, wide : wide + 4 + pc, :] = jnp.where(even_x, high, low)
        send1_ref[t, :, wide : wide + 4 + pc, :] = jnp.where(even_x, low, high)


def near_kernel(
    own_modes_ref, side_ref, pmodes_ref, llist_ref, plist_ref, lut, masks_ref, edge_ref, modes, flat
):
    rows, cols = own_modes_ref.shape[1:3]
    pr, pc = rows // 2, cols // 2
    gr, gc = pr // 2, pc // 2
    used = pr * pc + gr * gc
    high = lut.shape[2]
    count = masks_ref.shape[0] // 4

    for t in range(4):
        modes[t, 2 : 2 + rows, 8 : 8 + cols, :] = own_modes_ref[t]
        modes[t, 2 : 2 + rows, 4:8, :] = side_ref[t, :, 0:4]
        modes[t, 2 : 2 + rows, 8 + cols : 12 + cols, :] = side_ref[t, :, 4:8]
        edge_ref[t, 0:2] = modes[t, 2:4]
        edge_ref[t, 2:4] = modes[t, rows : rows + 2]

    def gather(i, carry):
        base = 2 * (i % 3) + i // 3
        for ds in range(2):
            for py in (-1, 0, 1):
                e = i * 6 + ds * 3 + py + 1
                for t in range(4):
                    x = jnp.concatenate(
                        [
                            modes[t, base + 2 * j, pl.ds(8 + 2 * py + ds, pc, stride=2), :]
                            for j in range(pr)
                        ]
                        + [
                            pmodes_ref[t, base + 2 * j, pl.ds(4 + 2 * py + ds, gc, stride=2), :]
                            for j in range(gr)
                        ]
                        + [jnp.zeros((high - used, 128), F32)],
                        axis=0,
                    )
                    lut[e, t // 2, :, 128 * (t % 2) : 128 * (t % 2) + 128] = x.astype(BF16)
        return carry

    lax.fori_loop(0, 6, gather, 0)

    flat[0, :, :, 0 : llist_ref.shape[2]] = llist_ref[...].astype(F32)
    flat[1, 0:pr, 0:pc, 0 : plist_ref.shape[2]] = plist_ref[...].astype(F32)
    for n, (c, d) in enumerate(class_pairs()):
        flag = jnp.concatenate(
            [flat[0, 2 * i + c, pl.ds(d, pc, stride=2), :] for i in range(pr)]
            + [flat[1, 2 * i + c, pl.ds(d, gc, stride=2), :] for i in range(gr)]
            + [jnp.zeros((high - used, 128), F32)],
            axis=0,
        )
        for k in range(count):
            o = plan()[count * n + k][0]
            masks_ref[count * n + k] = jnp.broadcast_to(flag[:, o : o + 1], (high, 128)).astype(BF16)


def close_kernel(
    even_ref,
    got0_ref, got1_ref, edge_ref, pside_ref, masks, lut,
    pin_ref, back, table, down_ref, inv_ref,
    out_ref,
    edge, pmodes, fresh, acc, flat, plocal,
):
    rows, cols, dens = out_ref.shape
    pr, pc = rows // 2, cols // 2
    gr, gc = pr // 2, pc // 2
    boxes, pboxes = pr * pc, gr * gc
    high = lut.shape[2]
    wide = cols + 4
    count = masks.shape[0] // 4
    even = even_ref[0] == 1
    for t in range(4):
        before = jnp.where(even, got1_ref[t], got0_ref[t])
        after = jnp.where(even, got0_ref[t], got1_ref[t])
        edge[t, 0:2, 6 : 6 + wide, :] = before[:, 0:wide]
        edge[t, 2:6] = edge_ref[t]
        edge[t, 6:8, 6 : 6 + wide, :] = after[:, 0:wide]
        pmodes[t, 0:2, 2 : 6 + pc, :] = before[:, wide : wide + 4 + pc]
        pmodes[t, 2 : 2 + pr] = pside_ref[t, 2 : 2 + pr]
        pmodes[t, 2 + pr :, 2 : 6 + pc, :] = after[:, wide : wide + 4 + pc]

    def patch(cs, carry):
        for ds in range(2):
            for py in (-1, 0, 1):
                for t in range(4):
                    at = slice(128 * (t % 2), 128 * (t % 2) + 128)
                    mine = pl.ds(8 + 2 * py + ds, pc, stride=2)
                    theirs = pl.ds(4 + 2 * py + ds, gc, stride=2)
                    e = cs * 6 + ds * 3 + py + 1
                    x = jnp.concatenate([edge[t, cs + 2 * j, mine, :] for j in range(2)], axis=0)
                    fresh[0, e, t // 2, 0:16, at] = x.astype(BF16)
                    x = jnp.concatenate([pmodes[t, cs + 2 * j, theirs, :] for j in range(4)], axis=0)
                    fresh[0, e, t // 2, 16:32, at] = x.astype(BF16)
                    x = jnp.concatenate([edge[t, 4 + cs + 2 * j, mine, :] for j in range(2)], axis=0)
                    fresh[1, e, t // 2, 0:16, at] = x.astype(BF16)
                    x = jnp.concatenate(
                        [pmodes[t, 4 + cs + 2 * j, theirs, :] for j in range(4, gr)]
                        + [jnp.zeros((high - boxes - pboxes, 128), F32)],
                        axis=0,
                    )
                    fresh[1, e, t // 2, 16:32, at] = x.astype(BF16)
        return carry

    lax.fori_loop(0, 2, patch, 0)

    shared = sum(abs(offset_table()[o][1]) < 3 for o, _ in plan()[:count])

    def listed(i, s):
        e = plan()[i][1]
        px = e // 6 % 3 - 1
        m = masks[i]
        if px == 0:
            x = lut[e, s]
        else:
            new = fresh[(px + 1) // 2, e // 18 * 6 + e % 6, s]
            if px < 0:
                pieces = [new[0:16], lut[e, s, 16:boxes], new[16:32], lut[e, s, boxes + 16 : high]]
            else:
                pieces = [lut[e, s, 0 : boxes - 16], new[0:16], lut[e, s, boxes : boxes + 16], new[16:32]]
            x = jnp.concatenate(pieces, axis=0)
        return jnp.concatenate([x[:, :128] * m, x[:, 128:] * m], axis=1)

    for c in range(2):

        def interact(s, carry):
            n = 2 * c
            total = jnp.zeros((2 * high, 256), F32)
            for k in range(shared):
                i = n * count + k
                x = jnp.concatenate([listed(i, s), listed(i + count, s)], axis=0)
                total = total + dot(x, table[s, plan()[i][0]])
            for d in range(2):
                part = total[high * d : high * (d + 1)]
                for k in range(shared, count):
                    i = (n + d) * count + k
                    part = part + dot(listed(i, s), table[s, plan()[i][0]])
                acc[s, n + d] = part
            return carry

        lax.fori_loop(0, 2, interact, 0)

    check = None
    for s in range(2):
        part = times_exact(acc[s].reshape(4 * high, 256), back[256 * s : 256 * (s + 1)])
        check = part if check is None else check + part

    inverse = parts(inv_ref[...])
    for n, (c, d) in enumerate(class_pairs()):
        for t, cut, to in cut_tiles(dens):
            for j in range(gr):
                r = high * n + boxes + gc * j
                plocal[t, 2 * j + c, pl.ds(d, gc, stride=2), to] = check[r : r + gc, cut]
    local = pin_ref[...].reshape(boxes, dens) + times_t(lanes(plocal)[:, :dens], inverse)
    x = jnp.concatenate(
        [
            check[high * n : high * n + boxes] + times_t(local, parts(down_ref[n]))
            for n in range(4)
        ],
        axis=0,
    )
    result = times_t(x, inverse)
    for n, (c, d) in enumerate(class_pairs()):
        for t, cut, to in cut_tiles(dens):
            for j in range(pr):
                r = boxes * n + pc * j
                flat[t, 2 * j + c, pl.ds(d, pc, stride=2), to] = result[r : r + pc, cut]
    for t, cut, to in cut_tiles(dens):
        out_ref[:, :, cut] = flat[t, :, :, to]


VMEM = pl.BlockSpec(memory_space=pltpu.VMEM)
SMEM = pl.BlockSpec(memory_space=pltpu.SMEM)


def params(mib):
    return pltpu.CompilerParams(vmem_limit_bytes=mib * 1024 * 1024)


def cost(rows, tiles, reads):
    return pl.CostEstimate(flops=2 * rows * tiles * 256 * 256, bytes_accessed=reads, transcendentals=0)


def height(boxes):
    return -(-(boxes * 5 // 4) // 16) * 16


def own_step(own, rotation):
    rows, cols, _ = own.shape
    tiled = jax.ShapeDtypeStruct((4, rows, cols, 128), F32)
    return pl.pallas_call(
        own_kernel,
        out_shape=(tiled, tiled, jax.ShapeDtypeStruct(rotation.shape, BF16)),
        in_specs=[VMEM] * 2,
        out_specs=(VMEM,) * 3,
        compiler_params=params(16),
        cost_estimate=cost(rows * cols, 48, 64 * 1024 * 1024),
    )(own, rotation)


def pass_step(even, strips, tiled, own_modes, rotation, up):
    rows, cols = tiled.shape[1:3]
    dens = up.shape[1]
    pr, pc = rows // 2, cols // 2
    send = jax.ShapeDtypeStruct((4, 2, -(-(cols + pc + 8) // 8) * 8, 128), F32)
    return pl.pallas_call(
        pass_kernel,
        out_shape=(
            jax.ShapeDtypeStruct((pr, pc, dens), F32),
            jax.ShapeDtypeStruct((4, rows, 2 * HALO, 128), F32),
            jax.ShapeDtypeStruct((4, pr + 4, pc + 8, 128), F32),
            send,
            send,
        ),
        in_specs=[SMEM] + [VMEM] * 6,
        out_specs=(VMEM,) * 5,
        scratch_shapes=[pltpu.VMEM((4, rows, 2 * HALO, 128), F32)],
        compiler_params=params(16),
        cost_estimate=cost(rows * cols, 32, up.size * 4),
    )(even, *strips, tiled, own_modes, rotation, up)


def near_step(own_modes, side, pmodes, llist, plist):
    rows, cols, _ = llist.shape
    high = height(rows * cols // 4)
    return pl.pallas_call(
        near_kernel,
        out_shape=(
            jax.ShapeDtypeStruct((36, 2, high, 256), BF16),
            jax.ShapeDtypeStruct((len(plan()), high, 128), BF16),
            jax.ShapeDtypeStruct((4, 4, cols + 16, 128), F32),
        ),
        in_specs=[VMEM] * 5,
        out_specs=(VMEM,) * 3,
        scratch_shapes=[
            pltpu.VMEM((4, rows + 4, cols + 16, 128), F32),
            pltpu.VMEM((2, rows, cols, 128), F32),
        ],
        compiler_params=params(16),
        cost_estimate=cost(rows * cols, 48, 16 * 1024 * 1024),
    )(own_modes, side, pmodes, llist, plist)


def close_step(even, ends, edge, pmodes, masks, lut, pin, back, table, down, inv, shape):
    rows, cols, dens = shape
    pr, pc = rows // 2, cols // 2
    high = height(pr * pc)
    return pl.pallas_call(
        close_kernel,
        out_shape=jax.ShapeDtypeStruct(shape, F32),
        in_specs=[SMEM] + [VMEM] * 11,
        out_specs=VMEM,
        scratch_shapes=[
            pltpu.VMEM((4, 8, cols + 16, 128), F32),
            pltpu.VMEM((4, pr + 4, pc + 8, 128), F32),
            pltpu.VMEM((2, 12, 2, 32, 256), BF16),
            pltpu.VMEM((2, 4, high, 256), F32),
            pltpu.VMEM((4, rows, cols, 128), F32),
            pltpu.VMEM((4, pr, pc, 128), F32),
        ],
        compiler_params=params(24),
        cost_estimate=cost(rows * cols, 150, table.size * 2),
    )(
        even, *ends, edge, pmodes, masks, lut, pin, back, table, down, inv,
    )


def swapped(strips, axis, odd_first):
    peers = lax.axis_size(axis)
    got = [None, None]
    for kind in (1, 0) if odd_first else (0, 1):
        pairs = [(i, i + 1) for i in range(kind, peers - 1, 2)]
        got[kind] = lax.ppermute(strips[kind], axis, pairs + [(j, i) for i, j in pairs])
    return got


def local(leaf_up, parent_in, leaf_lists, parent_lists, up_transfer, down_transfer, check_inverse):
    cols = leaf_up.shape[1]
    even = [lax.axis_index(axis) % 2 == 0 for axis in ("gx", "gy")]
    flag = jnp.stack(even).astype(jnp.int32)
    rotation, back, table = (jnp.asarray(x) for x in operators())
    low, high = leaf_up[:, :HALO], leaf_up[:, cols - HALO :]
    strips = (jnp.where(even[1], high, low), jnp.where(even[1], low, high))
    strips = swapped(strips, "gy", True)
    own_modes, tiled, rotation = own_step(leaf_up, rotation)
    parent_up, side, pmodes, *sends = pass_step(flag, strips, tiled, own_modes, rotation, up_transfer)
    ends = swapped(sends, "gx", False)
    lut, masks, edge = near_step(own_modes, side, pmodes, leaf_lists, parent_lists)
    leaf_down = close_step(
        flag, ends, edge, pmodes, masks, lut, parent_in, back, table,
        down_transfer, check_inverse, leaf_up.shape,
    )
    return leaf_down, parent_up


def solution(mesh):
    block = P("gx", "gy", None)
    return jax.shard_map(
        local,
        mesh=mesh,
        in_specs=(block,) * 4 + (P(),) * 3,
        out_specs=(block, block),
        check_vma=False,
    )
```

```python
import functools
import math

import jax
import jax.numpy as jnp
import ml_dtypes
import numpy as np
from jax import lax
from jax.experimental import pallas as pl
from jax.experimental.pallas import tpu as pltpu
from jax.sharding import PartitionSpec as P

ORDER = 6
HALO = 4
KEPT = 14
BF16, F32 = jnp.bfloat16, jnp.float32

PARTS = (
    [(a, -2) for a in range(-1, 2)],
    [(a, 2) for a in range(-1, 2)],
    [(-2, b) for b in range(-2, 3)],
    [(2, b) for b in range(-2, 3)],
    [(3, b) for b in range(-2, 3)],
    [(-3, b) for b in range(-2, 3)],
    [(a, 3) for a in range(-3, 4)],
    [(a, -3) for a in range(-3, 4)],
)


def offset_table():
    return [(a, b) for a in range(-3, 4) for b in range(-3, 4) if max(abs(a), abs(b)) >= 2]


BASES = sorted({(abs(a), abs(b)) for a, b in offset_table()})


def surface_points():
    grid = np.linspace(-1.0, 1.0, ORDER)
    keys = [
        (i, j, k)
        for i in range(ORDER)
        for j in range(ORDER)
        for k in range(ORDER)
        if min(i, j, k) == 0 or max(i, j, k) == ORDER - 1
    ]
    return keys, np.array([[grid[i] for i in key] for key in keys])


def translation(points, dx, dy):
    r = 0.525 * (points[:, None, :] - points[None, :, :]) - np.array([dx, dy, 0.0])
    dist = np.sqrt((r * r).sum(-1))
    n = len(points)
    out = np.zeros((3, n, 3, n))
    for a in range(3):
        for b in range(3):
            out[a, :, b, :] = (float(a == b) / dist + r[..., a] * r[..., b] / dist**3) / (8 * math.pi)
    return out.reshape(3 * n, 3 * n)


def split(x):
    high = x.astype(ml_dtypes.bfloat16)
    return high, (x - high.astype(np.float64)).astype(ml_dtypes.bfloat16)


@functools.lru_cache(maxsize=None)
def operators():
    keys, points = surface_points()
    n = len(keys)
    points_of = {key: i for i, key in enumerate(keys)}
    mirror = [points_of[(i, j, ORDER - 1 - k)] for i, j, k in keys]
    mats = {o: translation(points, *o) for o in offset_table()}
    half = 3 * n // 2
    rotation = np.zeros((3 * n, 512), ml_dtypes.bfloat16)
    back = np.zeros((512, 3 * n))
    table = np.zeros((2, len(BASES), 256, 256), ml_dtypes.bfloat16)
    signs = np.ones((4, 2, 256, 256), ml_dtypes.bfloat16)
    for s, sign in enumerate((1, -1)):
        pairs = np.zeros((3 * n, half))
        firsts = []
        for a in range(3):
            flip = sign if a < 2 else -sign
            for i in range(n):
                if i < mirror[i]:
                    pairs[a * n + i, len(firsts)] = 1.0
                    pairs[a * n + mirror[i], len(firsts)] = flip
                    firsts.append(a * n + i)
        blocks = {o: 0.25 * pairs.T @ m @ pairs for o, m in mats.items()}
        gram = sum(b.T @ b for b in blocks.values())
        place = {f: i for i, f in enumerate(firsts)}
        modes, parity, weight = [], [], []
        for sx in (1, -1):
            for sy in (1, -1):
                basis = []
                for i, f in enumerate(firsts):
                    a, (kx, ky, kz) = f // n, keys[f % n]
                    if kx < ORDER // 2 and ky < ORDER // 2:
                        v = np.zeros(half)
                        for fx in range(2):
                            for fy in range(2):
                                key = (ORDER - 1 - kx if fx else kx, ORDER - 1 - ky if fy else ky, kz)
                                sign_x = (sx if a != 0 else -sx) if fx else 1
                                sign_y = (sy if a != 1 else -sy) if fy else 1
                                v[place[a * n + points_of[key]]] = 0.5 * sign_x * sign_y
                        basis.append(v)
                basis = np.array(basis).T
                w, vecs = np.linalg.eigh(basis.T @ gram @ basis)
                vecs = basis @ vecs
                vecs = vecs * np.sign(vecs[np.abs(np.round(vecs, 9)).argmax(0), np.arange(len(w))])
                modes.append(vecs)
                weight.append(w)
                parity += [(sx, sy)] * len(w)
        order = np.argsort(-np.concatenate(weight), kind="stable")
        vecs = np.concatenate(modes, axis=1)[:, order]
        parity = np.array(parity)[order]
        modes = (pairs @ vecs / math.sqrt(2.0)).astype(ml_dtypes.bfloat16)
        lows = np.concatenate([modes, modes[:, :KEPT], modes[:, :KEPT]], axis=1)
        rotation[:, 256 * s : 256 * (s + 1)] = lows
        outs, out_parity = [], []
        for sx in (1, -1):
            for sy in (1, -1):
                for f in firsts:
                    a, (kx, ky, kz) = f // n, keys[f % n]
                    if kx < ORDER // 2 and ky < ORDER // 2:
                        v = np.zeros(half)
                        for fx in range(2):
                            for fy in range(2):
                                key = (ORDER - 1 - kx if fx else kx, ORDER - 1 - ky if fy else ky, kz)
                                sign_x = (sx if a != 0 else -sx) if fx else 1
                                sign_y = (sy if a != 1 else -sy) if fy else 1
                                v[place[a * n + points_of[key]]] = sign_x * sign_y
                        outs.append(v)
                        out_parity.append((sx, sy))
        outs = np.array(outs).T
        out_parity = np.array(out_parity)
        back[256 * s : 256 * s + half] = (pairs @ outs).T
        undo = np.linalg.inv(modes[firsts].astype(np.float64))
        for q, o in enumerate(BASES):
            high, low = split(undo @ blocks[o].T @ outs * 0.25)
            table[s, q, :half, :half] = high
            table[s, q, half : half + KEPT, :half] = high[:KEPT]
            table[s, q, half + KEPT : half + 2 * KEPT, :half] = low[:KEPT]
        ins = np.concatenate([parity, parity[:KEPT], parity[:KEPT]], axis=0)
        for f in range(4):
            row = np.ones(256)
            row[: len(ins)] = (ins[:, 0] if f // 2 else 1) * (ins[:, 1] if f % 2 else 1)
            col = np.ones(256)
            col[:half] = (out_parity[:, 0] if f // 2 else 1) * (out_parity[:, 1] if f % 2 else 1)
            signs[f, s] = row[:, None] * col[None, :]
    whole = [
        table[:, BASES.index((abs(a), abs(b)))] * signs[2 * (a < 0) + (b < 0)]
        for part in PARTS
        for a, b in part
    ]
    return rotation, back.astype(ml_dtypes.bfloat16), np.concatenate(whole, axis=1)


@functools.lru_cache(maxsize=None)
def plan():
    offsets = offset_table()
    sequence = [o for part in PARTS for o in part]
    products = []
    for c, d in class_pairs():
        for place, (dx, dy) in enumerate(sequence):
            px, cs = divmod(c + dx, 2)
            py, ds = divmod(d + dy, 2)
            if abs(px) <= 1 and abs(py) <= 1:
                entry = (cs * 3 + px + 1) * 6 + ds * 3 + py + 1
                products.append((offsets.index((dx, dy)), entry, place))
    return products


def class_pairs():
    return [(c, d) for c in range(2) for d in range(2)]


def dot(a, b):
    return lax.dot_general(a, b, (((1,), (0,)), ((), ())), preferred_element_type=F32)


def dot_t(a, b):
    return lax.dot_general(a, b, (((1,), (1,)), ((), ())), preferred_element_type=F32)


def parts(x):
    high = x.astype(BF16)
    return high, (x - high.astype(F32)).astype(BF16)


def times_t(x, weight):
    xh, xl = parts(x)
    wh, wl = weight
    both = dot_t(jnp.concatenate([xh, xl], axis=0), wh)
    return both[: x.shape[0]] + (both[x.shape[0] :] + dot_t(xh, wl))


def times_exact(x, weight):
    both = dot(jnp.concatenate(parts(x), axis=0), weight)
    return both[: x.shape[0]] + both[x.shape[0] :]


def lanes(ref, *at):
    pieces = [ref[(t,) + at] for t in range(4)]
    pieces = [p.reshape(-1, 128) for p in pieces]
    return jnp.concatenate(pieces, axis=1)


def cut_tiles(dens):
    return [(t, slice(128 * t, min(128 * t + 128, dens)), slice(0, min(128, dens - 128 * t))) for t in range(4)]


def modes_of(x, rot_ref, dens):
    y = times_exact(x[:, :dens], rot_ref[...])
    lane = lax.broadcasted_iota(jnp.int32, (1, 512), 1) % 256
    half = dens // 2
    is_low = (lane >= half) & (lane < half + KEPT)
    return jnp.where(is_low, y - y.astype(BF16).astype(F32), y)


def children(ref, dens, counts, c, d):
    return jnp.concatenate(
        [
            jnp.concatenate(
                [ref[t, 2 * i + c, pl.ds(d, counts[1], stride=2), :] for i in range(counts[0])],
                axis=0,
            )
            for t in range(4)
        ],
        axis=1,
    )[:, :dens]


def own_kernel(own_ref, rot_ref, modes_ref, tiled_ref, rot_out):
    rows, cols, dens = own_ref.shape
    rot_out[...] = rot_ref[...]
    y = modes_of(own_ref[...].reshape(rows * cols, dens), rot_ref, dens)
    for t, cut, to in cut_tiles(dens):
        modes_ref[t] = y[:, 128 * t : 128 * t + 128].reshape(rows, cols, 128)
        tiled_ref[t, :, :, to] = own_ref[:, :, cut]


def pass_kernel(
    even_ref, strip0_ref, strip1_ref, own_t, own_modes_ref, rot_ref, up_ref,
    pup_ref, side_ref, pmodes, send0_ref, send1_ref,
    strip_t,
):
    rows, _, dens = strip0_ref.shape
    cols = own_modes_ref.shape[2]
    pr, pc = rows // 2, cols // 2
    boxes = pr * pc
    even_x, even_y = even_ref[0] == 1, even_ref[1] == 1
    for t, cut, to in cut_tiles(dens):
        first, second = strip0_ref[:, :, cut], strip1_ref[:, :, cut]
        strip_t[t, :, 0:HALO, to] = jnp.where(even_y, second, first)
        strip_t[t, :, HALO:, to] = jnp.where(even_y, first, second)

    parent = None
    for n, (c, d) in enumerate(class_pairs()):
        x = jnp.concatenate(
            [children(own_t, dens, (pr, pc), c, d), children(strip_t, dens, (pr, HALO), c, d)],
            axis=0,
        )
        part = times_t(x, parts(up_ref[n]))
        parent = part if parent is None else parent + part
    pup_ref[...] = parent[:boxes].reshape(pr, pc, dens)
    z = modes_of(jnp.concatenate([lanes(strip_t)[:, :dens], parent], axis=0), rot_ref, dens)
    w, p = z[: rows * 8], z[rows * 8 :]
    for t in range(4):
        cut = slice(128 * t, 128 * t + 128)
        side = w[:, cut].reshape(rows, 8, 128)
        side_ref[t] = side
        pmodes[t, 2 : 2 + pr, 4 : 4 + pc, :] = p[:boxes, cut].reshape(pr, pc, 128)
        strip = p[boxes:, cut].reshape(pr, 4, 128)
        pmodes[t, 2 : 2 + pr, 2:4, :] = strip[:, 0:2]
        pmodes[t, 2 : 2 + pr, 4 + pc : 6 + pc, :] = strip[:, 2:4]
        own = p[:boxes, cut].reshape(pr, pc, 128)
        ends = []
        for x, to in ((slice(0, 2), slice(0, 2)), (slice(rows - 2, rows), slice(pr - 2, pr))):
            ends.append(
                jnp.concatenate(
                    [own_modes_ref[t, x], jnp.concatenate([side[x, 2:6], strip[to]], axis=1), own[to]],
                    axis=1,
                )
            )
        low, high = ends
        send0_ref[t] = jnp.where(even_x, high, low)
        send1_ref[t] = jnp.where(even_x, low, high)


def near_kernel(
    own_modes_ref, side_ref, pmodes_ref, llist_ref, plist_ref, lut, masks_ref, edge_ref, modes, flat
):
    rows, cols = own_modes_ref.shape[1:3]
    pr, pc = rows // 2, cols // 2
    gr, gc = pr // 2, pc // 2
    used = pr * pc + gr * gc
    high = lut.shape[2]
    count = masks_ref.shape[0] // 4

    for t in range(4):
        modes[t, 2 : 2 + rows, 8 : 8 + cols, :] = own_modes_ref[t]
        modes[t, 2 : 2 + rows, 4:8, :] = side_ref[t, :, 0:4]
        modes[t, 2 : 2 + rows, 8 + cols : 12 + cols, :] = side_ref[t, :, 4:8]
        edge_ref[t, 0:2] = modes[t, 2:4]
        edge_ref[t, 2:4] = modes[t, rows : rows + 2]

    def gather(i, carry):
        base = 2 * (i % 3) + i // 3
        for ds in range(2):
            for py in (-1, 0, 1):
                e = i * 6 + ds * 3 + py + 1
                for t in range(4):
                    x = jnp.concatenate(
                        [
                            modes[t, base + 2 * j, pl.ds(8 + 2 * py + ds, pc, stride=2), :]
                            for j in range(pr)
                        ]
                        + [
                            pmodes_ref[t, base + 2 * j, pl.ds(4 + 2 * py + ds, gc, stride=2), :]
                            for j in range(gr)
                        ]
                        + [jnp.zeros((high - used, 128), F32)],
                        axis=0,
                    )
                    lut[e, t // 2, :, 128 * (t % 2) : 128 * (t % 2) + 128] = x.astype(BF16)
        return carry

    lax.fori_loop(0, 6, gather, 0)

    flat[0, :, :, 0 : llist_ref.shape[2]] = llist_ref[...].astype(F32)
    flat[1, 0:pr, 0:pc, 0 : plist_ref.shape[2]] = plist_ref[...].astype(F32)
    for n, (c, d) in enumerate(class_pairs()):
        flag = jnp.concatenate(
            [flat[0, 2 * i + c, pl.ds(d, pc, stride=2), :] for i in range(pr)]
            + [flat[1, 2 * i + c, pl.ds(d, gc, stride=2), :] for i in range(gr)]
            + [jnp.zeros((high - used, 128), F32)],
            axis=0,
        )
        for k in range(count):
            o = plan()[count * n + k][0]
            masks_ref[count * n + k] = jnp.broadcast_to(flag[:, o : o + 1], (high, 128)).astype(BF16)


def close_kernel(
    even_ref,
    got0_ref, got1_ref, edge_ref, pside_ref, masks, lut,
    pin_ref, back, table, down_ref, inv_ref,
    out_ref,
    edge, pmodes, fresh, acc, flat, plocal,
):
    rows, cols, dens = out_ref.shape
    pr, pc = rows // 2, cols // 2
    gr, gc = pr // 2, pc // 2
    boxes, pboxes = pr * pc, gr * gc
    high = lut.shape[2]
    count = masks.shape[0] // 4
    even = even_ref[0] == 1
    for t in range(4):
        before = jnp.where(even, got1_ref[t], got0_ref[t])
        after = jnp.where(even, got0_ref[t], got1_ref[t])
        edge[t, 2:6] = edge_ref[t]
        pmodes[t, 2 : 2 + pr] = pside_ref[t, 2 : 2 + pr]
        for x, leaf, parent in ((before, slice(0, 2), slice(0, 2)), (after, slice(6, 8), slice(2 + pr, 4 + pr))):
            edge[t, leaf, 8 : 8 + cols, :] = x[:, 0:cols]
            edge[t, leaf, 6:8, :] = x[:, cols : cols + 2]
            edge[t, leaf, 8 + cols : 10 + cols, :] = x[:, cols + 2 : cols + 4]
            pmodes[t, parent, 2:4, :] = x[:, cols + 4 : cols + 6]
            pmodes[t, parent, 4 + pc : 6 + pc, :] = x[:, cols + 6 : cols + 8]
            pmodes[t, parent, 4 : 4 + pc, :] = x[:, cols + 8 :]

    def patch(cs, carry):
        for ds in range(2):
            for py in (-1, 0, 1):
                for t in range(4):
                    at = slice(128 * (t % 2), 128 * (t % 2) + 128)
                    mine = pl.ds(8 + 2 * py + ds, pc, stride=2)
                    theirs = pl.ds(4 + 2 * py + ds, gc, stride=2)
                    e = cs * 6 + ds * 3 + py + 1
                    x = jnp.concatenate([edge[t, cs + 2 * j, mine, :] for j in range(2)], axis=0)
                    fresh[0, e, t // 2, 0:16, at] = x.astype(BF16)
                    x = jnp.concatenate([pmodes[t, cs + 2 * j, theirs, :] for j in range(4)], axis=0)
                    fresh[0, e, t // 2, 16:32, at] = x.astype(BF16)
                    x = jnp.concatenate([edge[t, 4 + cs + 2 * j, mine, :] for j in range(2)], axis=0)
                    fresh[1, e, t // 2, 0:16, at] = x.astype(BF16)
                    x = jnp.concatenate(
                        [pmodes[t, 4 + cs + 2 * j, theirs, :] for j in range(4, gr)]
                        + [jnp.zeros((high - boxes - pboxes, 128), F32)],
                        axis=0,
                    )
                    fresh[1, e, t // 2, 16:32, at] = x.astype(BF16)
        return carry

    lax.fori_loop(0, 2, patch, 0)

    runs = [(0, 3), (3, 6), (6, 11), (11, 16), (16, 21)]

    def listed(i, s):
        e = plan()[i][1]
        px = e // 6 % 3 - 1
        m = masks[i]
        if px == 0:
            x = lut[e, s]
        else:
            new = fresh[(px + 1) // 2, e // 18 * 6 + e % 6, s]
            if px < 0:
                pieces = [new[0:16], lut[e, s, 16:boxes], new[16:32], lut[e, s, boxes + 16 : high]]
            else:
                pieces = [lut[e, s, 0 : boxes - 16], new[0:16], lut[e, s, boxes : boxes + 16], new[16:32]]
            x = jnp.concatenate(pieces, axis=0)
        return jnp.concatenate([x[:, :128] * m, x[:, 128:] * m], axis=1)

    for c in range(2):

        def interact(s, carry):
            n = 2 * c
            total = jnp.zeros((2 * high, 256), F32)

            def run(first, last, s):
                at = 256 * plan()[first][2]
                x = jnp.concatenate([listed(i, s) for i in range(first, last)], axis=1)
                return x, table[s, at : at + 256 * (last - first), :]

            for a, b in runs:
                x, weight = run(n * count + a, n * count + b, s)
                y, _ = run((n + 1) * count + a, (n + 1) * count + b, s)
                total = total + dot(jnp.concatenate([x, y], axis=0), weight)
            for d in range(2):
                x, weight = run((n + d) * count + runs[-1][1], (n + d + 1) * count, s)
                acc[s, n + d] = total[high * d : high * (d + 1)] + dot(x, weight)
            return carry

        lax.fori_loop(0, 2, interact, 0)

    def densities(rows):
        pieces = [
            times_exact(
                jnp.concatenate([acc[s, n, rows] for n in range(4)], axis=0),
                back[256 * s : 256 * (s + 1)],
            )
            for s in range(2)
        ]
        return pieces[0] + pieces[1]

    pcheck = densities(slice(boxes, high))
    check = densities(slice(0, boxes))

    inverse = parts(inv_ref[...])
    for n, (c, d) in enumerate(class_pairs()):
        for t, cut, to in cut_tiles(dens):
            for j in range(gr):
                r = (high - boxes) * n + gc * j
                plocal[t, 2 * j + c, pl.ds(d, gc, stride=2), to] = pcheck[r : r + gc, cut]
    local = pin_ref[...].reshape(boxes, dens) + times_t(lanes(plocal)[:, :dens], inverse)
    x = jnp.concatenate(
        [
            check[boxes * n : boxes * (n + 1)] + times_t(local, parts(down_ref[n]))
            for n in range(4)
        ],
        axis=0,
    )
    result = times_t(x, inverse)
    for n, (c, d) in enumerate(class_pairs()):
        for t, cut, to in cut_tiles(dens):
            for j in range(pr):
                r = boxes * n + pc * j
                flat[t, 2 * j + c, pl.ds(d, pc, stride=2), to] = result[r : r + pc, cut]
    for t, cut, to in cut_tiles(dens):
        out_ref[:, :, cut] = flat[t, :, :, to]


VMEM = pl.BlockSpec(memory_space=pltpu.VMEM)
SMEM = pl.BlockSpec(memory_space=pltpu.SMEM)


def params(mib):
    return pltpu.CompilerParams(vmem_limit_bytes=mib * 1024 * 1024)


def cost(rows, tiles, reads):
    return pl.CostEstimate(flops=2 * rows * tiles * 256 * 256, bytes_accessed=reads, transcendentals=0)


def height(boxes):
    return -(-(boxes * 5 // 4) // 16) * 16


def own_step(own, rotation):
    rows, cols, _ = own.shape
    tiled = jax.ShapeDtypeStruct((4, rows, cols, 128), F32)
    return pl.pallas_call(
        own_kernel,
        out_shape=(tiled, tiled, jax.ShapeDtypeStruct(rotation.shape, BF16)),
        in_specs=[VMEM] * 2,
        out_specs=(VMEM,) * 3,
        compiler_params=params(16),
        cost_estimate=cost(rows * cols, 48, 64 * 1024 * 1024),
    )(own, rotation)


def pass_step(even, strips, tiled, own_modes, rotation, up):
    rows, cols = tiled.shape[1:3]
    dens = up.shape[1]
    pr, pc = rows // 2, cols // 2
    send = jax.ShapeDtypeStruct((4, 2, cols + pc + 8, 128), F32)
    return pl.pallas_call(
        pass_kernel,
        out_shape=(
            jax.ShapeDtypeStruct((pr, pc, dens), F32),
            jax.ShapeDtypeStruct((4, rows, 2 * HALO, 128), F32),
            jax.ShapeDtypeStruct((4, pr + 4, pc + 8, 128), F32),
            send,
            send,
        ),
        in_specs=[SMEM] + [VMEM] * 6,
        out_specs=(VMEM,) * 5,
        scratch_shapes=[pltpu.VMEM((4, rows, 2 * HALO, 128), F32)],
        compiler_params=params(16),
        cost_estimate=cost(rows * cols, 32, up.size * 4),
    )(even, *strips, tiled, own_modes, rotation, up)


def near_step(own_modes, side, pmodes, llist, plist):
    rows, cols, _ = llist.shape
    high = height(rows * cols // 4)
    return pl.pallas_call(
        near_kernel,
        out_shape=(
            jax.ShapeDtypeStruct((36, 2, high, 256), BF16),
            jax.ShapeDtypeStruct((len(plan()), high, 128), BF16),
            jax.ShapeDtypeStruct((4, 4, cols + 16, 128), F32),
        ),
        in_specs=[VMEM] * 5,
        out_specs=(VMEM,) * 3,
        scratch_shapes=[
            pltpu.VMEM((4, rows + 4, cols + 16, 128), F32),
            pltpu.VMEM((2, rows, cols, 128), F32),
        ],
        compiler_params=params(16),
        cost_estimate=cost(rows * cols, 48, 16 * 1024 * 1024),
    )(own_modes, side, pmodes, llist, plist)


def close_step(even, ends, edge, pmodes, masks, lut, pin, back, table, down, inv, shape):
    rows, cols, dens = shape
    pr, pc = rows // 2, cols // 2
    high = height(pr * pc)
    return pl.pallas_call(
        close_kernel,
        out_shape=jax.ShapeDtypeStruct(shape, F32),
        in_specs=[SMEM] + [VMEM] * 11,
        out_specs=VMEM,
        scratch_shapes=[
            pltpu.VMEM((4, 8, cols + 16, 128), F32),
            pltpu.VMEM((4, pr + 4, pc + 8, 128), F32),
            pltpu.VMEM((2, 12, 2, 32, 256), BF16),
            pltpu.VMEM((2, 4, high, 256), F32),
            pltpu.VMEM((4, rows, cols, 128), F32),
            pltpu.VMEM((4, pr, pc, 128), F32),
        ],
        compiler_params=params(24),
        cost_estimate=cost(rows * cols, 150, table.size * 2),
    )(
        even, *ends, edge, pmodes, masks, lut, pin, back, table, down, inv,
    )


def swapped(strips, axis, odd_first):
    peers = lax.axis_size(axis)
    got = [None, None]
    for kind in (1, 0) if odd_first else (0, 1):
        pairs = [(i, i + 1) for i in range(kind, peers - 1, 2)]
        got[kind] = lax.ppermute(strips[kind], axis, pairs + [(j, i) for i, j in pairs])
    return got


def local(leaf_up, parent_in, leaf_lists, parent_lists, up_transfer, down_transfer, check_inverse):
    cols = leaf_up.shape[1]
    even = [lax.axis_index(axis) % 2 == 0 for axis in ("gx", "gy")]
    flag = jnp.stack(even).astype(jnp.int32)
    rotation, back, table = (jnp.asarray(x) for x in operators())
    low, high = leaf_up[:, :HALO], leaf_up[:, cols - HALO :]
    strips = (jnp.where(even[1], high, low), jnp.where(even[1], low, high))
    strips = swapped(strips, "gy", True)
    own_modes, tiled, rotation = own_step(leaf_up, rotation)
    parent_up, side, pmodes, *sends = pass_step(flag, strips, tiled, own_modes, rotation, up_transfer)
    ends = swapped(sends, "gx", False)
    lut, masks, edge = near_step(own_modes, side, pmodes, leaf_lists, parent_lists)
    leaf_down = close_step(
        flag, ends, edge, pmodes, masks, lut, parent_in, back, table,
        down_transfer, check_inverse, leaf_up.shape,
    )
    return leaf_down, parent_up


def solution(mesh):
    block = P("gx", "gy", None)
    return jax.shard_map(
        local,
        mesh=mesh,
        in_specs=(block,) * 4 + (P(),) * 3,
        out_specs=(block, block),
        check_vma=False,
    )
```

```python
import functools
import math

import jax
import jax.numpy as jnp
import ml_dtypes
import numpy as np
from jax import lax
from jax.experimental import pallas as pl
from jax.experimental.pallas import tpu as pltpu
from jax.sharding import PartitionSpec as P

ORDER = 6
HALO = 4
KEPT = 14
BF16, F32 = jnp.bfloat16, jnp.float32

PARTS = (
    [(a, -2) for a in range(-1, 2)],
    [(a, 2) for a in range(-1, 2)],
    [(-2, b) for b in range(-2, 3)],
    [(2, b) for b in range(-2, 3)],
    [(3, b) for b in range(-2, 3)],
    [(-3, b) for b in range(-2, 3)],
    [(a, 3) for a in range(-3, 4)],
    [(a, -3) for a in range(-3, 4)],
)


def offset_table():
    return [(a, b) for a in range(-3, 4) for b in range(-3, 4) if max(abs(a), abs(b)) >= 2]


BASES = sorted({(abs(a), abs(b)) for a, b in offset_table()})


def surface_points():
    grid = np.linspace(-1.0, 1.0, ORDER)
    keys = [
        (i, j, k)
        for i in range(ORDER)
        for j in range(ORDER)
        for k in range(ORDER)
        if min(i, j, k) == 0 or max(i, j, k) == ORDER - 1
    ]
    return keys, np.array([[grid[i] for i in key] for key in keys])


def translation(points, dx, dy):
    r = 0.525 * (points[:, None, :] - points[None, :, :]) - np.array([dx, dy, 0.0])
    dist = np.sqrt((r * r).sum(-1))
    n = len(points)
    out = np.zeros((3, n, 3, n))
    for a in range(3):
        for b in range(3):
            out[a, :, b, :] = (float(a == b) / dist + r[..., a] * r[..., b] / dist**3) / (8 * math.pi)
    return out.reshape(3 * n, 3 * n)


def split(x):
    high = x.astype(ml_dtypes.bfloat16)
    return high, (x - high.astype(np.float64)).astype(ml_dtypes.bfloat16)


@functools.lru_cache(maxsize=None)
def operators():
    keys, points = surface_points()
    n = len(keys)
    points_of = {key: i for i, key in enumerate(keys)}
    mirror = [points_of[(i, j, ORDER - 1 - k)] for i, j, k in keys]
    mats = {o: translation(points, *o) for o in offset_table()}
    half = 3 * n // 2
    rotation = np.zeros((3 * n, 512), ml_dtypes.bfloat16)
    back = np.zeros((512, 3 * n))
    table = np.zeros((2, len(BASES), 256, 256), ml_dtypes.bfloat16)
    signs = np.ones((4, 2, 256, 256), ml_dtypes.bfloat16)
    for s, sign in enumerate((1, -1)):
        pairs = np.zeros((3 * n, half))
        firsts = []
        for a in range(3):
            flip = sign if a < 2 else -sign
            for i in range(n):
                if i < mirror[i]:
                    pairs[a * n + i, len(firsts)] = 1.0
                    pairs[a * n + mirror[i], len(firsts)] = flip
                    firsts.append(a * n + i)
        blocks = {o: 0.25 * pairs.T @ m @ pairs for o, m in mats.items()}
        gram = sum(b.T @ b for b in blocks.values())
        place = {f: i for i, f in enumerate(firsts)}
        modes, parity, weight = [], [], []
        for sx in (1, -1):
            for sy in (1, -1):
                basis = []
                for i, f in enumerate(firsts):
                    a, (kx, ky, kz) = f // n, keys[f % n]
                    if kx < ORDER // 2 and ky < ORDER // 2:
                        v = np.zeros(half)
                        for fx in range(2):
                            for fy in range(2):
                                key = (ORDER - 1 - kx if fx else kx, ORDER - 1 - ky if fy else ky, kz)
                                sign_x = (sx if a != 0 else -sx) if fx else 1
                                sign_y = (sy if a != 1 else -sy) if fy else 1
                                v[place[a * n + points_of[key]]] = 0.5 * sign_x * sign_y
                        basis.append(v)
                basis = np.array(basis).T
                w, vecs = np.linalg.eigh(basis.T @ gram @ basis)
                vecs = basis @ vecs
                vecs = vecs * np.sign(vecs[np.abs(np.round(vecs, 9)).argmax(0), np.arange(len(w))])
                modes.append(vecs)
                weight.append(w)
                parity += [(sx, sy)] * len(w)
        order = np.argsort(-np.concatenate(weight), kind="stable")
        vecs = np.concatenate(modes, axis=1)[:, order]
        parity = np.array(parity)[order]
        modes = (pairs @ vecs / math.sqrt(2.0)).astype(ml_dtypes.bfloat16)
        lows = np.concatenate([modes, modes[:, :KEPT], modes[:, :KEPT]], axis=1)
        rotation[:, 256 * s : 256 * (s + 1)] = lows
        outs, out_parity = [], []
        for sx in (1, -1):
            for sy in (1, -1):
                for f in firsts:
                    a, (kx, ky, kz) = f // n, keys[f % n]
                    if kx < ORDER // 2 and ky < ORDER // 2:
                        v = np.zeros(half)
                        for fx in range(2):
                            for fy in range(2):
                                key = (ORDER - 1 - kx if fx else kx, ORDER - 1 - ky if fy else ky, kz)
                                sign_x = (sx if a != 0 else -sx) if fx else 1
                                sign_y = (sy if a != 1 else -sy) if fy else 1
                                v[place[a * n + points_of[key]]] = sign_x * sign_y
                        outs.append(v)
                        out_parity.append((sx, sy))
        outs = np.array(outs).T
        out_parity = np.array(out_parity)
        back[256 * s : 256 * s + half] = (pairs @ outs).T
        undo = np.linalg.inv(modes[firsts].astype(np.float64))
        for q, o in enumerate(BASES):
            high, low = split(undo @ blocks[o].T @ outs * 0.25)
            table[s, q, :half, :half] = high
            table[s, q, half : half + KEPT, :half] = high[:KEPT]
            table[s, q, half + KEPT : half + 2 * KEPT, :half] = low[:KEPT]
        ins = np.concatenate([parity, parity[:KEPT], parity[:KEPT]], axis=0)
        for f in range(4):
            row = np.ones(256)
            row[: len(ins)] = (ins[:, 0] if f // 2 else 1) * (ins[:, 1] if f % 2 else 1)
            col = np.ones(256)
            col[:half] = (out_parity[:, 0] if f // 2 else 1) * (out_parity[:, 1] if f % 2 else 1)
            signs[f, s] = row[:, None] * col[None, :]
    whole = [
        table[:, BASES.index((abs(a), abs(b)))] * signs[2 * (a < 0) + (b < 0)]
        for part in PARTS
        for a, b in part
    ]
    return rotation, back.astype(ml_dtypes.bfloat16), np.concatenate(whole, axis=1)


@functools.lru_cache(maxsize=None)
def plan():
    offsets = offset_table()
    sequence = [o for part in PARTS for o in part]
    products = []
    for c, d in class_pairs():
        for place, (dx, dy) in enumerate(sequence):
            px, cs = divmod(c + dx, 2)
            py, ds = divmod(d + dy, 2)
            if abs(px) <= 1 and abs(py) <= 1:
                entry = (cs * 3 + px + 1) * 6 + ds * 3 + py + 1
                products.append((offsets.index((dx, dy)), entry, place))
    return products


def class_pairs():
    return [(c, d) for c in range(2) for d in range(2)]


def dot(a, b):
    return lax.dot_general(a, b, (((1,), (0,)), ((), ())), preferred_element_type=F32)


def dot_t(a, b):
    return lax.dot_general(a, b, (((1,), (1,)), ((), ())), preferred_element_type=F32)


def parts(x):
    high = x.astype(BF16)
    return high, (x - high.astype(F32)).astype(BF16)


def times_t(x, weight):
    xh, xl = parts(x)
    wh, wl = weight
    both = dot_t(jnp.concatenate([xh, xl], axis=0), wh)
    return both[: x.shape[0]] + (both[x.shape[0] :] + dot_t(xh, wl))


def times_exact(x, weight):
    both = dot(jnp.concatenate(parts(x), axis=0), weight)
    return both[: x.shape[0]] + both[x.shape[0] :]


def lanes(ref, *at):
    pieces = [ref[(t,) + at] for t in range(4)]
    pieces = [p.reshape(-1, 128) for p in pieces]
    return jnp.concatenate(pieces, axis=1)


def cut_tiles(dens):
    return [(t, slice(128 * t, min(128 * t + 128, dens)), slice(0, min(128, dens - 128 * t))) for t in range(4)]


def modes_of(x, rot_ref, dens):
    y = times_exact(x[:, :dens], rot_ref[...])
    lane = lax.broadcasted_iota(jnp.int32, (1, 512), 1) % 256
    half = dens // 2
    is_low = (lane >= half) & (lane < half + KEPT)
    return jnp.where(is_low, y - y.astype(BF16).astype(F32), y)


def children(ref, dens, counts, c, d):
    return jnp.concatenate(
        [
            jnp.concatenate(
                [ref[t, 2 * i + c, pl.ds(d, counts[1], stride=2), :] for i in range(counts[0])],
                axis=0,
            )
            for t in range(4)
        ],
        axis=1,
    )[:, :dens]


def own_kernel(own_ref, rot_ref, modes_ref, tiled_ref, rot_out):
    rows, cols, dens = own_ref.shape
    rot_out[...] = rot_ref[...]
    y = modes_of(own_ref[...].reshape(rows * cols, dens), rot_ref, dens)
    for t, cut, to in cut_tiles(dens):
        modes_ref[t] = y[:, 128 * t : 128 * t + 128].reshape(rows, cols, 128)
        tiled_ref[t, :, :, to] = own_ref[:, :, cut]


def pass_kernel(
    even_ref, strip0_ref, strip1_ref, own_t, own_modes_ref, rot_ref, up_ref,
    parents_ref, side_ref, pmodes, send0_ref, send1_ref,
    strip_t,
):
    rows, _, dens = strip0_ref.shape
    cols = own_modes_ref.shape[2]
    pr, pc = rows // 2, cols // 2
    boxes = pr * pc
    even_x, even_y = even_ref[0] == 1, even_ref[1] == 1
    for t, cut, to in cut_tiles(dens):
        first, second = strip0_ref[:, :, cut], strip1_ref[:, :, cut]
        strip_t[t, :, 0:HALO, to] = jnp.where(even_y, second, first)
        strip_t[t, :, HALO:, to] = jnp.where(even_y, first, second)

    parent = None
    for n, (c, d) in enumerate(class_pairs()):
        x = jnp.concatenate(
            [children(own_t, dens, (pr, pc), c, d), children(strip_t, dens, (pr, HALO), c, d)],
            axis=0,
        )
        part = times_t(x, parts(up_ref[n]))
        parent = part if parent is None else parent + part
    parents_ref[...] = parent[:boxes].reshape(pr, pc, dens)
    z = modes_of(jnp.concatenate([lanes(strip_t)[:, :dens], parent], axis=0), rot_ref, dens)
    w, p = z[: rows * 8], z[rows * 8 :]
    for t in range(4):
        cut = slice(128 * t, 128 * t + 128)
        side = w[:, cut].reshape(rows, 8, 128)
        side_ref[t] = side
        pmodes[t, 2 : 2 + pr, 4 : 4 + pc, :] = p[:boxes, cut].reshape(pr, pc, 128)
        strip = p[boxes:, cut].reshape(pr, 4, 128)
        pmodes[t, 2 : 2 + pr, 2:4, :] = strip[:, 0:2]
        pmodes[t, 2 : 2 + pr, 4 + pc : 6 + pc, :] = strip[:, 2:4]
        own = p[:boxes, cut].reshape(pr, pc, 128)
        ends = []
        for x, to in ((slice(0, 2), slice(0, 2)), (slice(rows - 2, rows), slice(pr - 2, pr))):
            ends.append(
                jnp.concatenate(
                    [own_modes_ref[t, x], jnp.concatenate([side[x, 2:6], strip[to]], axis=1), own[to]],
                    axis=1,
                )
            )
        low, high = ends
        send0_ref[t] = jnp.where(even_x, high, low)
        send1_ref[t] = jnp.where(even_x, low, high)


def near_kernel(
    own_modes_ref, side_ref, pmodes_ref, parents_ref, llist_ref, plist_ref,
    pup_ref, lut, masks_ref, edge_ref,
    modes, flat,
):
    rows, cols = own_modes_ref.shape[1:3]
    pup_ref[...] = parents_ref[...]
    pr, pc = rows // 2, cols // 2
    gr, gc = pr // 2, pc // 2
    used = pr * pc + gr * gc
    high = lut.shape[2]
    count = masks_ref.shape[0] // 4

    for t in range(4):
        modes[t, 2 : 2 + rows, 8 : 8 + cols, :] = own_modes_ref[t]
        modes[t, 2 : 2 + rows, 4:8, :] = side_ref[t, :, 0:4]
        modes[t, 2 : 2 + rows, 8 + cols : 12 + cols, :] = side_ref[t, :, 4:8]
        edge_ref[t, 0:2] = modes[t, 2:4]
        edge_ref[t, 2:4] = modes[t, rows : rows + 2]

    def gather(i, carry):
        base = 2 * (i % 3) + i // 3
        for ds in range(2):
            for py in (-1, 0, 1):
                e = i * 6 + ds * 3 + py + 1
                for t in range(4):
                    x = jnp.concatenate(
                        [
                            modes[t, base + 2 * j, pl.ds(8 + 2 * py + ds, pc, stride=2), :]
                            for j in range(pr)
                        ]
                        + [
                            pmodes_ref[t, base + 2 * j, pl.ds(4 + 2 * py + ds, gc, stride=2), :]
                            for j in range(gr)
                        ]
                        + [jnp.zeros((high - used, 128), F32)],
                        axis=0,
                    )
                    lut[e, t // 2, :, 128 * (t % 2) : 128 * (t % 2) + 128] = x.astype(BF16)
        return carry

    lax.fori_loop(0, 6, gather, 0)

    flat[0, :, :, 0 : llist_ref.shape[2]] = llist_ref[...].astype(F32)
    flat[1, 0:pr, 0:pc, 0 : plist_ref.shape[2]] = plist_ref[...].astype(F32)
    for n, (c, d) in enumerate(class_pairs()):
        flag = jnp.concatenate(
            [flat[0, 2 * i + c, pl.ds(d, pc, stride=2), :] for i in range(pr)]
            + [flat[1, 2 * i + c, pl.ds(d, gc, stride=2), :] for i in range(gr)]
            + [jnp.zeros((high - used, 128), F32)],
            axis=0,
        )
        for k in range(count):
            o = plan()[count * n + k][0]
            masks_ref[count * n + k] = jnp.broadcast_to(flag[:, o : o + 1], (high, 128)).astype(BF16)


def close_kernel(
    even_ref,
    got0_ref, got1_ref, edge_ref, pside_ref, masks, lut,
    pin_ref, back, table, down_ref, inv_ref,
    out_ref,
    edge, pmodes, fresh, acc, flat, plocal,
):
    rows, cols, dens = out_ref.shape
    pr, pc = rows // 2, cols // 2
    gr, gc = pr // 2, pc // 2
    boxes, pboxes = pr * pc, gr * gc
    high = lut.shape[2]
    count = masks.shape[0] // 4
    even = even_ref[0] == 1
    for t in range(4):
        before = jnp.where(even, got1_ref[t], got0_ref[t])
        after = jnp.where(even, got0_ref[t], got1_ref[t])
        edge[t, 2:6] = edge_ref[t]
        pmodes[t, 2 : 2 + pr] = pside_ref[t, 2 : 2 + pr]
        for x, leaf, parent in ((before, slice(0, 2), slice(0, 2)), (after, slice(6, 8), slice(2 + pr, 4 + pr))):
            edge[t, leaf, 8 : 8 + cols, :] = x[:, 0:cols]
            edge[t, leaf, 6:8, :] = x[:, cols : cols + 2]
            edge[t, leaf, 8 + cols : 10 + cols, :] = x[:, cols + 2 : cols + 4]
            pmodes[t, parent, 2:4, :] = x[:, cols + 4 : cols + 6]
            pmodes[t, parent, 4 + pc : 6 + pc, :] = x[:, cols + 6 : cols + 8]
            pmodes[t, parent, 4 : 4 + pc, :] = x[:, cols + 8 :]

    def patch(cs, carry):
        for ds in range(2):
            for py in (-1, 0, 1):
                for t in range(4):
                    at = slice(128 * (t % 2), 128 * (t % 2) + 128)
                    mine = pl.ds(8 + 2 * py + ds, pc, stride=2)
                    theirs = pl.ds(4 + 2 * py + ds, gc, stride=2)
                    e = cs * 6 + ds * 3 + py + 1
                    x = jnp.concatenate([edge[t, cs + 2 * j, mine, :] for j in range(2)], axis=0)
                    fresh[0, e, t // 2, 0:16, at] = x.astype(BF16)
                    x = jnp.concatenate([pmodes[t, cs + 2 * j, theirs, :] for j in range(4)], axis=0)
                    fresh[0, e, t // 2, 16:32, at] = x.astype(BF16)
                    x = jnp.concatenate([edge[t, 4 + cs + 2 * j, mine, :] for j in range(2)], axis=0)
                    fresh[1, e, t // 2, 0:16, at] = x.astype(BF16)
                    x = jnp.concatenate(
                        [pmodes[t, 4 + cs + 2 * j, theirs, :] for j in range(4, gr)]
                        + [jnp.zeros((high - boxes - pboxes, 128), F32)],
                        axis=0,
                    )
                    fresh[1, e, t // 2, 16:32, at] = x.astype(BF16)
        return carry

    lax.fori_loop(0, 2, patch, 0)

    runs = [(0, 3), (3, 6), (6, 11), (11, 16), (16, 21)]

    def listed(i, s):
        e = plan()[i][1]
        px = e // 6 % 3 - 1
        m = masks[i]
        if px == 0:
            x = lut[e, s]
        else:
            new = fresh[(px + 1) // 2, e // 18 * 6 + e % 6, s]
            if px < 0:
                pieces = [new[0:16], lut[e, s, 16:boxes], new[16:32], lut[e, s, boxes + 16 : high]]
            else:
                pieces = [lut[e, s, 0 : boxes - 16], new[0:16], lut[e, s, boxes : boxes + 16], new[16:32]]
            x = jnp.concatenate(pieces, axis=0)
        return jnp.concatenate([x[:, :128] * m, x[:, 128:] * m], axis=1)

    for c in range(2):

        def interact(s, carry):
            n = 2 * c
            total = jnp.zeros((2 * high, 256), F32)

            def run(first, last, s):
                at = 256 * plan()[first][2]
                x = jnp.concatenate([listed(i, s) for i in range(first, last)], axis=1)
                return x, table[s, at : at + 256 * (last - first), :]

            for a, b in runs:
                x, weight = run(n * count + a, n * count + b, s)
                y, _ = run((n + 1) * count + a, (n + 1) * count + b, s)
                total = total + dot(jnp.concatenate([x, y], axis=0), weight)
            for d in range(2):
                x, weight = run((n + d) * count + runs[-1][1], (n + d + 1) * count, s)
                acc[s, n + d] = total[high * d : high * (d + 1)] + dot(x, weight)
            return carry

        lax.fori_loop(0, 2, interact, 0)

    def densities(rows):
        pieces = [
            times_exact(
                jnp.concatenate([acc[s, n, rows] for n in range(4)], axis=0),
                back[256 * s : 256 * (s + 1)],
            )
            for s in range(2)
        ]
        return pieces[0] + pieces[1]

    pcheck = densities(slice(boxes, high))
    check = densities(slice(0, boxes))

    inverse = parts(inv_ref[...])
    for n, (c, d) in enumerate(class_pairs()):
        for t, cut, to in cut_tiles(dens):
            for j in range(gr):
                r = (high - boxes) * n + gc * j
                plocal[t, 2 * j + c, pl.ds(d, gc, stride=2), to] = pcheck[r : r + gc, cut]
    local = pin_ref[...].reshape(boxes, dens) + times_t(lanes(plocal)[:, :dens], inverse)
    x = jnp.concatenate(
        [
            check[boxes * n : boxes * (n + 1)] + times_t(local, parts(down_ref[n]))
            for n in range(4)
        ],
        axis=0,
    )
    result = times_t(x, inverse)
    for n, (c, d) in enumerate(class_pairs()):
        for t, cut, to in cut_tiles(dens):
            for j in range(pr):
                r = boxes * n + pc * j
                flat[t, 2 * j + c, pl.ds(d, pc, stride=2), to] = result[r : r + pc, cut]
    for t, cut, to in cut_tiles(dens):
        out_ref[:, :, cut] = flat[t, :, :, to]


VMEM = pl.BlockSpec(memory_space=pltpu.VMEM)
SMEM = pl.BlockSpec(memory_space=pltpu.SMEM)


def params(mib):
    return pltpu.CompilerParams(vmem_limit_bytes=mib * 1024 * 1024)


def cost(rows, tiles, reads):
    return pl.CostEstimate(flops=2 * rows * tiles * 256 * 256, bytes_accessed=reads, transcendentals=0)


def height(boxes):
    return -(-(boxes * 5 // 4) // 16) * 16


def own_step(own, rotation):
    rows, cols, _ = own.shape
    tiled = jax.ShapeDtypeStruct((4, rows, cols, 128), F32)
    return pl.pallas_call(
        own_kernel,
        out_shape=(tiled, tiled, jax.ShapeDtypeStruct(rotation.shape, BF16)),
        in_specs=[VMEM] * 2,
        out_specs=(VMEM,) * 3,
        compiler_params=params(16),
        cost_estimate=cost(rows * cols, 48, 64 * 1024 * 1024),
    )(own, rotation)


def pass_step(even, strips, tiled, own_modes, rotation, up):
    rows, cols = tiled.shape[1:3]
    dens = up.shape[1]
    pr, pc = rows // 2, cols // 2
    send = jax.ShapeDtypeStruct((4, 2, cols + pc + 8, 128), F32)
    return pl.pallas_call(
        pass_kernel,
        out_shape=(
            jax.ShapeDtypeStruct((pr, pc, dens), F32),
            jax.ShapeDtypeStruct((4, rows, 2 * HALO, 128), F32),
            jax.ShapeDtypeStruct((4, pr + 4, pc + 8, 128), F32),
            send,
            send,
        ),
        in_specs=[SMEM] + [VMEM] * 6,
        out_specs=(VMEM,) * 5,
        scratch_shapes=[pltpu.VMEM((4, rows, 2 * HALO, 128), F32)],
        compiler_params=params(16),
        cost_estimate=cost(rows * cols, 32, up.size * 4),
    )(even, *strips, tiled, own_modes, rotation, up)


def near_step(own_modes, side, pmodes, parents, llist, plist):
    rows, cols, _ = llist.shape
    high = height(rows * cols // 4)
    return pl.pallas_call(
        near_kernel,
        out_shape=(
            jax.ShapeDtypeStruct(parents.shape, F32),
            jax.ShapeDtypeStruct((36, 2, high, 256), BF16),
            jax.ShapeDtypeStruct((len(plan()), high, 128), BF16),
            jax.ShapeDtypeStruct((4, 4, cols + 16, 128), F32),
        ),
        in_specs=[VMEM] * 6,
        out_specs=(VMEM,) * 4,
        scratch_shapes=[
            pltpu.VMEM((4, rows + 4, cols + 16, 128), F32),
            pltpu.VMEM((2, rows, cols, 128), F32),
        ],
        compiler_params=params(16),
        cost_estimate=cost(rows * cols, 48, 16 * 1024 * 1024),
    )(own_modes, side, pmodes, parents, llist, plist)


def close_step(even, ends, edge, pmodes, masks, lut, pin, back, table, down, inv, shape):
    rows, cols, dens = shape
    pr, pc = rows // 2, cols // 2
    high = height(pr * pc)
    return pl.pallas_call(
        close_kernel,
        out_shape=jax.ShapeDtypeStruct(shape, F32),
        in_specs=[SMEM] + [VMEM] * 11,
        out_specs=VMEM,
        scratch_shapes=[
            pltpu.VMEM((4, 8, cols + 16, 128), F32),
            pltpu.VMEM((4, pr + 4, pc + 8, 128), F32),
            pltpu.VMEM((2, 12, 2, 32, 256), BF16),
            pltpu.VMEM((2, 4, high, 256), F32),
            pltpu.VMEM((4, rows, cols, 128), F32),
            pltpu.VMEM((4, pr, pc, 128), F32),
        ],
        compiler_params=params(24),
        cost_estimate=cost(rows * cols, 150, table.size * 2),
    )(
        even, *ends, edge, pmodes, masks, lut, pin, back, table, down, inv,
    )


def swapped(strips, axis, odd_first):
    peers = lax.axis_size(axis)
    got = [None, None]
    for kind in (1, 0) if odd_first else (0, 1):
        pairs = [(i, i + 1) for i in range(kind, peers - 1, 2)]
        got[kind] = lax.ppermute(strips[kind], axis, pairs + [(j, i) for i, j in pairs])
    return got


def local(leaf_up, parent_in, leaf_lists, parent_lists, up_transfer, down_transfer, check_inverse):
    cols = leaf_up.shape[1]
    even = [lax.axis_index(axis) % 2 == 0 for axis in ("gx", "gy")]
    flag = jnp.stack(even).astype(jnp.int32)
    rotation, back, table = (jnp.asarray(x) for x in operators())
    low, high = leaf_up[:, :HALO], leaf_up[:, cols - HALO :]
    strips = (jnp.where(even[1], high, low), jnp.where(even[1], low, high))
    strips = swapped(strips, "gy", True)
    own_modes, tiled, rotation = own_step(leaf_up, rotation)
    parents, side, pmodes, *sends = pass_step(flag, strips, tiled, own_modes, rotation, up_transfer)
    ends = swapped(sends, "gx", False)
    parent_up, lut, masks, edge = near_step(
        own_modes, side, pmodes, parents, leaf_lists, parent_lists
    )
    leaf_down = close_step(
        flag, ends, edge, pmodes, masks, lut, parent_in, back, table,
        down_transfer, check_inverse, leaf_up.shape,
    )
    return leaf_down, parent_up


def solution(mesh):
    block = P("gx", "gy", None)
    return jax.shard_map(
        local,
        mesh=mesh,
        in_specs=(block,) * 4 + (P(),) * 3,
        out_specs=(block, block),
        check_vma=False,
    )
```

```python
import functools
import math

import jax
import jax.numpy as jnp
import ml_dtypes
import numpy as np
from jax import lax
from jax.experimental import pallas as pl
from jax.experimental.pallas import tpu as pltpu
from jax.sharding import PartitionSpec as P

ORDER = 6
HALO = 4
KEPT = 14
BF16, F32 = jnp.bfloat16, jnp.float32

PARTS = (
    [(a, -2) for a in range(-1, 2)],
    [(a, 2) for a in range(-1, 2)],
    [(-2, b) for b in range(-2, 3)],
    [(2, b) for b in range(-2, 3)],
    [(3, b) for b in range(-2, 3)],
    [(-3, b) for b in range(-2, 3)],
    [(a, 3) for a in range(-3, 4)],
    [(a, -3) for a in range(-3, 4)],
)


def offset_table():
    return [(a, b) for a in range(-3, 4) for b in range(-3, 4) if max(abs(a), abs(b)) >= 2]


BASES = sorted({(abs(a), abs(b)) for a, b in offset_table()})


def surface_points():
    grid = np.linspace(-1.0, 1.0, ORDER)
    keys = [
        (i, j, k)
        for i in range(ORDER)
        for j in range(ORDER)
        for k in range(ORDER)
        if min(i, j, k) == 0 or max(i, j, k) == ORDER - 1
    ]
    return keys, np.array([[grid[i] for i in key] for key in keys])


def translation(points, dx, dy):
    r = 0.525 * (points[:, None, :] - points[None, :, :]) - np.array([dx, dy, 0.0])
    dist = np.sqrt((r * r).sum(-1))
    n = len(points)
    out = np.zeros((3, n, 3, n))
    for a in range(3):
        for b in range(3):
            out[a, :, b, :] = (float(a == b) / dist + r[..., a] * r[..., b] / dist**3) / (8 * math.pi)
    return out.reshape(3 * n, 3 * n)


def split(x):
    high = x.astype(ml_dtypes.bfloat16)
    return high, (x - high.astype(np.float64)).astype(ml_dtypes.bfloat16)


@functools.lru_cache(maxsize=None)
def operators():
    keys, points = surface_points()
    n = len(keys)
    points_of = {key: i for i, key in enumerate(keys)}
    mirror = [points_of[(i, j, ORDER - 1 - k)] for i, j, k in keys]
    mats = {o: translation(points, *o) for o in offset_table()}
    half = 3 * n // 2
    rotation = np.zeros((3 * n, 512), ml_dtypes.bfloat16)
    back = np.zeros((512, 3 * n))
    table = np.zeros((2, len(BASES), 256, 256), ml_dtypes.bfloat16)
    signs = np.ones((4, 2, 256, 256), ml_dtypes.bfloat16)
    for s, sign in enumerate((1, -1)):
        pairs = np.zeros((3 * n, half))
        firsts = []
        for a in range(3):
            flip = sign if a < 2 else -sign
            for i in range(n):
                if i < mirror[i]:
                    pairs[a * n + i, len(firsts)] = 1.0
                    pairs[a * n + mirror[i], len(firsts)] = flip
                    firsts.append(a * n + i)
        blocks = {o: 0.25 * pairs.T @ m @ pairs for o, m in mats.items()}
        gram = sum(b.T @ b for b in blocks.values())
        place = {f: i for i, f in enumerate(firsts)}
        modes, parity, weight = [], [], []
        for sx in (1, -1):
            for sy in (1, -1):
                basis = []
                for i, f in enumerate(firsts):
                    a, (kx, ky, kz) = f // n, keys[f % n]
                    if kx < ORDER // 2 and ky < ORDER // 2:
                        v = np.zeros(half)
                        for fx in range(2):
                            for fy in range(2):
                                key = (ORDER - 1 - kx if fx else kx, ORDER - 1 - ky if fy else ky, kz)
                                sign_x = (sx if a != 0 else -sx) if fx else 1
                                sign_y = (sy if a != 1 else -sy) if fy else 1
                                v[place[a * n + points_of[key]]] = 0.5 * sign_x * sign_y
                        basis.append(v)
                basis = np.array(basis).T
                w, vecs = np.linalg.eigh(basis.T @ gram @ basis)
                vecs = basis @ vecs
                vecs = vecs * np.sign(vecs[np.abs(np.round(vecs, 9)).argmax(0), np.arange(len(w))])
                modes.append(vecs)
                weight.append(w)
                parity += [(sx, sy)] * len(w)
        order = np.argsort(-np.concatenate(weight), kind="stable")
        vecs = np.concatenate(modes, axis=1)[:, order]
        parity = np.array(parity)[order]
        modes = (pairs @ vecs / math.sqrt(2.0)).astype(ml_dtypes.bfloat16)
        lows = np.concatenate([modes, modes[:, :KEPT], modes[:, :KEPT]], axis=1)
        rotation[:, 256 * s : 256 * (s + 1)] = lows
        outs, out_parity = [], []
        for sx in (1, -1):
            for sy in (1, -1):
                for f in firsts:
                    a, (kx, ky, kz) = f // n, keys[f % n]
                    if kx < ORDER // 2 and ky < ORDER // 2:
                        v = np.zeros(half)
                        for fx in range(2):
                            for fy in range(2):
                                key = (ORDER - 1 - kx if fx else kx, ORDER - 1 - ky if fy else ky, kz)
                                sign_x = (sx if a != 0 else -sx) if fx else 1
                                sign_y = (sy if a != 1 else -sy) if fy else 1
                                v[place[a * n + points_of[key]]] = sign_x * sign_y
                        outs.append(v)
                        out_parity.append((sx, sy))
        outs = np.array(outs).T
        out_parity = np.array(out_parity)
        back[256 * s : 256 * s + half] = (pairs @ outs).T
        undo = np.linalg.inv(modes[firsts].astype(np.float64))
        for q, o in enumerate(BASES):
            high, low = split(undo @ blocks[o].T @ outs * 0.25)
            table[s, q, :half, :half] = high
            table[s, q, half : half + KEPT, :half] = high[:KEPT]
            table[s, q, half + KEPT : half + 2 * KEPT, :half] = low[:KEPT]
        ins = np.concatenate([parity, parity[:KEPT], parity[:KEPT]], axis=0)
        for f in range(4):
            row = np.ones(256)
            row[: len(ins)] = (ins[:, 0] if f // 2 else 1) * (ins[:, 1] if f % 2 else 1)
            col = np.ones(256)
            col[:half] = (out_parity[:, 0] if f // 2 else 1) * (out_parity[:, 1] if f % 2 else 1)
            signs[f, s] = row[:, None] * col[None, :]
    whole = [
        table[:, BASES.index((abs(a), abs(b)))] * signs[2 * (a < 0) + (b < 0)]
        for part in PARTS
        for a, b in part
    ]
    return rotation, back.astype(ml_dtypes.bfloat16), np.concatenate(whole, axis=1)


@functools.lru_cache(maxsize=None)
def plan():
    offsets = offset_table()
    sequence = [o for part in PARTS for o in part]
    products = []
    for c, d in class_pairs():
        for place, (dx, dy) in enumerate(sequence):
            px, cs = divmod(c + dx, 2)
            py, ds = divmod(d + dy, 2)
            if abs(px) <= 1 and abs(py) <= 1:
                entry = (cs * 3 + px + 1) * 6 + ds * 3 + py + 1
                products.append((offsets.index((dx, dy)), entry, place))
    return products


def class_pairs():
    return [(c, d) for c in range(2) for d in range(2)]


def dot(a, b):
    return lax.dot_general(a, b, (((1,), (0,)), ((), ())), preferred_element_type=F32)


def dot_t(a, b):
    return lax.dot_general(a, b, (((1,), (1,)), ((), ())), preferred_element_type=F32)


def parts(x):
    high = x.astype(BF16)
    return high, (x - high.astype(F32)).astype(BF16)


def times_t(x, weight):
    xh, xl = parts(x)
    wh, wl = weight
    both = dot_t(jnp.concatenate([xh, xl], axis=0), wh)
    return both[: x.shape[0]] + (both[x.shape[0] :] + dot_t(xh, wl))


def times_exact(x, weight):
    both = dot(jnp.concatenate(parts(x), axis=0), weight)
    return both[: x.shape[0]] + both[x.shape[0] :]


def lanes(ref, *at):
    pieces = [ref[(t,) + at] for t in range(4)]
    pieces = [p.reshape(-1, 128) for p in pieces]
    return jnp.concatenate(pieces, axis=1)


def cut_tiles(dens):
    return [(t, slice(128 * t, min(128 * t + 128, dens)), slice(0, min(128, dens - 128 * t))) for t in range(4)]


def modes_of(x, rot_ref, dens):
    y = times_exact(x[:, :dens], rot_ref[...])
    lane = lax.broadcasted_iota(jnp.int32, (1, 512), 1) % 256
    half = dens // 2
    is_low = (lane >= half) & (lane < half + KEPT)
    return jnp.where(is_low, y - y.astype(BF16).astype(F32), y)


def children(ref, dens, counts, c, d):
    return jnp.concatenate(
        [
            jnp.concatenate(
                [ref[t, 2 * i + c, pl.ds(d, counts[1], stride=2), :] for i in range(counts[0])],
                axis=0,
            )
            for t in range(4)
        ],
        axis=1,
    )[:, :dens]


def own_kernel(own_ref, rot_ref, modes_ref, tiled_ref, rot_out):
    rows, cols, dens = own_ref.shape
    rot_out[...] = rot_ref[...]
    y = modes_of(own_ref[...].reshape(rows * cols, dens), rot_ref, dens)
    for t, cut, to in cut_tiles(dens):
        modes_ref[t] = y[:, 128 * t : 128 * t + 128].reshape(rows, cols, 128)
        tiled_ref[t, :, :, to] = own_ref[:, :, cut]


def pass_kernel(
    even_ref, strip0_ref, strip1_ref, own_t, own_modes_ref, rot_ref, up_ref,
    parents_ref, side_ref, pmodes, send0_ref, send1_ref,
    strip_t,
):
    rows, _, dens = strip0_ref.shape
    cols = own_modes_ref.shape[2]
    pr, pc = rows // 2, cols // 2
    boxes = pr * pc
    even_x, even_y = even_ref[0] == 1, even_ref[1] == 1
    for t, cut, to in cut_tiles(dens):
        first, second = strip0_ref[:, :, cut], strip1_ref[:, :, cut]
        strip_t[t, :, 0:HALO, to] = jnp.where(even_y, second, first)
        strip_t[t, :, HALO:, to] = jnp.where(even_y, first, second)

    parent = None
    for n, (c, d) in enumerate(class_pairs()):
        x = jnp.concatenate(
            [children(own_t, dens, (pr, pc), c, d), children(strip_t, dens, (pr, HALO), c, d)],
            axis=0,
        )
        part = times_t(x, parts(up_ref[n]))
        parent = part if parent is None else parent + part
    parents_ref[...] = parent[:boxes].reshape(pr, pc, dens)
    z = modes_of(jnp.concatenate([lanes(strip_t)[:, :dens], parent], axis=0), rot_ref, dens)
    w, p = z[: rows * 8], z[rows * 8 :]
    for t in range(4):
        cut = slice(128 * t, 128 * t + 128)
        side = w[:, cut].reshape(rows, 8, 128)
        side_ref[t] = side
        pmodes[t, 2 : 2 + pr, 4 : 4 + pc, :] = p[:boxes, cut].reshape(pr, pc, 128)
        strip = p[boxes:, cut].reshape(pr, 4, 128)
        pmodes[t, 2 : 2 + pr, 2:4, :] = strip[:, 0:2]
        pmodes[t, 2 : 2 + pr, 4 + pc : 6 + pc, :] = strip[:, 2:4]
        own = p[:boxes, cut].reshape(pr, pc, 128)
        ends = []
        for x, to in ((slice(0, 2), slice(0, 2)), (slice(rows - 2, rows), slice(pr - 2, pr))):
            ends.append(
                jnp.concatenate(
                    [own_modes_ref[t, x], jnp.concatenate([side[x, 2:6], strip[to]], axis=1), own[to]],
                    axis=1,
                )
            )
        low, high = ends
        send0_ref[t] = jnp.where(even_x, high, low)
        send1_ref[t] = jnp.where(even_x, low, high)


def near_kernel(
    own_modes_ref, side_ref, pmodes_ref, parents_ref, llist_ref, plist_ref,
    pup_ref, lut, masks_ref, edge_ref,
    modes, flat,
):
    rows, cols = own_modes_ref.shape[1:3]
    pup_ref[...] = parents_ref[...]
    pr, pc = rows // 2, cols // 2
    gr, gc = pr // 2, pc // 2
    used = pr * pc + gr * gc
    high = lut.shape[2]
    count = masks_ref.shape[0] // 4

    for t in range(4):
        modes[t, 2 : 2 + rows, 8 : 8 + cols, :] = own_modes_ref[t]
        modes[t, 2 : 2 + rows, 4:8, :] = side_ref[t, :, 0:4]
        modes[t, 2 : 2 + rows, 8 + cols : 12 + cols, :] = side_ref[t, :, 4:8]
        edge_ref[t, 0:2] = modes[t, 2:4]
        edge_ref[t, 2:4] = modes[t, rows : rows + 2]

    def gather(i, carry):
        base = 2 * (i % 3) + i // 3
        for ds in range(2):
            for py in (-1, 0, 1):
                e = i * 6 + ds * 3 + py + 1
                for t in range(4):
                    x = jnp.concatenate(
                        [
                            modes[t, base + 2 * j, pl.ds(8 + 2 * py + ds, pc, stride=2), :]
                            for j in range(pr)
                        ]
                        + [
                            pmodes_ref[t, base + 2 * j, pl.ds(4 + 2 * py + ds, gc, stride=2), :]
                            for j in range(gr)
                        ]
                        + [jnp.zeros((high - used, 128), F32)],
                        axis=0,
                    )
                    lut[e, t // 2, :, 128 * (t % 2) : 128 * (t % 2) + 128] = x.astype(BF16)
        return carry

    lax.fori_loop(0, 6, gather, 0)

    flat[0, :, :, 0 : llist_ref.shape[2]] = llist_ref[...].astype(F32)
    flat[1, 0:pr, 0:pc, 0 : plist_ref.shape[2]] = plist_ref[...].astype(F32)
    for n, (c, d) in enumerate(class_pairs()):
        flag = jnp.concatenate(
            [flat[0, 2 * i + c, pl.ds(d, pc, stride=2), :] for i in range(pr)]
            + [flat[1, 2 * i + c, pl.ds(d, gc, stride=2), :] for i in range(gr)]
            + [jnp.zeros((high - used, 128), F32)],
            axis=0,
        )
        for k in range(count):
            o = plan()[count * n + k][0]
            masks_ref[count * n + k] = jnp.broadcast_to(flag[:, o : o + 1], (high, 128)).astype(BF16)


def close_kernel(
    even_ref,
    got0_ref, got1_ref, edge_ref, pside_ref, masks, lut,
    pin_ref, back, table, down_ref, inv_ref,
    out_ref,
    edge, pmodes, fresh, acc, flat, plocal,
):
    rows, cols, dens = out_ref.shape
    pr, pc = rows // 2, cols // 2
    gr, gc = pr // 2, pc // 2
    boxes, pboxes = pr * pc, gr * gc
    high = lut.shape[2]
    count = masks.shape[0] // 4
    even = even_ref[0] == 1
    for t in range(4):
        before = jnp.where(even, got1_ref[t], got0_ref[t])
        after = jnp.where(even, got0_ref[t], got1_ref[t])
        edge[t, 2:6] = edge_ref[t]
        pmodes[t, 2 : 2 + pr] = pside_ref[t, 2 : 2 + pr]
        for x, leaf, parent in ((before, slice(0, 2), slice(0, 2)), (after, slice(6, 8), slice(2 + pr, 4 + pr))):
            edge[t, leaf, 8 : 8 + cols, :] = x[:, 0:cols]
            edge[t, leaf, 6:8, :] = x[:, cols : cols + 2]
            edge[t, leaf, 8 + cols : 10 + cols, :] = x[:, cols + 2 : cols + 4]
            pmodes[t, parent, 2:4, :] = x[:, cols + 4 : cols + 6]
            pmodes[t, parent, 4 + pc : 6 + pc, :] = x[:, cols + 6 : cols + 8]
            pmodes[t, parent, 4 : 4 + pc, :] = x[:, cols + 8 :]

    def patch(cs, carry):
        for ds in range(2):
            for py in (-1, 0, 1):
                for t in range(4):
                    at = slice(128 * (t % 2), 128 * (t % 2) + 128)
                    mine = pl.ds(8 + 2 * py + ds, pc, stride=2)
                    theirs = pl.ds(4 + 2 * py + ds, gc, stride=2)
                    e = cs * 6 + ds * 3 + py + 1
                    x = jnp.concatenate([edge[t, cs + 2 * j, mine, :] for j in range(2)], axis=0)
                    fresh[0, e, t // 2, 0:16, at] = x.astype(BF16)
                    x = jnp.concatenate([pmodes[t, cs + 2 * j, theirs, :] for j in range(4)], axis=0)
                    fresh[0, e, t // 2, 16:32, at] = x.astype(BF16)
                    x = jnp.concatenate([edge[t, 4 + cs + 2 * j, mine, :] for j in range(2)], axis=0)
                    fresh[1, e, t // 2, 0:16, at] = x.astype(BF16)
                    x = jnp.concatenate(
                        [pmodes[t, 4 + cs + 2 * j, theirs, :] for j in range(4, gr)]
                        + [jnp.zeros((high - boxes - pboxes, 128), F32)],
                        axis=0,
                    )
                    fresh[1, e, t // 2, 16:32, at] = x.astype(BF16)
        return carry

    lax.fori_loop(0, 2, patch, 0)

    runs = [(0, 3), (3, 6), (6, 11), (11, 16), (16, 21)]

    def listed(i, s):
        e = plan()[i][1]
        px = e // 6 % 3 - 1
        m = masks[i]
        if px == 0:
            x = lut[e, s]
        else:
            new = fresh[(px + 1) // 2, e // 18 * 6 + e % 6, s]
            if px < 0:
                pieces = [new[0:16], lut[e, s, 16:boxes], new[16:32], lut[e, s, boxes + 16 : high]]
            else:
                pieces = [lut[e, s, 0 : boxes - 16], new[0:16], lut[e, s, boxes : boxes + 16], new[16:32]]
            x = jnp.concatenate(pieces, axis=0)
        return jnp.concatenate([x[:, :128] * m, x[:, 128:] * m], axis=1)

    for c in range(2):

        def interact(s, carry):
            n = 2 * c
            total = jnp.zeros((2 * high, 256), F32)

            def run(first, last, s):
                at = 256 * plan()[first][2]
                x = jnp.concatenate([listed(i, s) for i in range(first, last)], axis=1)
                return x, table[s, at : at + 256 * (last - first), :]

            for a, b in runs:
                x, weight = run(n * count + a, n * count + b, s)
                y, _ = run((n + 1) * count + a, (n + 1) * count + b, s)
                total = total + dot(jnp.concatenate([x, y], axis=0), weight)
            for d in range(2):
                x, weight = run((n + d) * count + runs[-1][1], (n + d + 1) * count, s)
                acc[s, n + d] = total[high * d : high * (d + 1)] + dot(x, weight)
            return carry

        for s in range(2):
            interact(s, 0)

    def densities(rows):
        pieces = [
            times_exact(
                jnp.concatenate([acc[s, n, rows] for n in range(4)], axis=0),
                back[256 * s : 256 * (s + 1)],
            )
            for s in range(2)
        ]
        return pieces[0] + pieces[1]

    pcheck = densities(slice(boxes, high))
    check = densities(slice(0, boxes))

    inverse = parts(inv_ref[...])
    for n, (c, d) in enumerate(class_pairs()):
        for t, cut, to in cut_tiles(dens):
            for j in range(gr):
                r = (high - boxes) * n + gc * j
                plocal[t, 2 * j + c, pl.ds(d, gc, stride=2), to] = pcheck[r : r + gc, cut]
    local = pin_ref[...].reshape(boxes, dens) + times_t(lanes(plocal)[:, :dens], inverse)
    x = jnp.concatenate(
        [
            check[boxes * n : boxes * (n + 1)] + times_t(local, parts(down_ref[n]))
            for n in range(4)
        ],
        axis=0,
    )
    result = times_t(x, inverse)
    for n, (c, d) in enumerate(class_pairs()):
        for t, cut, to in cut_tiles(dens):
            for j in range(pr):
                r = boxes * n + pc * j
                flat[t, 2 * j + c, pl.ds(d, pc, stride=2), to] = result[r : r + pc, cut]
    for t, cut, to in cut_tiles(dens):
        out_ref[:, :, cut] = flat[t, :, :, to]


VMEM = pl.BlockSpec(memory_space=pltpu.VMEM)
SMEM = pl.BlockSpec(memory_space=pltpu.SMEM)


def params(mib):
    return pltpu.CompilerParams(vmem_limit_bytes=mib * 1024 * 1024)


def cost(rows, tiles, reads):
    return pl.CostEstimate(flops=2 * rows * tiles * 256 * 256, bytes_accessed=reads, transcendentals=0)


def height(boxes):
    return -(-(boxes * 5 // 4) // 16) * 16


def own_step(own, rotation):
    rows, cols, _ = own.shape
    tiled = jax.ShapeDtypeStruct((4, rows, cols, 128), F32)
    return pl.pallas_call(
        own_kernel,
        out_shape=(tiled, tiled, jax.ShapeDtypeStruct(rotation.shape, BF16)),
        in_specs=[VMEM] * 2,
        out_specs=(VMEM,) * 3,
        compiler_params=params(16),
        cost_estimate=cost(rows * cols, 48, 64 * 1024 * 1024),
    )(own, rotation)


def pass_step(even, strips, tiled, own_modes, rotation, up):
    rows, cols = tiled.shape[1:3]
    dens = up.shape[1]
    pr, pc = rows // 2, cols // 2
    send = jax.ShapeDtypeStruct((4, 2, cols + pc + 8, 128), F32)
    return pl.pallas_call(
        pass_kernel,
        out_shape=(
            jax.ShapeDtypeStruct((pr, pc, dens), F32),
            jax.ShapeDtypeStruct((4, rows, 2 * HALO, 128), F32),
            jax.ShapeDtypeStruct((4, pr + 4, pc + 8, 128), F32),
            send,
            send,
        ),
        in_specs=[SMEM] + [VMEM] * 6,
        out_specs=(VMEM,) * 5,
        scratch_shapes=[pltpu.VMEM((4, rows, 2 * HALO, 128), F32)],
        compiler_params=params(16),
        cost_estimate=cost(rows * cols, 32, up.size * 4),
    )(even, *strips, tiled, own_modes, rotation, up)


def near_step(own_modes, side, pmodes, parents, llist, plist):
    rows, cols, _ = llist.shape
    high = height(rows * cols // 4)
    return pl.pallas_call(
        near_kernel,
        out_shape=(
            jax.ShapeDtypeStruct(parents.shape, F32),
            jax.ShapeDtypeStruct((36, 2, high, 256), BF16),
            jax.ShapeDtypeStruct((len(plan()), high, 128), BF16),
            jax.ShapeDtypeStruct((4, 4, cols + 16, 128), F32),
        ),
        in_specs=[VMEM] * 6,
        out_specs=(VMEM,) * 4,
        scratch_shapes=[
            pltpu.VMEM((4, rows + 4, cols + 16, 128), F32),
            pltpu.VMEM((2, rows, cols, 128), F32),
        ],
        compiler_params=params(16),
        cost_estimate=cost(rows * cols, 48, 16 * 1024 * 1024),
    )(own_modes, side, pmodes, parents, llist, plist)


def close_step(even, ends, edge, pmodes, masks, lut, pin, back, table, down, inv, shape):
    rows, cols, dens = shape
    pr, pc = rows // 2, cols // 2
    high = height(pr * pc)
    return pl.pallas_call(
        close_kernel,
        out_shape=jax.ShapeDtypeStruct(shape, F32),
        in_specs=[SMEM] + [VMEM] * 11,
        out_specs=VMEM,
        scratch_shapes=[
            pltpu.VMEM((4, 8, cols + 16, 128), F32),
            pltpu.VMEM((4, pr + 4, pc + 8, 128), F32),
            pltpu.VMEM((2, 12, 2, 32, 256), BF16),
            pltpu.VMEM((2, 4, high, 256), F32),
            pltpu.VMEM((4, rows, cols, 128), F32),
            pltpu.VMEM((4, pr, pc, 128), F32),
        ],
        compiler_params=params(24),
        cost_estimate=cost(rows * cols, 150, table.size * 2),
    )(
        even, *ends, edge, pmodes, masks, lut, pin, back, table, down, inv,
    )


def swapped(strips, axis, odd_first):
    peers = lax.axis_size(axis)
    got = [None, None]
    for kind in (1, 0) if odd_first else (0, 1):
        pairs = [(i, i + 1) for i in range(kind, peers - 1, 2)]
        got[kind] = lax.ppermute(strips[kind], axis, pairs + [(j, i) for i, j in pairs])
    return got


def local(leaf_up, parent_in, leaf_lists, parent_lists, up_transfer, down_transfer, check_inverse):
    cols = leaf_up.shape[1]
    even = [lax.axis_index(axis) % 2 == 0 for axis in ("gx", "gy")]
    flag = jnp.stack(even).astype(jnp.int32)
    rotation, back, table = (jnp.asarray(x) for x in operators())
    low, high = leaf_up[:, :HALO], leaf_up[:, cols - HALO :]
    strips = (jnp.where(even[1], high, low), jnp.where(even[1], low, high))
    strips = swapped(strips, "gy", True)
    own_modes, tiled, rotation = own_step(leaf_up, rotation)
    parents, side, pmodes, *sends = pass_step(flag, strips, tiled, own_modes, rotation, up_transfer)
    ends = swapped(sends, "gx", False)
    parent_up, lut, masks, edge = near_step(
        own_modes, side, pmodes, parents, leaf_lists, parent_lists
    )
    leaf_down = close_step(
        flag, ends, edge, pmodes, masks, lut, parent_in, back, table,
        down_transfer, check_inverse, leaf_up.shape,
    )
    return leaf_down, parent_up


def solution(mesh):
    block = P("gx", "gy", None)
    return jax.shard_map(
        local,
        mesh=mesh,
        in_specs=(block,) * 4 + (P(),) * 3,
        out_specs=(block, block),
        check_vma=False,
    )
```

```python
import functools
import math

import jax
import jax.numpy as jnp
import ml_dtypes
import numpy as np
from jax import lax
from jax.experimental import pallas as pl
from jax.experimental.pallas import tpu as pltpu
from jax.sharding import PartitionSpec as P

ORDER = 6
HALO = 4
KEPT = 14
BF16, F32 = jnp.bfloat16, jnp.float32

PARTS = (
    [(a, -2) for a in range(-1, 2)],
    [(a, 2) for a in range(-1, 2)],
    [(-2, b) for b in range(-2, 3)],
    [(2, b) for b in range(-2, 3)],
    [(3, b) for b in range(-2, 3)],
    [(-3, b) for b in range(-2, 3)],
    [(a, 3) for a in range(-3, 4)],
    [(a, -3) for a in range(-3, 4)],
)


def offset_table():
    return [(a, b) for a in range(-3, 4) for b in range(-3, 4) if max(abs(a), abs(b)) >= 2]


BASES = sorted({(abs(a), abs(b)) for a, b in offset_table()})


def surface_points():
    grid = np.linspace(-1.0, 1.0, ORDER)
    keys = [
        (i, j, k)
        for i in range(ORDER)
        for j in range(ORDER)
        for k in range(ORDER)
        if min(i, j, k) == 0 or max(i, j, k) == ORDER - 1
    ]
    return keys, np.array([[grid[i] for i in key] for key in keys])


def translation(points, dx, dy):
    r = 0.525 * (points[:, None, :] - points[None, :, :]) - np.array([dx, dy, 0.0])
    dist = np.sqrt((r * r).sum(-1))
    n = len(points)
    out = np.zeros((3, n, 3, n))
    for a in range(3):
        for b in range(3):
            out[a, :, b, :] = (float(a == b) / dist + r[..., a] * r[..., b] / dist**3) / (8 * math.pi)
    return out.reshape(3 * n, 3 * n)


def split(x):
    high = x.astype(ml_dtypes.bfloat16)
    return high, (x - high.astype(np.float64)).astype(ml_dtypes.bfloat16)


@functools.lru_cache(maxsize=None)
def operators():
    keys, points = surface_points()
    n = len(keys)
    points_of = {key: i for i, key in enumerate(keys)}
    mirror = [points_of[(i, j, ORDER - 1 - k)] for i, j, k in keys]
    mats = {o: translation(points, *o) for o in offset_table()}
    half = 3 * n // 2
    rotation = np.zeros((3 * n, 512), ml_dtypes.bfloat16)
    back = np.zeros((512, 3 * n))
    table = np.zeros((2, len(BASES), 256, 256), ml_dtypes.bfloat16)
    signs = np.ones((4, 2, 256, 256), ml_dtypes.bfloat16)
    for s, sign in enumerate((1, -1)):
        pairs = np.zeros((3 * n, half))
        firsts = []
        for a in range(3):
            flip = sign if a < 2 else -sign
            for i in range(n):
                if i < mirror[i]:
                    pairs[a * n + i, len(firsts)] = 1.0
                    pairs[a * n + mirror[i], len(firsts)] = flip
                    firsts.append(a * n + i)
        blocks = {o: 0.25 * pairs.T @ m @ pairs for o, m in mats.items()}
        gram = sum(b.T @ b for b in blocks.values())
        place = {f: i for i, f in enumerate(firsts)}
        modes, parity, weight = [], [], []
        for sx in (1, -1):
            for sy in (1, -1):
                basis = []
                for i, f in enumerate(firsts):
                    a, (kx, ky, kz) = f // n, keys[f % n]
                    if kx < ORDER // 2 and ky < ORDER // 2:
                        v = np.zeros(half)
                        for fx in range(2):
                            for fy in range(2):
                                key = (ORDER - 1 - kx if fx else kx, ORDER - 1 - ky if fy else ky, kz)
                                sign_x = (sx if a != 0 else -sx) if fx else 1
                                sign_y = (sy if a != 1 else -sy) if fy else 1
                                v[place[a * n + points_of[key]]] = 0.5 * sign_x * sign_y
                        basis.append(v)
                basis = np.array(basis).T
                w, vecs = np.linalg.eigh(basis.T @ gram @ basis)
                vecs = basis @ vecs
                vecs = vecs * np.sign(vecs[np.abs(np.round(vecs, 9)).argmax(0), np.arange(len(w))])
                modes.append(vecs)
                weight.append(w)
                parity += [(sx, sy)] * len(w)
        order = np.argsort(-np.concatenate(weight), kind="stable")
        vecs = np.concatenate(modes, axis=1)[:, order]
        parity = np.array(parity)[order]
        modes = (pairs @ vecs / math.sqrt(2.0)).astype(ml_dtypes.bfloat16)
        lows = np.concatenate([modes, modes[:, :KEPT], modes[:, :KEPT]], axis=1)
        rotation[:, 256 * s : 256 * (s + 1)] = lows
        outs, out_parity = [], []
        for sx in (1, -1):
            for sy in (1, -1):
                for f in firsts:
                    a, (kx, ky, kz) = f // n, keys[f % n]
                    if kx < ORDER // 2 and ky < ORDER // 2:
                        v = np.zeros(half)
                        for fx in range(2):
                            for fy in range(2):
                                key = (ORDER - 1 - kx if fx else kx, ORDER - 1 - ky if fy else ky, kz)
                                sign_x = (sx if a != 0 else -sx) if fx else 1
                                sign_y = (sy if a != 1 else -sy) if fy else 1
                                v[place[a * n + points_of[key]]] = sign_x * sign_y
                        outs.append(v)
                        out_parity.append((sx, sy))
        outs = np.array(outs).T
        out_parity = np.array(out_parity)
        back[256 * s : 256 * s + half] = (pairs @ outs).T
        undo = np.linalg.inv(modes[firsts].astype(np.float64))
        for q, o in enumerate(BASES):
            high, low = split(undo @ blocks[o].T @ outs * 0.25)
            table[s, q, :half, :half] = high
            table[s, q, half : half + KEPT, :half] = high[:KEPT]
            table[s, q, half + KEPT : half + 2 * KEPT, :half] = low[:KEPT]
        ins = np.concatenate([parity, parity[:KEPT], parity[:KEPT]], axis=0)
        for f in range(4):
            row = np.ones(256)
            row[: len(ins)] = (ins[:, 0] if f // 2 else 1) * (ins[:, 1] if f % 2 else 1)
            col = np.ones(256)
            col[:half] = (out_parity[:, 0] if f // 2 else 1) * (out_parity[:, 1] if f % 2 else 1)
            signs[f, s] = row[:, None] * col[None, :]
    whole = [
        table[:, BASES.index((abs(a), abs(b)))] * signs[2 * (a < 0) + (b < 0)]
        for part in PARTS
        for a, b in part
    ]
    return rotation, back.astype(ml_dtypes.bfloat16), np.concatenate(whole, axis=1)


@functools.lru_cache(maxsize=None)
def plan():
    offsets = offset_table()
    sequence = [o for part in PARTS for o in part]
    products = []
    for c, d in class_pairs():
        for place, (dx, dy) in enumerate(sequence):
            px, cs = divmod(c + dx, 2)
            py, ds = divmod(d + dy, 2)
            if abs(px) <= 1 and abs(py) <= 1:
                entry = (cs * 3 + px + 1) * 6 + ds * 3 + py + 1
                products.append((offsets.index((dx, dy)), entry, place))
    return products


def class_pairs():
    return [(c, d) for c in range(2) for d in range(2)]


def dot(a, b):
    return lax.dot_general(a, b, (((1,), (0,)), ((), ())), preferred_element_type=F32)


def dot_t(a, b):
    return lax.dot_general(a, b, (((1,), (1,)), ((), ())), preferred_element_type=F32)


def parts(x):
    high = x.astype(BF16)
    return high, (x - high.astype(F32)).astype(BF16)


def times_t(x, weight):
    xh, xl = parts(x)
    wh, wl = weight
    both = dot_t(jnp.concatenate([xh, xl], axis=0), wh)
    return both[: x.shape[0]] + (both[x.shape[0] :] + dot_t(xh, wl))


def times_exact(x, weight):
    both = dot(jnp.concatenate(parts(x), axis=0), weight)
    return both[: x.shape[0]] + both[x.shape[0] :]


def lanes(ref, *at):
    pieces = [ref[(t,) + at] for t in range(4)]
    pieces = [p.reshape(-1, 128) for p in pieces]
    return jnp.concatenate(pieces, axis=1)


def cut_tiles(dens):
    return [(t, slice(128 * t, min(128 * t + 128, dens)), slice(0, min(128, dens - 128 * t))) for t in range(4)]


def modes_of(x, rot_ref, dens):
    y = times_exact(x[:, :dens], rot_ref[...])
    lane = lax.broadcasted_iota(jnp.int32, (1, 512), 1) % 256
    half = dens // 2
    is_low = (lane >= half) & (lane < half + KEPT)
    return jnp.where(is_low, y - y.astype(BF16).astype(F32), y)


def children(ref, dens, counts, c, d):
    return jnp.concatenate(
        [
            jnp.concatenate(
                [ref[t, 2 * i + c, pl.ds(d, counts[1], stride=2), :] for i in range(counts[0])],
                axis=0,
            )
            for t in range(4)
        ],
        axis=1,
    )[:, :dens]


def own_kernel(own_ref, rot_ref, modes_ref, tiled_ref, rot_out):
    rows, cols, dens = own_ref.shape
    rot_out[...] = rot_ref[...]
    y = modes_of(own_ref[...].reshape(rows * cols, dens), rot_ref, dens)
    for t, cut, to in cut_tiles(dens):
        modes_ref[t] = y[:, 128 * t : 128 * t + 128].reshape(rows, cols, 128)
        tiled_ref[t, :, :, to] = own_ref[:, :, cut]


def pass_kernel(
    even_ref, strip0_ref, strip1_ref, own_t, own_modes_ref, rot_ref, up_ref,
    parents_ref, side_ref, pmodes, send0_ref, send1_ref,
    strip_t,
):
    rows, _, dens = strip0_ref.shape
    cols = own_modes_ref.shape[2]
    pr, pc = rows // 2, cols // 2
    boxes = pr * pc
    even_x, even_y = even_ref[0] == 1, even_ref[1] == 1
    for t, cut, to in cut_tiles(dens):
        first, second = strip0_ref[:, :, cut], strip1_ref[:, :, cut]
        strip_t[t, :, 0:HALO, to] = jnp.where(even_y, second, first)
        strip_t[t, :, HALO:, to] = jnp.where(even_y, first, second)

    parent = None
    for n, (c, d) in enumerate(class_pairs()):
        x = jnp.concatenate(
            [children(own_t, dens, (pr, pc), c, d), children(strip_t, dens, (pr, HALO), c, d)],
            axis=0,
        )
        part = times_t(x, parts(up_ref[n]))
        parent = part if parent is None else parent + part
    parents_ref[...] = parent[:boxes].reshape(pr, pc, dens)
    z = modes_of(jnp.concatenate([lanes(strip_t)[:, :dens], parent], axis=0), rot_ref, dens)
    w, p = z[: rows * 8], z[rows * 8 :]
    for t in range(4):
        cut = slice(128 * t, 128 * t + 128)
        side = w[:, cut].reshape(rows, 8, 128)
        side_ref[t] = side
        pmodes[t, 2 : 2 + pr, 4 : 4 + pc, :] = p[:boxes, cut].reshape(pr, pc, 128)
        strip = p[boxes:, cut].reshape(pr, 4, 128)
        pmodes[t, 2 : 2 + pr, 2:4, :] = strip[:, 0:2]
        pmodes[t, 2 : 2 + pr, 4 + pc : 6 + pc, :] = strip[:, 2:4]
        own = p[:boxes, cut].reshape(pr, pc, 128)
        ends = []
        for x, to in ((slice(0, 2), slice(0, 2)), (slice(rows - 2, rows), slice(pr - 2, pr))):
            ends.append(
                jnp.concatenate(
                    [own_modes_ref[t, x], jnp.concatenate([side[x, 2:6], strip[to]], axis=1), own[to]],
                    axis=1,
                )
            )
        low, high = ends
        send0_ref[t] = jnp.where(even_x, high, low)
        send1_ref[t] = jnp.where(even_x, low, high)


def near_kernel(
    own_modes_ref, side_ref, pmodes_ref, parents_ref, llist_ref, plist_ref,
    pup_ref, lut, masks_ref, edge_ref,
    modes, flat,
):
    rows, cols = own_modes_ref.shape[1:3]
    pup_ref[...] = parents_ref[...]
    pr, pc = rows // 2, cols // 2
    gr, gc = pr // 2, pc // 2
    used = pr * pc + gr * gc
    high = lut.shape[2]
    count = masks_ref.shape[0] // 4

    for t in range(4):
        modes[t, 2 : 2 + rows, 8 : 8 + cols, :] = own_modes_ref[t]
        modes[t, 2 : 2 + rows, 4:8, :] = side_ref[t, :, 0:4]
        modes[t, 2 : 2 + rows, 8 + cols : 12 + cols, :] = side_ref[t, :, 4:8]
        edge_ref[t, 0:2] = modes[t, 2:4]
        edge_ref[t, 2:4] = modes[t, rows : rows + 2]

    def gather(i, carry):
        base = 2 * (i % 3) + i // 3
        for ds in range(2):
            for py in (-1, 0, 1):
                e = i * 6 + ds * 3 + py + 1
                for t in range(4):
                    x = jnp.concatenate(
                        [
                            modes[t, base + 2 * j, pl.ds(8 + 2 * py + ds, pc, stride=2), :]
                            for j in range(pr)
                        ]
                        + [
                            pmodes_ref[t, base + 2 * j, pl.ds(4 + 2 * py + ds, gc, stride=2), :]
                            for j in range(gr)
                        ]
                        + [jnp.zeros((high - used, 128), F32)],
                        axis=0,
                    )
                    lut[e, t // 2, :, 128 * (t % 2) : 128 * (t % 2) + 128] = x.astype(BF16)
        return carry

    lax.fori_loop(0, 6, gather, 0)

    flat[0, :, :, 0 : llist_ref.shape[2]] = llist_ref[...].astype(F32)
    flat[1, 0:pr, 0:pc, 0 : plist_ref.shape[2]] = plist_ref[...].astype(F32)
    for n, (c, d) in enumerate(class_pairs()):
        flag = jnp.concatenate(
            [flat[0, 2 * i + c, pl.ds(d, pc, stride=2), :] for i in range(pr)]
            + [flat[1, 2 * i + c, pl.ds(d, gc, stride=2), :] for i in range(gr)]
            + [jnp.zeros((high - used, 128), F32)],
            axis=0,
        )
        for k in range(count):
            o = plan()[count * n + k][0]
            masks_ref[count * n + k] = jnp.broadcast_to(flag[:, o : o + 1], (high, 128)).astype(BF16)


def close_kernel(
    even_ref,
    got0_ref, got1_ref, edge_ref, pside_ref, masks, lut,
    pin_ref, back, table, down_ref, inv_ref,
    out_ref,
    edge, pmodes, fresh, acc, flat, plocal,
):
    rows, cols, dens = out_ref.shape
    pr, pc = rows // 2, cols // 2
    gr, gc = pr // 2, pc // 2
    boxes, pboxes = pr * pc, gr * gc
    high = lut.shape[2]
    count = masks.shape[0] // 4
    even = even_ref[0] == 1
    for t in range(4):
        before = jnp.where(even, got1_ref[t], got0_ref[t])
        after = jnp.where(even, got0_ref[t], got1_ref[t])
        edge[t, 2:6] = edge_ref[t]
        pmodes[t, 2 : 2 + pr] = pside_ref[t, 2 : 2 + pr]
        for x, leaf, parent in ((before, slice(0, 2), slice(0, 2)), (after, slice(6, 8), slice(2 + pr, 4 + pr))):
            edge[t, leaf, 8 : 8 + cols, :] = x[:, 0:cols]
            edge[t, leaf, 6:8, :] = x[:, cols : cols + 2]
            edge[t, leaf, 8 + cols : 10 + cols, :] = x[:, cols + 2 : cols + 4]
            pmodes[t, parent, 2:4, :] = x[:, cols + 4 : cols + 6]
            pmodes[t, parent, 4 + pc : 6 + pc, :] = x[:, cols + 6 : cols + 8]
            pmodes[t, parent, 4 : 4 + pc, :] = x[:, cols + 8 :]

    def patch(cs, carry):
        for ds in range(2):
            for py in (-1, 0, 1):
                for t in range(4):
                    at = slice(128 * (t % 2), 128 * (t % 2) + 128)
                    mine = pl.ds(8 + 2 * py + ds, pc, stride=2)
                    theirs = pl.ds(4 + 2 * py + ds, gc, stride=2)
                    e = cs * 6 + ds * 3 + py + 1
                    x = jnp.concatenate([edge[t, cs + 2 * j, mine, :] for j in range(2)], axis=0)
                    fresh[0, e, t // 2, 0:16, at] = x.astype(BF16)
                    x = jnp.concatenate([pmodes[t, cs + 2 * j, theirs, :] for j in range(4)], axis=0)
                    fresh[0, e, t // 2, 16:32, at] = x.astype(BF16)
                    x = jnp.concatenate([edge[t, 4 + cs + 2 * j, mine, :] for j in range(2)], axis=0)
                    fresh[1, e, t // 2, 0:16, at] = x.astype(BF16)
                    x = jnp.concatenate(
                        [pmodes[t, 4 + cs + 2 * j, theirs, :] for j in range(4, gr)]
                        + [jnp.zeros((high - boxes - pboxes, 128), F32)],
                        axis=0,
                    )
                    fresh[1, e, t // 2, 16:32, at] = x.astype(BF16)
        return carry

    for cs in range(2):
        patch(cs, 0)

    runs = [(0, 3), (3, 6), (6, 11), (11, 16), (16, 21)]

    def listed(i, s):
        e = plan()[i][1]
        px = e // 6 % 3 - 1
        m = masks[i]
        if px == 0:
            x = lut[e, s]
        else:
            new = fresh[(px + 1) // 2, e // 18 * 6 + e % 6, s]
            if px < 0:
                pieces = [new[0:16], lut[e, s, 16:boxes], new[16:32], lut[e, s, boxes + 16 : high]]
            else:
                pieces = [lut[e, s, 0 : boxes - 16], new[0:16], lut[e, s, boxes : boxes + 16], new[16:32]]
            x = jnp.concatenate(pieces, axis=0)
        return jnp.concatenate([x[:, :128] * m, x[:, 128:] * m], axis=1)

    for c in range(2):

        def interact(s, carry):
            n = 2 * c
            total = jnp.zeros((2 * high, 256), F32)

            def run(first, last, s):
                at = 256 * plan()[first][2]
                x = jnp.concatenate([listed(i, s) for i in range(first, last)], axis=1)
                return x, table[s, at : at + 256 * (last - first), :]

            for a, b in runs:
                x, weight = run(n * count + a, n * count + b, s)
                y, _ = run((n + 1) * count + a, (n + 1) * count + b, s)
                total = total + dot(jnp.concatenate([x, y], axis=0), weight)
            for d in range(2):
                x, weight = run((n + d) * count + runs[-1][1], (n + d + 1) * count, s)
                acc[s, n + d] = total[high * d : high * (d + 1)] + dot(x, weight)
            return carry

        for s in range(2):
            interact(s, 0)

    def densities(rows):
        pieces = [
            times_exact(
                jnp.concatenate([acc[s, n, rows] for n in range(4)], axis=0),
                back[256 * s : 256 * (s + 1)],
            )
            for s in range(2)
        ]
        return pieces[0] + pieces[1]

    pcheck = densities(slice(boxes, high))
    check = densities(slice(0, boxes))

    inverse = parts(inv_ref[...])
    for n, (c, d) in enumerate(class_pairs()):
        for t, cut, to in cut_tiles(dens):
            for j in range(gr):
                r = (high - boxes) * n + gc * j
                plocal[t, 2 * j + c, pl.ds(d, gc, stride=2), to] = pcheck[r : r + gc, cut]
    local = pin_ref[...].reshape(boxes, dens) + times_t(lanes(plocal)[:, :dens], inverse)
    x = jnp.concatenate(
        [
            check[boxes * n : boxes * (n + 1)] + times_t(local, parts(down_ref[n]))
            for n in range(4)
        ],
        axis=0,
    )
    result = times_t(x, inverse)
    for n, (c, d) in enumerate(class_pairs()):
        for t, cut, to in cut_tiles(dens):
            for j in range(pr):
                r = boxes * n + pc * j
                flat[t, 2 * j + c, pl.ds(d, pc, stride=2), to] = result[r : r + pc, cut]
    for t, cut, to in cut_tiles(dens):
        out_ref[:, :, cut] = flat[t, :, :, to]


VMEM = pl.BlockSpec(memory_space=pltpu.VMEM)
SMEM = pl.BlockSpec(memory_space=pltpu.SMEM)


def params(mib):
    return pltpu.CompilerParams(vmem_limit_bytes=mib * 1024 * 1024)


def cost(rows, tiles, reads):
    return pl.CostEstimate(flops=2 * rows * tiles * 256 * 256, bytes_accessed=reads, transcendentals=0)


def height(boxes):
    return -(-(boxes * 5 // 4) // 16) * 16


def own_step(own, rotation):
    rows, cols, _ = own.shape
    tiled = jax.ShapeDtypeStruct((4, rows, cols, 128), F32)
    return pl.pallas_call(
        own_kernel,
        out_shape=(tiled, tiled, jax.ShapeDtypeStruct(rotation.shape, BF16)),
        in_specs=[VMEM] * 2,
        out_specs=(VMEM,) * 3,
        compiler_params=params(16),
        cost_estimate=cost(rows * cols, 48, 64 * 1024 * 1024),
    )(own, rotation)


def pass_step(even, strips, tiled, own_modes, rotation, up):
    rows, cols = tiled.shape[1:3]
    dens = up.shape[1]
    pr, pc = rows // 2, cols // 2
    send = jax.ShapeDtypeStruct((4, 2, cols + pc + 8, 128), F32)
    return pl.pallas_call(
        pass_kernel,
        out_shape=(
            jax.ShapeDtypeStruct((pr, pc, dens), F32),
            jax.ShapeDtypeStruct((4, rows, 2 * HALO, 128), F32),
            jax.ShapeDtypeStruct((4, pr + 4, pc + 8, 128), F32),
            send,
            send,
        ),
        in_specs=[SMEM] + [VMEM] * 6,
        out_specs=(VMEM,) * 5,
        scratch_shapes=[pltpu.VMEM((4, rows, 2 * HALO, 128), F32)],
        compiler_params=params(16),
        cost_estimate=cost(rows * cols, 32, up.size * 4),
    )(even, *strips, tiled, own_modes, rotation, up)


def near_step(own_modes, side, pmodes, parents, llist, plist):
    rows, cols, _ = llist.shape
    high = height(rows * cols // 4)
    return pl.pallas_call(
        near_kernel,
        out_shape=(
            jax.ShapeDtypeStruct(parents.shape, F32),
            jax.ShapeDtypeStruct((36, 2, high, 256), BF16),
            jax.ShapeDtypeStruct((len(plan()), high, 128), BF16),
            jax.ShapeDtypeStruct((4, 4, cols + 16, 128), F32),
        ),
        in_specs=[VMEM] * 6,
        out_specs=(VMEM,) * 4,
        scratch_shapes=[
            pltpu.VMEM((4, rows + 4, cols + 16, 128), F32),
            pltpu.VMEM((2, rows, cols, 128), F32),
        ],
        compiler_params=params(16),
        cost_estimate=cost(rows * cols, 48, 16 * 1024 * 1024),
    )(own_modes, side, pmodes, parents, llist, plist)


def close_step(even, ends, edge, pmodes, masks, lut, pin, back, table, down, inv, shape):
    rows, cols, dens = shape
    pr, pc = rows // 2, cols // 2
    high = height(pr * pc)
    return pl.pallas_call(
        close_kernel,
        out_shape=jax.ShapeDtypeStruct(shape, F32),
        in_specs=[SMEM] + [VMEM] * 11,
        out_specs=VMEM,
        scratch_shapes=[
            pltpu.VMEM((4, 8, cols + 16, 128), F32),
            pltpu.VMEM((4, pr + 4, pc + 8, 128), F32),
            pltpu.VMEM((2, 12, 2, 32, 256), BF16),
            pltpu.VMEM((2, 4, high, 256), F32),
            pltpu.VMEM((4, rows, cols, 128), F32),
            pltpu.VMEM((4, pr, pc, 128), F32),
        ],
        compiler_params=params(24),
        cost_estimate=cost(rows * cols, 150, table.size * 2),
    )(
        even, *ends, edge, pmodes, masks, lut, pin, back, table, down, inv,
    )


def swapped(strips, axis, odd_first):
    peers = lax.axis_size(axis)
    got = [None, None]
    for kind in (1, 0) if odd_first else (0, 1):
        pairs = [(i, i + 1) for i in range(kind, peers - 1, 2)]
        got[kind] = lax.ppermute(strips[kind], axis, pairs + [(j, i) for i, j in pairs])
    return got


def local(leaf_up, parent_in, leaf_lists, parent_lists, up_transfer, down_transfer, check_inverse):
    cols = leaf_up.shape[1]
    even = [lax.axis_index(axis) % 2 == 0 for axis in ("gx", "gy")]
    flag = jnp.stack(even).astype(jnp.int32)
    rotation, back, table = (jnp.asarray(x) for x in operators())
    low, high = leaf_up[:, :HALO], leaf_up[:, cols - HALO :]
    strips = (jnp.where(even[1], high, low), jnp.where(even[1], low, high))
    strips = swapped(strips, "gy", True)
    own_modes, tiled, rotation = own_step(leaf_up, rotation)
    parents, side, pmodes, *sends = pass_step(flag, strips, tiled, own_modes, rotation, up_transfer)
    ends = swapped(sends, "gx", False)
    parent_up, lut, masks, edge = near_step(
        own_modes, side, pmodes, parents, leaf_lists, parent_lists
    )
    leaf_down = close_step(
        flag, ends, edge, pmodes, masks, lut, parent_in, back, table,
        down_transfer, check_inverse, leaf_up.shape,
    )
    return leaf_down, parent_up


def solution(mesh):
    block = P("gx", "gy", None)
    return jax.shard_map(
        local,
        mesh=mesh,
        in_specs=(block,) * 4 + (P(),) * 3,
        out_specs=(block, block),
        check_vma=False,
    )
```

```python
import functools
import math

import jax
import jax.numpy as jnp
import ml_dtypes
import numpy as np
from jax import lax
from jax.experimental import pallas as pl
from jax.experimental.pallas import tpu as pltpu
from jax.sharding import PartitionSpec as P

ORDER = 6
HALO = 4
KEPT = 14
BF16, F32 = jnp.bfloat16, jnp.float32

PARTS = (
    [(a, -2) for a in range(-1, 2)],
    [(a, 2) for a in range(-1, 2)],
    [(-2, b) for b in range(-2, 3)],
    [(2, b) for b in range(-2, 3)],
    [(3, b) for b in range(-2, 3)],
    [(-3, b) for b in range(-2, 3)],
    [(a, 3) for a in range(-3, 4)],
    [(a, -3) for a in range(-3, 4)],
)


def offset_table():
    return [(a, b) for a in range(-3, 4) for b in range(-3, 4) if max(abs(a), abs(b)) >= 2]


BASES = sorted({(abs(a), abs(b)) for a, b in offset_table()})


def surface_points():
    grid = np.linspace(-1.0, 1.0, ORDER)
    keys = [
        (i, j, k)
        for i in range(ORDER)
        for j in range(ORDER)
        for k in range(ORDER)
        if min(i, j, k) == 0 or max(i, j, k) == ORDER - 1
    ]
    return keys, np.array([[grid[i] for i in key] for key in keys])


def translation(points, dx, dy):
    r = 0.525 * (points[:, None, :] - points[None, :, :]) - np.array([dx, dy, 0.0])
    dist = np.sqrt((r * r).sum(-1))
    n = len(points)
    out = np.zeros((3, n, 3, n))
    for a in range(3):
        for b in range(3):
            out[a, :, b, :] = (float(a == b) / dist + r[..., a] * r[..., b] / dist**3) / (8 * math.pi)
    return out.reshape(3 * n, 3 * n)


def split(x):
    high = x.astype(ml_dtypes.bfloat16)
    return high, (x - high.astype(np.float64)).astype(ml_dtypes.bfloat16)


@functools.lru_cache(maxsize=None)
def operators():
    keys, points = surface_points()
    n = len(keys)
    points_of = {key: i for i, key in enumerate(keys)}
    mirror = [points_of[(i, j, ORDER - 1 - k)] for i, j, k in keys]
    mats = {o: translation(points, *o) for o in offset_table()}
    half = 3 * n // 2
    rotation = np.zeros((3 * n, 512), ml_dtypes.bfloat16)
    back = np.zeros((512, 3 * n))
    table = np.zeros((2, len(BASES), 256, 256), ml_dtypes.bfloat16)
    signs = np.ones((4, 2, 256, 256), ml_dtypes.bfloat16)
    for s, sign in enumerate((1, -1)):
        pairs = np.zeros((3 * n, half))
        firsts = []
        for a in range(3):
            flip = sign if a < 2 else -sign
            for i in range(n):
                if i < mirror[i]:
                    pairs[a * n + i, len(firsts)] = 1.0
                    pairs[a * n + mirror[i], len(firsts)] = flip
                    firsts.append(a * n + i)
        blocks = {o: 0.25 * pairs.T @ m @ pairs for o, m in mats.items()}
        gram = sum(b.T @ b for b in blocks.values())
        place = {f: i for i, f in enumerate(firsts)}
        modes, parity, weight = [], [], []
        for sx in (1, -1):
            for sy in (1, -1):
                basis = []
                for i, f in enumerate(firsts):
                    a, (kx, ky, kz) = f // n, keys[f % n]
                    if kx < ORDER // 2 and ky < ORDER // 2:
                        v = np.zeros(half)
                        for fx in range(2):
                            for fy in range(2):
                                key = (ORDER - 1 - kx if fx else kx, ORDER - 1 - ky if fy else ky, kz)
                                sign_x = (sx if a != 0 else -sx) if fx else 1
                                sign_y = (sy if a != 1 else -sy) if fy else 1
                                v[place[a * n + points_of[key]]] = 0.5 * sign_x * sign_y
                        basis.append(v)
                basis = np.array(basis).T
                w, vecs = np.linalg.eigh(basis.T @ gram @ basis)
                vecs = basis @ vecs
                vecs = vecs * np.sign(vecs[np.abs(np.round(vecs, 9)).argmax(0), np.arange(len(w))])
                modes.append(vecs)
                weight.append(w)
                parity += [(sx, sy)] * len(w)
        order = np.argsort(-np.concatenate(weight), kind="stable")
        vecs = np.concatenate(modes, axis=1)[:, order]
        parity = np.array(parity)[order]
        modes = (pairs @ vecs / math.sqrt(2.0)).astype(ml_dtypes.bfloat16)
        lows = np.concatenate([modes, modes[:, :KEPT], modes[:, :KEPT]], axis=1)
        rotation[:, 256 * s : 256 * (s + 1)] = lows
        outs, out_parity = [], []
        for sx in (1, -1):
            for sy in (1, -1):
                for f in firsts:
                    a, (kx, ky, kz) = f // n, keys[f % n]
                    if kx < ORDER // 2 and ky < ORDER // 2:
                        v = np.zeros(half)
                        for fx in range(2):
                            for fy in range(2):
                                key = (ORDER - 1 - kx if fx else kx, ORDER - 1 - ky if fy else ky, kz)
                                sign_x = (sx if a != 0 else -sx) if fx else 1
                                sign_y = (sy if a != 1 else -sy) if fy else 1
                                v[place[a * n + points_of[key]]] = sign_x * sign_y
                        outs.append(v)
                        out_parity.append((sx, sy))
        outs = np.array(outs).T
        out_parity = np.array(out_parity)
        back[256 * s : 256 * s + half] = (pairs @ outs).T
        undo = np.linalg.inv(modes[firsts].astype(np.float64))
        for q, o in enumerate(BASES):
            high, low = split(undo @ blocks[o].T @ outs * 0.25)
            table[s, q, :half, :half] = high
            table[s, q, half : half + KEPT, :half] = high[:KEPT]
            table[s, q, half + KEPT : half + 2 * KEPT, :half] = low[:KEPT]
        ins = np.concatenate([parity, parity[:KEPT], parity[:KEPT]], axis=0)
        for f in range(4):
            row = np.ones(256)
            row[: len(ins)] = (ins[:, 0] if f // 2 else 1) * (ins[:, 1] if f % 2 else 1)
            col = np.ones(256)
            col[:half] = (out_parity[:, 0] if f // 2 else 1) * (out_parity[:, 1] if f % 2 else 1)
            signs[f, s] = row[:, None] * col[None, :]
    whole = [
        table[:, BASES.index((abs(a), abs(b)))] * signs[2 * (a < 0) + (b < 0)]
        for part in PARTS
        for a, b in part
    ]
    return rotation, back.astype(ml_dtypes.bfloat16), np.concatenate(whole, axis=1)


@functools.lru_cache(maxsize=None)
def plan():
    offsets = offset_table()
    sequence = [o for part in PARTS for o in part]
    products = []
    for c, d in class_pairs():
        for place, (dx, dy) in enumerate(sequence):
            px, cs = divmod(c + dx, 2)
            py, ds = divmod(d + dy, 2)
            if abs(px) <= 1 and abs(py) <= 1:
                entry = (cs * 3 + px + 1) * 6 + ds * 3 + py + 1
                products.append((offsets.index((dx, dy)), entry, place))
    return products


def class_pairs():
    return [(c, d) for c in range(2) for d in range(2)]


def dot(a, b):
    return lax.dot_general(a, b, (((1,), (0,)), ((), ())), preferred_element_type=F32)


def dot_t(a, b):
    return lax.dot_general(a, b, (((1,), (1,)), ((), ())), preferred_element_type=F32)


def parts(x):
    high = x.astype(BF16)
    return high, (x - high.astype(F32)).astype(BF16)


def times_t(x, weight):
    xh, xl = parts(x)
    wh, wl = weight
    both = dot_t(jnp.concatenate([xh, xl], axis=0), wh)
    return both[: x.shape[0]] + (both[x.shape[0] :] + dot_t(xh, wl))


def times_exact(x, weight):
    both = dot(jnp.concatenate(parts(x), axis=0), weight)
    return both[: x.shape[0]] + both[x.shape[0] :]


def lanes(ref, *at):
    pieces = [ref[(t,) + at] for t in range(4)]
    pieces = [p.reshape(-1, 128) for p in pieces]
    return jnp.concatenate(pieces, axis=1)


def cut_tiles(dens):
    return [(t, slice(128 * t, min(128 * t + 128, dens)), slice(0, min(128, dens - 128 * t))) for t in range(4)]


def modes_of(x, rot_ref, dens):
    y = times_exact(x[:, :dens], rot_ref[...])
    lane = lax.broadcasted_iota(jnp.int32, (1, 512), 1) % 256
    half = dens // 2
    is_low = (lane >= half) & (lane < half + KEPT)
    return jnp.where(is_low, y - y.astype(BF16).astype(F32), y)


def children(ref, dens, counts, c, d):
    return jnp.concatenate(
        [
            jnp.concatenate(
                [ref[t, 2 * i + c, pl.ds(d, counts[1], stride=2), :] for i in range(counts[0])],
                axis=0,
            )
            for t in range(4)
        ],
        axis=1,
    )[:, :dens]


def own_kernel(own_ref, rot_ref, modes_ref, tiled_ref, rot_out):
    rows, cols, dens = own_ref.shape
    rot_out[...] = rot_ref[...]
    y = modes_of(own_ref[...].reshape(rows * cols, dens), rot_ref, dens)
    for t, cut, to in cut_tiles(dens):
        modes_ref[t] = y[:, 128 * t : 128 * t + 128].reshape(rows, cols, 128)
        tiled_ref[t, :, :, to] = own_ref[:, :, cut]


def pass_kernel(
    even_ref, strip0_ref, strip1_ref, own_t, own_modes_ref, rot_ref, up_ref,
    parents_ref, side_ref, pmodes, send0_ref, send1_ref,
    strip_t,
):
    rows, _, dens = strip0_ref.shape
    cols = own_modes_ref.shape[2]
    pr, pc = rows // 2, cols // 2
    boxes = pr * pc
    even_x, even_y = even_ref[0] == 1, even_ref[1] == 1
    for t, cut, to in cut_tiles(dens):
        first, second = strip0_ref[:, :, cut], strip1_ref[:, :, cut]
        strip_t[t, :, 0:HALO, to] = jnp.where(even_y, second, first)
        strip_t[t, :, HALO:, to] = jnp.where(even_y, first, second)

    parent = None
    for n, (c, d) in enumerate(class_pairs()):
        x = jnp.concatenate(
            [children(own_t, dens, (pr, pc), c, d), children(strip_t, dens, (pr, HALO), c, d)],
            axis=0,
        )
        part = times_t(x, parts(up_ref[n]))
        parent = part if parent is None else parent + part
    parents_ref[...] = parent[:boxes].reshape(pr, pc, dens)
    z = modes_of(jnp.concatenate([lanes(strip_t)[:, :dens], parent], axis=0), rot_ref, dens)
    w, p = z[: rows * 8], z[rows * 8 :]
    for t in range(4):
        cut = slice(128 * t, 128 * t + 128)
        side = w[:, cut].reshape(rows, 8, 128)
        side_ref[t] = side
        pmodes[t, 2 : 2 + pr, 4 : 4 + pc, :] = p[:boxes, cut].reshape(pr, pc, 128)
        strip = p[boxes:, cut].reshape(pr, 4, 128)
        pmodes[t, 2 : 2 + pr, 2:4, :] = strip[:, 0:2]
        pmodes[t, 2 : 2 + pr, 4 + pc : 6 + pc, :] = strip[:, 2:4]
        own = p[:boxes, cut].reshape(pr, pc, 128)
        ends = []
        for x, to in ((slice(0, 2), slice(0, 2)), (slice(rows - 2, rows), slice(pr - 2, pr))):
            ends.append(
                jnp.concatenate(
                    [own_modes_ref[t, x], jnp.concatenate([side[x, 2:6], strip[to]], axis=1), own[to]],
                    axis=1,
                )
            )
        low, high = ends
        send0_ref[t] = jnp.where(even_x, high, low)
        send1_ref[t] = jnp.where(even_x, low, high)


def near_kernel(
    own_modes_ref, side_ref, pmodes_ref, parents_ref, llist_ref, plist_ref,
    pup_ref, lut, masks_ref, edge_ref,
    modes, flat,
):
    rows, cols = own_modes_ref.shape[1:3]
    pup_ref[...] = parents_ref[...]
    pr, pc = rows // 2, cols // 2
    gr, gc = pr // 2, pc // 2
    used = pr * pc + gr * gc
    high = lut.shape[2]
    count = masks_ref.shape[0] // 4

    for t in range(4):
        modes[t, 2 : 2 + rows, 8 : 8 + cols, :] = own_modes_ref[t]
        modes[t, 2 : 2 + rows, 4:8, :] = side_ref[t, :, 0:4]
        modes[t, 2 : 2 + rows, 8 + cols : 12 + cols, :] = side_ref[t, :, 4:8]
        edge_ref[t, 0:2] = modes[t, 2:4]
        edge_ref[t, 2:4] = modes[t, rows : rows + 2]

    def gather(i, carry):
        base = 2 * (i % 3) + i // 3
        for ds in range(2):
            for py in (-1, 0, 1):
                e = i * 6 + ds * 3 + py + 1
                for t in range(4):
                    x = jnp.concatenate(
                        [
                            modes[t, base + 2 * j, pl.ds(8 + 2 * py + ds, pc, stride=2), :]
                            for j in range(pr)
                        ]
                        + [
                            pmodes_ref[t, base + 2 * j, pl.ds(4 + 2 * py + ds, gc, stride=2), :]
                            for j in range(gr)
                        ]
                        + [jnp.zeros((high - used, 128), F32)],
                        axis=0,
                    )
                    lut[e, t // 2, :, 128 * (t % 2) : 128 * (t % 2) + 128] = x.astype(BF16)
        return carry

    lax.fori_loop(0, 6, gather, 0)

    flat[0, :, :, 0 : llist_ref.shape[2]] = llist_ref[...].astype(F32)
    flat[1, 0:pr, 0:pc, 0 : plist_ref.shape[2]] = plist_ref[...].astype(F32)
    for n, (c, d) in enumerate(class_pairs()):
        flag = jnp.concatenate(
            [flat[0, 2 * i + c, pl.ds(d, pc, stride=2), :] for i in range(pr)]
            + [flat[1, 2 * i + c, pl.ds(d, gc, stride=2), :] for i in range(gr)]
            + [jnp.zeros((high - used, 128), F32)],
            axis=0,
        )
        for k in range(count):
            o = plan()[count * n + k][0]
            masks_ref[count * n + k] = jnp.broadcast_to(flag[:, o : o + 1], (high, 128)).astype(BF16)


def close_kernel(
    even_ref,
    got0_ref, got1_ref, edge_ref, pside_ref, masks, lut,
    pin_ref, back, table, down_ref, inv_ref,
    out_ref,
    edge, pmodes, fresh, flat, plocal,
):
    rows, cols, dens = out_ref.shape
    pr, pc = rows // 2, cols // 2
    gr, gc = pr // 2, pc // 2
    boxes, pboxes = pr * pc, gr * gc
    high = lut.shape[2]
    count = masks.shape[0] // 4
    even = even_ref[0] == 1
    for t in range(4):
        before = jnp.where(even, got1_ref[t], got0_ref[t])
        after = jnp.where(even, got0_ref[t], got1_ref[t])
        edge[t, 2:6] = edge_ref[t]
        pmodes[t, 2 : 2 + pr] = pside_ref[t, 2 : 2 + pr]
        for x, leaf, parent in ((before, slice(0, 2), slice(0, 2)), (after, slice(6, 8), slice(2 + pr, 4 + pr))):
            edge[t, leaf, 8 : 8 + cols, :] = x[:, 0:cols]
            edge[t, leaf, 6:8, :] = x[:, cols : cols + 2]
            edge[t, leaf, 8 + cols : 10 + cols, :] = x[:, cols + 2 : cols + 4]
            pmodes[t, parent, 2:4, :] = x[:, cols + 4 : cols + 6]
            pmodes[t, parent, 4 + pc : 6 + pc, :] = x[:, cols + 6 : cols + 8]
            pmodes[t, parent, 4 : 4 + pc, :] = x[:, cols + 8 :]

    def patch(cs, carry):
        for ds in range(2):
            for py in (-1, 0, 1):
                for t in range(4):
                    at = slice(128 * (t % 2), 128 * (t % 2) + 128)
                    mine = pl.ds(8 + 2 * py + ds, pc, stride=2)
                    theirs = pl.ds(4 + 2 * py + ds, gc, stride=2)
                    e = cs * 6 + ds * 3 + py + 1
                    x = jnp.concatenate([edge[t, cs + 2 * j, mine, :] for j in range(2)], axis=0)
                    fresh[0, e, t // 2, 0:16, at] = x.astype(BF16)
                    x = jnp.concatenate([pmodes[t, cs + 2 * j, theirs, :] for j in range(4)], axis=0)
                    fresh[0, e, t // 2, 16:32, at] = x.astype(BF16)
                    x = jnp.concatenate([edge[t, 4 + cs + 2 * j, mine, :] for j in range(2)], axis=0)
                    fresh[1, e, t // 2, 0:16, at] = x.astype(BF16)
                    x = jnp.concatenate(
                        [pmodes[t, 4 + cs + 2 * j, theirs, :] for j in range(4, gr)]
                        + [jnp.zeros((high - boxes - pboxes, 128), F32)],
                        axis=0,
                    )
                    fresh[1, e, t // 2, 16:32, at] = x.astype(BF16)
        return carry

    for cs in range(2):
        patch(cs, 0)

    runs = [(0, 3), (3, 6), (6, 11), (11, 16), (16, 21)]

    def listed(i, s):
        e = plan()[i][1]
        px = e // 6 % 3 - 1
        m = masks[i]
        if px == 0:
            x = lut[e, s]
        else:
            new = fresh[(px + 1) // 2, e // 18 * 6 + e % 6, s]
            if px < 0:
                pieces = [new[0:16], lut[e, s, 16:boxes], new[16:32], lut[e, s, boxes + 16 : high]]
            else:
                pieces = [lut[e, s, 0 : boxes - 16], new[0:16], lut[e, s, boxes : boxes + 16], new[16:32]]
            x = jnp.concatenate(pieces, axis=0)
        return jnp.concatenate([x[:, :128] * m, x[:, 128:] * m], axis=1)

    checks, pchecks = [], []
    for c in range(2):

        def interact(s):
            n = 2 * c
            total = jnp.zeros((2 * high, 256), F32)

            def run(first, last, s):
                at = 256 * plan()[first][2]
                x = jnp.concatenate([listed(i, s) for i in range(first, last)], axis=1)
                return x, table[s, at : at + 256 * (last - first), :]

            for a, b in runs:
                x, weight = run(n * count + a, n * count + b, s)
                y, _ = run((n + 1) * count + a, (n + 1) * count + b, s)
                total = total + dot(jnp.concatenate([x, y], axis=0), weight)
            ends = []
            for d in range(2):
                x, weight = run((n + d) * count + runs[-1][1], (n + d + 1) * count, s)
                ends.append(dot(x, weight))
            return total + jnp.concatenate(ends, axis=0)

        mapped = [times_exact(interact(s), back[256 * s : 256 * (s + 1)]) for s in range(2)]
        mapped = mapped[0] + mapped[1]
        for d in range(2):
            checks.append(mapped[high * d : high * d + boxes])
            pchecks.append(mapped[high * d + boxes : high * (d + 1)])

    inverse = parts(inv_ref[...])
    for n, (c, d) in enumerate(class_pairs()):
        for t, cut, to in cut_tiles(dens):
            for j in range(gr):
                plocal[t, 2 * j + c, pl.ds(d, gc, stride=2), to] = pchecks[n][
                    gc * j : gc * (j + 1), cut
                ]
    local = pin_ref[...].reshape(boxes, dens) + times_t(lanes(plocal)[:, :dens], inverse)
    x = jnp.concatenate(
        [
            checks[n] + times_t(local, parts(down_ref[n]))
            for n in range(4)
        ],
        axis=0,
    )
    result = times_t(x, inverse)
    for n, (c, d) in enumerate(class_pairs()):
        for t, cut, to in cut_tiles(dens):
            for j in range(pr):
                r = boxes * n + pc * j
                flat[t, 2 * j + c, pl.ds(d, pc, stride=2), to] = result[r : r + pc, cut]
    for t, cut, to in cut_tiles(dens):
        out_ref[:, :, cut] = flat[t, :, :, to]


VMEM = pl.BlockSpec(memory_space=pltpu.VMEM)
SMEM = pl.BlockSpec(memory_space=pltpu.SMEM)


def params(mib):
    return pltpu.CompilerParams(vmem_limit_bytes=mib * 1024 * 1024)


def cost(rows, tiles, reads):
    return pl.CostEstimate(flops=2 * rows * tiles * 256 * 256, bytes_accessed=reads, transcendentals=0)


def height(boxes):
    return -(-(boxes * 5 // 4) // 16) * 16


def own_step(own, rotation):
    rows, cols, _ = own.shape
    tiled = jax.ShapeDtypeStruct((4, rows, cols, 128), F32)
    return pl.pallas_call(
        own_kernel,
        out_shape=(tiled, tiled, jax.ShapeDtypeStruct(rotation.shape, BF16)),
        in_specs=[VMEM] * 2,
        out_specs=(VMEM,) * 3,
        compiler_params=params(16),
        cost_estimate=cost(rows * cols, 48, 64 * 1024 * 1024),
    )(own, rotation)


def pass_step(even, strips, tiled, own_modes, rotation, up):
    rows, cols = tiled.shape[1:3]
    dens = up.shape[1]
    pr, pc = rows // 2, cols // 2
    send = jax.ShapeDtypeStruct((4, 2, cols + pc + 8, 128), F32)
    return pl.pallas_call(
        pass_kernel,
        out_shape=(
            jax.ShapeDtypeStruct((pr, pc, dens), F32),
            jax.ShapeDtypeStruct((4, rows, 2 * HALO, 128), F32),
            jax.ShapeDtypeStruct((4, pr + 4, pc + 8, 128), F32),
            send,
            send,
        ),
        in_specs=[SMEM] + [VMEM] * 6,
        out_specs=(VMEM,) * 5,
        scratch_shapes=[pltpu.VMEM((4, rows, 2 * HALO, 128), F32)],
        compiler_params=params(16),
        cost_estimate=cost(rows * cols, 32, up.size * 4),
    )(even, *strips, tiled, own_modes, rotation, up)


def near_step(own_modes, side, pmodes, parents, llist, plist):
    rows, cols, _ = llist.shape
    high = height(rows * cols // 4)
    return pl.pallas_call(
        near_kernel,
        out_shape=(
            jax.ShapeDtypeStruct(parents.shape, F32),
            jax.ShapeDtypeStruct((36, 2, high, 256), BF16),
            jax.ShapeDtypeStruct((len(plan()), high, 128), BF16),
            jax.ShapeDtypeStruct((4, 4, cols + 16, 128), F32),
        ),
        in_specs=[VMEM] * 6,
        out_specs=(VMEM,) * 4,
        scratch_shapes=[
            pltpu.VMEM((4, rows + 4, cols + 16, 128), F32),
            pltpu.VMEM((2, rows, cols, 128), F32),
        ],
        compiler_params=params(16),
        cost_estimate=cost(rows * cols, 48, 16 * 1024 * 1024),
    )(own_modes, side, pmodes, parents, llist, plist)


def close_step(even, ends, edge, pmodes, masks, lut, pin, back, table, down, inv, shape):
    rows, cols, dens = shape
    pr, pc = rows // 2, cols // 2
    high = height(pr * pc)
    return pl.pallas_call(
        close_kernel,
        out_shape=jax.ShapeDtypeStruct(shape, F32),
        in_specs=[SMEM] + [VMEM] * 11,
        out_specs=VMEM,
        scratch_shapes=[
            pltpu.VMEM((4, 8, cols + 16, 128), F32),
            pltpu.VMEM((4, pr + 4, pc + 8, 128), F32),
            pltpu.VMEM((2, 12, 2, 32, 256), BF16),
            pltpu.VMEM((4, rows, cols, 128), F32),
            pltpu.VMEM((4, pr, pc, 128), F32),
        ],
        compiler_params=params(24),
        cost_estimate=cost(rows * cols, 150, table.size * 2),
    )(
        even, *ends, edge, pmodes, masks, lut, pin, back, table, down, inv,
    )


def swapped(strips, axis, odd_first):
    peers = lax.axis_size(axis)
    got = [None, None]
    for kind in (1, 0) if odd_first else (0, 1):
        pairs = [(i, i + 1) for i in range(kind, peers - 1, 2)]
        got[kind] = lax.ppermute(strips[kind], axis, pairs + [(j, i) for i, j in pairs])
    return got


def local(leaf_up, parent_in, leaf_lists, parent_lists, up_transfer, down_transfer, check_inverse):
    cols = leaf_up.shape[1]
    even = [lax.axis_index(axis) % 2 == 0 for axis in ("gx", "gy")]
    flag = jnp.stack(even).astype(jnp.int32)
    rotation, back, table = (jnp.asarray(x) for x in operators())
    low, high = leaf_up[:, :HALO], leaf_up[:, cols - HALO :]
    strips = (jnp.where(even[1], high, low), jnp.where(even[1], low, high))
    strips = swapped(strips, "gy", True)
    own_modes, tiled, rotation = own_step(leaf_up, rotation)
    parents, side, pmodes, *sends = pass_step(flag, strips, tiled, own_modes, rotation, up_transfer)
    ends = swapped(sends, "gx", False)
    parent_up, lut, masks, edge = near_step(
        own_modes, side, pmodes, parents, leaf_lists, parent_lists
    )
    leaf_down = close_step(
        flag, ends, edge, pmodes, masks, lut, parent_in, back, table,
        down_transfer, check_inverse, leaf_up.shape,
    )
    return leaf_down, parent_up


def solution(mesh):
    block = P("gx", "gy", None)
    return jax.shard_map(
        local,
        mesh=mesh,
        in_specs=(block,) * 4 + (P(),) * 3,
        out_specs=(block, block),
        check_vma=False,
    )
```
